32 devices in a mesh: groups: 2 (over x), pool: 8 (over z, y), tp: 2 (over core).
Axes of the slice: x: 2, y: 2, z: 4, core: 2. Of those that a mesh axis runs over, the one named last changes fastest.
Arguments:
- tokens: bfloat16 [2048, 5120], P(('groups', 'pool'), 'tp'), parts along dimension 0, may hold values from -6 to 6
- row_adapters: int32 [2048, 1], P(('groups', 'pool')), parts along dimension 0, may hold values from 0 to 7; in each aligned block of 128 rows (0 to 127, 128 to 255, ...) at most 32 rows name the same one
- positions: int32 [2048], P(('groups', 'pool')), parts along dimension 0, may hold values from 0 to 4095
- key_value_weight: bfloat16 [5120, 2048], P('tp'), may hold values from -0.078125 to 0.078125
- adapter_down: bfloat16 [8, 5120, 128], P('pool', 'tp'), may hold values from -0.078125 to 0.078125
- adapter_up: bfloat16 [8, 128, 2048], P('pool'), may hold values from -0.5 to 0.5
- ranks: int32 [8], P('pool'), may hold values from 16 to 128, as said below
- key_norm_gain: bfloat16 [128], replicated, may hold values from 0.099609375 to 1.8984375
Outputs:
- kv_entries: bfloat16 [2048, 8, 2, 128], P(('groups', 'pool'), 'tp'), parts along dimension 0
The draws below stay inside these ranges and needn't reach their ends.
There are 2 independent parts, one for each index of `groups`. The reference program is written for one: setup_inputs(seed, part) draws one part's arguments, and reference() takes and returns one part's arrays. A program takes and returns all parts, laid end to end along the dimension named above; an argument that names none is the same for every part. Nothing has to cross between parts.
Inputs may be any that keep to these rules, and one draw needn't show every extreme that they name: `row_adapters`: in the rows of one device (aligned blocks of 128 rows) no adapter is named by more than 32 rows, a bound that some block reaches. `ranks`: each rank is 128 // 8 times 1, 2, 4 or 8; some adapter has rank 128 and some 128 // 8.
All inputs are finite; a program needn't handle non-finite values.
Results may differ from the reference program's by a relative error of at most 0.001.
Values may be sent and summed in bfloat16 or wider, within the bound.
No kernel may reach another device: no remote copies, remote signals or barrier semaphores. Data moves between devices by JAX's collectives and lax.ppermute only.
A program may use at most 64 MiB of HBM per device.

```python
import math
import jax
import jax.numpy as jnp
import numpy as np
from jax import lax

MODEL_WIDTH = 5120
HD = 128
PADDED_RANK = 128
ALPHA = 32
CONTEXT = 4096
ROWS_DEV = 128
KEY_VALUE_COLUMNS = 2048
ADAPTER_TOTAL = 8
ROWS = 1024
MOST = 32


def draw_ranks(key, part):
    key = jax.random.fold_in(key, 7)
    level_key, order_key = jax.random.split(key)
    levels = jax.random.randint(level_key, (ADAPTER_TOTAL,), 0, 4)
    order = jax.random.permutation(order_key, ADAPTER_TOTAL)
    levels = levels.at[order[0]].set(3)
    levels = levels.at[order[1]].set(0)
    powers = jnp.array([1, 2, 4, 8], dtype=jnp.int32)
    return (powers[levels] * (PADDED_RANK // 8)).astype(jnp.int32)


def place_ends(values, stream_key, least, top_value):
    longest = values.shape.index(max(values.shape))
    spots = []
    for shift in (0, 1):
        where = [jax.random.randint(jax.random.fold_in(stream_key, axis), (), 0, length) for axis, length in enumerate(values.shape)]
        where[longest] = (where[longest] + shift) % values.shape[longest]
        spots.append(tuple(where))
    return values.at[spots[0]].set(least).at[spots[1]].set(top_value)


def level_of(key, dims, cuts, low, top_value):
    loudness = 1.0
    for dim, shards_of in cuts:
        heights = jax.random.uniform(jax.random.fold_in(jax.random.fold_in(key, 6), dim), (shards_of,), jnp.float32, low / len(cuts), top_value / len(cuts))
        loudness = loudness * jnp.repeat(jnp.exp(heights), dims[dim] // shards_of).reshape((-1,) + (1,) * (len(dims) - 1 - dim))
    return loudness


def deal_out(stream_key, own, number, rows, count, top, bound, slope):
    sequence = jax.random.permutation(stream_key, count)
    packed, common = load_shares(count, rows * top, bound, slope, True), load_shares(count, rows * top, bound, slope, False)
    places = jnp.arange(count)

    def named(sizes, offset_by):
        used = int((sizes > 0).sum())
        fixed = max(1, used // 4)
        moved = fixed + (places - fixed + offset_by * (used - fixed)) % max(1, count - fixed)
        return jnp.zeros((count,), jnp.int32).at[sequence[jnp.where(places < fixed, places, moved)]].set(jnp.asarray(sizes, jnp.int32))

    sizes = jnp.where(number % 4 == 0, named(packed, number // 4), named(common, number - number // 4 - 1))
    mixed = jax.random.permutation(jax.random.fold_in(own, 3), count)
    giver, taker = mixed[0:count // 2 * 2:2], mixed[1:count // 2 * 2:2]
    slack = jnp.minimum(sizes[giver] - 1, bound - sizes[taker]) // 2
    slack = jnp.where((giver == sequence[0]) | (taker == sequence[0]) | (sizes[taker] == 0), 0, jnp.maximum(slack, 0))
    moved = jax.random.randint(jax.random.fold_in(own, 4), (count // 2,), 0, 1 << 20) % (slack + 1)
    sizes = sizes.at[giver].add(-moved).at[taker].add(moved)
    members = jnp.searchsorted(jnp.cumsum(sizes), jnp.arange(rows * top), side="right").astype(jnp.int32)
    grid = members.reshape(top, rows).T
    grid = grid[jax.random.permutation(jax.random.fold_in(own, 1), rows)]
    offset_by = jax.random.randint(jax.random.fold_in(own, 2), (rows, 1), 0, top)
    return jnp.take_along_axis(grid, (jnp.arange(top)[None, :] + offset_by) % top, axis=1)


def load_shares(number_of, total, reach, lean, full):
    loads = [(1 << 20) // math.isqrt(grade ** lean) + 1 for grade in range(1, number_of + 1)]
    largest = reach if full else min(reach, max(-(-total // number_of), total * loads[0] // sum(loads)))
    least = 1 if total - largest >= number_of - 1 else 0
    counts, surplus = [largest] + [least] * (number_of - 1), total - largest - least * (number_of - 1)
    while surplus > 0:
        candidates = [i for i in range(1, number_of) if counts[i] < largest] or [i for i in range(1, number_of) if counts[i] < reach]
        pool, budget = sum([loads[i] for i in candidates]), surplus
        for i in candidates:
            more = min(reach - counts[i], max(1, budget * loads[i] // pool), surplus)
            counts[i] = counts[i] + more
            surplus = surplus - more
    return np.array(counts)


def centred(rng, dims, spread, reach, pieces=(), kind=jnp.bfloat16):
    entries = jax.random.normal(rng, dims, jnp.float32) * spread
    if len(pieces) > 0:
        entries = level_of(rng, dims, pieces, -0.22, 0.18) * entries
    return jnp.clip(entries, min=-reach, max=reach).astype(kind)


def setup_inputs(seed: int = 0, part: int = 0) -> dict:
    key_list = jax.random.split(jax.random.key(seed), 9)
    own_keys = jax.random.split(jax.random.fold_in(key_list[8], part), 9)
    tokens = centred(own_keys[0], (ROWS, MODEL_WIDTH), 1.0, 6.0, ((0, 8), (1, 2)))
    row_adapters_keys = jax.random.split(jax.random.fold_in(own_keys[1], 1), ROWS // ROWS_DEV)
    row_adapters_turns = jax.random.permutation(jax.random.fold_in(own_keys[1], 3), ROWS // ROWS_DEV)
    row_adapters = jax.vmap(lambda own, number: deal_out(jax.random.fold_in(own_keys[1], 2), own, number, ROWS_DEV, ADAPTER_TOTAL, 1, MOST, 2))(row_adapters_keys, row_adapters_turns).reshape((ROWS, 1))
    positions = place_ends(jax.random.randint(own_keys[2], (ROWS,), 0, CONTEXT), jax.random.fold_in(own_keys[2], 1), 0, CONTEXT - 1).astype(jnp.int32)
    key_value_weight = centred(key_list[3], (MODEL_WIDTH, KEY_VALUE_COLUMNS), MODEL_WIDTH ** -0.5, 0.078125, ((0, 2),))
    adapter_down = centred(key_list[4], (ADAPTER_TOTAL, MODEL_WIDTH, PADDED_RANK), MODEL_WIDTH ** -0.5, 0.078125, ((0, 8), (1, 2)))
    adapter_up = centred(key_list[5], (ADAPTER_TOTAL, PADDED_RANK, KEY_VALUE_COLUMNS), PADDED_RANK ** -0.5, 0.5, ((0, 8),))
    ranks = draw_ranks(jax.random.fold_in(key_list[8], 71), part)
    key_norm_gain = jnp.clip(1.0 + 0.18 * jax.random.normal(key_list[7], (HD,), jnp.float32), 0.099609375, 1.8984375).astype(jnp.bfloat16)
    return {"tokens": tokens, "row_adapters": row_adapters, "positions": positions, "key_value_weight": key_value_weight, "adapter_down": adapter_down, "adapter_up": adapter_up, "ranks": ranks, "key_norm_gain": key_norm_gain}


rope_theta = 1000000.0
norm_eps = 1e-06

def rotate_keys(keys, positions):
    head_size = keys.shape[-1]
    half_dim = head_size // 2
    exponent = jnp.arange(half_dim, dtype=jnp.float32) * (2.0 / head_size)
    frequency = jnp.power(jnp.float32(rope_theta), -exponent)
    angles = positions.astype(jnp.float32)[:, None] * frequency[None, :]
    cosine = jnp.cos(angles)[:, None, :]
    sine = jnp.sin(angles)[:, None, :]
    lower = keys[..., :half_dim]
    upper = keys[..., half_dim:]
    return jnp.concatenate([lower * cosine - upper * sine, upper * cosine + lower * sine], axis=-1)

def finish_rows(projected, positions, key_norm_gain):
    head_size = key_norm_gain.shape[0]
    row_count = projected.shape[0]
    shaped = projected.reshape(row_count, -1, 2, head_size)
    keys = shaped[:, :, 0, :]
    values_part = shaped[:, :, 1, :]
    mean_square = lax.optimization_barrier(jnp.mean(keys * keys, axis=-1, keepdims=True))
    normed = keys * lax.rsqrt(mean_square + norm_eps) * key_norm_gain.astype(jnp.float32)
    rotated = rotate_keys(normed, positions)
    return jnp.stack([rotated, values_part], axis=2).astype(jnp.bfloat16)

def reference(tokens, row_adapters, positions, key_value_weight, adapter_down, adapter_up, ranks, key_norm_gain):
    base_projected = jnp.dot(tokens, key_value_weight, preferred_element_type=jnp.float32)
    row_adapter = row_adapters[:, 0]

    def adapter_outputs(running_total, adapter_choice):
        down_factor = lax.dynamic_index_in_dim(adapter_down, adapter_choice, 0, keepdims=False)
        up_matrix = lax.dynamic_index_in_dim(adapter_up, adapter_choice, 0, keepdims=False)
        adapter_rank = lax.dynamic_index_in_dim(ranks, adapter_choice, 0, keepdims=False)
        rank_reduced = jnp.dot(tokens, down_factor, preferred_element_type=jnp.float32)
        rank_mask = (jnp.arange(PADDED_RANK, dtype=jnp.int32) < adapter_rank).astype(jnp.float32)
        scaling = jnp.float32(ALPHA) / adapter_rank.astype(jnp.float32)
        rank_reduced = rank_reduced * (rank_mask * scaling)[None, :]
        adapter_term = jnp.dot(rank_reduced, up_matrix.astype(jnp.float32), precision=lax.Precision.HIGHEST)
        adapter_row_mask = (row_adapter == adapter_choice).astype(jnp.float32)[:, None]
        return (running_total + adapter_row_mask * adapter_term, None)
    adapter_delta, unused_slot = lax.scan(adapter_outputs, jnp.zeros(base_projected.shape, jnp.float32), jnp.arange(ADAPTER_TOTAL, dtype=jnp.int32))
    return finish_rows(base_projected + adapter_delta, positions, key_norm_gain)
```

```python
import functools

import jax
import jax.numpy as jnp
from jax import lax
from jax.experimental import pallas as pl
from jax.experimental.pallas import tpu as pltpu
from jax.sharding import PartitionSpec as P

ALPHA = 32
ROPE_THETA = 1000000.0
NORM_EPS = 1e-06
VMEM_LIMIT = 48 * 1024 * 1024

VMEM = pl.BlockSpec(memory_space=pltpu.VMEM)


def params(**kw):
    return pltpu.CompilerParams(vmem_limit_bytes=VMEM_LIMIT, **kw)


def cost(flops, bytes_accessed):
    return pl.CostEstimate(flops=flops, bytes_accessed=bytes_accessed, transcendentals=0)


def slot_places(adapter, me_ref, local, depth):
    rows = adapter.shape[0]
    r0 = lax.broadcasted_iota(jnp.int32, (rows, rows), 0)
    r1 = lax.broadcasted_iota(jnp.int32, (rows, rows), 1)
    column = jnp.broadcast_to(adapter, (rows, rows))
    row = jnp.sum(jnp.where(r0 == r1, column, 0), axis=0, keepdims=True)
    slot = jnp.sum(jnp.where((column == row) & (r0 < r1), 1, 0), axis=0, keepdims=True)
    holder = row // local
    return ((holder ^ me_ref[0]) * local + (row - holder * local)) * depth + slot


def pick_kernel(local, depth, me_ref, adapter_ref, tokens_ref, *outs):
    rows = tokens_ref.shape[0]
    place = slot_places(adapter_ref[...], me_ref, local, depth)
    size = local * depth
    slots = len(outs) * size
    picker = jnp.where(
        lax.broadcasted_iota(jnp.int32, (slots, rows), 0) == place, 1.0, 0.0
    ).astype(jnp.bfloat16)
    width = tokens_ref.shape[1]
    step = 512
    for at in range(0, width, step):
        block = jnp.dot(
            picker, tokens_ref[:, at : at + step], preferred_element_type=jnp.float32
        )
        for j, out in enumerate(outs):
            out[:, at : at + step] = block[j * size : (j + 1) * size].astype(jnp.bfloat16)


def down_kernel(local, depth, factor_ref, down_ref, *refs):
    count = len(refs) // 2
    ins, outs = refs[:count], refs[count:]
    for a in range(local):
        rows = jnp.concatenate([x[a * depth : (a + 1) * depth, :] for x in ins], axis=0)
        low = jnp.dot(rows, down_ref[a], preferred_element_type=jnp.float32)
        low = low * factor_ref[a : a + 1, :]
        for j, out in enumerate(outs):
            out[a * depth : (a + 1) * depth, :] = low[j * depth : (j + 1) * depth]


def halves(x):
    high = x.astype(jnp.bfloat16)
    low = (x - high.astype(jnp.float32)).astype(jnp.bfloat16)
    return high, low


def return_kernel(local, depth, me_ref, adapter_ref, *refs):
    ins, out = refs[:-1], refs[-1]
    place = slot_places(adapter_ref[...], me_ref, local, depth)
    slots = len(ins) * local * depth
    picker = jnp.where(
        lax.broadcasted_iota(jnp.int32, (slots, place.shape[1]), 0) == place, 1.0, 0.0
    ).astype(jnp.bfloat16)
    slot = jnp.concatenate([x[...] for x in ins], axis=0)
    high, low = halves(slot)
    rest = (slot - high.astype(jnp.float32) - low.astype(jnp.float32)).astype(jnp.bfloat16)
    total = None
    for part in (rest, low, high):
        term = lax.dot_general(
            picker, part, (((0,), (0,)), ((), ())), preferred_element_type=jnp.float32
        )
        total = term if total is None else total + term
    out[...] = total


def base_kernel(half_ref, tokens_ref, weight_ref, out_ref):
    @pl.when(pl.program_id(0) == 0)
    def _():
        out_ref[...] = jnp.zeros_like(out_ref)

    out_ref[...] += jnp.dot(
        tokens_ref[...], weight_ref[...], preferred_element_type=jnp.float32
    )


def base_half(tokens, weight, half, columns):
    rows, width = tokens.shape
    step = 512
    return pl.pallas_call(
        base_kernel,
        grid_spec=pltpu.PrefetchScalarGridSpec(
            num_scalar_prefetch=1,
            grid=(width // step,),
            in_specs=[
                pl.BlockSpec((rows, step), lambda k, h: (0, k)),
                pl.BlockSpec((step, columns), lambda k, h: (k, h[0])),
            ],
            out_specs=pl.BlockSpec((rows, columns), lambda k, h: (0, 0)),
        ),
        out_shape=jax.ShapeDtypeStruct((rows, columns), jnp.float32),
        compiler_params=params(),
        cost_estimate=cost(2 * rows * width * columns, 2 * width * (rows + columns)),
        name="base_half",
    )(half, tokens, weight)


def finish_kernel(
    adapter_ref, mine_ref, other_ref, low_ref, low_other_ref, up_ref, cos_ref, sin_ref, gain_ref, out_ref
):
    rows, columns = mine_ref.shape
    count, rank, _ = up_ref.shape
    head = cos_ref.shape[1]
    high, low = halves(low_ref[...] + low_other_ref[...])
    both = jnp.concatenate([high, low], axis=0)
    adapter = jnp.concatenate([adapter_ref[...], adapter_ref[...]], axis=0)
    blocks = [
        jnp.where(adapter == a, both, jnp.zeros_like(both)) for a in range(count)
    ]
    spread = jnp.concatenate(blocks, axis=1)
    cosine, sine, gain = cos_ref[...], sin_ref[...], gain_ref[...]
    for at in range(0, columns, 2 * head):
        up = up_ref[:, :, at : at + 2 * head].reshape(count * rank, 2 * head)
        delta = jnp.dot(spread, up, preferred_element_type=jnp.float32)
        delta = delta[:rows] + delta[rows:]
        projected = mine_ref[:, at : at + 2 * head] + other_ref[:, at : at + 2 * head] + delta
        key, value = projected[:, :head], projected[:, head:]
        mean = jnp.mean(key * key, axis=1, keepdims=True)
        normed = key * lax.rsqrt(mean + NORM_EPS) * gain
        rotated = normed * cosine + pltpu.roll(normed, head // 2, 1) * sine
        out_ref[:, at : at + head] = rotated.astype(jnp.bfloat16)
        out_ref[:, at + head : at + 2 * head] = value.astype(jnp.bfloat16)


def body(
    tokens,
    row_adapters,
    positions,
    key_value_weight,
    adapter_down,
    adapter_up,
    ranks,
    key_norm_gain,
):
    pool_size = lax.axis_size("pool")
    tp_size = lax.axis_size("tp")
    rows, width = tokens.shape
    local = adapter_down.shape[0]
    adapters = local * pool_size
    columns = key_value_weight.shape[1] // tp_size
    rank = adapter_down.shape[2]
    head = key_norm_gain.shape[0]
    depth = max(2, 2 * rows // adapters)
    size = local * depth
    f32, bf16 = jnp.float32, jnp.bfloat16

    me = lax.axis_index("pool").astype(jnp.int32)[None]
    core = lax.axis_index("tp").astype(jnp.int32)[None]
    smem = pl.BlockSpec(memory_space=pltpu.SMEM)

    own_up = lax.dynamic_slice_in_dim(adapter_up, core[0] * columns, columns, 2)
    ups = lax.all_gather(own_up, "pool", axis=0, tiled=True)

    picked = pl.pallas_call(
        functools.partial(pick_kernel, local, depth),
        in_specs=[smem, VMEM, VMEM],
        out_specs=[VMEM] * pool_size,
        out_shape=[jax.ShapeDtypeStruct((size, width), bf16)] * pool_size,
        compiler_params=params(),
        cost_estimate=cost(2 * pool_size * size * rows * width, 2 * (rows + pool_size * size) * width),
        name="pick",
    )(me, row_adapters, tokens)

    def across(x, j):
        return lax.ppermute(x, "pool", [(p, p ^ j) for p in range(pool_size)])

    def swap(x):
        return lax.ppermute(x, "tp", [(c, (c + 1) % tp_size) for c in range(tp_size)])

    arrived = [picked[0]] + [None] * (pool_size - 1)
    for j in range(pool_size - 1, 0, -1):
        arrived[j] = across(picked[j], j)

    theirs = base_half(tokens, key_value_weight, 1 - core, columns)
    mine = base_half(tokens, key_value_weight, core, columns)
    other = swap(theirs)

    mask = (jnp.arange(rank, dtype=jnp.int32)[None, :] < ranks[:, None]).astype(f32)
    factor = mask * (f32(ALPHA) / ranks.astype(f32))[:, None]

    half_dim = head // 2
    frequency = jnp.power(
        f32(ROPE_THETA), -jnp.arange(half_dim, dtype=f32) * (2.0 / head)
    )
    angles = positions.astype(f32)[:, None] * frequency[None, :]
    cosine, sine = jnp.cos(angles), jnp.sin(angles)
    cosine = jnp.concatenate([cosine, cosine], axis=1)
    sine = jnp.concatenate([-sine, sine], axis=1)

    low = pl.pallas_call(
        functools.partial(down_kernel, local, depth),
        in_specs=[VMEM] * (2 + pool_size),
        out_specs=[VMEM] * pool_size,
        out_shape=[jax.ShapeDtypeStruct((size, rank), f32)] * pool_size,
        compiler_params=params(),
        cost_estimate=cost(2 * pool_size * size * rank * width, 2 * (pool_size * size + rank) * width),
        name="down",
    )(factor, adapter_down, *arrived)

    back = [low[0]] + [None] * (pool_size - 1)
    for j in range(pool_size - 1, 0, -1):
        back[j] = across(low[j], j)
    row_low = pl.pallas_call(
        functools.partial(return_kernel, local, depth),
        in_specs=[smem] + [VMEM] * (1 + pool_size),
        out_specs=VMEM,
        out_shape=jax.ShapeDtypeStruct((rows, rank), f32),
        compiler_params=params(),
        cost_estimate=cost(6 * pool_size * size * rank * rows, 4 * pool_size * size * rank),
        name="collect",
    )(me, row_adapters, *back)
    row_low_other = swap(row_low)

    out = pl.pallas_call(
        finish_kernel,
        in_specs=[VMEM] * 9,
        out_specs=VMEM,
        out_shape=jax.ShapeDtypeStruct((rows, columns), bf16),
        compiler_params=params(),
        cost_estimate=cost(4 * rows * adapters * rank * columns, 2 * adapters * rank * columns),
        name="finish",
    )(
        row_adapters,
        mine,
        other,
        row_low,
        row_low_other,
        ups,
        cosine,
        sine,
        key_norm_gain.astype(f32)[None, :],
    )
    return out.reshape(rows, columns // (2 * head), 2, head)


def solution(mesh):
    return jax.shard_map(
        body,
        mesh=mesh,
        in_specs=(
            P(("groups", "pool"), "tp"),
            P(("groups", "pool"), None),
            P(("groups", "pool")),
            P("tp", None),
            P("pool", "tp", None),
            P("pool", None, None),
            P("pool"),
            P(),
        ),
        out_specs=P(("groups", "pool"), "tp", None, None),
        check_vma=False,
    )
```

```python
import functools

import jax
import jax.numpy as jnp
from jax import lax
from jax.experimental import pallas as pl
from jax.experimental.pallas import tpu as pltpu
from jax.sharding import PartitionSpec as P

ALPHA = 32
ROPE_THETA = 1000000.0
NORM_EPS = 1e-06
VMEM_LIMIT = 48 * 1024 * 1024
LANES = 128

VMEM = pl.BlockSpec(memory_space=pltpu.VMEM)
SMEM = pl.BlockSpec(memory_space=pltpu.SMEM)


def params(**kw):
    return pltpu.CompilerParams(vmem_limit_bytes=VMEM_LIMIT, **kw)


def cost(flops, bytes_accessed):
    return pl.CostEstimate(flops=flops, bytes_accessed=bytes_accessed, transcendentals=0)


def iota(shape, dim):
    return lax.broadcasted_iota(jnp.int32, shape, dim)


def to_column(row):
    n = row.shape[1]
    return jnp.sum(
        jnp.where(iota((n, n), 0) == iota((n, n), 1), row, 0), axis=1, keepdims=True
    )


def slot_places(row, me, pool, local, depth):
    n = row.shape[1]
    column = to_column(row)
    earlier = (column == row) & (iota((n, n), 0) < iota((n, n), 1))
    slot = jnp.sum(jnp.where(earlier, 1, 0), axis=0, keepdims=True)
    holder = row // local
    apart = holder ^ me
    buffer, far = apart % (pool // 2), apart // (pool // 2)
    return ((buffer * 2 + far) * local + (row - holder * local)) * depth + slot


def halves(x):
    high = x.astype(jnp.bfloat16)
    low = (x - high.astype(jnp.float32)).astype(jnp.bfloat16)
    return high, low


def pick_kernel(pool, local, depth, me_ref, adapter_ref, tokens_ref, *outs):
    rows, width = tokens_ref.shape
    place = slot_places(adapter_ref[...], me_ref[0], pool, local, depth)
    size = outs[0].shape[0]
    slots = len(outs) * size
    picker = jnp.where(iota((slots, rows), 0) == place, 1.0, 0.0).astype(jnp.bfloat16)
    step = 512
    for at in range(0, width, step):
        block = jnp.dot(
            picker, tokens_ref[:, at : at + step], preferred_element_type=jnp.float32
        )
        for j, out in enumerate(outs):
            out[:, at : at + step] = block[j * size : (j + 1) * size].astype(jnp.bfloat16)


def base_kernel(half_ref, tokens_ref, weight_ref, out_ref):
    @pl.when(pl.program_id(0) == 0)
    def _():
        out_ref[...] = jnp.zeros_like(out_ref)

    out_ref[...] += jnp.dot(
        tokens_ref[...], weight_ref[...], preferred_element_type=jnp.float32
    )


def base_half(tokens, weight, half, columns):
    rows, width = tokens.shape
    step = 512
    return pl.pallas_call(
        base_kernel,
        grid_spec=pltpu.PrefetchScalarGridSpec(
            num_scalar_prefetch=1,
            grid=(width // step,),
            in_specs=[
                pl.BlockSpec((rows, step), lambda k, h: (0, k)),
                pl.BlockSpec((step, columns), lambda k, h: (k, h[0])),
            ],
            out_specs=pl.BlockSpec((rows, columns), lambda k, h: (0, 0)),
        ),
        out_shape=jax.ShapeDtypeStruct((rows, columns), jnp.float32),
        compiler_params=params(),
        cost_estimate=cost(2 * rows * width * columns, 2 * width * (rows + columns)),
        name="base_half",
    )(half, tokens, weight)


def down_kernel(buffers, groups, local, depth, group_ref, down_ref, *refs):
    ins, shares, out = refs[:buffers], refs[buffers : buffers + groups], refs[-1]
    rank = out.shape[1]
    share = shares[0].shape[1]
    total = None
    for k in range(groups):
        at = pl.multiple_of((group_ref[0] ^ k) * share, share)
        rows = jnp.concatenate([x[:, pl.ds(at, share)] for x in ins], axis=0)
        factors = [down_ref[a, pl.ds(at, share), :] for a in range(local)]
        factors += [shares[k][a] for a in range(local)]
        term = jnp.dot(
            rows, jnp.concatenate(factors, axis=1), preferred_element_type=jnp.float32
        )
        total = term if total is None else total + term
    which = (iota((total.shape[0], 1), 0) // depth) % (2 * local)
    low = total[:, :rank]
    for i in range(1, 2 * local):
        low = jnp.where(which == i, total[:, i * rank : (i + 1) * rank], low)
    out[...] = low


def up_kernel(
    buffers, groups, local, depth, group_ref, core_ref, low_ref, other_ref, factor_ref, up_ref, *refs
):
    shares, outs, term_ref = refs[:groups], refs[groups : groups + buffers], refs[-1]
    rows, rank = low_ref.shape
    size = rows // buffers
    columns = term_ref.shape[1]
    share = columns // groups
    which = (iota((rows, 1), 0) // depth) % (2 * local)
    low = low_ref[...] + other_ref[...]
    for a in range(local):
        low = jnp.where(which == a, low * factor_ref[a : a + 1, :], low)
    both = jnp.concatenate(halves(low), axis=0)
    which = jnp.concatenate([which, which], axis=0)
    spread = jnp.concatenate(
        [jnp.where(which == i, both, jnp.zeros_like(both)) for i in range(2 * local)], axis=1
    )
    for k in range(groups):
        at = pl.multiple_of((group_ref[0] ^ k) * share, share)
        own_at = pl.multiple_of(core_ref[0] * columns + at, share)
        factors = [up_ref[a, :, pl.ds(own_at, share)] for a in range(local)]
        factors += [shares[k][a] for a in range(local)]
        term = jnp.dot(
            spread, jnp.concatenate(factors, axis=0), preferred_element_type=jnp.float32
        )
        term_ref[:, pl.ds(at, share)] = term[:rows] + term[rows:]
    for j, out in enumerate(outs):
        term = term_ref[j * size : (j + 1) * size, :]
        top = jnp.max(jnp.abs(term), axis=1, keepdims=True)
        exponent = jnp.ceil(jnp.log2(jnp.maximum(top, 1e-30)) + 1e-3)
        code = jnp.round(term * jnp.exp2(15.0 - exponent))
        code = jnp.clip(code, -32767.0, 32767.0)
        out[:, :columns] = code.astype(jnp.int32).astype(jnp.int16)
        out[:, columns:] = jnp.broadcast_to(
            exponent.astype(jnp.int32), (size, LANES)
        ).astype(jnp.int16)


def finish_kernel(
    buffers, pool, local, depth, me_ref, adapter_ref, mine_ref, other_ref, cos_ref, sin_ref, gain_ref, *refs
):
    ins, out_ref = refs[:buffers], refs[-1]
    rows, columns = mine_ref.shape
    head = cos_ref.shape[1]
    place = to_column(slot_places(adapter_ref[...], me_ref[0], pool, local, depth))
    slots = buffers * ins[0].shape[0]
    picker = jnp.where(iota((rows, slots), 1) == place, 1.0, 0.0).astype(jnp.bfloat16)

    def picked(at, size):
        code = jnp.concatenate([x[:, at : at + size] for x in ins], axis=0).astype(jnp.int32)
        high = (code >> 8).astype(jnp.float32).astype(jnp.bfloat16)
        low = (code & 255).astype(jnp.float32).astype(jnp.bfloat16)
        high = jnp.dot(picker, high, preferred_element_type=jnp.float32)
        low = jnp.dot(picker, low, preferred_element_type=jnp.float32)
        return high * 256.0 + low

    scale = jnp.exp2(picked(columns, LANES)[:, :1] - 15.0)
    cosine, sine, gain = cos_ref[...], sin_ref[...], gain_ref[...]
    for at in range(0, columns, 2 * head):
        projected = mine_ref[:, at : at + 2 * head] + other_ref[:, at : at + 2 * head]
        projected = projected + picked(at, 2 * head) * scale
        key, value = projected[:, :head], projected[:, head:]
        mean = jnp.mean(key * key, axis=1, keepdims=True)
        normed = key * lax.rsqrt(mean + NORM_EPS) * gain
        rotated = normed * cosine + pltpu.roll(normed, head // 2, 1) * sine
        out_ref[:, at : at + head] = rotated.astype(jnp.bfloat16)
        out_ref[:, at + head : at + 2 * head] = value.astype(jnp.bfloat16)


def body(
    tokens,
    row_adapters,
    positions,
    key_value_weight,
    adapter_down,
    adapter_up,
    ranks,
    key_norm_gain,
):
    pool = lax.axis_size("pool")
    groups = lax.axis_size("groups")
    cores = lax.axis_size("tp")
    rows, width = tokens.shape
    local = adapter_down.shape[0]
    adapters = local * pool
    columns = key_value_weight.shape[1] // cores
    rank = adapter_down.shape[2]
    head = key_norm_gain.shape[0]
    depth = max(2, 2 * rows // adapters)
    buffers = pool // 2
    size = 2 * local * depth
    f32, bf16 = jnp.float32, jnp.bfloat16

    me = lax.axis_index("pool").astype(jnp.int32)[None]
    core = lax.axis_index("tp").astype(jnp.int32)[None]
    group = lax.axis_index("groups").astype(jnp.int32)[None]

    def exchange(x, axis, count, j):
        return lax.ppermute(x, axis, [(p, p ^ j) for p in range(count)])

    def hand_round(share):
        return [share] + [exchange(share, "groups", groups, k) for k in range(1, groups)]

    mask = (jnp.arange(rank, dtype=jnp.int32)[None, :] < ranks[:, None]).astype(f32)
    factor = mask * (f32(ALPHA) / ranks.astype(f32))[:, None]

    down_share = width // groups
    down_part = lax.dynamic_slice_in_dim(adapter_down, group[0] * down_share, down_share, 1)
    far_down = exchange(down_part, "pool", pool, pool // 2)
    up_share = columns // groups
    up_part = lax.dynamic_slice_in_dim(
        adapter_up, core[0] * columns + group[0] * up_share, up_share, 2
    )
    up_part = (up_part.astype(f32) * factor[:, :, None]).astype(bf16)
    far_up = exchange(up_part, "pool", pool, pool // 2)

    adapter_row = row_adapters.reshape(1, rows)
    picked = pl.pallas_call(
        functools.partial(pick_kernel, pool, local, depth),
        in_specs=[SMEM, VMEM, VMEM],
        out_specs=[VMEM] * buffers,
        out_shape=[jax.ShapeDtypeStruct((size, width), bf16)] * buffers,
        compiler_params=params(),
        cost_estimate=cost(2 * buffers * size * rows * width, 2 * (rows + buffers * size) * width),
        name="pick",
    )(me, adapter_row, tokens)
    arrived = [picked[0]] + [None] * (buffers - 1)
    for j in range(buffers - 1, 0, -1):
        arrived[j] = exchange(picked[j], "pool", pool, j)

    far_downs = hand_round(far_down)
    far_ups = hand_round(far_up)

    theirs = base_half(tokens, key_value_weight, 1 - core, columns)
    mine = base_half(tokens, key_value_weight, core, columns)
    other = exchange(theirs, "tp", cores, 1)

    half_dim = head // 2
    frequency = jnp.power(
        f32(ROPE_THETA), -jnp.arange(half_dim, dtype=f32) * (2.0 / head)
    )
    angles = positions.astype(f32)[:, None] * frequency[None, :]
    cosine, sine = jnp.cos(angles), jnp.sin(angles)
    cosine = jnp.concatenate([cosine, cosine], axis=1)
    sine = jnp.concatenate([-sine, sine], axis=1)

    arrived, mine, cosine, sine = lax.optimization_barrier((arrived, mine, cosine, sine))
    slots = buffers * size
    low = pl.pallas_call(
        functools.partial(down_kernel, buffers, groups, local, depth),
        in_specs=[SMEM] + [VMEM] * (1 + buffers + groups),
        out_specs=VMEM,
        out_shape=jax.ShapeDtypeStruct((slots, rank), f32),
        compiler_params=params(),
        cost_estimate=cost(4 * local * slots * rank * width, 2 * (slots + rank) * width),
        name="down",
    )(group, adapter_down, *arrived, *far_downs)
    low_other = exchange(low, "tp", cores, 1)

    terms = pl.pallas_call(
        functools.partial(up_kernel, buffers, groups, local, depth),
        in_specs=[SMEM] * 2 + [VMEM] * (4 + groups),
        out_specs=[VMEM] * buffers,
        out_shape=[jax.ShapeDtypeStruct((size, columns + LANES), jnp.int16)] * buffers,
        scratch_shapes=[pltpu.VMEM((slots, columns), f32)],
        compiler_params=params(),
        cost_estimate=cost(8 * local * slots * rank * columns, 2 * slots * columns),
        name="up",
    )(group, core, low, low_other, factor, adapter_up, *far_ups)
    returned = [terms[0]] + [None] * (buffers - 1)
    for j in range(buffers - 1, 0, -1):
        returned[j] = exchange(terms[j], "pool", pool, j)

    out = pl.pallas_call(
        functools.partial(finish_kernel, buffers, pool, local, depth),
        in_specs=[SMEM] + [VMEM] * (6 + buffers),
        out_specs=VMEM,
        out_shape=jax.ShapeDtypeStruct((rows, columns), bf16),
        compiler_params=params(),
        cost_estimate=cost(4 * rows * slots * columns, 2 * slots * columns),
        name="finish",
    )(
        me,
        adapter_row,
        mine,
        other,
        cosine,
        sine,
        key_norm_gain.astype(f32)[None, :],
        *returned,
    )
    return out.reshape(rows, columns // (2 * head), 2, head)


def solution(mesh):
    return jax.shard_map(
        body,
        mesh=mesh,
        in_specs=(
            P(("groups", "pool"), "tp"),
            P(("groups", "pool"), None),
            P(("groups", "pool")),
            P("tp", None),
            P("pool", "tp", None),
            P("pool", None, None),
            P("pool"),
            P(),
        ),
        out_specs=P(("groups", "pool"), "tp", None, None),
        check_vma=False,
    )
```

```python
import functools

import jax
import jax.numpy as jnp
from jax import lax
from jax.experimental import pallas as pl
from jax.experimental.pallas import tpu as pltpu
from jax.sharding import PartitionSpec as P

ALPHA = 32
ROPE_THETA = 1000000.0
NORM_EPS = 1e-06
VMEM_LIMIT = 48 * 1024 * 1024
LANES = 128

VMEM = pl.BlockSpec(memory_space=pltpu.VMEM)
HBM = pl.BlockSpec(memory_space=pltpu.HBM)
SMEM = pl.BlockSpec(memory_space=pltpu.SMEM)


def params(**kw):
    return pltpu.CompilerParams(vmem_limit_bytes=VMEM_LIMIT, **kw)


def cost(flops, bytes_accessed):
    return pl.CostEstimate(flops=flops, bytes_accessed=bytes_accessed, transcendentals=0)


def in_hbm(x):
    return pltpu.with_memory_space_constraint(x, pltpu.HBM)


def iota(shape, dim):
    return lax.broadcasted_iota(jnp.int32, shape, dim)


def to_column(row):
    n = row.shape[1]
    return jnp.sum(
        jnp.where(iota((n, n), 0) == iota((n, n), 1), row, 0), axis=1, keepdims=True
    )


def slot_places(row, me, pool, local, depth):
    n = row.shape[1]
    column = to_column(row)
    earlier = (column == row) & (iota((n, n), 0) < iota((n, n), 1))
    slot = jnp.sum(jnp.where(earlier, 1, 0), axis=0, keepdims=True)
    holder = row // local
    apart = holder ^ me
    buffer, far = apart % (pool // 2), apart // (pool // 2)
    return ((buffer * 2 + far) * local + (row - holder * local)) * depth + slot


def halves(x):
    high = x.astype(jnp.bfloat16)
    low = (x - high.astype(jnp.float32)).astype(jnp.bfloat16)
    return high, low


def prepare_kernel(
    local, group_ref, core_ref, ranks_ref, down_ref, up_ref, down_out, up_out, up_own, sems
):
    down_share, up_share = down_out.shape[1], up_out.shape[2]
    rank, columns = up_out.shape[1], up_ref.shape[2] // lax.axis_size("tp")
    at = pl.multiple_of(group_ref[0] * down_share, down_share)
    up_at = pl.multiple_of(core_ref[0] * columns + group_ref[0] * up_share, up_share)
    down_copy = pltpu.make_async_copy(
        down_ref.at[:, pl.ds(at, down_share), :], down_out, sems.at[0]
    )
    up_copy = pltpu.make_async_copy(
        up_ref.at[:, :, pl.ds(up_at, up_share)], up_own, sems.at[1]
    )
    down_copy.start()
    up_copy.start()
    up_copy.wait()
    for a in range(local):
        used = jnp.full((rank, 1), ranks_ref[a], jnp.int32)
        factor = jnp.where(
            iota((rank, 1), 0) < used, jnp.float32(ALPHA) / used.astype(jnp.float32), 0.0
        )
        up_out[a] = (up_own[a].astype(jnp.float32) * factor).astype(jnp.bfloat16)
    down_copy.wait()


def pick_kernel(
    pool, local, depth, me_ref, adapter_hbm, tokens_hbm, *refs
):
    outs, (adapter_ref, tokens_ref, adapter_sem, sems) = refs[:-4], refs[-4:]
    rows, width = tokens_ref.shape
    step = width // sems.shape[0]
    adapter_copy = pltpu.make_async_copy(adapter_hbm, adapter_ref, adapter_sem)
    adapter_copy.start()
    copies = [
        pltpu.make_async_copy(
            tokens_hbm.at[:, pl.ds(i * step, step)],
            tokens_ref.at[:, pl.ds(i * step, step)],
            sems.at[i],
        )
        for i in range(sems.shape[0])
    ]
    for copy in copies:
        copy.start()
    adapter_copy.wait()
    place = slot_places(adapter_ref[...], me_ref[0], pool, local, depth)
    size = outs[0].shape[0]
    slots = len(outs) * size
    picker = jnp.where(iota((slots, rows), 0) == place, 1.0, 0.0).astype(jnp.bfloat16)
    for i, copy in enumerate(copies):
        copy.wait()
        at = i * step
        block = jnp.dot(
            picker, tokens_ref[:, at : at + step], preferred_element_type=jnp.float32
        )
        for j, out in enumerate(outs):
            out[:, at : at + step] = block[j * size : (j + 1) * size].astype(jnp.bfloat16)


def base_kernel(
    core_ref, tokens_hbm, weight_hbm, theirs_ref, mine_ref, tokens_ref, weight_ref, tokens_sem, sems
):
    rows, columns = mine_ref.shape
    steps = sems.shape[1]
    step = tokens_ref.shape[1] // steps
    copies = []
    for half in range(2):
        start = (1 - core_ref[0] if half == 0 else core_ref[0]) * columns
        start = pl.multiple_of(start, columns)
        for k in range(steps):
            copies.append(
                pltpu.make_async_copy(
                    weight_hbm.at[pl.ds(k * step, step), pl.ds(start, columns)],
                    weight_ref.at[half, pl.ds(k * step, step), :],
                    sems.at[half, k],
                )
            )
    tokens_copy = pltpu.make_async_copy(tokens_hbm, tokens_ref, tokens_sem)
    tokens_copy.start()
    for copy in copies:
        copy.start()
    tokens_copy.wait()
    for half, out in enumerate((theirs_ref, mine_ref)):
        for k in range(steps):
            copies[half * steps + k].wait()
            term = jnp.dot(
                tokens_ref[:, k * step : (k + 1) * step],
                weight_ref[half, k * step : (k + 1) * step, :],
                preferred_element_type=jnp.float32,
            )
            if k == 0:
                out[...] = term
            else:
                out[...] += term


def down_kernel(buffers, groups, local, depth, group_ref, down_ref, *refs):
    ins, shares, out = refs[:buffers], refs[buffers : buffers + groups], refs[-1]
    rank = out.shape[1]
    share = shares[0].shape[1]
    total = None
    for k in range(groups):
        at = pl.multiple_of((group_ref[0] ^ k) * share, share)
        rows = jnp.concatenate([x[:, pl.ds(at, share)] for x in ins], axis=0)
        factors = [down_ref[a, pl.ds(at, share), :] for a in range(local)]
        factors += [shares[k][a] for a in range(local)]
        term = jnp.dot(
            rows, jnp.concatenate(factors, axis=1), preferred_element_type=jnp.float32
        )
        total = term if total is None else total + term
    which = (iota((total.shape[0], 1), 0) // depth) % (2 * local)
    low = total[:, :rank]
    for i in range(1, 2 * local):
        low = jnp.where(which == i, total[:, i * rank : (i + 1) * rank], low)
    out[...] = low


def up_kernel(
    buffers, groups, local, depth, group_ref, core_ref, low_ref, other_ref, factor_ref, up_ref, *refs
):
    shares, outs, term_ref = refs[:groups], refs[groups : groups + buffers], refs[-1]
    rows, rank = low_ref.shape
    size = rows // buffers
    columns = term_ref.shape[1]
    share = columns // groups
    which = (iota((rows, 1), 0) // depth) % (2 * local)
    low = low_ref[...] + other_ref[...]
    for a in range(local):
        low = jnp.where(which == a, low * factor_ref[a : a + 1, :], low)
    both = jnp.concatenate(halves(low), axis=0)
    which = jnp.concatenate([which, which], axis=0)
    spread = jnp.concatenate(
        [jnp.where(which == i, both, jnp.zeros_like(both)) for i in range(2 * local)], axis=1
    )
    for k in range(groups):
        at = pl.multiple_of((group_ref[0] ^ k) * share, share)
        own_at = pl.multiple_of(core_ref[0] * columns + at, share)
        factors = [up_ref[a, :, pl.ds(own_at, share)] for a in range(local)]
        factors += [shares[k][a] for a in range(local)]
        term = jnp.dot(
            spread, jnp.concatenate(factors, axis=0), preferred_element_type=jnp.float32
        )
        term_ref[:, pl.ds(at, share)] = term[:rows] + term[rows:]
    for j, out in enumerate(outs):
        term = term_ref[j * size : (j + 1) * size, :]
        top = jnp.max(jnp.abs(term), axis=1, keepdims=True)
        exponent = jnp.ceil(jnp.log2(jnp.maximum(top, 1e-30)) + 1e-3)
        code = jnp.round(term * jnp.exp2(15.0 - exponent))
        code = jnp.clip(code, -32767.0, 32767.0)
        out[:, :columns] = code.astype(jnp.int32).astype(jnp.int16)
        out[:, columns:] = jnp.broadcast_to(
            exponent.astype(jnp.int32), (size, LANES)
        ).astype(jnp.int16)


def finish_kernel(
    buffers, pool, local, depth, me_ref, adapter_ref, mine_ref, other_ref, cos_ref, sin_ref, gain_ref, *refs
):
    ins, out_ref = refs[:buffers], refs[-1]
    rows, columns = mine_ref.shape
    head = cos_ref.shape[1]
    place = to_column(slot_places(adapter_ref[...], me_ref[0], pool, local, depth))
    slots = buffers * ins[0].shape[0]
    picker = jnp.where(iota((rows, slots), 1) == place, 1.0, 0.0).astype(jnp.bfloat16)

    def picked(at, size):
        code = jnp.concatenate([x[:, at : at + size] for x in ins], axis=0).astype(jnp.int32)
        high = (code >> 8).astype(jnp.float32).astype(jnp.bfloat16)
        low = (code & 255).astype(jnp.float32).astype(jnp.bfloat16)
        high = jnp.dot(picker, high, preferred_element_type=jnp.float32)
        low = jnp.dot(picker, low, preferred_element_type=jnp.float32)
        return high * 256.0 + low

    scale = jnp.exp2(picked(columns, LANES)[:, :1] - 15.0)
    cosine, sine, gain = cos_ref[...], sin_ref[...], gain_ref[...]
    for at in range(0, columns, 2 * head):
        projected = mine_ref[:, at : at + 2 * head] + other_ref[:, at : at + 2 * head]
        projected = projected + picked(at, 2 * head) * scale
        key, value = projected[:, :head], projected[:, head:]
        mean = jnp.mean(key * key, axis=1, keepdims=True)
        normed = key * lax.rsqrt(mean + NORM_EPS) * gain
        rotated = normed * cosine + pltpu.roll(normed, head // 2, 1) * sine
        entry = jnp.stack([rotated, value], axis=1)
        out_ref[:, at // (2 * head)] = entry.astype(jnp.bfloat16)


def body(
    tokens,
    row_adapters,
    positions,
    key_value_weight,
    adapter_down,
    adapter_up,
    ranks,
    key_norm_gain,
):
    pool = lax.axis_size("pool")
    groups = lax.axis_size("groups")
    cores = lax.axis_size("tp")
    rows, width = tokens.shape
    local = adapter_down.shape[0]
    adapters = local * pool
    columns = key_value_weight.shape[1] // cores
    rank = adapter_down.shape[2]
    head = key_norm_gain.shape[0]
    depth = max(2, 2 * rows // adapters)
    buffers = pool // 2
    size = 2 * local * depth
    f32, bf16 = jnp.float32, jnp.bfloat16

    me = lax.axis_index("pool").astype(jnp.int32)[None]
    core = lax.axis_index("tp").astype(jnp.int32)[None]
    group = lax.axis_index("groups").astype(jnp.int32)[None]

    def exchange(x, axis, count, j):
        return lax.ppermute(x, axis, [(p, p ^ j) for p in range(count)])

    def hand_round(share):
        return [share] + [exchange(share, "groups", groups, k) for k in range(1, groups)]

    mask = (jnp.arange(rank, dtype=jnp.int32)[None, :] < ranks[:, None]).astype(f32)
    factor = mask * (f32(ALPHA) / ranks.astype(f32))[:, None]

    down_share = width // groups
    up_share = columns // groups
    down_part, up_part = pl.pallas_call(
        functools.partial(prepare_kernel, local),
        in_specs=[SMEM] * 3 + [HBM] * 2,
        out_specs=[VMEM] * 2,
        out_shape=[
            jax.ShapeDtypeStruct((local, down_share, rank), bf16),
            jax.ShapeDtypeStruct((local, rank, up_share), bf16),
        ],
        scratch_shapes=[
            pltpu.VMEM((local, rank, up_share), bf16),
            pltpu.SemaphoreType.DMA((2,)),
        ],
        compiler_params=params(),
        cost_estimate=cost(local * rank * up_share, 4 * local * rank * (down_share + up_share)),
        name="prepare",
    )(group, core, ranks, in_hbm(adapter_down), in_hbm(adapter_up))
    far_down = exchange(down_part, "pool", pool, pool // 2)
    far_up = exchange(up_part, "pool", pool, pool // 2)

    adapter_row = row_adapters.reshape(1, rows)
    steps = 5
    tokens_now, _, _ = lax.optimization_barrier((tokens, down_part, up_part))
    picked = pl.pallas_call(
        functools.partial(pick_kernel, pool, local, depth),
        in_specs=[SMEM, HBM, HBM],
        out_specs=[VMEM] * buffers,
        out_shape=[jax.ShapeDtypeStruct((size, width), bf16)] * buffers,
        scratch_shapes=[
            pltpu.VMEM((1, rows), jnp.int32),
            pltpu.VMEM((rows, width), bf16),
            pltpu.SemaphoreType.DMA,
            pltpu.SemaphoreType.DMA((steps,)),
        ],
        compiler_params=params(),
        cost_estimate=cost(2 * buffers * size * rows * width, 2 * (rows + buffers * size) * width),
        name="pick",
    )(me, in_hbm(adapter_row), in_hbm(tokens_now))
    arrived = [picked[0]] + [None] * (buffers - 1)
    for j in range(buffers - 1, 0, -1):
        arrived[j] = exchange(picked[j], "pool", pool, j)

    theirs, mine = pl.pallas_call(
        base_kernel,
        in_specs=[SMEM, HBM, HBM],
        out_specs=[VMEM] * 2,
        out_shape=[jax.ShapeDtypeStruct((rows, columns), f32)] * 2,
        scratch_shapes=[
            pltpu.VMEM((rows, width), bf16),
            pltpu.VMEM((2, width, columns), bf16),
            pltpu.SemaphoreType.DMA,
            pltpu.SemaphoreType.DMA((2, steps)),
        ],
        compiler_params=params(),
        cost_estimate=cost(4 * rows * width * columns, 4 * width * columns),
        name="base",
    )(core, in_hbm(tokens), in_hbm(key_value_weight))
    far_down, far_up, theirs = lax.optimization_barrier((far_down, far_up, theirs))
    far_downs = hand_round(far_down)
    far_ups = hand_round(far_up)
    half_dim = head // 2
    frequency = jnp.power(
        f32(ROPE_THETA), -jnp.arange(half_dim, dtype=f32) * (2.0 / head)
    )
    angles = positions.astype(f32)[:, None] * frequency[None, :]
    cosine, sine = jnp.cos(angles), jnp.sin(angles)
    cosine = jnp.concatenate([cosine, cosine], axis=1)
    sine = jnp.concatenate([-sine, sine], axis=1)

    arrived, far_ups, theirs, mine, cosine, sine = lax.optimization_barrier(
        (arrived, far_ups, theirs, mine, cosine, sine)
    )
    other = exchange(theirs, "tp", cores, 1)
    slots = buffers * size
    low = pl.pallas_call(
        functools.partial(down_kernel, buffers, groups, local, depth),
        in_specs=[SMEM] + [VMEM] * (1 + buffers + groups),
        out_specs=VMEM,
        out_shape=jax.ShapeDtypeStruct((slots, rank), f32),
        compiler_params=params(),
        cost_estimate=cost(4 * local * slots * rank * width, 2 * (slots + rank) * width),
        name="down",
    )(group, adapter_down, *arrived, *far_downs)
    low_other = exchange(low, "tp", cores, 1)

    terms = pl.pallas_call(
        functools.partial(up_kernel, buffers, groups, local, depth),
        in_specs=[SMEM] * 2 + [VMEM] * (4 + groups),
        out_specs=[VMEM] * buffers,
        out_shape=[jax.ShapeDtypeStruct((size, columns + LANES), jnp.int16)] * buffers,
        scratch_shapes=[pltpu.VMEM((slots, columns), f32)],
        compiler_params=params(),
        cost_estimate=cost(8 * local * slots * rank * columns, 2 * slots * columns),
        name="up",
    )(group, core, low, low_other, factor, adapter_up, *far_ups)
    returned = [terms[0]] + [None] * (buffers - 1)
    for j in range(buffers - 1, 0, -1):
        returned[j] = exchange(terms[j], "pool", pool, j)

    out = pl.pallas_call(
        functools.partial(finish_kernel, buffers, pool, local, depth),
        in_specs=[SMEM] + [VMEM] * (6 + buffers),
        out_specs=VMEM,
        out_shape=jax.ShapeDtypeStruct((rows, columns // (2 * head), 2, head), bf16),
        compiler_params=params(),
        cost_estimate=cost(4 * rows * slots * columns, 2 * slots * columns),
        name="finish",
    )(
        me,
        adapter_row,
        mine,
        other,
        cosine,
        sine,
        key_norm_gain.astype(f32)[None, :],
        *returned,
    )
    return out


def solution(mesh):
    return jax.shard_map(
        body,
        mesh=mesh,
        in_specs=(
            P(("groups", "pool"), "tp"),
            P(("groups", "pool"), None),
            P(("groups", "pool")),
            P("tp", None),
            P("pool", "tp", None),
            P("pool", None, None),
            P("pool"),
            P(),
        ),
        out_specs=P(("groups", "pool"), "tp", None, None),
        check_vma=False,
    )
```

```python
import functools

import jax
import jax.numpy as jnp
from jax import lax
from jax.experimental import pallas as pl
from jax.experimental.pallas import tpu as pltpu
from jax.sharding import PartitionSpec as P

ALPHA = 32
ROPE_THETA = 1000000.0
NORM_EPS = 1e-06
VMEM_LIMIT = 48 * 1024 * 1024
LANES = 128

VMEM = pl.BlockSpec(memory_space=pltpu.VMEM)
HBM = pl.BlockSpec(memory_space=pltpu.HBM)
SMEM = pl.BlockSpec(memory_space=pltpu.SMEM)


def params(**kw):
    return pltpu.CompilerParams(vmem_limit_bytes=VMEM_LIMIT, **kw)


def cost(flops, bytes_accessed):
    return pl.CostEstimate(flops=flops, bytes_accessed=bytes_accessed, transcendentals=0)


def in_hbm(x):
    return pltpu.with_memory_space_constraint(x, pltpu.HBM)


def iota(shape, dim):
    return lax.broadcasted_iota(jnp.int32, shape, dim)


def to_column(row):
    n = row.shape[1]
    return jnp.sum(
        jnp.where(iota((n, n), 0) == iota((n, n), 1), row, 0), axis=1, keepdims=True
    )


def slot_places(row, me, pool, local, depth):
    n = row.shape[1]
    column = to_column(row)
    earlier = (column == row) & (iota((n, n), 0) < iota((n, n), 1))
    slot = jnp.sum(jnp.where(earlier, 1, 0), axis=0, keepdims=True)
    holder = row // local
    apart = holder ^ me
    buffer, far = apart % (pool // 2), apart // (pool // 2)
    return ((buffer * 2 + far) * local + (row - holder * local)) * depth + slot


def far_first(count):
    return sorted(range(1, count), key=lambda j: (-bin(j).count("1"), j))


def return_order(count):
    order = far_first(count)
    return order[-1:] + order[:-1]


def halves(x):
    high = x.astype(jnp.bfloat16)
    low = (x - high.astype(jnp.float32)).astype(jnp.bfloat16)
    return high, low


def down_share_kernel(group_ref, down_hbm, out_ref, sem):
    share = out_ref.shape[1]
    at = pl.multiple_of(group_ref[0] * share, share)
    copy = pltpu.make_async_copy(down_hbm.at[:, pl.ds(at, share), :], out_ref, sem)
    copy.start()
    copy.wait()


def up_share_kernel(cores, group_ref, core_ref, ranks_ref, up_hbm, out_ref, factor_ref, own_ref, sem):
    local, rank, share = out_ref.shape
    at = core_ref[0] * (up_hbm.shape[2] // cores) + group_ref[0] * share
    copy = pltpu.make_async_copy(
        up_hbm.at[:, :, pl.ds(pl.multiple_of(at, share), share)], own_ref, sem
    )
    copy.start()
    copy.wait()
    for a in range(local):
        used = ranks_ref[a]

        def factor(shape, dim):
            scale = jnp.float32(ALPHA) / jnp.full(shape, used, jnp.int32).astype(jnp.float32)
            return jnp.where(iota(shape, dim) < used, scale, 0.0)

        factor_ref[a : a + 1, :] = factor((1, rank), 1)
        out_ref[a] = (own_ref[a].astype(jnp.float32) * factor((rank, 1), 0)).astype(jnp.bfloat16)


def pick_kernel(
    pool, local, depth, me_ref, adapter_hbm, tokens_hbm, *refs
):
    outs, (adapter_ref, tokens_ref, adapter_sem, sems) = refs[:-4], refs[-4:]
    rows, width = tokens_ref.shape
    step = width // sems.shape[0]
    adapter_copy = pltpu.make_async_copy(adapter_hbm, adapter_ref, adapter_sem)
    adapter_copy.start()
    copies = [
        pltpu.make_async_copy(
            tokens_hbm.at[:, pl.ds(i * step, step)],
            tokens_ref.at[:, pl.ds(i * step, step)],
            sems.at[i],
        )
        for i in range(sems.shape[0])
    ]
    for copy in copies:
        copy.start()
    adapter_copy.wait()
    place = slot_places(adapter_ref[...], me_ref[0], pool, local, depth)
    size = outs[0].shape[0]
    slots = len(outs) * size
    picker = jnp.where(iota((slots, rows), 0) == place, 1.0, 0.0).astype(jnp.bfloat16)
    for i, copy in enumerate(copies):
        copy.wait()
        at = i * step
        block = jnp.dot(
            picker, tokens_ref[:, at : at + step], preferred_element_type=jnp.float32
        )
        for j, out in enumerate(outs):
            out[:, at : at + step] = block[j * size : (j + 1) * size].astype(jnp.bfloat16)


def base_kernel(
    core_ref, tokens_hbm, weight_hbm, theirs_ref, mine_ref, tokens_ref, weight_ref, tokens_sem, sems
):
    rows, columns = mine_ref.shape
    steps = sems.shape[1]
    step = tokens_ref.shape[1] // steps
    copies = []
    for half in range(2):
        start = (1 - core_ref[0] if half == 0 else core_ref[0]) * columns
        start = pl.multiple_of(start, columns)
        for k in range(steps):
            copies.append(
                pltpu.make_async_copy(
                    weight_hbm.at[pl.ds(k * step, step), pl.ds(start, columns)],
                    weight_ref.at[half, pl.ds(k * step, step), :],
                    sems.at[half, k],
                )
            )
    tokens_copy = pltpu.make_async_copy(tokens_hbm, tokens_ref, tokens_sem)
    tokens_copy.start()
    for copy in copies:
        copy.start()
    tokens_copy.wait()
    for half, out in enumerate((theirs_ref, mine_ref)):
        for k in range(steps):
            copies[half * steps + k].wait()
            term = jnp.dot(
                tokens_ref[:, k * step : (k + 1) * step],
                weight_ref[half, k * step : (k + 1) * step, :],
                preferred_element_type=jnp.float32,
            )
            if k == 0:
                out[...] = term
            else:
                out[...] += term


def down_kernel(buffers, groups, local, depth, group_ref, down_ref, *refs):
    order = [0] + far_first(buffers)
    ins = [refs[order.index(j)] for j in range(buffers)]
    shares, out = refs[buffers : buffers + groups], refs[-1]
    rank = out.shape[1]
    share = shares[0].shape[1]
    total = None
    for k in range(groups):
        at = pl.multiple_of((group_ref[0] ^ k) * share, share)
        rows = jnp.concatenate([x[:, pl.ds(at, share)] for x in ins], axis=0)
        factors = [down_ref[a, pl.ds(at, share), :] for a in range(local)]
        factors += [shares[k][a] for a in range(local)]
        term = jnp.dot(
            rows, jnp.concatenate(factors, axis=1), preferred_element_type=jnp.float32
        )
        total = term if total is None else total + term
    which = (iota((total.shape[0], 1), 0) // depth) % (2 * local)
    low = total[:, :rank]
    for i in range(1, 2 * local):
        low = jnp.where(which == i, total[:, i * rank : (i + 1) * rank], low)
    out[...] = low


def up_kernel(
    buffers, groups, local, depth, group_ref, core_ref, low_ref, other_ref, factor_ref, up_ref, *refs
):
    shares, outs, term_ref = refs[:groups], refs[groups : groups + buffers], refs[-1]
    rows, rank = low_ref.shape
    size = rows // buffers
    columns = term_ref.shape[1]
    share = columns // groups
    which = (iota((rows, 1), 0) // depth) % (2 * local)
    low = low_ref[...] + other_ref[...]
    for a in range(local):
        low = jnp.where(which == a, low * factor_ref[a : a + 1, :], low)
    both = jnp.concatenate(halves(low), axis=0)
    which = jnp.concatenate([which, which], axis=0)
    spread = jnp.concatenate(
        [jnp.where(which == i, both, jnp.zeros_like(both)) for i in range(2 * local)], axis=1
    )
    for k in range(groups):
        at = pl.multiple_of((group_ref[0] ^ k) * share, share)
        own_at = pl.multiple_of(core_ref[0] * columns + at, share)
        factors = [up_ref[a, :, pl.ds(own_at, share)] for a in range(local)]
        factors += [shares[k][a] for a in range(local)]
        term = jnp.dot(
            spread, jnp.concatenate(factors, axis=0), preferred_element_type=jnp.float32
        )
        term_ref[:, pl.ds(at, share)] = term[:rows] + term[rows:]
    for j, out in enumerate(outs):
        term = term_ref[j * size : (j + 1) * size, :]
        top = jnp.max(jnp.abs(term), axis=1, keepdims=True)
        exponent = jnp.ceil(jnp.log2(jnp.maximum(top, 1e-30)) + 1e-3)
        code = jnp.round(term * jnp.exp2(15.0 - exponent))
        code = jnp.clip(code, -32767.0, 32767.0)
        out[:, :columns] = code.astype(jnp.int32).astype(jnp.int16)
        out[:, columns:] = jnp.broadcast_to(
            exponent.astype(jnp.int32), (size, LANES)
        ).astype(jnp.int16)


def finish_kernel(
    buffers, pool, local, depth, me_ref, adapter_ref, mine_ref, other_ref, cos_ref, sin_ref, gain_ref, *refs
):
    order = [0] + return_order(buffers)
    ins, out_ref = [refs[order.index(j)] for j in range(buffers)], refs[-1]
    rows, columns = mine_ref.shape
    head = cos_ref.shape[1]
    place = to_column(slot_places(adapter_ref[...], me_ref[0], pool, local, depth))
    slots = buffers * ins[0].shape[0]
    picker = jnp.where(iota((rows, slots), 1) == place, 1.0, 0.0).astype(jnp.bfloat16)

    def picked(at, size):
        code = jnp.concatenate([x[:, at : at + size] for x in ins], axis=0).astype(jnp.int32)
        high = (code >> 8).astype(jnp.float32).astype(jnp.bfloat16)
        low = (code & 255).astype(jnp.float32).astype(jnp.bfloat16)
        high = jnp.dot(picker, high, preferred_element_type=jnp.float32)
        low = jnp.dot(picker, low, preferred_element_type=jnp.float32)
        return high * 256.0 + low

    scale = jnp.exp2(picked(columns, LANES)[:, :1] - 15.0)
    cosine, sine, gain = cos_ref[...], sin_ref[...], gain_ref[...]
    for at in range(0, columns, 2 * head):
        projected = mine_ref[:, at : at + 2 * head] + other_ref[:, at : at + 2 * head]
        projected = projected + picked(at, 2 * head) * scale
        key, value = projected[:, :head], projected[:, head:]
        mean = jnp.mean(key * key, axis=1, keepdims=True)
        normed = key * lax.rsqrt(mean + NORM_EPS) * gain
        rotated = normed * cosine + pltpu.roll(normed, head // 2, 1) * sine
        entry = jnp.stack([rotated, value], axis=1)
        out_ref[:, at // (2 * head)] = entry.astype(jnp.bfloat16)


def body(
    tokens,
    row_adapters,
    positions,
    key_value_weight,
    adapter_down,
    adapter_up,
    ranks,
    key_norm_gain,
):
    pool = lax.axis_size("pool")
    groups = lax.axis_size("groups")
    cores = lax.axis_size("tp")
    rows, width = tokens.shape
    local = adapter_down.shape[0]
    adapters = local * pool
    columns = key_value_weight.shape[1] // cores
    rank = adapter_down.shape[2]
    head = key_norm_gain.shape[0]
    depth = max(2, 2 * rows // adapters)
    buffers = pool // 2
    size = 2 * local * depth
    f32, bf16 = jnp.float32, jnp.bfloat16

    me = lax.axis_index("pool").astype(jnp.int32)[None]
    core = lax.axis_index("tp").astype(jnp.int32)[None]
    group = lax.axis_index("groups").astype(jnp.int32)[None]

    def exchange(x, axis, count, j):
        return lax.ppermute(x, axis, [(p, p ^ j) for p in range(count)])

    def hand_round(share):
        return [share] + [exchange(share, "groups", groups, k) for k in range(1, groups)]

    down_share = width // groups
    down_part = pl.pallas_call(
        down_share_kernel,
        in_specs=[SMEM, HBM],
        out_specs=VMEM,
        out_shape=jax.ShapeDtypeStruct((local, down_share, rank), bf16),
        scratch_shapes=[pltpu.SemaphoreType.DMA],
        compiler_params=params(),
        cost_estimate=cost(0, 4 * local * rank * down_share),
        name="down_share",
    )(group, in_hbm(adapter_down))
    far_down = exchange(down_part, "pool", pool, pool // 2)

    adapter_row = row_adapters.reshape(1, rows)
    steps = 5
    tokens_now, _ = lax.optimization_barrier((tokens, down_part))
    picked = pl.pallas_call(
        functools.partial(pick_kernel, pool, local, depth),
        in_specs=[SMEM, HBM, HBM],
        out_specs=[VMEM] * buffers,
        out_shape=[jax.ShapeDtypeStruct((size, width), bf16)] * buffers,
        scratch_shapes=[
            pltpu.VMEM((1, rows), jnp.int32),
            pltpu.VMEM((rows, width), bf16),
            pltpu.SemaphoreType.DMA,
            pltpu.SemaphoreType.DMA((steps,)),
        ],
        compiler_params=params(),
        cost_estimate=cost(2 * buffers * size * rows * width, 2 * (rows + buffers * size) * width),
        name="pick",
    )(me, in_hbm(adapter_row), in_hbm(tokens_now))
    order = far_first(buffers)
    arrived = [picked[0]] + [exchange(picked[j], "pool", pool, j) for j in order]

    up_share = columns // groups
    ranks_now, adapter_up_now, _ = lax.optimization_barrier((ranks, adapter_up, picked))
    up_part, factor = pl.pallas_call(
        functools.partial(up_share_kernel, cores),
        in_specs=[SMEM] * 3 + [HBM],
        out_specs=[VMEM] * 2,
        out_shape=[
            jax.ShapeDtypeStruct((local, rank, up_share), bf16),
            jax.ShapeDtypeStruct((local, rank), f32),
        ],
        scratch_shapes=[
            pltpu.VMEM((local, rank, up_share), bf16),
            pltpu.SemaphoreType.DMA,
        ],
        compiler_params=params(),
        cost_estimate=cost(local * rank * up_share, 4 * local * rank * up_share),
        name="up_share",
    )(group, core, ranks_now, in_hbm(adapter_up_now))
    far_up = exchange(up_part, "pool", pool, pool // 2)

    theirs, mine = pl.pallas_call(
        base_kernel,
        in_specs=[SMEM, HBM, HBM],
        out_specs=[VMEM] * 2,
        out_shape=[jax.ShapeDtypeStruct((rows, columns), f32)] * 2,
        scratch_shapes=[
            pltpu.VMEM((rows, width), bf16),
            pltpu.VMEM((2, width, columns), bf16),
            pltpu.SemaphoreType.DMA,
            pltpu.SemaphoreType.DMA((2, steps)),
        ],
        compiler_params=params(),
        cost_estimate=cost(4 * rows * width * columns, 4 * width * columns),
        name="base",
    )(core, in_hbm(tokens), in_hbm(key_value_weight))
    far_down, theirs = lax.optimization_barrier((far_down, theirs))
    far_downs = hand_round(far_down)
    far_up, _ = lax.optimization_barrier((far_up, far_down))
    far_ups = hand_round(far_up)
    half_dim = head // 2
    frequency = jnp.power(
        f32(ROPE_THETA), -jnp.arange(half_dim, dtype=f32) * (2.0 / head)
    )
    angles = positions.astype(f32)[:, None] * frequency[None, :]
    cosine, sine = jnp.cos(angles), jnp.sin(angles)
    cosine = jnp.concatenate([cosine, cosine], axis=1)
    sine = jnp.concatenate([-sine, sine], axis=1)

    arrived, far_ups, theirs, mine, cosine, sine = lax.optimization_barrier(
        (arrived, far_ups, theirs, mine, cosine, sine)
    )
    other = exchange(theirs, "tp", cores, 1)
    slots = buffers * size
    low = pl.pallas_call(
        functools.partial(down_kernel, buffers, groups, local, depth),
        in_specs=[SMEM] + [VMEM] * (1 + buffers + groups),
        out_specs=VMEM,
        out_shape=jax.ShapeDtypeStruct((slots, rank), f32),
        compiler_params=params(),
        cost_estimate=cost(4 * local * slots * rank * width, 2 * (slots + rank) * width),
        name="down",
    )(group, adapter_down, *arrived, *far_downs)
    low_other = exchange(low, "tp", cores, 1)

    terms = pl.pallas_call(
        functools.partial(up_kernel, buffers, groups, local, depth),
        in_specs=[SMEM] * 2 + [VMEM] * (4 + groups),
        out_specs=[VMEM] * buffers,
        out_shape=[jax.ShapeDtypeStruct((size, columns + LANES), jnp.int16)] * buffers,
        scratch_shapes=[pltpu.VMEM((slots, columns), f32)],
        compiler_params=params(),
        cost_estimate=cost(8 * local * slots * rank * columns, 2 * slots * columns),
        name="up",
    )(group, core, low, low_other, factor, adapter_up, *far_ups)
    order = return_order(buffers)
    returned = [terms[0]] + [exchange(terms[j], "pool", pool, j) for j in order]

    out = pl.pallas_call(
        functools.partial(finish_kernel, buffers, pool, local, depth),
        in_specs=[SMEM] + [VMEM] * (6 + buffers),
        out_specs=VMEM,
        out_shape=jax.ShapeDtypeStruct((rows, columns // (2 * head), 2, head), bf16),
        compiler_params=params(),
        cost_estimate=cost(4 * rows * slots * columns, 2 * slots * columns),
        name="finish",
    )(
        me,
        adapter_row,
        mine,
        other,
        cosine,
        sine,
        key_norm_gain.astype(f32)[None, :],
        *returned,
    )
    return out


def solution(mesh):
    return jax.shard_map(
        body,
        mesh=mesh,
        in_specs=(
            P(("groups", "pool"), "tp"),
            P(("groups", "pool"), None),
            P(("groups", "pool")),
            P("tp", None),
            P("pool", "tp", None),
            P("pool", None, None),
            P("pool"),
            P(),
        ),
        out_specs=P(("groups", "pool"), "tp", None, None),
        check_vma=False,
    )
```

```python
import functools

import jax
import jax.numpy as jnp
from jax import lax
from jax.experimental import pallas as pl
from jax.experimental.pallas import tpu as pltpu
from jax.sharding import PartitionSpec as P

ALPHA = 32
ROPE_THETA = 1000000.0
NORM_EPS = 1e-06
VMEM_LIMIT = 48 * 1024 * 1024
LANES = 128

VMEM = pl.BlockSpec(memory_space=pltpu.VMEM)
HBM = pl.BlockSpec(memory_space=pltpu.HBM)
SMEM = pl.BlockSpec(memory_space=pltpu.SMEM)


def params(**kw):
    return pltpu.CompilerParams(vmem_limit_bytes=VMEM_LIMIT, **kw)


def cost(flops, bytes_accessed):
    return pl.CostEstimate(flops=flops, bytes_accessed=bytes_accessed, transcendentals=0)


def in_hbm(x):
    return pltpu.with_memory_space_constraint(x, pltpu.HBM)


def iota(shape, dim):
    return lax.broadcasted_iota(jnp.int32, shape, dim)


def to_column(row):
    n = row.shape[1]
    return jnp.sum(
        jnp.where(iota((n, n), 0) == iota((n, n), 1), row, 0), axis=1, keepdims=True
    )


def slot_places(row, me, pool, local, depth):
    n = row.shape[1]
    column = to_column(row)
    earlier = (column == row) & (iota((n, n), 0) < iota((n, n), 1))
    slot = jnp.sum(jnp.where(earlier, 1, 0), axis=0, keepdims=True)
    holder = row // local
    apart = holder ^ me
    buffer, far = apart % (pool // 2), apart // (pool // 2)
    return ((buffer * 2 + far) * local + (row - holder * local)) * depth + slot


def far_first(count):
    return sorted(range(1, count), key=lambda j: (-bin(j).count("1"), j))


def return_order(count):
    order = far_first(count)
    return order[-1:] + order[:-1]


def halves(x):
    high = x.astype(jnp.bfloat16)
    low = (x - high.astype(jnp.float32)).astype(jnp.bfloat16)
    return high, low


def up_share_kernel(cores, group_ref, core_ref, ranks_ref, up_hbm, out_ref, factor_ref, own_ref, sem):
    local, rank, share = out_ref.shape
    at = core_ref[0] * (up_hbm.shape[2] // cores) + group_ref[0] * share
    copy = pltpu.make_async_copy(
        up_hbm.at[:, :, pl.ds(pl.multiple_of(at, share), share)], own_ref, sem
    )
    copy.start()
    copy.wait()
    for a in range(local):
        used = ranks_ref[a]

        def factor(shape, dim):
            scale = jnp.float32(ALPHA) / jnp.full(shape, used, jnp.int32).astype(jnp.float32)
            return jnp.where(iota(shape, dim) < used, scale, 0.0)

        factor_ref[a : a + 1, :] = factor((1, rank), 1)
        out_ref[a] = (own_ref[a].astype(jnp.float32) * factor((rank, 1), 0)).astype(jnp.bfloat16)


def pick_kernel(
    pool, local, depth, me_ref, group_ref, adapter_hbm, tokens_hbm, down_hbm, *refs
):
    share_ref, outs = refs[0], refs[1:-4]
    adapter_ref, tokens_ref, share_sem, sems = refs[-4:]
    rows, width = tokens_ref.shape
    share = share_ref.shape[1]
    parts = sems.shape[0] - 1
    part = rows // parts
    adapter_copy = pltpu.make_async_copy(adapter_hbm, adapter_ref, sems.at[parts])
    adapter_copy.start()
    copies = [
        pltpu.make_async_copy(
            tokens_hbm.at[pl.ds(i * part, part), :],
            tokens_ref.at[pl.ds(i * part, part), :],
            sems.at[i],
        )
        for i in range(parts)
    ]
    for copy in copies:
        copy.start()
    at = pl.multiple_of(group_ref[0] * share, share)
    share_copy = pltpu.make_async_copy(down_hbm.at[:, pl.ds(at, share), :], share_ref, share_sem)
    share_copy.start()
    adapter_copy.wait()
    place = slot_places(adapter_ref[...], me_ref[0], pool, local, depth)
    size = outs[0].shape[0]
    slots = len(outs) * size
    picker = jnp.where(iota((slots, rows), 0) == place, 1.0, 0.0).astype(jnp.bfloat16)
    for copy in copies:
        copy.wait()
    step = 512
    for at in range(0, width, step):
        block = jnp.dot(
            picker, tokens_ref[:, at : at + step], preferred_element_type=jnp.float32
        )
        for j, out in enumerate(outs):
            out[:, at : at + step] = block[j * size : (j + 1) * size].astype(jnp.bfloat16)
    share_copy.wait()


def base_kernel(
    core_ref,
    tokens_hbm,
    weight_hbm,
    down_hbm,
    up_hbm,
    theirs_ref,
    mine_ref,
    down_ref,
    up_ref,
    tokens_ref,
    weight_ref,
    other_sems,
    sems,
):
    rows, columns = mine_ref.shape
    steps = sems.shape[1]
    step = tokens_ref.shape[1] // steps
    copies = []
    for half in range(2):
        start = (1 - core_ref[0] if half == 0 else core_ref[0]) * columns
        start = pl.multiple_of(start, columns)
        for k in range(steps):
            copies.append(
                pltpu.make_async_copy(
                    weight_hbm.at[pl.ds(k * step, step), pl.ds(start, columns)],
                    weight_ref.at[half, pl.ds(k * step, step), :],
                    sems.at[half, k],
                )
            )
    tokens_copy = pltpu.make_async_copy(tokens_hbm, tokens_ref, other_sems.at[0])
    own = pl.multiple_of(core_ref[0] * columns, columns)
    factor_copies = [
        pltpu.make_async_copy(down_hbm, down_ref, other_sems.at[1]),
        pltpu.make_async_copy(up_hbm.at[:, :, pl.ds(own, columns)], up_ref, other_sems.at[2]),
    ]
    for copy in [tokens_copy] + copies + factor_copies:
        copy.start()
    tokens_copy.wait()
    for half, out in enumerate((theirs_ref, mine_ref)):
        for k in range(steps):
            copies[half * steps + k].wait()
            term = jnp.dot(
                tokens_ref[:, k * step : (k + 1) * step],
                weight_ref[half, k * step : (k + 1) * step, :],
                preferred_element_type=jnp.float32,
            )
            if k == 0:
                out[...] = term
            else:
                out[...] += term
    for copy in factor_copies:
        copy.wait()


def down_kernel(buffers, groups, local, depth, group_ref, down_ref, *refs):
    order = [0] + far_first(buffers)
    ins = [refs[order.index(j)] for j in range(buffers)]
    shares, out = refs[buffers : buffers + groups], refs[-1]
    rank = out.shape[1]
    share = shares[0].shape[1]
    total = None
    for k in range(groups):
        at = pl.multiple_of((group_ref[0] ^ k) * share, share)
        rows = jnp.concatenate([x[:, pl.ds(at, share)] for x in ins], axis=0)
        factors = [down_ref[a, pl.ds(at, share), :] for a in range(local)]
        factors += [shares[k][a] for a in range(local)]
        term = jnp.dot(
            rows, jnp.concatenate(factors, axis=1), preferred_element_type=jnp.float32
        )
        total = term if total is None else total + term
    which = (iota((total.shape[0], 1), 0) // depth) % (2 * local)
    low = total[:, :rank]
    for i in range(1, 2 * local):
        low = jnp.where(which == i, total[:, i * rank : (i + 1) * rank], low)
    out[...] = low


def up_kernel(
    buffers, groups, local, depth, group_ref, low_ref, other_ref, factor_ref, up_ref, *refs
):
    shares, outs, term_ref = refs[:groups], refs[groups : groups + buffers], refs[-1]
    rows, rank = low_ref.shape
    size = rows // buffers
    columns = term_ref.shape[1]
    share = columns // groups
    which = (iota((rows, 1), 0) // depth) % (2 * local)
    low = low_ref[...] + other_ref[...]
    for a in range(local):
        low = jnp.where(which == a, low * factor_ref[a : a + 1, :], low)
    both = jnp.concatenate(halves(low), axis=0)
    which = jnp.concatenate([which, which], axis=0)
    spread = jnp.concatenate(
        [jnp.where(which == i, both, jnp.zeros_like(both)) for i in range(2 * local)], axis=1
    )
    for k in range(groups):
        at = pl.multiple_of((group_ref[0] ^ k) * share, share)
        factors = [up_ref[a, :, pl.ds(at, share)] for a in range(local)]
        factors += [shares[k][a] for a in range(local)]
        term = jnp.dot(
            spread, jnp.concatenate(factors, axis=0), preferred_element_type=jnp.float32
        )
        term_ref[:, pl.ds(at, share)] = term[:rows] + term[rows:]
    for j, out in enumerate(outs):
        term = term_ref[j * size : (j + 1) * size, :]
        top = jnp.max(jnp.abs(term), axis=1, keepdims=True)
        exponent = jnp.ceil(jnp.log2(jnp.maximum(top, 1e-30)) + 1e-3)
        code = jnp.round(term * jnp.exp2(15.0 - exponent))
        code = jnp.clip(code, -32767.0, 32767.0)
        out[:, :columns] = code.astype(jnp.int32).astype(jnp.int16)
        out[:, columns:] = jnp.broadcast_to(
            exponent.astype(jnp.int32), (size, LANES)
        ).astype(jnp.int16)


def finish_kernel(
    buffers, pool, local, depth, me_ref, adapter_ref, mine_ref, other_ref, cos_ref, sin_ref, gain_ref, *refs
):
    order = [0] + return_order(buffers)
    ins, out_ref = [refs[order.index(j)] for j in range(buffers)], refs[-1]
    rows, columns = mine_ref.shape
    head = cos_ref.shape[1]
    place = to_column(slot_places(adapter_ref[...], me_ref[0], pool, local, depth))
    slots = buffers * ins[0].shape[0]
    picker = jnp.where(iota((rows, slots), 1) == place, 1.0, 0.0).astype(jnp.bfloat16)

    def picked(at, size):
        code = jnp.concatenate([x[:, at : at + size] for x in ins], axis=0).astype(jnp.int32)
        high = (code >> 8).astype(jnp.float32).astype(jnp.bfloat16)
        low = (code & 255).astype(jnp.float32).astype(jnp.bfloat16)
        high = jnp.dot(picker, high, preferred_element_type=jnp.float32)
        low = jnp.dot(picker, low, preferred_element_type=jnp.float32)
        return high * 256.0 + low

    scale = jnp.exp2(picked(columns, LANES)[:, :1] - 15.0)
    cosine, sine, gain = cos_ref[...], sin_ref[...], gain_ref[...]
    entries = []
    for at in range(0, columns, 2 * head):
        projected = mine_ref[:, at : at + 2 * head] + other_ref[:, at : at + 2 * head]
        projected = projected + picked(at, 2 * head) * scale
        key, value = projected[:, :head], projected[:, head:]
        mean = jnp.mean(key * key, axis=1, keepdims=True)
        normed = key * lax.rsqrt(mean + NORM_EPS) * gain
        rotated = normed * cosine + pltpu.roll(normed, head // 2, 1) * sine
        entries += [rotated.astype(jnp.bfloat16), value.astype(jnp.bfloat16)]
    kinds, block = len(entries), 16
    n = kinds * block
    source = (iota((n, n), 0) % kinds) * block + iota((n, n), 0) // kinds
    order = jnp.where(iota((n, n), 1) == source, 1.0, 0.0).astype(jnp.bfloat16)
    for i in range(rows // block):
        stacked = jnp.concatenate([e[i * block : (i + 1) * block] for e in entries], axis=0)
        mixed = jnp.dot(order, stacked, preferred_element_type=jnp.float32)
        out_ref[i * n : (i + 1) * n, :] = mixed.astype(jnp.bfloat16)


def body(
    tokens,
    row_adapters,
    positions,
    key_value_weight,
    adapter_down,
    adapter_up,
    ranks,
    key_norm_gain,
):
    pool = lax.axis_size("pool")
    groups = lax.axis_size("groups")
    cores = lax.axis_size("tp")
    rows, width = tokens.shape
    local = adapter_down.shape[0]
    adapters = local * pool
    columns = key_value_weight.shape[1] // cores
    rank = adapter_down.shape[2]
    head = key_norm_gain.shape[0]
    depth = max(2, 2 * rows // adapters)
    buffers = pool // 2
    size = 2 * local * depth
    f32, bf16 = jnp.float32, jnp.bfloat16

    me = lax.axis_index("pool").astype(jnp.int32)[None]
    core = lax.axis_index("tp").astype(jnp.int32)[None]
    group = lax.axis_index("groups").astype(jnp.int32)[None]

    def exchange(x, axis, count, j):
        return lax.ppermute(x, axis, [(p, p ^ j) for p in range(count)])

    def hand_round(share):
        return [share] + [exchange(share, "groups", groups, k) for k in range(1, groups)]

    adapter_row = row_adapters.reshape(1, rows)
    down_share = width // groups
    parts = rows // 16
    down_part, *picked = pl.pallas_call(
        functools.partial(pick_kernel, pool, local, depth),
        in_specs=[SMEM] * 2 + [HBM] * 3,
        out_specs=[VMEM] * (1 + buffers),
        out_shape=[jax.ShapeDtypeStruct((local, down_share, rank), bf16)]
        + [jax.ShapeDtypeStruct((size, width), bf16)] * buffers,
        scratch_shapes=[
            pltpu.VMEM((1, rows), jnp.int32),
            pltpu.VMEM((rows, width), bf16),
            pltpu.SemaphoreType.DMA,
            pltpu.SemaphoreType.DMA((parts + 1,)),
        ],
        compiler_params=params(),
        cost_estimate=cost(2 * buffers * size * rows * width, 2 * (rows + buffers * size) * width),
        name="pick",
    )(me, group, in_hbm(adapter_row), in_hbm(tokens), in_hbm(adapter_down))
    far_down = exchange(down_part, "pool", pool, pool // 2)
    order = far_first(buffers)
    arrived = [picked[0]] + [exchange(picked[j], "pool", pool, j) for j in order]

    up_share = columns // groups
    ranks_now, adapter_up_now, _ = lax.optimization_barrier((ranks, adapter_up, picked))
    up_part, factor = pl.pallas_call(
        functools.partial(up_share_kernel, cores),
        in_specs=[SMEM] * 3 + [HBM],
        out_specs=[VMEM] * 2,
        out_shape=[
            jax.ShapeDtypeStruct((local, rank, up_share), bf16),
            jax.ShapeDtypeStruct((local, rank), f32),
        ],
        scratch_shapes=[
            pltpu.VMEM((local, rank, up_share), bf16),
            pltpu.SemaphoreType.DMA,
        ],
        compiler_params=params(),
        cost_estimate=cost(local * rank * up_share, 4 * local * rank * up_share),
        name="up_share",
    )(group, core, ranks_now, in_hbm(adapter_up_now))
    far_up = exchange(up_part, "pool", pool, pool // 2)

    steps = 5
    theirs, mine, own_down, own_up = pl.pallas_call(
        base_kernel,
        in_specs=[SMEM] + [HBM] * 4,
        out_specs=[VMEM] * 4,
        out_shape=[jax.ShapeDtypeStruct((rows, columns), f32)] * 2
        + [
            jax.ShapeDtypeStruct(adapter_down.shape, bf16),
            jax.ShapeDtypeStruct((local, rank, columns), bf16),
        ],
        scratch_shapes=[
            pltpu.VMEM((rows, width), bf16),
            pltpu.VMEM((2, width, columns), bf16),
            pltpu.SemaphoreType.DMA((3,)),
            pltpu.SemaphoreType.DMA((2, steps)),
        ],
        compiler_params=params(),
        cost_estimate=cost(4 * rows * width * columns, 4 * width * columns),
        name="base",
    )(
        core,
        in_hbm(tokens),
        in_hbm(key_value_weight),
        in_hbm(adapter_down),
        in_hbm(adapter_up),
    )
    far_down, theirs = lax.optimization_barrier((far_down, theirs))
    far_downs = hand_round(far_down)
    far_up, _ = lax.optimization_barrier((far_up, far_down))
    far_ups = hand_round(far_up)
    half_dim = head // 2
    frequency = jnp.power(
        f32(ROPE_THETA), -jnp.arange(half_dim, dtype=f32) * (2.0 / head)
    )
    angles = positions.astype(f32)[:, None] * frequency[None, :]
    cosine, sine = jnp.cos(angles), jnp.sin(angles)
    cosine = jnp.concatenate([cosine, cosine], axis=1)
    sine = jnp.concatenate([-sine, sine], axis=1)

    arrived, far_ups, mine, cosine, sine = lax.optimization_barrier(
        (arrived, far_ups, mine, cosine, sine)
    )
    slots = buffers * size
    low = pl.pallas_call(
        functools.partial(down_kernel, buffers, groups, local, depth),
        in_specs=[SMEM] + [VMEM] * (1 + buffers + groups),
        out_specs=VMEM,
        out_shape=jax.ShapeDtypeStruct((slots, rank), f32),
        compiler_params=params(),
        cost_estimate=cost(4 * local * slots * rank * width, 2 * (slots + rank) * width),
        name="down",
    )(group, own_down, *arrived, *far_downs)
    low_other = exchange(low, "tp", cores, 1)

    terms = pl.pallas_call(
        functools.partial(up_kernel, buffers, groups, local, depth),
        in_specs=[SMEM] + [VMEM] * (4 + groups),
        out_specs=[VMEM] * buffers,
        out_shape=[jax.ShapeDtypeStruct((size, columns + LANES), jnp.int16)] * buffers,
        scratch_shapes=[pltpu.VMEM((slots, columns), f32)],
        compiler_params=params(),
        cost_estimate=cost(8 * local * slots * rank * columns, 2 * slots * columns),
        name="up",
    )(group, low, low_other, factor, own_up, *far_ups)
    terms, theirs = lax.optimization_barrier((terms, theirs))
    other = exchange(theirs, "tp", cores, 1)
    order = return_order(buffers)
    returned = [terms[0]] + [exchange(terms[j], "pool", pool, j) for j in order]

    out = pl.pallas_call(
        functools.partial(finish_kernel, buffers, pool, local, depth),
        in_specs=[SMEM] + [VMEM] * (6 + buffers),
        out_specs=VMEM,
        out_shape=jax.ShapeDtypeStruct((rows * columns // head, head), bf16),
        compiler_params=params(),
        cost_estimate=cost(4 * rows * slots * columns, 2 * slots * columns),
        name="finish",
    )(
        me,
        adapter_row,
        mine,
        other,
        cosine,
        sine,
        key_norm_gain.astype(f32)[None, :],
        *returned,
    )
    return out.reshape(rows, columns // (2 * head), 2, head)


def solution(mesh):
    return jax.shard_map(
        body,
        mesh=mesh,
        in_specs=(
            P(("groups", "pool"), "tp"),
            P(("groups", "pool"), None),
            P(("groups", "pool")),
            P("tp", None),
            P("pool", "tp", None),
            P("pool", None, None),
            P("pool"),
            P(),
        ),
        out_specs=P(("groups", "pool"), "tp", None, None),
        check_vma=False,
    )
```

```python
import functools

import jax
import jax.numpy as jnp
from jax import lax
from jax.experimental import pallas as pl
from jax.experimental.pallas import tpu as pltpu
from jax.sharding import PartitionSpec as P

ALPHA = 32
ROPE_THETA = 1000000.0
NORM_EPS = 1e-06
VMEM_LIMIT = 48 * 1024 * 1024
LANES = 128

VMEM = pl.BlockSpec(memory_space=pltpu.VMEM)
HBM = pl.BlockSpec(memory_space=pltpu.HBM)
SMEM = pl.BlockSpec(memory_space=pltpu.SMEM)


def params(**kw):
    return pltpu.CompilerParams(vmem_limit_bytes=VMEM_LIMIT, **kw)


def cost(flops, bytes_accessed):
    return pl.CostEstimate(flops=flops, bytes_accessed=bytes_accessed, transcendentals=0)


def in_hbm(x):
    return pltpu.with_memory_space_constraint(x, pltpu.HBM)


def iota(shape, dim):
    return lax.broadcasted_iota(jnp.int32, shape, dim)


def to_column(row):
    n = row.shape[1]
    return jnp.sum(
        jnp.where(iota((n, n), 0) == iota((n, n), 1), row, 0), axis=1, keepdims=True
    )


def slot_places(row, me, pool, local, depth):
    n = row.shape[1]
    column = to_column(row)
    earlier = (column == row) & (iota((n, n), 0) < iota((n, n), 1))
    slot = jnp.sum(jnp.where(earlier, 1, 0), axis=0, keepdims=True)
    holder = row // local
    apart = holder ^ me
    buffer, far = apart % (pool // 2), apart // (pool // 2)
    return ((buffer * 2 + far) * local + (row - holder * local)) * depth + slot


def far_first(count):
    return sorted(range(1, count), key=lambda j: (-bin(j).count("1"), j))


def return_order(count):
    order = far_first(count)
    return order[1:] + order[:1]


def halves(x):
    high = x.astype(jnp.bfloat16)
    low = (x - high.astype(jnp.float32)).astype(jnp.bfloat16)
    return high, low


def scale_up_kernel(core_ref, ranks_ref, up_hbm, out_ref, own_ref, sem):
    local, rank, columns = out_ref.shape
    at = pl.multiple_of(core_ref[0] * columns, columns)
    copy = pltpu.make_async_copy(up_hbm.at[:, :, pl.ds(at, columns)], own_ref, sem)
    copy.start()
    copy.wait()
    for a in range(local):
        used = ranks_ref[a]

        scale = jnp.float32(ALPHA) / jnp.full((rank, 1), used, jnp.int32).astype(jnp.float32)
        factor = jnp.where(iota((rank, 1), 0) < used, scale, 0.0)
        out_ref[a] = (own_ref[a].astype(jnp.float32) * factor).astype(jnp.bfloat16)


def pick_kernel(
    pool, local, depth, me_ref, group_ref, adapter_hbm, tokens_hbm, down_hbm, *refs
):
    share_ref, outs = refs[0], refs[1:-4]
    adapter_ref, tokens_ref, share_sem, sems = refs[-4:]
    rows, width = tokens_ref.shape
    share = share_ref.shape[1]
    parts = sems.shape[0] - 1
    part = rows // parts
    adapter_copy = pltpu.make_async_copy(adapter_hbm, adapter_ref, sems.at[parts])
    adapter_copy.start()
    copies = [
        pltpu.make_async_copy(
            tokens_hbm.at[pl.ds(i * part, part), :],
            tokens_ref.at[pl.ds(i * part, part), :],
            sems.at[i],
        )
        for i in range(parts)
    ]
    for copy in copies:
        copy.start()
    at = pl.multiple_of(group_ref[0] * share, share)
    share_copy = pltpu.make_async_copy(down_hbm.at[:, pl.ds(at, share), :], share_ref, share_sem)
    share_copy.start()
    adapter_copy.wait()
    place = slot_places(adapter_ref[...], me_ref[0], pool, local, depth)
    size = outs[0].shape[0]
    slots = len(outs) * size
    picker = jnp.where(iota((slots, rows), 0) == place, 1.0, 0.0).astype(jnp.bfloat16)
    for copy in copies:
        copy.wait()
    step = 512
    for at in range(0, width, step):
        block = jnp.dot(
            picker, tokens_ref[:, at : at + step], preferred_element_type=jnp.float32
        )
        for j, out in enumerate(outs):
            out[:, at : at + step] = block[j * size : (j + 1) * size].astype(jnp.bfloat16)
    share_copy.wait()


def base_kernel(
    core_ref,
    tokens_hbm,
    weight_hbm,
    down_hbm,
    theirs_ref,
    mine_ref,
    down_ref,
    tokens_ref,
    weight_ref,
    other_sems,
    sems,
):
    rows, columns = mine_ref.shape
    steps = sems.shape[1]
    step = tokens_ref.shape[1] // steps
    copies = []
    for half in range(2):
        start = (1 - core_ref[0] if half == 0 else core_ref[0]) * columns
        start = pl.multiple_of(start, columns)
        for k in range(steps):
            copies.append(
                pltpu.make_async_copy(
                    weight_hbm.at[pl.ds(k * step, step), pl.ds(start, columns)],
                    weight_ref.at[half, pl.ds(k * step, step), :],
                    sems.at[half, k],
                )
            )
    tokens_copy = pltpu.make_async_copy(tokens_hbm, tokens_ref, other_sems.at[0])
    down_copy = pltpu.make_async_copy(down_hbm, down_ref, other_sems.at[1])
    for copy in [tokens_copy] + copies + [down_copy]:
        copy.start()
    tokens_copy.wait()
    for half, out in enumerate((theirs_ref, mine_ref)):
        for k in range(steps):
            copies[half * steps + k].wait()
            term = jnp.dot(
                tokens_ref[:, k * step : (k + 1) * step],
                weight_ref[half, k * step : (k + 1) * step, :],
                preferred_element_type=jnp.float32,
            )
            if k == 0:
                out[...] = term
            else:
                out[...] += term
    down_copy.wait()


def down_kernel(buffers, groups, local, depth, group_ref, down_ref, *refs):
    order = [0] + far_first(buffers)
    ins = [refs[order.index(j)] for j in range(buffers)]
    shares, out = refs[buffers : buffers + groups], refs[-1]
    rank = out.shape[1]
    share = shares[0].shape[1]
    total = None
    for k in range(groups):
        at = pl.multiple_of((group_ref[0] ^ k) * share, share)
        rows = jnp.concatenate([x[:, pl.ds(at, share)] for x in ins], axis=0)
        factors = [down_ref[a, pl.ds(at, share), :] for a in range(local)]
        factors += [shares[k][a] for a in range(local)]
        term = jnp.dot(
            rows, jnp.concatenate(factors, axis=1), preferred_element_type=jnp.float32
        )
        total = term if total is None else total + term
    which = (iota((total.shape[0], 1), 0) // depth) % (2 * local)
    low = total[:, :rank]
    for i in range(1, 2 * local):
        low = jnp.where(which == i, total[:, i * rank : (i + 1) * rank], low)
    out[...] = low


def up_kernel(buffers, local, depth, low_ref, other_ref, up_ref, far_ref, *outs):
    rows, rank = low_ref.shape
    size = rows // buffers
    columns = up_ref.shape[2]
    both = jnp.concatenate(halves(low_ref[...] + other_ref[...]), axis=0)
    which = (iota((2 * rows, 1), 0) // depth) % (2 * local)
    spread = jnp.concatenate(
        [jnp.where(which == i, both, jnp.zeros_like(both)) for i in range(2 * local)], axis=1
    )
    factors = [up_ref[a] for a in range(local)] + [far_ref[a] for a in range(local)]
    term = jnp.dot(
        spread, jnp.concatenate(factors, axis=0), preferred_element_type=jnp.float32
    )
    term = term[:rows] + term[rows:]
    top = jnp.max(jnp.abs(term), axis=1, keepdims=True)
    exponent = jnp.ceil(jnp.log2(jnp.maximum(top, 1e-30)) + 1e-3)
    code = jnp.clip(jnp.round(term * jnp.exp2(15.0 - exponent)), -32767.0, 32767.0)
    code = code.astype(jnp.int32).astype(jnp.int16)
    exponent = jnp.broadcast_to(exponent.astype(jnp.int32), (rows, LANES)).astype(jnp.int16)
    for j, out in enumerate(outs):
        out[:, :columns] = code[j * size : (j + 1) * size]
        out[:, columns:] = exponent[j * size : (j + 1) * size]


def finish_kernel(
    buffers, pool, local, depth, me_ref, adapter_ref, mine_ref, other_ref, cos_ref, sin_ref, gain_ref, *refs
):
    order = [0] + return_order(buffers)
    ins = [refs[order.index(j)] for j in range(buffers)]
    out_hbm, out_ref, sems = refs[-3:]
    rows, columns = mine_ref.shape
    head = cos_ref.shape[1]
    place = to_column(slot_places(adapter_ref[...], me_ref[0], pool, local, depth))
    slots = buffers * ins[0].shape[0]
    picker = jnp.where(iota((rows, slots), 1) == place, 1.0, 0.0).astype(jnp.bfloat16)

    def picked(at, size):
        code = jnp.concatenate([x[:, at : at + size] for x in ins], axis=0).astype(jnp.int32)
        high = (code >> 8).astype(jnp.float32).astype(jnp.bfloat16)
        low = (code & 255).astype(jnp.float32).astype(jnp.bfloat16)
        high = jnp.dot(picker, high, preferred_element_type=jnp.float32)
        low = jnp.dot(picker, low, preferred_element_type=jnp.float32)
        return high * 256.0 + low

    scale = jnp.exp2(picked(columns, LANES)[:, :1] - 15.0)
    cosine, sine, gain = cos_ref[...], sin_ref[...], gain_ref[...]
    entries = []
    for at in range(0, columns, 2 * head):
        projected = mine_ref[:, at : at + 2 * head] + other_ref[:, at : at + 2 * head]
        projected = projected + picked(at, 2 * head) * scale
        key, value = projected[:, :head], projected[:, head:]
        mean = jnp.mean(key * key, axis=1, keepdims=True)
        normed = key * lax.rsqrt(mean + NORM_EPS) * gain
        rotated = normed * cosine + pltpu.roll(normed, head // 2, 1) * sine
        entries += [rotated.astype(jnp.bfloat16), value.astype(jnp.bfloat16)]
    kinds, block = len(entries), 16
    n = kinds * block
    source = (iota((n, n), 0) % kinds) * block + iota((n, n), 0) // kinds
    order = jnp.where(iota((n, n), 1) == source, 1.0, 0.0).astype(jnp.bfloat16)
    copies = []
    for i in range(rows // block):
        stacked = jnp.concatenate([e[i * block : (i + 1) * block] for e in entries], axis=0)
        mixed = jnp.dot(order, stacked, preferred_element_type=jnp.float32)
        out_ref[i * n : (i + 1) * n, :] = mixed.astype(jnp.bfloat16)
        if i % 2:
            done = pl.ds((i - 1) * n, 2 * n)
            copies.append(
                pltpu.make_async_copy(out_ref.at[done, :], out_hbm.at[done, :], sems.at[i // 2])
            )
            copies[-1].start()
    for copy in copies:
        copy.wait()


def body(
    tokens,
    row_adapters,
    positions,
    key_value_weight,
    adapter_down,
    adapter_up,
    ranks,
    key_norm_gain,
):
    pool = lax.axis_size("pool")
    groups = lax.axis_size("groups")
    cores = lax.axis_size("tp")
    rows, width = tokens.shape
    local = adapter_down.shape[0]
    adapters = local * pool
    columns = key_value_weight.shape[1] // cores
    rank = adapter_down.shape[2]
    head = key_norm_gain.shape[0]
    depth = max(2, 2 * rows // adapters)
    buffers = pool // 2
    size = 2 * local * depth
    f32, bf16 = jnp.float32, jnp.bfloat16

    me = lax.axis_index("pool").astype(jnp.int32)[None]
    core = lax.axis_index("tp").astype(jnp.int32)[None]
    group = lax.axis_index("groups").astype(jnp.int32)[None]

    def exchange(x, axis, count, j):
        return lax.ppermute(x, axis, [(p, p ^ j) for p in range(count)])

    def hand_round(share):
        return [share] + [exchange(share, "groups", groups, k) for k in range(1, groups)]

    adapter_row = row_adapters.reshape(1, rows)
    down_share = width // groups
    parts = rows // 16
    down_part, *picked = pl.pallas_call(
        functools.partial(pick_kernel, pool, local, depth),
        in_specs=[SMEM] * 2 + [HBM] * 3,
        out_specs=[VMEM] * (1 + buffers),
        out_shape=[jax.ShapeDtypeStruct((local, down_share, rank), bf16)]
        + [jax.ShapeDtypeStruct((size, width), bf16)] * buffers,
        scratch_shapes=[
            pltpu.VMEM((1, rows), jnp.int32),
            pltpu.VMEM((rows, width), bf16),
            pltpu.SemaphoreType.DMA,
            pltpu.SemaphoreType.DMA((parts + 1,)),
        ],
        compiler_params=params(),
        cost_estimate=cost(2 * buffers * size * rows * width, 2 * (rows + buffers * size) * width),
        name="pick",
    )(me, group, in_hbm(adapter_row), in_hbm(tokens), in_hbm(adapter_down))
    far_down = exchange(down_part, "pool", pool, pool // 2)
    order = far_first(buffers)
    arrived = [picked[0]] + [exchange(picked[j], "pool", pool, j) for j in order]

    ranks_now, adapter_up_now, _ = lax.optimization_barrier((ranks, adapter_up, picked))
    own_up = pl.pallas_call(
        scale_up_kernel,
        in_specs=[SMEM] * 2 + [HBM],
        out_specs=VMEM,
        out_shape=jax.ShapeDtypeStruct((local, rank, columns), bf16),
        scratch_shapes=[
            pltpu.VMEM((local, rank, columns), bf16),
            pltpu.SemaphoreType.DMA,
        ],
        compiler_params=params(),
        cost_estimate=cost(local * rank * columns, 4 * local * rank * columns),
        name="scale_up",
    )(core, ranks_now, in_hbm(adapter_up_now))
    far_up = exchange(own_up, "pool", pool, pool // 2)

    steps = 5
    theirs, mine, own_down = pl.pallas_call(
        base_kernel,
        in_specs=[SMEM] + [HBM] * 3,
        out_specs=[VMEM] * 3,
        out_shape=[jax.ShapeDtypeStruct((rows, columns), f32)] * 2
        + [jax.ShapeDtypeStruct(adapter_down.shape, bf16)],
        scratch_shapes=[
            pltpu.VMEM((rows, width), bf16),
            pltpu.VMEM((2, width, columns), bf16),
            pltpu.SemaphoreType.DMA((2,)),
            pltpu.SemaphoreType.DMA((2, steps)),
        ],
        compiler_params=params(),
        cost_estimate=cost(4 * rows * width * columns, 4 * width * columns),
        name="base",
    )(core, in_hbm(tokens), in_hbm(key_value_weight), in_hbm(adapter_down))
    far_down, theirs = lax.optimization_barrier((far_down, theirs))
    far_downs = hand_round(far_down)
    half_dim = head // 2
    frequency = jnp.power(
        f32(ROPE_THETA), -jnp.arange(half_dim, dtype=f32) * (2.0 / head)
    )
    angles = positions.astype(f32)[:, None] * frequency[None, :]
    cosine, sine = jnp.cos(angles), jnp.sin(angles)
    cosine = jnp.concatenate([cosine, cosine], axis=1)
    sine = jnp.concatenate([-sine, sine], axis=1)

    arrived, mine, cosine, sine = lax.optimization_barrier((arrived, mine, cosine, sine))
    slots = buffers * size
    low = pl.pallas_call(
        functools.partial(down_kernel, buffers, groups, local, depth),
        in_specs=[SMEM] + [VMEM] * (1 + buffers + groups),
        out_specs=VMEM,
        out_shape=jax.ShapeDtypeStruct((slots, rank), f32),
        compiler_params=params(),
        cost_estimate=cost(4 * local * slots * rank * width, 2 * (slots + rank) * width),
        name="down",
    )(group, own_down, *arrived, *far_downs)
    low_other = exchange(low, "tp", cores, 1)

    terms = pl.pallas_call(
        functools.partial(up_kernel, buffers, local, depth),
        in_specs=[VMEM] * 4,
        out_specs=[VMEM] * buffers,
        out_shape=[jax.ShapeDtypeStruct((size, columns + LANES), jnp.int16)] * buffers,
        compiler_params=params(),
        cost_estimate=cost(8 * local * slots * rank * columns, 2 * slots * columns),
        name="up",
    )(low, low_other, own_up, far_up)
    terms, theirs = lax.optimization_barrier((terms, theirs))
    other = exchange(theirs, "tp", cores, 1)
    order = return_order(buffers)
    returned = [terms[0]] + [exchange(terms[j], "pool", pool, j) for j in order]

    out = pl.pallas_call(
        functools.partial(finish_kernel, buffers, pool, local, depth),
        in_specs=[SMEM] + [VMEM] * (6 + buffers),
        out_specs=HBM,
        out_shape=jax.ShapeDtypeStruct((rows * columns // head, head), bf16),
        scratch_shapes=[
            pltpu.VMEM((rows * columns // head, head), bf16),
            pltpu.SemaphoreType.DMA((rows // 32,)),
        ],
        compiler_params=params(),
        cost_estimate=cost(4 * rows * slots * columns, 2 * slots * columns),
        name="finish",
    )(
        me,
        adapter_row,
        mine,
        other,
        cosine,
        sine,
        key_norm_gain.astype(f32)[None, :],
        *returned,
    )
    return out.reshape(rows, columns // (2 * head), 2, head)


def solution(mesh):
    return jax.shard_map(
        body,
        mesh=mesh,
        in_specs=(
            P(("groups", "pool"), "tp"),
            P(("groups", "pool"), None),
            P(("groups", "pool")),
            P("tp", None),
            P("pool", "tp", None),
            P("pool", None, None),
            P("pool"),
            P(),
        ),
        out_specs=P(("groups", "pool"), "tp", None, None),
        check_vma=False,
    )
```

```python
import functools

import jax
import jax.numpy as jnp
from jax import lax
from jax.experimental import pallas as pl
from jax.experimental.pallas import tpu as pltpu
from jax.sharding import PartitionSpec as P

ALPHA = 32
ROPE_THETA = 1000000.0
NORM_EPS = 1e-06
VMEM_LIMIT = 48 * 1024 * 1024
LANES = 128

VMEM = pl.BlockSpec(memory_space=pltpu.VMEM)
HBM = pl.BlockSpec(memory_space=pltpu.HBM)
SMEM = pl.BlockSpec(memory_space=pltpu.SMEM)


def params(**kw):
    return pltpu.CompilerParams(vmem_limit_bytes=VMEM_LIMIT, **kw)


def cost(flops, bytes_accessed):
    return pl.CostEstimate(flops=flops, bytes_accessed=bytes_accessed, transcendentals=0)


def in_hbm(x):
    return pltpu.with_memory_space_constraint(x, pltpu.HBM)


def iota(shape, dim):
    return lax.broadcasted_iota(jnp.int32, shape, dim)


def to_column(row):
    n = row.shape[1]
    return jnp.sum(
        jnp.where(iota((n, n), 0) == iota((n, n), 1), row, 0), axis=1, keepdims=True
    )


def slot_places(row, me, pool, local, depth):
    n = row.shape[1]
    column = to_column(row)
    earlier = (column == row) & (iota((n, n), 0) < iota((n, n), 1))
    slot = jnp.sum(jnp.where(earlier, 1, 0), axis=0, keepdims=True)
    holder = row // local
    apart = holder ^ me
    buffer, far = apart % (pool // 2), apart // (pool // 2)
    return ((buffer * 2 + far) * local + (row - holder * local)) * depth + slot


def far_first(count):
    return sorted(range(1, count), key=lambda j: (-bin(j).count("1"), -j))


def return_order(count):
    order = far_first(count)
    return order[1:] + order[:1]


def halves(x):
    high = x.astype(jnp.bfloat16)
    low = (x - high.astype(jnp.float32)).astype(jnp.bfloat16)
    return high, low


def scale_up_kernel(core_ref, ranks_ref, up_hbm, out_ref, own_ref, sem):
    local, rank, columns = out_ref.shape
    at = pl.multiple_of(core_ref[0] * columns, columns)
    copy = pltpu.make_async_copy(up_hbm.at[:, :, pl.ds(at, columns)], own_ref, sem)
    copy.start()
    copy.wait()
    for a in range(local):
        used = ranks_ref[a]

        scale = jnp.float32(ALPHA) / jnp.full((rank, 1), used, jnp.int32).astype(jnp.float32)
        factor = jnp.where(iota((rank, 1), 0) < used, scale, 0.0)
        out_ref[a] = (own_ref[a].astype(jnp.float32) * factor).astype(jnp.bfloat16)


def pick_kernel(
    pool, local, depth, me_ref, group_ref, adapter_hbm, tokens_hbm, down_hbm, *refs
):
    share_ref, outs = refs[0], refs[1:-4]
    adapter_ref, tokens_ref, share_sem, sems = refs[-4:]
    rows, width = tokens_ref.shape
    share = share_ref.shape[1]
    parts = sems.shape[0] - 1
    part = rows // parts
    adapter_copy = pltpu.make_async_copy(adapter_hbm, adapter_ref, sems.at[parts])
    adapter_copy.start()
    copies = [
        pltpu.make_async_copy(
            tokens_hbm.at[pl.ds(i * part, part), :],
            tokens_ref.at[pl.ds(i * part, part), :],
            sems.at[i],
        )
        for i in range(parts)
    ]
    for copy in copies:
        copy.start()
    at = pl.multiple_of(group_ref[0] * share, share)
    share_copy = pltpu.make_async_copy(down_hbm.at[:, pl.ds(at, share), :], share_ref, share_sem)
    share_copy.start()
    adapter_copy.wait()
    place = slot_places(adapter_ref[...], me_ref[0], pool, local, depth)
    size = outs[0].shape[0]
    slots = len(outs) * size
    picker = jnp.where(iota((slots, rows), 0) == place, 1.0, 0.0).astype(jnp.bfloat16)
    for copy in copies:
        copy.wait()
    step = 512
    for at in range(0, width, step):
        block = jnp.dot(
            picker, tokens_ref[:, at : at + step], preferred_element_type=jnp.float32
        )
        for j, out in enumerate(outs):
            out[:, at : at + step] = block[j * size : (j + 1) * size].astype(jnp.bfloat16)
    share_copy.wait()


def base_kernel(
    core_ref,
    tokens_hbm,
    weight_hbm,
    down_hbm,
    theirs_ref,
    mine_ref,
    down_ref,
    tokens_ref,
    weight_ref,
    other_sems,
    sems,
):
    rows, columns = mine_ref.shape
    steps = sems.shape[1]
    step = tokens_ref.shape[1] // steps
    copies = []
    for half in range(2):
        start = (1 - core_ref[0] if half == 0 else core_ref[0]) * columns
        start = pl.multiple_of(start, columns)
        for k in range(steps):
            copies.append(
                pltpu.make_async_copy(
                    weight_hbm.at[pl.ds(k * step, step), pl.ds(start, columns)],
                    weight_ref.at[half, pl.ds(k * step, step), :],
                    sems.at[half, k],
                )
            )
    tokens_copy = pltpu.make_async_copy(tokens_hbm, tokens_ref, other_sems.at[0])
    down_copy = pltpu.make_async_copy(down_hbm, down_ref, other_sems.at[1])
    for copy in [tokens_copy] + copies + [down_copy]:
        copy.start()
    tokens_copy.wait()
    for half, out in enumerate((theirs_ref, mine_ref)):
        for k in range(steps):
            copies[half * steps + k].wait()
            term = jnp.dot(
                tokens_ref[:, k * step : (k + 1) * step],
                weight_ref[half, k * step : (k + 1) * step, :],
                preferred_element_type=jnp.float32,
            )
            if k == 0:
                out[...] = term
            else:
                out[...] += term
    down_copy.wait()


def down_kernel(buffers, groups, local, depth, group_ref, down_ref, *refs):
    order = [0] + far_first(buffers)
    ins = [refs[order.index(j)] for j in range(buffers)]
    shares, out = refs[buffers : buffers + groups], refs[-1]
    rank = out.shape[1]
    share = shares[0].shape[1]
    total = None
    for k in range(groups):
        at = pl.multiple_of((group_ref[0] ^ k) * share, share)
        rows = jnp.concatenate([x[:, pl.ds(at, share)] for x in ins], axis=0)
        factors = [down_ref[a, pl.ds(at, share), :] for a in range(local)]
        factors += [shares[k][a] for a in range(local)]
        term = jnp.dot(
            rows, jnp.concatenate(factors, axis=1), preferred_element_type=jnp.float32
        )
        total = term if total is None else total + term
    which = (iota((total.shape[0], 1), 0) // depth) % (2 * local)
    low = total[:, :rank]
    for i in range(1, 2 * local):
        low = jnp.where(which == i, total[:, i * rank : (i + 1) * rank], low)
    out[...] = low


def up_kernel(buffers, local, depth, low_ref, other_ref, up_ref, far_ref, *outs):
    rows, rank = low_ref.shape
    size = rows // buffers
    columns = up_ref.shape[2]
    both = jnp.concatenate(halves(low_ref[...] + other_ref[...]), axis=0)
    which = (iota((2 * rows, 1), 0) // depth) % (2 * local)
    spread = jnp.concatenate(
        [jnp.where(which == i, both, jnp.zeros_like(both)) for i in range(2 * local)], axis=1
    )
    factors = [up_ref[a] for a in range(local)] + [far_ref[a] for a in range(local)]
    term = jnp.dot(
        spread, jnp.concatenate(factors, axis=0), preferred_element_type=jnp.float32
    )
    term = term[:rows] + term[rows:]
    top = jnp.max(jnp.abs(term), axis=1, keepdims=True)
    exponent = jnp.ceil(jnp.log2(jnp.maximum(top, 1e-30)) + 1e-3)
    code = jnp.clip(jnp.round(term * jnp.exp2(15.0 - exponent)), -32767.0, 32767.0)
    code = code.astype(jnp.int32).astype(jnp.int16)
    exponent = jnp.broadcast_to(exponent.astype(jnp.int32), (rows, LANES)).astype(jnp.int16)
    for j, out in enumerate(outs):
        out[:, :columns] = code[j * size : (j + 1) * size]
        out[:, columns:] = exponent[j * size : (j + 1) * size]


def finish_kernel(
    buffers, pool, local, depth, me_ref, adapter_ref, mine_ref, other_ref, cos_ref, sin_ref, gain_ref, *refs
):
    order = [0] + return_order(buffers)
    ins = [refs[order.index(j)] for j in range(buffers)]
    out_hbm, out_ref, sems = refs[-3:]
    rows, columns = mine_ref.shape
    head = cos_ref.shape[1]
    place = to_column(slot_places(adapter_ref[...], me_ref[0], pool, local, depth))
    slots = buffers * ins[0].shape[0]
    picker = jnp.where(iota((rows, slots), 1) == place, 1.0, 0.0).astype(jnp.bfloat16)

    def picked(at, size):
        code = jnp.concatenate([x[:, at : at + size] for x in ins], axis=0).astype(jnp.int32)
        high = (code >> 8).astype(jnp.float32).astype(jnp.bfloat16)
        low = (code & 255).astype(jnp.float32).astype(jnp.bfloat16)
        high = jnp.dot(picker, high, preferred_element_type=jnp.float32)
        low = jnp.dot(picker, low, preferred_element_type=jnp.float32)
        return high * 256.0 + low

    scale = jnp.exp2(picked(columns, LANES)[:, :1] - 15.0)
    cosine, sine, gain = cos_ref[...], sin_ref[...], gain_ref[...]
    entries = []
    for at in range(0, columns, 2 * head):
        projected = mine_ref[:, at : at + 2 * head] + other_ref[:, at : at + 2 * head]
        projected = projected + picked(at, 2 * head) * scale
        key, value = projected[:, :head], projected[:, head:]
        mean = jnp.mean(key * key, axis=1, keepdims=True)
        normed = key * lax.rsqrt(mean + NORM_EPS) * gain
        rotated = normed * cosine + pltpu.roll(normed, head // 2, 1) * sine
        entries += [rotated.astype(jnp.bfloat16), value.astype(jnp.bfloat16)]
    kinds, block = len(entries), 16
    n = kinds * block
    source = (iota((n, n), 0) % kinds) * block + iota((n, n), 0) // kinds
    order = jnp.where(iota((n, n), 1) == source, 1.0, 0.0).astype(jnp.bfloat16)
    copies = []
    for i in range(rows // block):
        stacked = jnp.concatenate([e[i * block : (i + 1) * block] for e in entries], axis=0)
        mixed = jnp.dot(order, stacked, preferred_element_type=jnp.float32)
        out_ref[i * n : (i + 1) * n, :] = mixed.astype(jnp.bfloat16)
        if i % 2:
            done = pl.ds((i - 1) * n, 2 * n)
            copies.append(
                pltpu.make_async_copy(out_ref.at[done, :], out_hbm.at[done, :], sems.at[i // 2])
            )
            copies[-1].start()
    for copy in copies:
        copy.wait()


def body(
    tokens,
    row_adapters,
    positions,
    key_value_weight,
    adapter_down,
    adapter_up,
    ranks,
    key_norm_gain,
):
    pool = lax.axis_size("pool")
    groups = lax.axis_size("groups")
    cores = lax.axis_size("tp")
    rows, width = tokens.shape
    local = adapter_down.shape[0]
    adapters = local * pool
    columns = key_value_weight.shape[1] // cores
    rank = adapter_down.shape[2]
    head = key_norm_gain.shape[0]
    depth = max(2, 2 * rows // adapters)
    buffers = pool // 2
    size = 2 * local * depth
    f32, bf16 = jnp.float32, jnp.bfloat16

    me = lax.axis_index("pool").astype(jnp.int32)[None]
    core = lax.axis_index("tp").astype(jnp.int32)[None]
    group = lax.axis_index("groups").astype(jnp.int32)[None]

    def exchange(x, axis, count, j):
        return lax.ppermute(x, axis, [(p, p ^ j) for p in range(count)])

    def hand_round(share):
        return [share] + [exchange(share, "groups", groups, k) for k in range(1, groups)]

    adapter_row = row_adapters.reshape(1, rows)
    down_share = width // groups
    parts = rows // 16
    down_part, *picked = pl.pallas_call(
        functools.partial(pick_kernel, pool, local, depth),
        in_specs=[SMEM] * 2 + [HBM] * 3,
        out_specs=[VMEM] * (1 + buffers),
        out_shape=[jax.ShapeDtypeStruct((local, down_share, rank), bf16)]
        + [jax.ShapeDtypeStruct((size, width), bf16)] * buffers,
        scratch_shapes=[
            pltpu.VMEM((1, rows), jnp.int32),
            pltpu.VMEM((rows, width), bf16),
            pltpu.SemaphoreType.DMA,
            pltpu.SemaphoreType.DMA((parts + 1,)),
        ],
        compiler_params=params(),
        cost_estimate=cost(2 * buffers * size * rows * width, 2 * (rows + buffers * size) * width),
        name="pick",
    )(me, group, in_hbm(adapter_row), in_hbm(tokens), in_hbm(adapter_down))
    far_down = exchange(down_part, "pool", pool, pool // 2)
    order = far_first(buffers)
    arrived = [picked[0]] + [exchange(picked[j], "pool", pool, j) for j in order]

    ranks_now, adapter_up_now, _ = lax.optimization_barrier((ranks, adapter_up, picked))
    own_up = pl.pallas_call(
        scale_up_kernel,
        in_specs=[SMEM] * 2 + [HBM],
        out_specs=VMEM,
        out_shape=jax.ShapeDtypeStruct((local, rank, columns), bf16),
        scratch_shapes=[
            pltpu.VMEM((local, rank, columns), bf16),
            pltpu.SemaphoreType.DMA,
        ],
        compiler_params=params(),
        cost_estimate=cost(local * rank * columns, 4 * local * rank * columns),
        name="scale_up",
    )(core, ranks_now, in_hbm(adapter_up_now))
    far_up = exchange(own_up, "pool", pool, pool // 2)

    steps = 5
    theirs, mine, own_down = pl.pallas_call(
        base_kernel,
        in_specs=[SMEM] + [HBM] * 3,
        out_specs=[VMEM] * 3,
        out_shape=[jax.ShapeDtypeStruct((rows, columns), f32)] * 2
        + [jax.ShapeDtypeStruct(adapter_down.shape, bf16)],
        scratch_shapes=[
            pltpu.VMEM((rows, width), bf16),
            pltpu.VMEM((2, width, columns), bf16),
            pltpu.SemaphoreType.DMA((2,)),
            pltpu.SemaphoreType.DMA((2, steps)),
        ],
        compiler_params=params(),
        cost_estimate=cost(4 * rows * width * columns, 4 * width * columns),
        name="base",
    )(core, in_hbm(tokens), in_hbm(key_value_weight), in_hbm(adapter_down))
    far_down, theirs = lax.optimization_barrier((far_down, theirs))
    far_downs = hand_round(far_down)
    half_dim = head // 2
    frequency = jnp.power(
        f32(ROPE_THETA), -jnp.arange(half_dim, dtype=f32) * (2.0 / head)
    )
    angles = positions.astype(f32)[:, None] * frequency[None, :]
    cosine, sine = jnp.cos(angles), jnp.sin(angles)
    cosine = jnp.concatenate([cosine, cosine], axis=1)
    sine = jnp.concatenate([-sine, sine], axis=1)

    arrived[1], theirs = lax.optimization_barrier((arrived[1], theirs))
    other = exchange(theirs, "tp", cores, 1)
    arrived, mine, cosine, sine = lax.optimization_barrier((arrived, mine, cosine, sine))
    slots = buffers * size
    low = pl.pallas_call(
        functools.partial(down_kernel, buffers, groups, local, depth),
        in_specs=[SMEM] + [VMEM] * (1 + buffers + groups),
        out_specs=VMEM,
        out_shape=jax.ShapeDtypeStruct((slots, rank), f32),
        compiler_params=params(),
        cost_estimate=cost(4 * local * slots * rank * width, 2 * (slots + rank) * width),
        name="down",
    )(group, own_down, *arrived, *far_downs)
    low_other = exchange(low, "tp", cores, 1)

    terms = pl.pallas_call(
        functools.partial(up_kernel, buffers, local, depth),
        in_specs=[VMEM] * 4,
        out_specs=[VMEM] * buffers,
        out_shape=[jax.ShapeDtypeStruct((size, columns + LANES), jnp.int16)] * buffers,
        compiler_params=params(),
        cost_estimate=cost(8 * local * slots * rank * columns, 2 * slots * columns),
        name="up",
    )(low, low_other, own_up, far_up)
    order = return_order(buffers)
    returned = [terms[0]] + [exchange(terms[j], "pool", pool, j) for j in order]

    out = pl.pallas_call(
        functools.partial(finish_kernel, buffers, pool, local, depth),
        in_specs=[SMEM] + [VMEM] * (6 + buffers),
        out_specs=HBM,
        out_shape=jax.ShapeDtypeStruct((rows * columns // head, head), bf16),
        scratch_shapes=[
            pltpu.VMEM((rows * columns // head, head), bf16),
            pltpu.SemaphoreType.DMA((rows // 32,)),
        ],
        compiler_params=params(),
        cost_estimate=cost(4 * rows * slots * columns, 2 * slots * columns),
        name="finish",
    )(
        me,
        adapter_row,
        mine,
        other,
        cosine,
        sine,
        key_norm_gain.astype(f32)[None, :],
        *returned,
    )
    return out.reshape(rows, columns // (2 * head), 2, head)


def solution(mesh):
    return jax.shard_map(
        body,
        mesh=mesh,
        in_specs=(
            P(("groups", "pool"), "tp"),
            P(("groups", "pool"), None),
            P(("groups", "pool")),
            P("tp", None),
            P("pool", "tp", None),
            P("pool", None, None),
            P("pool"),
            P(),
        ),
        out_specs=P(("groups", "pool"), "tp", None, None),
        check_vma=False,
    )
```

```python
import functools

import jax
import jax.numpy as jnp
from jax import lax
from jax.experimental import pallas as pl
from jax.experimental.pallas import tpu as pltpu
from jax.sharding import PartitionSpec as P

ALPHA = 32
ROPE_THETA = 1000000.0
NORM_EPS = 1e-06
VMEM_LIMIT = 48 * 1024 * 1024
LANES = 128
EXPONENT_BITS = 8
EXPONENT_BIAS = 128

VMEM = pl.BlockSpec(memory_space=pltpu.VMEM)
HBM = pl.BlockSpec(memory_space=pltpu.HBM)
SMEM = pl.BlockSpec(memory_space=pltpu.SMEM)


def params(**kw):
    return pltpu.CompilerParams(vmem_limit_bytes=VMEM_LIMIT, **kw)


def cost(flops, bytes_accessed):
    return pl.CostEstimate(flops=flops, bytes_accessed=bytes_accessed, transcendentals=0)


def in_hbm(x):
    return pltpu.with_memory_space_constraint(x, pltpu.HBM)


def iota(shape, dim):
    return lax.broadcasted_iota(jnp.int32, shape, dim)


def to_column(row):
    n = row.shape[1]
    return jnp.sum(
        jnp.where(iota((n, n), 0) == iota((n, n), 1), row, 0), axis=1, keepdims=True
    )


def slot_places(row, me, pool, local, depth):
    n = row.shape[1]
    column = to_column(row)
    earlier = (column == row) & (iota((n, n), 0) < iota((n, n), 1))
    slot = jnp.sum(jnp.where(earlier, 1, 0), axis=0, keepdims=True)
    holder = row // local
    apart = holder ^ me
    buffer, far = apart % (pool // 2), apart // (pool // 2)
    return ((buffer * 2 + far) * local + (row - holder * local)) * depth + slot


def far_first(count):
    return sorted(range(1, count), key=lambda j: (-bin(j).count("1"), -j))


def return_order(count):
    order = far_first(count)
    return order


def halves(x):
    high = x.astype(jnp.bfloat16)
    low = (x - high.astype(jnp.float32)).astype(jnp.bfloat16)
    return high, low


def pick_kernel(
    pool, local, depth, columns, me_ref, group_ref, core_ref, adapter_hbm, tokens_hbm, down_hbm, up_hbm, *refs
):
    down_ref, up_ref, outs = refs[0], refs[1], refs[2:-4]
    adapter_ref, tokens_ref, share_sems, sems = refs[-4:]
    rows, width = tokens_ref.shape
    down_share, up_share = down_ref.shape[1], up_ref.shape[2]
    parts = sems.shape[0] - 1
    part = rows // parts
    adapter_copy = pltpu.make_async_copy(adapter_hbm, adapter_ref, sems.at[parts])
    adapter_copy.start()
    copies = [
        pltpu.make_async_copy(
            tokens_hbm.at[pl.ds(i * part, part), :],
            tokens_ref.at[pl.ds(i * part, part), :],
            sems.at[i],
        )
        for i in range(parts)
    ]
    for copy in copies:
        copy.start()
    at = pl.multiple_of(group_ref[0] * down_share, down_share)
    up_at = pl.multiple_of(core_ref[0] * columns + group_ref[0] * up_share, up_share)
    share_copies = [
        pltpu.make_async_copy(
            down_hbm.at[:, pl.ds(at, down_share), :], down_ref, share_sems.at[0]
        ),
        pltpu.make_async_copy(
            up_hbm.at[:, :, pl.ds(up_at, up_share)], up_ref, share_sems.at[1]
        ),
    ]
    for copy in share_copies:
        copy.start()
    adapter_copy.wait()
    place = slot_places(adapter_ref[...], me_ref[0], pool, local, depth)
    size = outs[0].shape[0]
    slots = len(outs) * size
    picker = jnp.where(iota((slots, rows), 0) == place, 1.0, 0.0).astype(jnp.bfloat16)
    for copy in copies:
        copy.wait()
    step = 512
    for at in range(0, width, step):
        block = jnp.dot(
            picker, tokens_ref[:, at : at + step], preferred_element_type=jnp.float32
        )
        for j, out in enumerate(outs):
            out[:, at : at + step] = block[j * size : (j + 1) * size].astype(jnp.bfloat16)
    for copy in share_copies:
        copy.wait()


def base_kernel(
    core_ref,
    tokens_hbm,
    weight_hbm,
    down_hbm,
    up_hbm,
    theirs_ref,
    mine_ref,
    down_ref,
    up_ref,
    tokens_ref,
    weight_ref,
    other_sems,
    sems,
):
    rows, columns = mine_ref.shape
    steps = sems.shape[1]
    step = tokens_ref.shape[1] // steps
    copies = []
    for half in range(2):
        start = (1 - core_ref[0] if half == 0 else core_ref[0]) * columns
        start = pl.multiple_of(start, columns)
        for k in range(steps):
            copies.append(
                pltpu.make_async_copy(
                    weight_hbm.at[pl.ds(k * step, step), pl.ds(start, columns)],
                    weight_ref.at[half, pl.ds(k * step, step), :],
                    sems.at[half, k],
                )
            )
    tokens_copy = pltpu.make_async_copy(tokens_hbm, tokens_ref, other_sems.at[0])
    own = pl.multiple_of(core_ref[0] * columns, columns)
    factor_copies = [
        pltpu.make_async_copy(down_hbm, down_ref, other_sems.at[1]),
        pltpu.make_async_copy(up_hbm.at[:, :, pl.ds(own, columns)], up_ref, other_sems.at[2]),
    ]
    for copy in [tokens_copy] + copies + factor_copies:
        copy.start()
    tokens_copy.wait()
    for half, out in enumerate((theirs_ref, mine_ref)):
        for k in range(steps):
            copies[half * steps + k].wait()
            term = jnp.dot(
                tokens_ref[:, k * step : (k + 1) * step],
                weight_ref[half, k * step : (k + 1) * step, :],
                preferred_element_type=jnp.float32,
            )
            if k == 0:
                out[...] = term
            else:
                out[...] += term
    for copy in factor_copies:
        copy.wait()


def down_kernel(buffers, groups, local, depth, group_ref, down_ref, *refs):
    order = [0] + far_first(buffers)
    ins = [refs[order.index(j)] for j in range(buffers)]
    shares, out = refs[buffers : buffers + groups], refs[-1]
    rank = out.shape[1]
    share = shares[0].shape[1]
    total = None
    for k in range(groups):
        at = pl.multiple_of((group_ref[0] ^ k) * share, share)
        rows = jnp.concatenate([x[:, pl.ds(at, share)] for x in ins], axis=0)
        factors = [down_ref[a, pl.ds(at, share), :] for a in range(local)]
        factors += [shares[k][a] for a in range(local)]
        term = jnp.dot(
            rows, jnp.concatenate(factors, axis=1), preferred_element_type=jnp.float32
        )
        total = term if total is None else total + term
    which = (iota((total.shape[0], 1), 0) // depth) % (2 * local)
    low = total[:, :rank]
    for i in range(1, 2 * local):
        low = jnp.where(which == i, total[:, i * rank : (i + 1) * rank], low)
    out[...] = low


def up_kernel(
    buffers, groups, local, depth, group_ref, low_ref, other_ref, factor_ref, far_factor_ref, up_ref, *refs
):
    shares, outs, term_ref = refs[:groups], refs[groups : groups + buffers], refs[-1]
    rows, rank = low_ref.shape
    size = rows // buffers
    columns = up_ref.shape[2]
    share = columns // groups
    which = (iota((rows, 1), 0) // depth) % (2 * local)
    low = low_ref[...] + other_ref[...]
    factors = [factor_ref[a : a + 1, :] for a in range(local)]
    factors += [far_factor_ref[a : a + 1, :] for a in range(local)]
    scale = factors[0]
    for i in range(1, 2 * local):
        scale = jnp.where(which == i, factors[i], scale)
    both = jnp.concatenate(halves(low * scale), axis=0)
    which = jnp.concatenate([which, which], axis=0)
    spread = jnp.concatenate(
        [jnp.where(which == i, both, jnp.zeros_like(both)) for i in range(2 * local)], axis=1
    )
    for k in range(groups):
        at = pl.multiple_of((group_ref[0] ^ k) * share, share)
        up = [up_ref[a, :, pl.ds(at, share)] for a in range(local)]
        up += [shares[k][a] for a in range(local)]
        term = jnp.dot(
            spread, jnp.concatenate(up, axis=0), preferred_element_type=jnp.float32
        )
        term_ref[:, pl.ds(at, share)] = term[:rows] + term[rows:]
    lane = iota((1, LANES), 1)
    for j, out in enumerate(outs):
        term = term_ref[j * size : (j + 1) * size, :]
        top = jnp.max(jnp.abs(term), axis=1, keepdims=True)
        exponent = jnp.ceil(jnp.log2(jnp.maximum(top, 1e-30)) + 1e-3)
        code = jnp.clip(jnp.round(term * jnp.exp2(15.0 - exponent)), -32767.0, 32767.0)
        code = code.astype(jnp.int32)
        biased = exponent.astype(jnp.int32) + EXPONENT_BIAS
        first = code[:, :LANES]
        marked = (first & -2) | ((biased >> jnp.minimum(lane, EXPONENT_BITS - 1)) & 1)
        first = jnp.where(lane < EXPONENT_BITS, marked, first)
        out[:, :LANES] = first.astype(jnp.int16)
        out[:, LANES:] = code[:, LANES:].astype(jnp.int16)


def finish_kernel(
    buffers, pool, local, depth, me_ref, adapter_ref, mine_ref, other_ref, cos_ref, sin_ref, gain_ref, *refs
):
    order = [0] + return_order(buffers)
    ins = [refs[order.index(j)] for j in range(buffers)]
    out_hbm, out_ref, sems = refs[-3:]
    rows, columns = mine_ref.shape
    head = cos_ref.shape[1]
    place = to_column(slot_places(adapter_ref[...], me_ref[0], pool, local, depth))
    slots = buffers * ins[0].shape[0]
    picker = jnp.where(iota((rows, slots), 1) == place, 1.0, 0.0).astype(jnp.bfloat16)

    def picked(at, size):
        code = jnp.concatenate([x[:, at : at + size] for x in ins], axis=0).astype(jnp.int32)
        high = (code >> 8).astype(jnp.float32).astype(jnp.bfloat16)
        low = (code & 255).astype(jnp.float32).astype(jnp.bfloat16)
        high = jnp.dot(picker, high, preferred_element_type=jnp.float32)
        low = jnp.dot(picker, low, preferred_element_type=jnp.float32)
        return high * 256.0 + low

    lane = iota((1, LANES), 1)
    bits = picked(0, LANES).astype(jnp.int32) & 1
    bits = jnp.where(lane < EXPONENT_BITS, bits << jnp.minimum(lane, EXPONENT_BITS - 1), 0)
    exponent = jnp.sum(bits.astype(jnp.float32), axis=1, keepdims=True) - EXPONENT_BIAS
    scale = jnp.exp2(exponent - 15.0)
    cosine, sine, gain = cos_ref[...], sin_ref[...], gain_ref[...]
    entries = []
    for at in range(0, columns, 2 * head):
        projected = mine_ref[:, at : at + 2 * head] + other_ref[:, at : at + 2 * head]
        projected = projected + picked(at, 2 * head) * scale
        key, value = projected[:, :head], projected[:, head:]
        mean = jnp.mean(key * key, axis=1, keepdims=True)
        normed = key * lax.rsqrt(mean + NORM_EPS) * gain
        rotated = normed * cosine + pltpu.roll(normed, head // 2, 1) * sine
        entries += [rotated.astype(jnp.bfloat16), value.astype(jnp.bfloat16)]
    kinds, block = len(entries), 16
    n = kinds * block
    source = (iota((n, n), 0) % kinds) * block + iota((n, n), 0) // kinds
    order = jnp.where(iota((n, n), 1) == source, 1.0, 0.0).astype(jnp.bfloat16)
    copies = []
    for i in range(rows // block):
        stacked = jnp.concatenate([e[i * block : (i + 1) * block] for e in entries], axis=0)
        mixed = jnp.dot(order, stacked, preferred_element_type=jnp.float32)
        out_ref[i * n : (i + 1) * n, :] = mixed.astype(jnp.bfloat16)
        if i % 2:
            done = pl.ds((i - 1) * n, 2 * n)
            copies.append(
                pltpu.make_async_copy(out_ref.at[done, :], out_hbm.at[done, :], sems.at[i // 2])
            )
            copies[-1].start()
    for copy in copies:
        copy.wait()


def body(
    tokens,
    row_adapters,
    positions,
    key_value_weight,
    adapter_down,
    adapter_up,
    ranks,
    key_norm_gain,
):
    pool = lax.axis_size("pool")
    groups = lax.axis_size("groups")
    cores = lax.axis_size("tp")
    rows, width = tokens.shape
    local = adapter_down.shape[0]
    adapters = local * pool
    columns = key_value_weight.shape[1] // cores
    rank = adapter_down.shape[2]
    head = key_norm_gain.shape[0]
    depth = max(2, 2 * rows // adapters)
    buffers = pool // 2
    size = 2 * local * depth
    f32, bf16 = jnp.float32, jnp.bfloat16

    me = lax.axis_index("pool").astype(jnp.int32)[None]
    core = lax.axis_index("tp").astype(jnp.int32)[None]
    group = lax.axis_index("groups").astype(jnp.int32)[None]

    def exchange(x, axis, count, j):
        return lax.ppermute(x, axis, [(p, p ^ j) for p in range(count)])

    def hand_round(share):
        return [share] + [exchange(share, "groups", groups, k) for k in range(1, groups)]

    adapter_row = row_adapters.reshape(1, rows)
    down_share = width // groups
    parts = rows // 16
    up_share = columns // groups
    down_part, up_part, *picked = pl.pallas_call(
        functools.partial(pick_kernel, pool, local, depth, columns),
        in_specs=[SMEM] * 3 + [HBM] * 4,
        out_specs=[VMEM] * (2 + buffers),
        out_shape=[
            jax.ShapeDtypeStruct((local, down_share, rank), bf16),
            jax.ShapeDtypeStruct((local, rank, up_share), bf16),
        ]
        + [jax.ShapeDtypeStruct((size, width), bf16)] * buffers,
        scratch_shapes=[
            pltpu.VMEM((1, rows), jnp.int32),
            pltpu.VMEM((rows, width), bf16),
            pltpu.SemaphoreType.DMA((2,)),
            pltpu.SemaphoreType.DMA((parts + 1,)),
        ],
        compiler_params=params(),
        cost_estimate=cost(2 * buffers * size * rows * width, 2 * (rows + buffers * size) * width),
        name="pick",
    )(
        me,
        group,
        core,
        in_hbm(adapter_row),
        in_hbm(tokens),
        in_hbm(adapter_down),
        in_hbm(adapter_up),
    )
    far_down = exchange(down_part, "pool", pool, pool // 2)
    far_up = exchange(up_part, "pool", pool, pool // 2)
    order = far_first(buffers)
    arrived = [picked[0]] + [exchange(picked[j], "pool", pool, j) for j in order]

    steps = 5
    theirs, mine, own_down, own_up = pl.pallas_call(
        base_kernel,
        in_specs=[SMEM] + [HBM] * 4,
        out_specs=[VMEM] * 4,
        out_shape=[jax.ShapeDtypeStruct((rows, columns), f32)] * 2
        + [
            jax.ShapeDtypeStruct(adapter_down.shape, bf16),
            jax.ShapeDtypeStruct((local, rank, columns), bf16),
        ],
        scratch_shapes=[
            pltpu.VMEM((rows, width), bf16),
            pltpu.VMEM((2, width, columns), bf16),
            pltpu.SemaphoreType.DMA((3,)),
            pltpu.SemaphoreType.DMA((2, steps)),
        ],
        compiler_params=params(),
        cost_estimate=cost(4 * rows * width * columns, 4 * width * columns),
        name="base",
    )(
        core,
        in_hbm(tokens),
        in_hbm(key_value_weight),
        in_hbm(adapter_down),
        in_hbm(adapter_up),
    )
    far_down, theirs = lax.optimization_barrier((far_down, theirs))
    far_downs = hand_round(far_down)
    far_up, _ = lax.optimization_barrier((far_up, far_down))
    far_ups = hand_round(far_up)
    mask = (jnp.arange(rank, dtype=jnp.int32)[None, :] < ranks[:, None]).astype(f32)
    factor = mask * (f32(ALPHA) / ranks.astype(f32))[:, None]
    factor, _ = lax.optimization_barrier((factor, arrived[1]))
    far_factor = exchange(factor, "pool", pool, pool // 2)

    half_dim = head // 2
    frequency = jnp.power(
        f32(ROPE_THETA), -jnp.arange(half_dim, dtype=f32) * (2.0 / head)
    )
    angles = positions.astype(f32)[:, None] * frequency[None, :]
    cosine, sine = jnp.cos(angles), jnp.sin(angles)
    cosine = jnp.concatenate([cosine, cosine], axis=1)
    sine = jnp.concatenate([-sine, sine], axis=1)

    arrived[-1], theirs = lax.optimization_barrier((arrived[-1], theirs))
    other = exchange(theirs, "tp", cores, 1)
    arrived, far_ups, far_factor, mine, cosine, sine = lax.optimization_barrier(
        (arrived, far_ups, far_factor, mine, cosine, sine)
    )
    slots = buffers * size
    low = pl.pallas_call(
        functools.partial(down_kernel, buffers, groups, local, depth),
        in_specs=[SMEM] + [VMEM] * (1 + buffers + groups),
        out_specs=VMEM,
        out_shape=jax.ShapeDtypeStruct((slots, rank), f32),
        compiler_params=params(),
        cost_estimate=cost(4 * local * slots * rank * width, 2 * (slots + rank) * width),
        name="down",
    )(group, own_down, *arrived, *far_downs)
    low_other = exchange(low, "tp", cores, 1)

    terms = pl.pallas_call(
        functools.partial(up_kernel, buffers, groups, local, depth),
        in_specs=[SMEM] + [VMEM] * (5 + groups),
        out_specs=[VMEM] * buffers,
        out_shape=[jax.ShapeDtypeStruct((size, columns), jnp.int16)] * buffers,
        scratch_shapes=[pltpu.VMEM((slots, columns), f32)],
        compiler_params=params(),
        cost_estimate=cost(8 * local * slots * rank * columns, 2 * slots * columns),
        name="up",
    )(group, low, low_other, factor, far_factor, own_up, *far_ups)
    order = return_order(buffers)
    returned = [terms[0]] + [exchange(terms[j], "pool", pool, j) for j in order]

    out = pl.pallas_call(
        functools.partial(finish_kernel, buffers, pool, local, depth),
        in_specs=[SMEM] + [VMEM] * (6 + buffers),
        out_specs=HBM,
        out_shape=jax.ShapeDtypeStruct((rows * columns // head, head), bf16),
        scratch_shapes=[
            pltpu.VMEM((rows * columns // head, head), bf16),
            pltpu.SemaphoreType.DMA((rows // 32,)),
        ],
        compiler_params=params(),
        cost_estimate=cost(4 * rows * slots * columns, 2 * slots * columns),
        name="finish",
    )(
        me,
        adapter_row,
        mine,
        other,
        cosine,
        sine,
        key_norm_gain.astype(f32)[None, :],
        *returned,
    )
    return out.reshape(rows, columns // (2 * head), 2, head)


def solution(mesh):
    return jax.shard_map(
        body,
        mesh=mesh,
        in_specs=(
            P(("groups", "pool"), "tp"),
            P(("groups", "pool"), None),
            P(("groups", "pool")),
            P("tp", None),
            P("pool", "tp", None),
            P("pool", None, None),
            P("pool"),
            P(),
        ),
        out_specs=P(("groups", "pool"), "tp", None, None),
        check_vma=False,
    )
```

```python
import functools

import jax
import jax.numpy as jnp
from jax import lax
from jax.experimental import pallas as pl
from jax.experimental.pallas import tpu as pltpu
from jax.sharding import PartitionSpec as P

ALPHA = 32
ROPE_THETA = 1000000.0
NORM_EPS = 1e-06
VMEM_LIMIT = 48 * 1024 * 1024
LANES = 128
CHUNKS = 2
EXPONENT_BITS = 8
EXPONENT_BIAS = 128

VMEM = pl.BlockSpec(memory_space=pltpu.VMEM)
HBM = pl.BlockSpec(memory_space=pltpu.HBM)
SMEM = pl.BlockSpec(memory_space=pltpu.SMEM)


def params(**kw):
    return pltpu.CompilerParams(vmem_limit_bytes=VMEM_LIMIT, **kw)


def cost(flops, bytes_accessed):
    return pl.CostEstimate(flops=flops, bytes_accessed=bytes_accessed, transcendentals=0)


def in_hbm(x):
    return pltpu.with_memory_space_constraint(x, pltpu.HBM)


def iota(shape, dim):
    return lax.broadcasted_iota(jnp.int32, shape, dim)


def to_column(row):
    n = row.shape[1]
    return jnp.sum(
        jnp.where(iota((n, n), 0) == iota((n, n), 1), row, 0), axis=1, keepdims=True
    )


def slot_places(row, me, pool, local, depth):
    n = row.shape[1]
    column = to_column(row)
    earlier = (column == row) & (iota((n, n), 0) < iota((n, n), 1))
    slot = jnp.sum(jnp.where(earlier, 1, 0), axis=0, keepdims=True)
    holder = row // local
    apart = holder ^ me
    buffer, far = apart % (pool // 2), apart // (pool // 2)
    return ((buffer * 2 + far) * local + (row - holder * local)) * depth + slot


def chunk_places(share):
    first = (share // LANES + 1) // 2 * LANES
    return [(0, first), (first, share - first)]


def far_first(count):
    return sorted(range(1, count), key=lambda j: (-bin(j).count("1"), -j))


def return_order(count):
    order = far_first(count)
    return order


def halves(x):
    high = x.astype(jnp.bfloat16)
    low = (x - high.astype(jnp.float32)).astype(jnp.bfloat16)
    return high, low


def pick_kernel(
    pool, local, depth, columns, me_ref, group_ref, core_ref, adapter_hbm, tokens_hbm, down_hbm, up_hbm, *refs
):
    up_ref, down_refs, outs = refs[0], refs[1 : 1 + CHUNKS], refs[1 + CHUNKS : -4]
    adapter_ref, tokens_ref, share_sems, sems = refs[-4:]
    rows, width = tokens_ref.shape
    up_share = up_ref.shape[2]
    parts = sems.shape[0] - 1
    part = rows // parts
    adapter_copy = pltpu.make_async_copy(adapter_hbm, adapter_ref, sems.at[parts])
    adapter_copy.start()
    copies = [
        pltpu.make_async_copy(
            tokens_hbm.at[pl.ds(i * part, part), :],
            tokens_ref.at[pl.ds(i * part, part), :],
            sems.at[i],
        )
        for i in range(parts)
    ]
    for copy in copies:
        copy.start()
    up_at = pl.multiple_of(core_ref[0] * columns + group_ref[0] * up_share, up_share)
    share_copies = [
        pltpu.make_async_copy(
            up_hbm.at[:, :, pl.ds(up_at, up_share)], up_ref, share_sems.at[0]
        ),
    ]
    share = sum(ref.shape[1] for ref in down_refs)
    for c, (offset, chunk) in enumerate(chunk_places(share)):
        at = pl.multiple_of(group_ref[0] * share + offset, LANES)
        share_copies.append(
            pltpu.make_async_copy(
                down_hbm.at[:, pl.ds(at, chunk), :], down_refs[c], share_sems.at[1 + c]
            )
        )
    for copy in share_copies:
        copy.start()
    adapter_copy.wait()
    place = slot_places(adapter_ref[...], me_ref[0], pool, local, depth)
    size = outs[0].shape[0]
    slots = len(outs) * size
    picker = jnp.where(iota((slots, rows), 0) == place, 1.0, 0.0).astype(jnp.bfloat16)
    for copy in copies:
        copy.wait()
    step = 512
    for at in range(0, width, step):
        block = jnp.dot(
            picker, tokens_ref[:, at : at + step], preferred_element_type=jnp.float32
        )
        for j, out in enumerate(outs):
            out[:, at : at + step] = block[j * size : (j + 1) * size].astype(jnp.bfloat16)
    for copy in share_copies:
        copy.wait()


def base_kernel(
    core_ref,
    tokens_hbm,
    weight_hbm,
    down_hbm,
    up_hbm,
    theirs_ref,
    mine_ref,
    down_ref,
    up_ref,
    tokens_ref,
    weight_ref,
    other_sems,
    sems,
):
    rows, columns = mine_ref.shape
    steps = sems.shape[1]
    step = tokens_ref.shape[1] // steps
    copies = []
    for half in range(2):
        start = (1 - core_ref[0] if half == 0 else core_ref[0]) * columns
        start = pl.multiple_of(start, columns)
        for k in range(steps):
            copies.append(
                pltpu.make_async_copy(
                    weight_hbm.at[pl.ds(k * step, step), pl.ds(start, columns)],
                    weight_ref.at[half, pl.ds(k * step, step), :],
                    sems.at[half, k],
                )
            )
    tokens_copy = pltpu.make_async_copy(tokens_hbm, tokens_ref, other_sems.at[0])
    own = pl.multiple_of(core_ref[0] * columns, columns)
    factor_copies = [
        pltpu.make_async_copy(down_hbm, down_ref, other_sems.at[1]),
        pltpu.make_async_copy(up_hbm.at[:, :, pl.ds(own, columns)], up_ref, other_sems.at[2]),
    ]
    for copy in [tokens_copy] + copies + factor_copies:
        copy.start()
    tokens_copy.wait()
    for half, out in enumerate((theirs_ref, mine_ref)):
        for k in range(steps):
            copies[half * steps + k].wait()
            term = jnp.dot(
                tokens_ref[:, k * step : (k + 1) * step],
                weight_ref[half, k * step : (k + 1) * step, :],
                preferred_element_type=jnp.float32,
            )
            if k == 0:
                out[...] = term
            else:
                out[...] += term
    for copy in factor_copies:
        copy.wait()


def down_kernel(buffers, groups, local, depth, group_ref, down_ref, *refs):
    order = [0] + far_first(buffers)
    ins = [refs[order.index(j)] for j in range(buffers)]
    shares, out = refs[buffers:-1], refs[-1]
    rank = out.shape[1]
    share = ins[0].shape[1] // groups
    total = None
    for k in range(groups * CHUNKS):
        offset, chunk = chunk_places(share)[k // groups]
        at = pl.multiple_of((group_ref[0] ^ (k % groups)) * share + offset, LANES)
        rows = jnp.concatenate([x[:, pl.ds(at, chunk)] for x in ins], axis=0)
        factors = [down_ref[a, pl.ds(at, chunk), :] for a in range(local)]
        factors += [shares[k][a] for a in range(local)]
        term = jnp.dot(
            rows, jnp.concatenate(factors, axis=1), preferred_element_type=jnp.float32
        )
        total = term if total is None else total + term
    which = (iota((total.shape[0], 1), 0) // depth) % (2 * local)
    low = total[:, :rank]
    for i in range(1, 2 * local):
        low = jnp.where(which == i, total[:, i * rank : (i + 1) * rank], low)
    out[...] = low


def up_kernel(
    buffers, groups, local, depth, group_ref, low_ref, other_ref, factor_ref, far_factor_ref, up_ref, *refs
):
    shares, outs, term_ref = refs[:groups], refs[groups : groups + buffers], refs[-1]
    rows, rank = low_ref.shape
    size = rows // buffers
    columns = up_ref.shape[2]
    share = columns // groups
    which = (iota((rows, 1), 0) // depth) % (2 * local)
    low = low_ref[...] + other_ref[...]
    factors = [factor_ref[a : a + 1, :] for a in range(local)]
    factors += [far_factor_ref[a : a + 1, :] for a in range(local)]
    scale = factors[0]
    for i in range(1, 2 * local):
        scale = jnp.where(which == i, factors[i], scale)
    both = jnp.concatenate(halves(low * scale), axis=0)
    which = jnp.concatenate([which, which], axis=0)
    spread = jnp.concatenate(
        [jnp.where(which == i, both, jnp.zeros_like(both)) for i in range(2 * local)], axis=1
    )
    for k in range(groups):
        at = pl.multiple_of((group_ref[0] ^ k) * share, share)
        up = [up_ref[a, :, pl.ds(at, share)] for a in range(local)]
        up += [shares[k][a] for a in range(local)]
        term = jnp.dot(
            spread, jnp.concatenate(up, axis=0), preferred_element_type=jnp.float32
        )
        term_ref[:, pl.ds(at, share)] = term[:rows] + term[rows:]
    lane = iota((1, LANES), 1)
    for j, out in enumerate(outs):
        term = term_ref[j * size : (j + 1) * size, :]
        top = jnp.max(jnp.abs(term), axis=1, keepdims=True)
        exponent = jnp.ceil(jnp.log2(jnp.maximum(top, 1e-30)) + 1e-3)
        code = jnp.clip(jnp.round(term * jnp.exp2(15.0 - exponent)), -32767.0, 32767.0)
        code = code.astype(jnp.int32)
        biased = exponent.astype(jnp.int32) + EXPONENT_BIAS
        first = code[:, :LANES]
        marked = (first & -2) | ((biased >> jnp.minimum(lane, EXPONENT_BITS - 1)) & 1)
        first = jnp.where(lane < EXPONENT_BITS, marked, first)
        out[:, :LANES] = first.astype(jnp.int16)
        out[:, LANES:] = code[:, LANES:].astype(jnp.int16)


def finish_kernel(
    buffers, pool, local, depth, me_ref, adapter_ref, mine_ref, other_ref, cos_ref, sin_ref, gain_ref, *refs
):
    order = [0] + return_order(buffers)
    ins = [refs[order.index(j)] for j in range(buffers)]
    out_hbm, out_ref, sems = refs[-3:]
    rows, columns = mine_ref.shape
    head = cos_ref.shape[1]
    place = to_column(slot_places(adapter_ref[...], me_ref[0], pool, local, depth))
    slots = buffers * ins[0].shape[0]
    picker = jnp.where(iota((rows, slots), 1) == place, 1.0, 0.0).astype(jnp.bfloat16)

    def picked(at, size):
        code = jnp.concatenate([x[:, at : at + size] for x in ins], axis=0).astype(jnp.int32)
        high = (code >> 8).astype(jnp.float32).astype(jnp.bfloat16)
        low = (code & 255).astype(jnp.float32).astype(jnp.bfloat16)
        high = jnp.dot(picker, high, preferred_element_type=jnp.float32)
        low = jnp.dot(picker, low, preferred_element_type=jnp.float32)
        return high * 256.0 + low

    lane = iota((1, LANES), 1)
    bits = picked(0, LANES).astype(jnp.int32) & 1
    bits = jnp.where(lane < EXPONENT_BITS, bits << jnp.minimum(lane, EXPONENT_BITS - 1), 0)
    exponent = jnp.sum(bits.astype(jnp.float32), axis=1, keepdims=True) - EXPONENT_BIAS
    scale = jnp.exp2(exponent - 15.0)
    cosine, sine, gain = cos_ref[...], sin_ref[...], gain_ref[...]
    entries = []
    for at in range(0, columns, 2 * head):
        projected = mine_ref[:, at : at + 2 * head] + other_ref[:, at : at + 2 * head]
        projected = projected + picked(at, 2 * head) * scale
        key, value = projected[:, :head], projected[:, head:]
        mean = jnp.mean(key * key, axis=1, keepdims=True)
        normed = key * lax.rsqrt(mean + NORM_EPS) * gain
        rotated = normed * cosine + pltpu.roll(normed, head // 2, 1) * sine
        entries += [rotated.astype(jnp.bfloat16), value.astype(jnp.bfloat16)]
    kinds, block = len(entries), 16
    n = kinds * block
    source = (iota((n, n), 0) % kinds) * block + iota((n, n), 0) // kinds
    order = jnp.where(iota((n, n), 1) == source, 1.0, 0.0).astype(jnp.bfloat16)
    copies = []
    for i in range(rows // block):
        stacked = jnp.concatenate([e[i * block : (i + 1) * block] for e in entries], axis=0)
        mixed = jnp.dot(order, stacked, preferred_element_type=jnp.float32)
        out_ref[i * n : (i + 1) * n, :] = mixed.astype(jnp.bfloat16)
        if i % 2:
            done = pl.ds((i - 1) * n, 2 * n)
            copies.append(
                pltpu.make_async_copy(out_ref.at[done, :], out_hbm.at[done, :], sems.at[i // 2])
            )
            copies[-1].start()
    for copy in copies:
        copy.wait()


def body(
    tokens,
    row_adapters,
    positions,
    key_value_weight,
    adapter_down,
    adapter_up,
    ranks,
    key_norm_gain,
):
    pool = lax.axis_size("pool")
    groups = lax.axis_size("groups")
    cores = lax.axis_size("tp")
    rows, width = tokens.shape
    local = adapter_down.shape[0]
    adapters = local * pool
    columns = key_value_weight.shape[1] // cores
    rank = adapter_down.shape[2]
    head = key_norm_gain.shape[0]
    depth = max(2, 2 * rows // adapters)
    buffers = pool // 2
    size = 2 * local * depth
    f32, bf16 = jnp.float32, jnp.bfloat16

    me = lax.axis_index("pool").astype(jnp.int32)[None]
    core = lax.axis_index("tp").astype(jnp.int32)[None]
    group = lax.axis_index("groups").astype(jnp.int32)[None]

    def exchange(x, axis, count, j):
        return lax.ppermute(x, axis, [(p, p ^ j) for p in range(count)])

    def hand_round(share):
        return [share] + [exchange(share, "groups", groups, k) for k in range(1, groups)]

    adapter_row = row_adapters.reshape(1, rows)
    chunks = [size for _, size in chunk_places(width // groups)]
    parts = rows // 16
    up_share = columns // groups
    up_part, *parts_picked = pl.pallas_call(
        functools.partial(pick_kernel, pool, local, depth, columns),
        in_specs=[SMEM] * 3 + [HBM] * 4,
        out_specs=[VMEM] * (1 + CHUNKS + buffers),
        out_shape=[jax.ShapeDtypeStruct((local, rank, up_share), bf16)]
        + [jax.ShapeDtypeStruct((local, chunk, rank), bf16) for chunk in chunks]
        + [jax.ShapeDtypeStruct((size, width), bf16)] * buffers,
        scratch_shapes=[
            pltpu.VMEM((1, rows), jnp.int32),
            pltpu.VMEM((rows, width), bf16),
            pltpu.SemaphoreType.DMA((1 + CHUNKS,)),
            pltpu.SemaphoreType.DMA((parts + 1,)),
        ],
        compiler_params=params(),
        cost_estimate=cost(2 * buffers * size * rows * width, 2 * (rows + buffers * size) * width),
        name="pick",
    )(
        me,
        group,
        core,
        in_hbm(adapter_row),
        in_hbm(tokens),
        in_hbm(adapter_down),
        in_hbm(adapter_up),
    )
    down_parts, picked = parts_picked[:CHUNKS], parts_picked[CHUNKS:]
    far_up = exchange(up_part, "pool", pool, pool // 2)
    far_down = exchange(down_parts[0], "pool", pool, pool // 2)
    order = far_first(buffers)
    arrived = [picked[0]] + [exchange(picked[j], "pool", pool, j) for j in order]

    steps = 5
    theirs, mine, own_down, own_up = pl.pallas_call(
        base_kernel,
        in_specs=[SMEM] + [HBM] * 4,
        out_specs=[VMEM] * 4,
        out_shape=[jax.ShapeDtypeStruct((rows, columns), f32)] * 2
        + [
            jax.ShapeDtypeStruct(adapter_down.shape, bf16),
            jax.ShapeDtypeStruct((local, rank, columns), bf16),
        ],
        scratch_shapes=[
            pltpu.VMEM((rows, width), bf16),
            pltpu.VMEM((2, width, columns), bf16),
            pltpu.SemaphoreType.DMA((3,)),
            pltpu.SemaphoreType.DMA((2, steps)),
        ],
        compiler_params=params(),
        cost_estimate=cost(4 * rows * width * columns, 4 * width * columns),
        name="base",
    )(
        core,
        in_hbm(tokens),
        in_hbm(key_value_weight),
        in_hbm(adapter_down),
        in_hbm(adapter_up),
    )
    far_up, far_down, theirs = lax.optimization_barrier((far_up, far_down, theirs))
    far_ups = hand_round(far_up)
    far_downs = hand_round(far_down)
    for part in down_parts[1:]:
        part, _ = lax.optimization_barrier((part, far_down))
        far_down = exchange(part, "pool", pool, pool // 2)
        far_downs += hand_round(far_down)
    mask = (jnp.arange(rank, dtype=jnp.int32)[None, :] < ranks[:, None]).astype(f32)
    factor = mask * (f32(ALPHA) / ranks.astype(f32))[:, None]
    factor, _ = lax.optimization_barrier((factor, arrived[1]))
    far_factor = exchange(factor, "pool", pool, pool // 2)

    half_dim = head // 2
    frequency = jnp.power(
        f32(ROPE_THETA), -jnp.arange(half_dim, dtype=f32) * (2.0 / head)
    )
    angles = positions.astype(f32)[:, None] * frequency[None, :]
    cosine, sine = jnp.cos(angles), jnp.sin(angles)
    cosine = jnp.concatenate([cosine, cosine], axis=1)
    sine = jnp.concatenate([-sine, sine], axis=1)

    arrived[-1], theirs = lax.optimization_barrier((arrived[-1], theirs))
    other = exchange(theirs, "tp", cores, 1)
    arrived, far_ups, far_factor, mine, cosine, sine = lax.optimization_barrier(
        (arrived, far_ups, far_factor, mine, cosine, sine)
    )
    slots = buffers * size
    low = pl.pallas_call(
        functools.partial(down_kernel, buffers, groups, local, depth),
        in_specs=[SMEM] + [VMEM] * (1 + buffers + groups * CHUNKS),
        out_specs=VMEM,
        out_shape=jax.ShapeDtypeStruct((slots, rank), f32),
        compiler_params=params(),
        cost_estimate=cost(4 * local * slots * rank * width, 2 * (slots + rank) * width),
        name="down",
    )(group, own_down, *arrived, *far_downs)
    low_other = exchange(low, "tp", cores, 1)

    terms = pl.pallas_call(
        functools.partial(up_kernel, buffers, groups, local, depth),
        in_specs=[SMEM] + [VMEM] * (5 + groups),
        out_specs=[VMEM] * buffers,
        out_shape=[jax.ShapeDtypeStruct((size, columns), jnp.int16)] * buffers,
        scratch_shapes=[pltpu.VMEM((slots, columns), f32)],
        compiler_params=params(),
        cost_estimate=cost(8 * local * slots * rank * columns, 2 * slots * columns),
        name="up",
    )(group, low, low_other, factor, far_factor, own_up, *far_ups)
    order = return_order(buffers)
    returned = [terms[0]] + [exchange(terms[j], "pool", pool, j) for j in order]

    out = pl.pallas_call(
        functools.partial(finish_kernel, buffers, pool, local, depth),
        in_specs=[SMEM] + [VMEM] * (6 + buffers),
        out_specs=HBM,
        out_shape=jax.ShapeDtypeStruct((rows * columns // head, head), bf16),
        scratch_shapes=[
            pltpu.VMEM((rows * columns // head, head), bf16),
            pltpu.SemaphoreType.DMA((rows // 32,)),
        ],
        compiler_params=params(),
        cost_estimate=cost(4 * rows * slots * columns, 2 * slots * columns),
        name="finish",
    )(
        me,
        adapter_row,
        mine,
        other,
        cosine,
        sine,
        key_norm_gain.astype(f32)[None, :],
        *returned,
    )
    return out.reshape(rows, columns // (2 * head), 2, head)


def solution(mesh):
    return jax.shard_map(
        body,
        mesh=mesh,
        in_specs=(
            P(("groups", "pool"), "tp"),
            P(("groups", "pool"), None),
            P(("groups", "pool")),
            P("tp", None),
            P("pool", "tp", None),
            P("pool", None, None),
            P("pool"),
            P(),
        ),
        out_specs=P(("groups", "pool"), "tp", None, None),
        check_vma=False,
    )
```

```python
import functools

import jax
import jax.numpy as jnp
from jax import lax
from jax.experimental import pallas as pl
from jax.experimental.pallas import tpu as pltpu
from jax.sharding import PartitionSpec as P

ALPHA = 32
ROPE_THETA = 1000000.0
NORM_EPS = 1e-06
VMEM_LIMIT = 48 * 1024 * 1024
LANES = 128
EXPONENT_BITS = 8
EXPONENT_BIAS = 128

VMEM = pl.BlockSpec(memory_space=pltpu.VMEM)
HBM = pl.BlockSpec(memory_space=pltpu.HBM)
SMEM = pl.BlockSpec(memory_space=pltpu.SMEM)


def params(**kw):
    return pltpu.CompilerParams(vmem_limit_bytes=VMEM_LIMIT, **kw)


def cost(flops, bytes_accessed):
    return pl.CostEstimate(flops=flops, bytes_accessed=bytes_accessed, transcendentals=0)


def in_hbm(x):
    return pltpu.with_memory_space_constraint(x, pltpu.HBM)


def iota(shape, dim):
    return lax.broadcasted_iota(jnp.int32, shape, dim)


def to_column(row):
    n = row.shape[1]
    return jnp.sum(
        jnp.where(iota((n, n), 0) == iota((n, n), 1), row, 0), axis=1, keepdims=True
    )


def slot_places(row, me, pool, local, depth):
    n = row.shape[1]
    column = to_column(row)
    earlier = (column == row) & (iota((n, n), 0) < iota((n, n), 1))
    slot = jnp.sum(jnp.where(earlier, 1, 0), axis=0, keepdims=True)
    holder = row // local
    apart = holder ^ me
    buffer, far = apart % (pool // 2), apart // (pool // 2)
    return ((buffer * 2 + far) * local + (row - holder * local)) * depth + slot


def far_first(count):
    return sorted(range(1, count), key=lambda j: (-bin(j).count("1"), -j))


def return_order(count):
    order = far_first(count)
    return order[-1:] + order[:-1]


def halves(x):
    high = x.astype(jnp.bfloat16)
    low = (x - high.astype(jnp.float32)).astype(jnp.bfloat16)
    return high, low


def up_share_kernel(cores, group_ref, core_ref, ranks_ref, up_hbm, out_ref, factor_ref, own_ref, sem):
    local, rank, share = out_ref.shape
    at = core_ref[0] * (up_hbm.shape[2] // cores) + group_ref[0] * share
    copy = pltpu.make_async_copy(
        up_hbm.at[:, :, pl.ds(pl.multiple_of(at, share), share)], own_ref, sem
    )
    copy.start()
    copy.wait()
    for a in range(local):
        used = ranks_ref[a]

        def factor(shape, dim):
            scale = jnp.float32(ALPHA) / jnp.full(shape, used, jnp.int32).astype(jnp.float32)
            return jnp.where(iota(shape, dim) < used, scale, 0.0)

        factor_ref[a : a + 1, :] = factor((1, rank), 1)
        out_ref[a] = (own_ref[a].astype(jnp.float32) * factor((rank, 1), 0)).astype(jnp.bfloat16)


def pick_kernel(
    pool, local, depth, me_ref, group_ref, adapter_hbm, tokens_hbm, down_hbm, *refs
):
    share_ref, outs = refs[0], refs[1:-4]
    adapter_ref, tokens_ref, share_sem, sems = refs[-4:]
    rows, width = tokens_ref.shape
    share = share_ref.shape[1]
    parts = sems.shape[0] - 1
    part = rows // parts
    adapter_copy = pltpu.make_async_copy(adapter_hbm, adapter_ref, sems.at[parts])
    adapter_copy.start()
    copies = [
        pltpu.make_async_copy(
            tokens_hbm.at[pl.ds(i * part, part), :],
            tokens_ref.at[pl.ds(i * part, part), :],
            sems.at[i],
        )
        for i in range(parts)
    ]
    for copy in copies:
        copy.start()
    at = pl.multiple_of(group_ref[0] * share, share)
    share_copy = pltpu.make_async_copy(down_hbm.at[:, pl.ds(at, share), :], share_ref, share_sem)
    share_copy.start()
    adapter_copy.wait()
    place = slot_places(adapter_ref[...], me_ref[0], pool, local, depth)
    size = outs[0].shape[0]
    slots = len(outs) * size
    picker = jnp.where(iota((slots, rows), 0) == place, 1.0, 0.0).astype(jnp.bfloat16)
    for copy in copies:
        copy.wait()
    step = 512
    for at in range(0, width, step):
        block = jnp.dot(
            picker, tokens_ref[:, at : at + step], preferred_element_type=jnp.float32
        )
        for j, out in enumerate(outs):
            out[:, at : at + step] = block[j * size : (j + 1) * size].astype(jnp.bfloat16)
    share_copy.wait()


def base_kernel(
    core_ref,
    tokens_hbm,
    weight_hbm,
    down_hbm,
    up_hbm,
    theirs_ref,
    mine_ref,
    down_ref,
    up_ref,
    tokens_ref,
    weight_ref,
    other_sems,
    sems,
):
    rows, columns = mine_ref.shape
    steps = sems.shape[1]
    step = tokens_ref.shape[1] // steps
    copies = []
    for half in range(2):
        start = (1 - core_ref[0] if half == 0 else core_ref[0]) * columns
        start = pl.multiple_of(start, columns)
        for k in range(steps):
            copies.append(
                pltpu.make_async_copy(
                    weight_hbm.at[pl.ds(k * step, step), pl.ds(start, columns)],
                    weight_ref.at[half, pl.ds(k * step, step), :],
                    sems.at[half, k],
                )
            )
    tokens_copy = pltpu.make_async_copy(tokens_hbm, tokens_ref, other_sems.at[0])
    own = pl.multiple_of(core_ref[0] * columns, columns)
    factor_copies = [
        pltpu.make_async_copy(down_hbm, down_ref, other_sems.at[1]),
        pltpu.make_async_copy(up_hbm.at[:, :, pl.ds(own, columns)], up_ref, other_sems.at[2]),
    ]
    for copy in [tokens_copy] + copies + factor_copies:
        copy.start()
    tokens_copy.wait()
    for half, out in enumerate((theirs_ref, mine_ref)):
        for k in range(steps):
            copies[half * steps + k].wait()
            term = jnp.dot(
                tokens_ref[:, k * step : (k + 1) * step],
                weight_ref[half, k * step : (k + 1) * step, :],
                preferred_element_type=jnp.float32,
            )
            if k == 0:
                out[...] = term
            else:
                out[...] += term
    for copy in factor_copies:
        copy.wait()


def down_kernel(buffers, groups, local, depth, group_ref, down_ref, *refs):
    order = [0] + far_first(buffers)
    ins = [refs[order.index(j)] for j in range(buffers)]
    shares, out = refs[buffers : buffers + groups], refs[-1]
    rank = out.shape[1]
    share = shares[0].shape[1]
    total = None
    for k in range(groups):
        at = pl.multiple_of((group_ref[0] ^ k) * share, share)
        rows = jnp.concatenate([x[:, pl.ds(at, share)] for x in ins], axis=0)
        factors = [down_ref[a, pl.ds(at, share), :] for a in range(local)]
        factors += [shares[k][a] for a in range(local)]
        term = jnp.dot(
            rows, jnp.concatenate(factors, axis=1), preferred_element_type=jnp.float32
        )
        total = term if total is None else total + term
    which = (iota((total.shape[0], 1), 0) // depth) % (2 * local)
    low = total[:, :rank]
    for i in range(1, 2 * local):
        low = jnp.where(which == i, total[:, i * rank : (i + 1) * rank], low)
    out[...] = low


def up_kernel(
    buffers, groups, local, depth, group_ref, low_ref, other_ref, factor_ref, up_ref, *refs
):
    shares, outs, term_ref = refs[:groups], refs[groups : groups + buffers], refs[-1]
    rows, rank = low_ref.shape
    size = rows // buffers
    columns = up_ref.shape[2]
    share = columns // groups
    which = (iota((rows, 1), 0) // depth) % (2 * local)
    low = low_ref[...] + other_ref[...]
    for a in range(local):
        low = jnp.where(which == a, low * factor_ref[a : a + 1, :], low)
    both = jnp.concatenate(halves(low), axis=0)
    which = jnp.concatenate([which, which], axis=0)
    spread = jnp.concatenate(
        [jnp.where(which == i, both, jnp.zeros_like(both)) for i in range(2 * local)], axis=1
    )
    for k in range(groups):
        at = pl.multiple_of((group_ref[0] ^ k) * share, share)
        up = [up_ref[a, :, pl.ds(at, share)] for a in range(local)]
        up += [shares[k][a] for a in range(local)]
        term = jnp.dot(
            spread, jnp.concatenate(up, axis=0), preferred_element_type=jnp.float32
        )
        term_ref[:, pl.ds(at, share)] = term[:rows] + term[rows:]
    lane = iota((1, LANES), 1)
    for j, out in enumerate(outs):
        term = term_ref[j * size : (j + 1) * size, :]
        top = jnp.max(jnp.abs(term), axis=1, keepdims=True)
        exponent = jnp.ceil(jnp.log2(jnp.maximum(top, 1e-30)) + 1e-3)
        code = jnp.clip(jnp.round(term * jnp.exp2(15.0 - exponent)), -32767.0, 32767.0)
        code = code.astype(jnp.int32)
        biased = exponent.astype(jnp.int32) + EXPONENT_BIAS
        first = code[:, :LANES]
        marked = (first & -2) | ((biased >> jnp.minimum(lane, EXPONENT_BITS - 1)) & 1)
        first = jnp.where(lane < EXPONENT_BITS, marked, first)
        out[:, :LANES] = first.astype(jnp.int16)
        out[:, LANES:] = code[:, LANES:].astype(jnp.int16)


def finish_kernel(
    buffers, pool, local, depth, me_ref, adapter_ref, mine_ref, other_ref, cos_ref, sin_ref, gain_ref, *refs
):
    order = [0] + return_order(buffers)
    ins = [refs[order.index(j)] for j in range(buffers)]
    out_hbm, out_ref, sems = refs[-3:]
    rows, columns = mine_ref.shape
    head = cos_ref.shape[1]
    place = to_column(slot_places(adapter_ref[...], me_ref[0], pool, local, depth))
    slots = buffers * ins[0].shape[0]
    picker = jnp.where(iota((rows, slots), 1) == place, 1.0, 0.0).astype(jnp.bfloat16)

    def picked(at, size):
        code = jnp.concatenate([x[:, at : at + size] for x in ins], axis=0).astype(jnp.int32)
        high = (code >> 8).astype(jnp.float32).astype(jnp.bfloat16)
        low = (code & 255).astype(jnp.float32).astype(jnp.bfloat16)
        high = jnp.dot(picker, high, preferred_element_type=jnp.float32)
        low = jnp.dot(picker, low, preferred_element_type=jnp.float32)
        return high * 256.0 + low

    lane = iota((1, LANES), 1)
    bits = picked(0, LANES).astype(jnp.int32) & 1
    bits = jnp.where(lane < EXPONENT_BITS, bits << jnp.minimum(lane, EXPONENT_BITS - 1), 0)
    exponent = jnp.sum(bits.astype(jnp.float32), axis=1, keepdims=True) - EXPONENT_BIAS
    scale = jnp.exp2(exponent - 15.0)
    cosine, sine, gain = cos_ref[...], sin_ref[...], gain_ref[...]
    entries = []
    for at in range(0, columns, 2 * head):
        projected = mine_ref[:, at : at + 2 * head] + other_ref[:, at : at + 2 * head]
        projected = projected + picked(at, 2 * head) * scale
        key, value = projected[:, :head], projected[:, head:]
        mean = jnp.mean(key * key, axis=1, keepdims=True)
        normed = key * lax.rsqrt(mean + NORM_EPS) * gain
        rotated = normed * cosine + pltpu.roll(normed, head // 2, 1) * sine
        entries += [rotated.astype(jnp.bfloat16), value.astype(jnp.bfloat16)]
    kinds, block = len(entries), 16
    n = kinds * block
    source = (iota((n, n), 0) % kinds) * block + iota((n, n), 0) // kinds
    order = jnp.where(iota((n, n), 1) == source, 1.0, 0.0).astype(jnp.bfloat16)
    copies = []
    for i in range(rows // block):
        stacked = jnp.concatenate([e[i * block : (i + 1) * block] for e in entries], axis=0)
        mixed = jnp.dot(order, stacked, preferred_element_type=jnp.float32)
        out_ref[i * n : (i + 1) * n, :] = mixed.astype(jnp.bfloat16)
        if i % 2:
            done = pl.ds((i - 1) * n, 2 * n)
            copies.append(
                pltpu.make_async_copy(out_ref.at[done, :], out_hbm.at[done, :], sems.at[i // 2])
            )
            copies[-1].start()
    for copy in copies:
        copy.wait()


def body(
    tokens,
    row_adapters,
    positions,
    key_value_weight,
    adapter_down,
    adapter_up,
    ranks,
    key_norm_gain,
):
    pool = lax.axis_size("pool")
    groups = lax.axis_size("groups")
    cores = lax.axis_size("tp")
    rows, width = tokens.shape
    local = adapter_down.shape[0]
    adapters = local * pool
    columns = key_value_weight.shape[1] // cores
    rank = adapter_down.shape[2]
    head = key_norm_gain.shape[0]
    depth = max(2, 2 * rows // adapters)
    buffers = pool // 2
    size = 2 * local * depth
    f32, bf16 = jnp.float32, jnp.bfloat16

    me = lax.axis_index("pool").astype(jnp.int32)[None]
    core = lax.axis_index("tp").astype(jnp.int32)[None]
    group = lax.axis_index("groups").astype(jnp.int32)[None]

    def exchange(x, axis, count, j):
        return lax.ppermute(x, axis, [(p, p ^ j) for p in range(count)])

    def hand_round(share):
        return [share] + [exchange(share, "groups", groups, k) for k in range(1, groups)]

    adapter_row = row_adapters.reshape(1, rows)
    down_share = width // groups
    parts = rows // 16
    down_part, *picked = pl.pallas_call(
        functools.partial(pick_kernel, pool, local, depth),
        in_specs=[SMEM] * 2 + [HBM] * 3,
        out_specs=[VMEM] * (1 + buffers),
        out_shape=[jax.ShapeDtypeStruct((local, down_share, rank), bf16)]
        + [jax.ShapeDtypeStruct((size, width), bf16)] * buffers,
        scratch_shapes=[
            pltpu.VMEM((1, rows), jnp.int32),
            pltpu.VMEM((rows, width), bf16),
            pltpu.SemaphoreType.DMA,
            pltpu.SemaphoreType.DMA((parts + 1,)),
        ],
        compiler_params=params(),
        cost_estimate=cost(2 * buffers * size * rows * width, 2 * (rows + buffers * size) * width),
        name="pick",
    )(me, group, in_hbm(adapter_row), in_hbm(tokens), in_hbm(adapter_down))
    far_down = exchange(down_part, "pool", pool, pool // 2)
    order = far_first(buffers)
    arrived = [picked[0]] + [exchange(picked[j], "pool", pool, j) for j in order]

    up_share = columns // groups
    ranks_now, adapter_up_now, _ = lax.optimization_barrier((ranks, adapter_up, picked))
    up_part, factor = pl.pallas_call(
        functools.partial(up_share_kernel, cores),
        in_specs=[SMEM] * 3 + [HBM],
        out_specs=[VMEM] * 2,
        out_shape=[
            jax.ShapeDtypeStruct((local, rank, up_share), bf16),
            jax.ShapeDtypeStruct((local, rank), f32),
        ],
        scratch_shapes=[
            pltpu.VMEM((local, rank, up_share), bf16),
            pltpu.SemaphoreType.DMA,
        ],
        compiler_params=params(),
        cost_estimate=cost(local * rank * up_share, 4 * local * rank * up_share),
        name="up_share",
    )(group, core, ranks_now, in_hbm(adapter_up_now))
    far_up = exchange(up_part, "pool", pool, pool // 2)

    steps = 5
    theirs, mine, own_down, own_up = pl.pallas_call(
        base_kernel,
        in_specs=[SMEM] + [HBM] * 4,
        out_specs=[VMEM] * 4,
        out_shape=[jax.ShapeDtypeStruct((rows, columns), f32)] * 2
        + [
            jax.ShapeDtypeStruct(adapter_down.shape, bf16),
            jax.ShapeDtypeStruct((local, rank, columns), bf16),
        ],
        scratch_shapes=[
            pltpu.VMEM((rows, width), bf16),
            pltpu.VMEM((2, width, columns), bf16),
            pltpu.SemaphoreType.DMA((3,)),
            pltpu.SemaphoreType.DMA((2, steps)),
        ],
        compiler_params=params(),
        cost_estimate=cost(4 * rows * width * columns, 4 * width * columns),
        name="base",
    )(
        core,
        in_hbm(tokens),
        in_hbm(key_value_weight),
        in_hbm(adapter_down),
        in_hbm(adapter_up),
    )
    far_down, theirs = lax.optimization_barrier((far_down, theirs))
    far_downs = hand_round(far_down)
    far_up, _ = lax.optimization_barrier((far_up, far_down))
    far_ups = hand_round(far_up)
    half_dim = head // 2
    frequency = jnp.power(
        f32(ROPE_THETA), -jnp.arange(half_dim, dtype=f32) * (2.0 / head)
    )
    angles = positions.astype(f32)[:, None] * frequency[None, :]
    cosine, sine = jnp.cos(angles), jnp.sin(angles)
    cosine = jnp.concatenate([cosine, cosine], axis=1)
    sine = jnp.concatenate([-sine, sine], axis=1)

    arrived[1], theirs = lax.optimization_barrier((arrived[1], theirs))
    other = exchange(theirs, "tp", cores, 1)
    arrived, mine, cosine, sine = lax.optimization_barrier((arrived, mine, cosine, sine))
    slots = buffers * size
    low = pl.pallas_call(
        functools.partial(down_kernel, buffers, groups, local, depth),
        in_specs=[SMEM] + [VMEM] * (1 + buffers + groups),
        out_specs=VMEM,
        out_shape=jax.ShapeDtypeStruct((slots, rank), f32),
        compiler_params=params(),
        cost_estimate=cost(4 * local * slots * rank * width, 2 * (slots + rank) * width),
        name="down",
    )(group, own_down, *arrived, *far_downs)
    low_other = exchange(low, "tp", cores, 1)

    terms = pl.pallas_call(
        functools.partial(up_kernel, buffers, groups, local, depth),
        in_specs=[SMEM] + [VMEM] * (4 + groups),
        out_specs=[VMEM] * buffers,
        out_shape=[jax.ShapeDtypeStruct((size, columns), jnp.int16)] * buffers,
        scratch_shapes=[pltpu.VMEM((slots, columns), f32)],
        compiler_params=params(),
        cost_estimate=cost(8 * local * slots * rank * columns, 2 * slots * columns),
        name="up",
    )(group, low, low_other, factor, own_up, *far_ups)
    order = return_order(buffers)
    returned = [terms[0]] + [exchange(terms[j], "pool", pool, j) for j in order]

    out = pl.pallas_call(
        functools.partial(finish_kernel, buffers, pool, local, depth),
        in_specs=[SMEM] + [VMEM] * (6 + buffers),
        out_specs=HBM,
        out_shape=jax.ShapeDtypeStruct((rows * columns // head, head), bf16),
        scratch_shapes=[
            pltpu.VMEM((rows * columns // head, head), bf16),
            pltpu.SemaphoreType.DMA((rows // 32,)),
        ],
        compiler_params=params(),
        cost_estimate=cost(4 * rows * slots * columns, 2 * slots * columns),
        name="finish",
    )(
        me,
        adapter_row,
        mine,
        other,
        cosine,
        sine,
        key_norm_gain.astype(f32)[None, :],
        *returned,
    )
    return out.reshape(rows, columns // (2 * head), 2, head)


def solution(mesh):
    return jax.shard_map(
        body,
        mesh=mesh,
        in_specs=(
            P(("groups", "pool"), "tp"),
            P(("groups", "pool"), None),
            P(("groups", "pool")),
            P("tp", None),
            P("pool", "tp", None),
            P("pool", None, None),
            P("pool"),
            P(),
        ),
        out_specs=P(("groups", "pool"), "tp", None, None),
        check_vma=False,
    )
```

```python
import functools

import jax
import jax.numpy as jnp
from jax import lax
from jax.experimental import pallas as pl
from jax.experimental.pallas import tpu as pltpu
from jax.sharding import PartitionSpec as P

ALPHA = 32
ROPE_THETA = 1000000.0
NORM_EPS = 1e-06
VMEM_LIMIT = 48 * 1024 * 1024
LANES = 128
EXPONENT_BITS = 8
EXPONENT_BIAS = 128

VMEM = pl.BlockSpec(memory_space=pltpu.VMEM)
HBM = pl.BlockSpec(memory_space=pltpu.HBM)
SMEM = pl.BlockSpec(memory_space=pltpu.SMEM)


def params(**kw):
    return pltpu.CompilerParams(vmem_limit_bytes=VMEM_LIMIT, **kw)


def cost(flops, bytes_accessed):
    return pl.CostEstimate(flops=flops, bytes_accessed=bytes_accessed, transcendentals=0)


def in_hbm(x):
    return pltpu.with_memory_space_constraint(x, pltpu.HBM)


def iota(shape, dim):
    return lax.broadcasted_iota(jnp.int32, shape, dim)


def to_column(row):
    n = row.shape[1]
    return jnp.sum(
        jnp.where(iota((n, n), 0) == iota((n, n), 1), row, 0), axis=1, keepdims=True
    )


def slot_places(row, me, pool, local, depth):
    n = row.shape[1]
    column = to_column(row)
    earlier = (column == row) & (iota((n, n), 0) < iota((n, n), 1))
    slot = jnp.sum(jnp.where(earlier, 1, 0), axis=0, keepdims=True)
    holder = row // local
    apart = holder ^ me
    buffer, far = apart % (pool // 2), apart // (pool // 2)
    return ((buffer * 2 + far) * local + (row - holder * local)) * depth + slot


def far_first(count):
    return sorted(range(1, count), key=lambda j: (-bin(j).count("1"), -j))


def return_order(count):
    order = far_first(count)
    return order[-1:] + order[:-1]


def halves(x):
    high = x.astype(jnp.bfloat16)
    low = (x - high.astype(jnp.float32)).astype(jnp.bfloat16)
    return high, low


def up_share_kernel(cores, group_ref, core_ref, ranks_ref, up_hbm, out_ref, factor_ref, own_ref, sem):
    local, rank, share = out_ref.shape
    at = core_ref[0] * (up_hbm.shape[2] // cores) + group_ref[0] * share
    copy = pltpu.make_async_copy(
        up_hbm.at[:, :, pl.ds(pl.multiple_of(at, share), share)], own_ref, sem
    )
    copy.start()
    copy.wait()
    for a in range(local):
        used = ranks_ref[a]

        def factor(shape, dim):
            scale = jnp.float32(ALPHA) / jnp.full(shape, used, jnp.int32).astype(jnp.float32)
            return jnp.where(iota(shape, dim) < used, scale, 0.0)

        factor_ref[a : a + 1, :] = factor((1, rank), 1)
        out_ref[a] = (own_ref[a].astype(jnp.float32) * factor((rank, 1), 0)).astype(jnp.bfloat16)


def pick_kernel(
    pool, local, depth, me_ref, group_ref, adapter_hbm, tokens_hbm, down_hbm, *refs
):
    share_ref, outs = refs[0], refs[1:-4]
    adapter_ref, tokens_ref, share_sem, sems = refs[-4:]
    rows, width = tokens_ref.shape
    share = share_ref.shape[1]
    parts = sems.shape[0] - 1
    part = rows // parts
    adapter_copy = pltpu.make_async_copy(adapter_hbm, adapter_ref, sems.at[parts])
    adapter_copy.start()
    copies = [
        pltpu.make_async_copy(
            tokens_hbm.at[pl.ds(i * part, part), :],
            tokens_ref.at[pl.ds(i * part, part), :],
            sems.at[i],
        )
        for i in range(parts)
    ]
    for copy in copies:
        copy.start()
    at = pl.multiple_of(group_ref[0] * share, share)
    share_copy = pltpu.make_async_copy(down_hbm.at[:, pl.ds(at, share), :], share_ref, share_sem)
    share_copy.start()
    adapter_copy.wait()
    place = slot_places(adapter_ref[...], me_ref[0], pool, local, depth)
    size = outs[0].shape[0]
    slots = len(outs) * size
    picker = jnp.where(iota((slots, rows), 0) == place, 1.0, 0.0).astype(jnp.bfloat16)
    for copy in copies:
        copy.wait()
    step = 512
    for at in range(0, width, step):
        block = jnp.dot(
            picker, tokens_ref[:, at : at + step], preferred_element_type=jnp.float32
        )
        for j, out in enumerate(outs):
            out[:, at : at + step] = block[j * size : (j + 1) * size].astype(jnp.bfloat16)
    share_copy.wait()


def base_kernel(
    core_ref,
    tokens_hbm,
    weight_hbm,
    down_hbm,
    up_hbm,
    theirs_ref,
    mine_ref,
    down_ref,
    up_ref,
    tokens_ref,
    weight_ref,
    other_sems,
    sems,
):
    rows, columns = mine_ref.shape
    steps = sems.shape[1]
    step = tokens_ref.shape[1] // steps
    copies = []
    for half in range(2):
        start = (1 - core_ref[0] if half == 0 else core_ref[0]) * columns
        start = pl.multiple_of(start, columns)
        for k in range(steps):
            copies.append(
                pltpu.make_async_copy(
                    weight_hbm.at[pl.ds(k * step, step), pl.ds(start, columns)],
                    weight_ref.at[half, pl.ds(k * step, step), :],
                    sems.at[half, k],
                )
            )
    tokens_copy = pltpu.make_async_copy(tokens_hbm, tokens_ref, other_sems.at[0])
    own = pl.multiple_of(core_ref[0] * columns, columns)
    factor_copies = [
        pltpu.make_async_copy(down_hbm, down_ref, other_sems.at[1]),
        pltpu.make_async_copy(up_hbm.at[:, :, pl.ds(own, columns)], up_ref, other_sems.at[2]),
    ]
    for copy in [tokens_copy] + copies + factor_copies:
        copy.start()
    tokens_copy.wait()
    for half, out in enumerate((theirs_ref, mine_ref)):
        for k in range(steps):
            copies[half * steps + k].wait()
            term = jnp.dot(
                tokens_ref[:, k * step : (k + 1) * step],
                weight_ref[half, k * step : (k + 1) * step, :],
                preferred_element_type=jnp.float32,
            )
            if k == 0:
                out[...] = term
            else:
                out[...] += term
    for copy in factor_copies:
        copy.wait()


def down_kernel(buffers, groups, local, depth, group_ref, down_ref, *refs):
    order = [0] + far_first(buffers)
    ins = [refs[order.index(j)] for j in range(buffers)]
    shares, out = refs[buffers : buffers + groups], refs[-1]
    rank = out.shape[1]
    share = shares[0].shape[1]
    total = None
    for k in range(groups):
        at = pl.multiple_of((group_ref[0] ^ k) * share, share)
        rows = jnp.concatenate([x[:, pl.ds(at, share)] for x in ins], axis=0)
        factors = [down_ref[a, pl.ds(at, share), :] for a in range(local)]
        factors += [shares[k][a] for a in range(local)]
        term = jnp.dot(
            rows, jnp.concatenate(factors, axis=1), preferred_element_type=jnp.float32
        )
        total = term if total is None else total + term
    which = (iota((total.shape[0], 1), 0) // depth) % (2 * local)
    low = total[:, :rank]
    for i in range(1, 2 * local):
        low = jnp.where(which == i, total[:, i * rank : (i + 1) * rank], low)
    out[...] = low


def up_kernel(
    buffers, groups, local, depth, group_ref, low_ref, other_ref, factor_ref, up_ref, *refs
):
    shares, outs, term_ref = refs[:groups], refs[groups : groups + buffers], refs[-1]
    rows, rank = low_ref.shape
    size = rows // buffers
    columns = up_ref.shape[2]
    share = columns // groups
    which = (iota((rows, 1), 0) // depth) % (2 * local)
    low = low_ref[...] + other_ref[...]
    for a in range(local):
        low = jnp.where(which == a, low * factor_ref[a : a + 1, :], low)
    both = jnp.concatenate(halves(low), axis=0)
    which = jnp.concatenate([which, which], axis=0)
    spread = jnp.concatenate(
        [jnp.where(which == i, both, jnp.zeros_like(both)) for i in range(2 * local)], axis=1
    )
    for k in range(groups):
        at = pl.multiple_of((group_ref[0] ^ k) * share, share)
        up = [up_ref[a, :, pl.ds(at, share)] for a in range(local)]
        up += [shares[k][a] for a in range(local)]
        term = jnp.dot(
            spread, jnp.concatenate(up, axis=0), preferred_element_type=jnp.float32
        )
        term_ref[:, pl.ds(at, share)] = term[:rows] + term[rows:]
    lane = iota((1, LANES), 1)
    for j, out in enumerate(outs):
        term = term_ref[j * size : (j + 1) * size, :]
        top = jnp.max(jnp.abs(term), axis=1, keepdims=True)
        exponent = jnp.ceil(jnp.log2(jnp.maximum(top, 1e-30)) + 1e-3)
        code = jnp.clip(jnp.round(term * jnp.exp2(15.0 - exponent)), -32767.0, 32767.0)
        code = code.astype(jnp.int32)
        biased = exponent.astype(jnp.int32) + EXPONENT_BIAS
        first = code[:, :LANES]
        marked = (first & -2) | ((biased >> jnp.minimum(lane, EXPONENT_BITS - 1)) & 1)
        first = jnp.where(lane < EXPONENT_BITS, marked, first)
        out[:, :LANES] = first.astype(jnp.int16)
        out[:, LANES:] = code[:, LANES:].astype(jnp.int16)


def finish_kernel(
    buffers, pool, local, depth, me_ref, adapter_ref, mine_ref, other_ref, cos_ref, sin_ref, gain_ref, *refs
):
    order = [0] + return_order(buffers)
    ins = [refs[order.index(j)] for j in range(buffers)]
    out_hbm, out_ref, sems = refs[-3:]
    rows, columns = mine_ref.shape
    head = cos_ref.shape[1]
    place = to_column(slot_places(adapter_ref[...], me_ref[0], pool, local, depth))
    slots = buffers * ins[0].shape[0]
    picker = jnp.where(iota((rows, slots), 1) == place, 1.0, 0.0).astype(jnp.bfloat16)

    def picked(at, size):
        code = jnp.concatenate([x[:, at : at + size] for x in ins], axis=0).astype(jnp.int32)
        high = (code >> 8).astype(jnp.float32).astype(jnp.bfloat16)
        low = (code & 255).astype(jnp.float32).astype(jnp.bfloat16)
        high = jnp.dot(picker, high, preferred_element_type=jnp.float32)
        low = jnp.dot(picker, low, preferred_element_type=jnp.float32)
        return high * 256.0 + low

    lane = iota((1, LANES), 1)
    bits = picked(0, LANES).astype(jnp.int32) & 1
    bits = jnp.where(lane < EXPONENT_BITS, bits << jnp.minimum(lane, EXPONENT_BITS - 1), 0)
    exponent = jnp.sum(bits.astype(jnp.float32), axis=1, keepdims=True) - EXPONENT_BIAS
    scale = jnp.exp2(exponent - 15.0)
    cosine, sine, gain = cos_ref[...], sin_ref[...], gain_ref[...]
    entries = []
    for at in range(0, columns, 2 * head):
        projected = mine_ref[:, at : at + 2 * head] + other_ref[:, at : at + 2 * head]
        projected = projected + picked(at, 2 * head) * scale
        key, value = projected[:, :head], projected[:, head:]
        mean = jnp.mean(key * key, axis=1, keepdims=True)
        normed = key * lax.rsqrt(mean + NORM_EPS) * gain
        rotated = normed * cosine + pltpu.roll(normed, head // 2, 1) * sine
        entries += [rotated.astype(jnp.bfloat16), value.astype(jnp.bfloat16)]
    kinds, block = len(entries), 16
    n = kinds * block
    source = (iota((n, n), 0) % kinds) * block + iota((n, n), 0) // kinds
    order = jnp.where(iota((n, n), 1) == source, 1.0, 0.0).astype(jnp.bfloat16)
    copies = []
    for i in range(rows // block):
        stacked = jnp.concatenate([e[i * block : (i + 1) * block] for e in entries], axis=0)
        mixed = jnp.dot(order, stacked, preferred_element_type=jnp.float32)
        out_ref[i * n : (i + 1) * n, :] = mixed.astype(jnp.bfloat16)
        if i % 2:
            done = pl.ds((i - 1) * n, 2 * n)
            copies.append(
                pltpu.make_async_copy(out_ref.at[done, :], out_hbm.at[done, :], sems.at[i // 2])
            )
            copies[-1].start()
    for copy in copies:
        copy.wait()


def body(
    tokens,
    row_adapters,
    positions,
    key_value_weight,
    adapter_down,
    adapter_up,
    ranks,
    key_norm_gain,
):
    pool = lax.axis_size("pool")
    groups = lax.axis_size("groups")
    cores = lax.axis_size("tp")
    rows, width = tokens.shape
    local = adapter_down.shape[0]
    adapters = local * pool
    columns = key_value_weight.shape[1] // cores
    rank = adapter_down.shape[2]
    head = key_norm_gain.shape[0]
    depth = max(2, 2 * rows // adapters)
    buffers = pool // 2
    size = 2 * local * depth
    f32, bf16 = jnp.float32, jnp.bfloat16

    me = lax.axis_index("pool").astype(jnp.int32)[None]
    core = lax.axis_index("tp").astype(jnp.int32)[None]
    group = lax.axis_index("groups").astype(jnp.int32)[None]

    def exchange(x, axis, count, j):
        return lax.ppermute(x, axis, [(p, p ^ j) for p in range(count)])

    def hand_round(share):
        return [share] + [exchange(share, "groups", groups, k) for k in range(1, groups)]

    adapter_row = row_adapters.reshape(1, rows)
    down_share = width // groups
    parts = rows // 16
    down_part, *picked = pl.pallas_call(
        functools.partial(pick_kernel, pool, local, depth),
        in_specs=[SMEM] * 2 + [HBM] * 3,
        out_specs=[VMEM] * (1 + buffers),
        out_shape=[jax.ShapeDtypeStruct((local, down_share, rank), bf16)]
        + [jax.ShapeDtypeStruct((size, width), bf16)] * buffers,
        scratch_shapes=[
            pltpu.VMEM((1, rows), jnp.int32),
            pltpu.VMEM((rows, width), bf16),
            pltpu.SemaphoreType.DMA,
            pltpu.SemaphoreType.DMA((parts + 1,)),
        ],
        compiler_params=params(),
        cost_estimate=cost(2 * buffers * size * rows * width, 2 * (rows + buffers * size) * width),
        name="pick",
    )(me, group, in_hbm(adapter_row), in_hbm(tokens), in_hbm(adapter_down))
    far_down = exchange(down_part, "pool", pool, pool // 2)
    order = far_first(buffers)
    arrived = [picked[0]] + [exchange(picked[j], "pool", pool, j) for j in order]

    up_share = columns // groups
    ranks_now, adapter_up_now, _ = lax.optimization_barrier((ranks, adapter_up, picked))
    up_part, factor = pl.pallas_call(
        functools.partial(up_share_kernel, cores),
        in_specs=[SMEM] * 3 + [HBM],
        out_specs=[VMEM] * 2,
        out_shape=[
            jax.ShapeDtypeStruct((local, rank, up_share), bf16),
            jax.ShapeDtypeStruct((local, rank), f32),
        ],
        scratch_shapes=[
            pltpu.VMEM((local, rank, up_share), bf16),
            pltpu.SemaphoreType.DMA,
        ],
        compiler_params=params(),
        cost_estimate=cost(local * rank * up_share, 4 * local * rank * up_share),
        name="up_share",
    )(group, core, ranks_now, in_hbm(adapter_up_now))
    far_up = exchange(up_part, "pool", pool, pool // 2)

    steps = 5
    theirs, mine, own_down, own_up = pl.pallas_call(
        base_kernel,
        in_specs=[SMEM] + [HBM] * 4,
        out_specs=[VMEM] * 4,
        out_shape=[jax.ShapeDtypeStruct((rows, columns), f32)] * 2
        + [
            jax.ShapeDtypeStruct(adapter_down.shape, bf16),
            jax.ShapeDtypeStruct((local, rank, columns), bf16),
        ],
        scratch_shapes=[
            pltpu.VMEM((rows, width), bf16),
            pltpu.VMEM((2, width, columns), bf16),
            pltpu.SemaphoreType.DMA((3,)),
            pltpu.SemaphoreType.DMA((2, steps)),
        ],
        compiler_params=params(),
        cost_estimate=cost(4 * rows * width * columns, 4 * width * columns),
        name="base",
    )(
        core,
        in_hbm(tokens),
        in_hbm(key_value_weight),
        in_hbm(adapter_down),
        in_hbm(adapter_up),
    )
    far_down, theirs = lax.optimization_barrier((far_down, theirs))
    far_downs = hand_round(far_down)
    far_up, _ = lax.optimization_barrier((far_up, far_down))
    far_ups = hand_round(far_up)
    half_dim = head // 2
    frequency = jnp.power(
        f32(ROPE_THETA), -jnp.arange(half_dim, dtype=f32) * (2.0 / head)
    )
    angles = positions.astype(f32)[:, None] * frequency[None, :]
    cosine, sine = jnp.cos(angles), jnp.sin(angles)
    cosine = jnp.concatenate([cosine, cosine], axis=1)
    sine = jnp.concatenate([-sine, sine], axis=1)

    far_up, theirs = lax.optimization_barrier((far_up, theirs))
    other = exchange(theirs, "tp", cores, 1)
    arrived, mine, cosine, sine = lax.optimization_barrier((arrived, mine, cosine, sine))
    slots = buffers * size
    low = pl.pallas_call(
        functools.partial(down_kernel, buffers, groups, local, depth),
        in_specs=[SMEM] + [VMEM] * (1 + buffers + groups),
        out_specs=VMEM,
        out_shape=jax.ShapeDtypeStruct((slots, rank), f32),
        compiler_params=params(),
        cost_estimate=cost(4 * local * slots * rank * width, 2 * (slots + rank) * width),
        name="down",
    )(group, own_down, *arrived, *far_downs)
    low_other = exchange(low, "tp", cores, 1)

    terms = pl.pallas_call(
        functools.partial(up_kernel, buffers, groups, local, depth),
        in_specs=[SMEM] + [VMEM] * (4 + groups),
        out_specs=[VMEM] * buffers,
        out_shape=[jax.ShapeDtypeStruct((size, columns), jnp.int16)] * buffers,
        scratch_shapes=[pltpu.VMEM((slots, columns), f32)],
        compiler_params=params(),
        cost_estimate=cost(8 * local * slots * rank * columns, 2 * slots * columns),
        name="up",
    )(group, low, low_other, factor, own_up, *far_ups)
    order = return_order(buffers)
    returned = [terms[0]] + [exchange(terms[j], "pool", pool, j) for j in order]

    out = pl.pallas_call(
        functools.partial(finish_kernel, buffers, pool, local, depth),
        in_specs=[SMEM] + [VMEM] * (6 + buffers),
        out_specs=HBM,
        out_shape=jax.ShapeDtypeStruct((rows * columns // head, head), bf16),
        scratch_shapes=[
            pltpu.VMEM((rows * columns // head, head), bf16),
            pltpu.SemaphoreType.DMA((rows // 32,)),
        ],
        compiler_params=params(),
        cost_estimate=cost(4 * rows * slots * columns, 2 * slots * columns),
        name="finish",
    )(
        me,
        adapter_row,
        mine,
        other,
        cosine,
        sine,
        key_norm_gain.astype(f32)[None, :],
        *returned,
    )
    return out.reshape(rows, columns // (2 * head), 2, head)


def solution(mesh):
    return jax.shard_map(
        body,
        mesh=mesh,
        in_specs=(
            P(("groups", "pool"), "tp"),
            P(("groups", "pool"), None),
            P(("groups", "pool")),
            P("tp", None),
            P("pool", "tp", None),
            P("pool", None, None),
            P("pool"),
            P(),
        ),
        out_specs=P(("groups", "pool"), "tp", None, None),
        check_vma=False,
    )
```

```python
import functools

import jax
import jax.numpy as jnp
from jax import lax
from jax.experimental import pallas as pl
from jax.experimental.pallas import tpu as pltpu
from jax.sharding import PartitionSpec as P

ALPHA = 32
ROPE_THETA = 1000000.0
NORM_EPS = 1e-06
VMEM_LIMIT = 48 * 1024 * 1024
LANES = 128
EXPONENT_BITS = 8
EXPONENT_BIAS = 128

VMEM = pl.BlockSpec(memory_space=pltpu.VMEM)
HBM = pl.BlockSpec(memory_space=pltpu.HBM)
SMEM = pl.BlockSpec(memory_space=pltpu.SMEM)


def params(**kw):
    return pltpu.CompilerParams(vmem_limit_bytes=VMEM_LIMIT, **kw)


def cost(flops, bytes_accessed):
    return pl.CostEstimate(flops=flops, bytes_accessed=bytes_accessed, transcendentals=0)


def in_hbm(x):
    return pltpu.with_memory_space_constraint(x, pltpu.HBM)


def iota(shape, dim):
    return lax.broadcasted_iota(jnp.int32, shape, dim)


def to_column(row):
    n = row.shape[1]
    return jnp.sum(
        jnp.where(iota((n, n), 0) == iota((n, n), 1), row, 0), axis=1, keepdims=True
    )


def slot_places(row, me, pool, local, depth):
    n = row.shape[1]
    column = to_column(row)
    earlier = (column == row) & (iota((n, n), 0) < iota((n, n), 1))
    slot = jnp.sum(jnp.where(earlier, 1, 0), axis=0, keepdims=True)
    holder = row // local
    apart = holder ^ me
    buffer, far = apart % (pool // 2), apart // (pool // 2)
    return ((buffer * 2 + far) * local + (row - holder * local)) * depth + slot


def far_first(count):
    return sorted(range(1, count), key=lambda j: (-bin(j).count("1"), -j))


def return_order(count):
    order = far_first(count)
    return order[-1:] + order[:-1]


def halves(x):
    high = x.astype(jnp.bfloat16)
    low = (x - high.astype(jnp.float32)).astype(jnp.bfloat16)
    return high, low


def up_share_kernel(cores, group_ref, core_ref, ranks_ref, up_hbm, out_ref, factor_ref, own_ref, sem):
    local, rank, share = out_ref.shape
    at = core_ref[0] * (up_hbm.shape[2] // cores) + group_ref[0] * share
    copy = pltpu.make_async_copy(
        up_hbm.at[:, :, pl.ds(pl.multiple_of(at, share), share)], own_ref, sem
    )
    copy.start()
    copy.wait()
    for a in range(local):
        used = ranks_ref[a]

        def factor(shape, dim):
            scale = jnp.float32(ALPHA) / jnp.full(shape, used, jnp.int32).astype(jnp.float32)
            return jnp.where(iota(shape, dim) < used, scale, 0.0)

        factor_ref[a : a + 1, :] = factor((1, rank), 1)
        out_ref[a] = (own_ref[a].astype(jnp.float32) * factor((rank, 1), 0)).astype(jnp.bfloat16)


def pick_kernel(
    pool, local, depth, me_ref, group_ref, adapter_hbm, tokens_hbm, down_hbm, *refs
):
    share_ref, outs = refs[0], refs[1:-4]
    adapter_ref, tokens_ref, share_sem, sems = refs[-4:]
    rows, width = tokens_ref.shape
    share = share_ref.shape[1]
    parts = sems.shape[0] - 1
    part = rows // parts
    adapter_copy = pltpu.make_async_copy(adapter_hbm, adapter_ref, sems.at[parts])
    adapter_copy.start()
    copies = [
        pltpu.make_async_copy(
            tokens_hbm.at[pl.ds(i * part, part), :],
            tokens_ref.at[pl.ds(i * part, part), :],
            sems.at[i],
        )
        for i in range(parts)
    ]
    for copy in copies:
        copy.start()
    at = pl.multiple_of(group_ref[0] * share, share)
    share_copy = pltpu.make_async_copy(down_hbm.at[:, pl.ds(at, share), :], share_ref, share_sem)
    share_copy.start()
    adapter_copy.wait()
    place = slot_places(adapter_ref[...], me_ref[0], pool, local, depth)
    size = outs[0].shape[0]
    slots = len(outs) * size
    picker = jnp.where(iota((slots, rows), 0) == place, 1.0, 0.0).astype(jnp.bfloat16)
    for copy in copies:
        copy.wait()
    step = 512
    for at in range(0, width, step):
        block = jnp.dot(
            picker, tokens_ref[:, at : at + step], preferred_element_type=jnp.float32
        )
        for j, out in enumerate(outs):
            out[:, at : at + step] = block[j * size : (j + 1) * size].astype(jnp.bfloat16)
    share_copy.wait()


def base_kernel(
    core_ref,
    tokens_hbm,
    weight_hbm,
    down_hbm,
    up_hbm,
    theirs_ref,
    mine_ref,
    down_ref,
    up_ref,
    tokens_ref,
    weight_ref,
    other_sems,
    sems,
):
    rows, columns = mine_ref.shape
    steps = sems.shape[1]
    step = tokens_ref.shape[1] // steps
    copies = []
    for half in range(2):
        start = (1 - core_ref[0] if half == 0 else core_ref[0]) * columns
        start = pl.multiple_of(start, columns)
        for k in range(steps):
            copies.append(
                pltpu.make_async_copy(
                    weight_hbm.at[pl.ds(k * step, step), pl.ds(start, columns)],
                    weight_ref.at[half, pl.ds(k * step, step), :],
                    sems.at[half, k],
                )
            )
    tokens_copy = pltpu.make_async_copy(tokens_hbm, tokens_ref, other_sems.at[0])
    own = pl.multiple_of(core_ref[0] * columns, columns)
    factor_copies = [
        pltpu.make_async_copy(down_hbm, down_ref, other_sems.at[1]),
        pltpu.make_async_copy(up_hbm.at[:, :, pl.ds(own, columns)], up_ref, other_sems.at[2]),
    ]
    for copy in [tokens_copy] + copies + factor_copies:
        copy.start()
    tokens_copy.wait()
    for half, out in enumerate((theirs_ref, mine_ref)):
        for k in range(steps):
            copies[half * steps + k].wait()
            term = jnp.dot(
                tokens_ref[:, k * step : (k + 1) * step],
                weight_ref[half, k * step : (k + 1) * step, :],
                preferred_element_type=jnp.float32,
            )
            if k == 0:
                out[...] = term
            else:
                out[...] += term
    for copy in factor_copies:
        copy.wait()


def down_kernel(buffers, groups, local, depth, group_ref, down_ref, *refs):
    order = [0] + far_first(buffers)
    ins = [refs[order.index(j)] for j in range(buffers)]
    shares, out = refs[buffers : buffers + groups], refs[-1]
    rank = out.shape[1]
    share = shares[0].shape[1]
    total = None
    for k in range(groups):
        at = pl.multiple_of((group_ref[0] ^ k) * share, share)
        rows = jnp.concatenate([x[:, pl.ds(at, share)] for x in ins], axis=0)
        factors = [down_ref[a, pl.ds(at, share), :] for a in range(local)]
        factors += [shares[k][a] for a in range(local)]
        term = jnp.dot(
            rows, jnp.concatenate(factors, axis=1), preferred_element_type=jnp.float32
        )
        total = term if total is None else total + term
    which = (iota((total.shape[0], 1), 0) // depth) % (2 * local)
    low = total[:, :rank]
    for i in range(1, 2 * local):
        low = jnp.where(which == i, total[:, i * rank : (i + 1) * rank], low)
    out[...] = low


def up_kernel(
    buffers, groups, local, depth, group_ref, low_ref, other_ref, factor_ref, up_ref, *refs
):
    shares, outs, term_ref = refs[:groups], refs[groups : groups + buffers], refs[-1]
    rows, rank = low_ref.shape
    size = rows // buffers
    columns = up_ref.shape[2]
    share = columns // groups
    which = (iota((rows, 1), 0) // depth) % (2 * local)
    low = low_ref[...] + other_ref[...]
    for a in range(local):
        low = jnp.where(which == a, low * factor_ref[a : a + 1, :], low)
    both = jnp.concatenate(halves(low), axis=0)
    which = jnp.concatenate([which, which], axis=0)
    spread = jnp.concatenate(
        [jnp.where(which == i, both, jnp.zeros_like(both)) for i in range(2 * local)], axis=1
    )
    for k in range(groups):
        at = pl.multiple_of((group_ref[0] ^ k) * share, share)
        up = [up_ref[a, :, pl.ds(at, share)] for a in range(local)]
        up += [shares[k][a] for a in range(local)]
        term = jnp.dot(
            spread, jnp.concatenate(up, axis=0), preferred_element_type=jnp.float32
        )
        term_ref[:, pl.ds(at, share)] = term[:rows] + term[rows:]
    lane = iota((1, LANES), 1)
    for j, out in enumerate(outs):
        term = term_ref[j * size : (j + 1) * size, :]
        top = jnp.max(jnp.abs(term), axis=1, keepdims=True)
        exponent = jnp.ceil(jnp.log2(jnp.maximum(top, 1e-30)) + 1e-3)
        code = jnp.clip(jnp.round(term * jnp.exp2(15.0 - exponent)), -32767.0, 32767.0)
        code = code.astype(jnp.int32)
        biased = exponent.astype(jnp.int32) + EXPONENT_BIAS
        first = code[:, :LANES]
        marked = (first & -2) | ((biased >> jnp.minimum(lane, EXPONENT_BITS - 1)) & 1)
        first = jnp.where(lane < EXPONENT_BITS, marked, first)
        out[:, :LANES] = first.astype(jnp.int16)
        out[:, LANES:] = code[:, LANES:].astype(jnp.int16)


def finish_kernel(
    buffers, pool, local, depth, me_ref, adapter_ref, mine_ref, other_ref, cos_ref, sin_ref, gain_ref, *refs
):
    order = [0] + return_order(buffers)
    ins = [refs[order.index(j)] for j in range(buffers)]
    out_hbm, out_ref, sems = refs[-3:]
    rows, columns = mine_ref.shape
    head = cos_ref.shape[1]
    place = to_column(slot_places(adapter_ref[...], me_ref[0], pool, local, depth))
    slots = buffers * ins[0].shape[0]
    picker = jnp.where(iota((rows, slots), 1) == place, 1.0, 0.0).astype(jnp.bfloat16)

    def picked(at, size):
        code = jnp.concatenate([x[:, at : at + size] for x in ins], axis=0).astype(jnp.int32)
        high = (code >> 8).astype(jnp.float32).astype(jnp.bfloat16)
        low = (code & 255).astype(jnp.float32).astype(jnp.bfloat16)
        high = jnp.dot(picker, high, preferred_element_type=jnp.float32)
        low = jnp.dot(picker, low, preferred_element_type=jnp.float32)
        return high * 256.0 + low

    lane = iota((1, LANES), 1)
    bits = picked(0, LANES).astype(jnp.int32) & 1
    bits = jnp.where(lane < EXPONENT_BITS, bits << jnp.minimum(lane, EXPONENT_BITS - 1), 0)
    exponent = jnp.sum(bits.astype(jnp.float32), axis=1, keepdims=True) - EXPONENT_BIAS
    scale = jnp.exp2(exponent - 15.0)
    cosine, sine, gain = cos_ref[...], sin_ref[...], gain_ref[...]
    entries = []
    for at in range(0, columns, 2 * head):
        projected = mine_ref[:, at : at + 2 * head] + other_ref[:, at : at + 2 * head]
        projected = projected + picked(at, 2 * head) * scale
        key, value = projected[:, :head], projected[:, head:]
        mean = jnp.mean(key * key, axis=1, keepdims=True)
        normed = key * lax.rsqrt(mean + NORM_EPS) * gain
        rotated = normed * cosine + pltpu.roll(normed, head // 2, 1) * sine
        entries += [rotated.astype(jnp.bfloat16), value.astype(jnp.bfloat16)]
    kinds, block = len(entries), 16
    n = kinds * block
    source = (iota((n, n), 0) % kinds) * block + iota((n, n), 0) // kinds
    order = jnp.where(iota((n, n), 1) == source, 1.0, 0.0).astype(jnp.bfloat16)
    copies = []
    for i in range(rows // block):
        stacked = jnp.concatenate([e[i * block : (i + 1) * block] for e in entries], axis=0)
        mixed = jnp.dot(order, stacked, preferred_element_type=jnp.float32)
        out_ref[i * n : (i + 1) * n, :] = mixed.astype(jnp.bfloat16)
        if i % 2:
            done = pl.ds((i - 1) * n, 2 * n)
            copies.append(
                pltpu.make_async_copy(out_ref.at[done, :], out_hbm.at[done, :], sems.at[i // 2])
            )
            copies[-1].start()
    for copy in copies:
        copy.wait()


def body(
    tokens,
    row_adapters,
    positions,
    key_value_weight,
    adapter_down,
    adapter_up,
    ranks,
    key_norm_gain,
):
    pool = lax.axis_size("pool")
    groups = lax.axis_size("groups")
    cores = lax.axis_size("tp")
    rows, width = tokens.shape
    local = adapter_down.shape[0]
    adapters = local * pool
    columns = key_value_weight.shape[1] // cores
    rank = adapter_down.shape[2]
    head = key_norm_gain.shape[0]
    depth = max(2, 2 * rows // adapters)
    buffers = pool // 2
    size = 2 * local * depth
    f32, bf16 = jnp.float32, jnp.bfloat16

    me = lax.axis_index("pool").astype(jnp.int32)[None]
    core = lax.axis_index("tp").astype(jnp.int32)[None]
    group = lax.axis_index("groups").astype(jnp.int32)[None]

    def exchange(x, axis, count, j):
        return lax.ppermute(x, axis, [(p, p ^ j) for p in range(count)])

    def hand_round(share):
        return [share] + [exchange(share, "groups", groups, k) for k in range(1, groups)]

    adapter_row = row_adapters.reshape(1, rows)
    down_share = width // groups
    parts = rows // 16
    down_part, *picked = pl.pallas_call(
        functools.partial(pick_kernel, pool, local, depth),
        in_specs=[SMEM] * 2 + [HBM] * 3,
        out_specs=[VMEM] * (1 + buffers),
        out_shape=[jax.ShapeDtypeStruct((local, down_share, rank), bf16)]
        + [jax.ShapeDtypeStruct((size, width), bf16)] * buffers,
        scratch_shapes=[
            pltpu.VMEM((1, rows), jnp.int32),
            pltpu.VMEM((rows, width), bf16),
            pltpu.SemaphoreType.DMA,
            pltpu.SemaphoreType.DMA((parts + 1,)),
        ],
        compiler_params=params(),
        cost_estimate=cost(2 * buffers * size * rows * width, 2 * (rows + buffers * size) * width),
        name="pick",
    )(me, group, in_hbm(adapter_row), in_hbm(tokens), in_hbm(adapter_down))
    far_down = exchange(down_part, "pool", pool, pool // 2)
    up_share = columns // groups
    ranks_now, adapter_up_now, _ = lax.optimization_barrier((ranks, adapter_up, picked))
    up_part, factor = pl.pallas_call(
        functools.partial(up_share_kernel, cores),
        in_specs=[SMEM] * 3 + [HBM],
        out_specs=[VMEM] * 2,
        out_shape=[
            jax.ShapeDtypeStruct((local, rank, up_share), bf16),
            jax.ShapeDtypeStruct((local, rank), f32),
        ],
        scratch_shapes=[
            pltpu.VMEM((local, rank, up_share), bf16),
            pltpu.SemaphoreType.DMA,
        ],
        compiler_params=params(),
        cost_estimate=cost(local * rank * up_share, 4 * local * rank * up_share),
        name="up_share",
    )(group, core, ranks_now, in_hbm(adapter_up_now))
    far_up = exchange(up_part, "pool", pool, pool // 2)

    order = far_first(buffers)
    early, late = order[:1], order[1:]
    late_rows, _ = lax.optimization_barrier(([picked[j] for j in late], up_part))
    leaving = [picked[j] for j in early] + late_rows
    arrived = [picked[0]] + [exchange(x, "pool", pool, j) for x, j in zip(leaving, order)]

    steps = 5
    theirs, mine, own_down, own_up = pl.pallas_call(
        base_kernel,
        in_specs=[SMEM] + [HBM] * 4,
        out_specs=[VMEM] * 4,
        out_shape=[jax.ShapeDtypeStruct((rows, columns), f32)] * 2
        + [
            jax.ShapeDtypeStruct(adapter_down.shape, bf16),
            jax.ShapeDtypeStruct((local, rank, columns), bf16),
        ],
        scratch_shapes=[
            pltpu.VMEM((rows, width), bf16),
            pltpu.VMEM((2, width, columns), bf16),
            pltpu.SemaphoreType.DMA((3,)),
            pltpu.SemaphoreType.DMA((2, steps)),
        ],
        compiler_params=params(),
        cost_estimate=cost(4 * rows * width * columns, 4 * width * columns),
        name="base",
    )(
        core,
        in_hbm(tokens),
        in_hbm(key_value_weight),
        in_hbm(adapter_down),
        in_hbm(adapter_up),
    )
    far_down, theirs = lax.optimization_barrier((far_down, theirs))
    far_downs = hand_round(far_down)
    far_up, _ = lax.optimization_barrier((far_up, far_down))
    far_ups = hand_round(far_up)
    half_dim = head // 2
    frequency = jnp.power(
        f32(ROPE_THETA), -jnp.arange(half_dim, dtype=f32) * (2.0 / head)
    )
    angles = positions.astype(f32)[:, None] * frequency[None, :]
    cosine, sine = jnp.cos(angles), jnp.sin(angles)
    cosine = jnp.concatenate([cosine, cosine], axis=1)
    sine = jnp.concatenate([-sine, sine], axis=1)

    far_ups, theirs = lax.optimization_barrier((far_ups, theirs))
    other = exchange(theirs, "tp", cores, 1)
    arrived, mine, cosine, sine = lax.optimization_barrier((arrived, mine, cosine, sine))
    slots = buffers * size
    low = pl.pallas_call(
        functools.partial(down_kernel, buffers, groups, local, depth),
        in_specs=[SMEM] + [VMEM] * (1 + buffers + groups),
        out_specs=VMEM,
        out_shape=jax.ShapeDtypeStruct((slots, rank), f32),
        compiler_params=params(),
        cost_estimate=cost(4 * local * slots * rank * width, 2 * (slots + rank) * width),
        name="down",
    )(group, own_down, *arrived, *far_downs)
    low_other = exchange(low, "tp", cores, 1)

    terms = pl.pallas_call(
        functools.partial(up_kernel, buffers, groups, local, depth),
        in_specs=[SMEM] + [VMEM] * (4 + groups),
        out_specs=[VMEM] * buffers,
        out_shape=[jax.ShapeDtypeStruct((size, columns), jnp.int16)] * buffers,
        scratch_shapes=[pltpu.VMEM((slots, columns), f32)],
        compiler_params=params(),
        cost_estimate=cost(8 * local * slots * rank * columns, 2 * slots * columns),
        name="up",
    )(group, low, low_other, factor, own_up, *far_ups)
    order = return_order(buffers)
    returned = [terms[0]] + [exchange(terms[j], "pool", pool, j) for j in order]

    out = pl.pallas_call(
        functools.partial(finish_kernel, buffers, pool, local, depth),
        in_specs=[SMEM] + [VMEM] * (6 + buffers),
        out_specs=HBM,
        out_shape=jax.ShapeDtypeStruct((rows * columns // head, head), bf16),
        scratch_shapes=[
            pltpu.VMEM((rows * columns // head, head), bf16),
            pltpu.SemaphoreType.DMA((rows // 32,)),
        ],
        compiler_params=params(),
        cost_estimate=cost(4 * rows * slots * columns, 2 * slots * columns),
        name="finish",
    )(
        me,
        adapter_row,
        mine,
        other,
        cosine,
        sine,
        key_norm_gain.astype(f32)[None, :],
        *returned,
    )
    return out.reshape(rows, columns // (2 * head), 2, head)


def solution(mesh):
    return jax.shard_map(
        body,
        mesh=mesh,
        in_specs=(
            P(("groups", "pool"), "tp"),
            P(("groups", "pool"), None),
            P(("groups", "pool")),
            P("tp", None),
            P("pool", "tp", None),
            P("pool", None, None),
            P("pool"),
            P(),
        ),
        out_specs=P(("groups", "pool"), "tp", None, None),
        check_vma=False,
    )
```

```python
import functools

import jax
import jax.numpy as jnp
from jax import lax
from jax.experimental import pallas as pl
from jax.experimental.pallas import tpu as pltpu
from jax.sharding import PartitionSpec as P

ALPHA = 32
ROPE_THETA = 1000000.0
NORM_EPS = 1e-06
VMEM_LIMIT = 48 * 1024 * 1024
LANES = 128
EXPONENT_BITS = 8
EXPONENT_BIAS = 128

VMEM = pl.BlockSpec(memory_space=pltpu.VMEM)
HBM = pl.BlockSpec(memory_space=pltpu.HBM)
SMEM = pl.BlockSpec(memory_space=pltpu.SMEM)


def params(**kw):
    return pltpu.CompilerParams(vmem_limit_bytes=VMEM_LIMIT, **kw)


def cost(flops, bytes_accessed):
    return pl.CostEstimate(flops=flops, bytes_accessed=bytes_accessed, transcendentals=0)


def in_hbm(x):
    return pltpu.with_memory_space_constraint(x, pltpu.HBM)


def iota(shape, dim):
    return lax.broadcasted_iota(jnp.int32, shape, dim)


def to_column(row):
    n = row.shape[1]
    return jnp.sum(
        jnp.where(iota((n, n), 0) == iota((n, n), 1), row, 0), axis=1, keepdims=True
    )


def slot_places(row, me, pool, local, depth, far_outer):
    n = row.shape[1]
    column = to_column(row)
    earlier = (column == row) & (iota((n, n), 0) < iota((n, n), 1))
    slot = jnp.sum(jnp.where(earlier, 1, 0), axis=0, keepdims=True)
    holder = row // local
    apart = holder ^ me
    buffer, far = apart % (pool // 2), apart // (pool // 2)
    block = far * (pool // 2) + buffer if far_outer else buffer * 2 + far
    return (block * local + (row - holder * local)) * depth + slot


def far_first(count):
    return sorted(range(1, count), key=lambda j: (-bin(j).count("1"), -j))


def return_order(count):
    order = far_first(count)
    return order[-1:] + order[:-1]


def halves(x):
    high = x.astype(jnp.bfloat16)
    low = (x - high.astype(jnp.float32)).astype(jnp.bfloat16)
    return high, low


def up_share_kernel(cores, group_ref, core_ref, ranks_ref, up_hbm, out_ref, factor_ref, own_ref, sem):
    local, rank, share = out_ref.shape
    at = core_ref[0] * (up_hbm.shape[2] // cores) + group_ref[0] * share
    copy = pltpu.make_async_copy(
        up_hbm.at[:, :, pl.ds(pl.multiple_of(at, share), share)], own_ref, sem
    )
    copy.start()
    copy.wait()
    for a in range(local):
        used = ranks_ref[a]

        def factor(shape, dim):
            scale = jnp.float32(ALPHA) / jnp.full(shape, used, jnp.int32).astype(jnp.float32)
            return jnp.where(iota(shape, dim) < used, scale, 0.0)

        factor_ref[a : a + 1, :] = factor((1, rank), 1)
        out_ref[a] = (own_ref[a].astype(jnp.float32) * factor((rank, 1), 0)).astype(jnp.bfloat16)


def pick_kernel(
    pool, local, depth, me_ref, group_ref, adapter_hbm, tokens_hbm, down_hbm, *refs
):
    share_ref, outs = refs[0], refs[1:-4]
    adapter_ref, tokens_ref, share_sem, sems = refs[-4:]
    rows, width = tokens_ref.shape
    share = share_ref.shape[1]
    parts = sems.shape[0] - 1
    part = rows // parts
    adapter_copy = pltpu.make_async_copy(adapter_hbm, adapter_ref, sems.at[parts])
    adapter_copy.start()
    copies = [
        pltpu.make_async_copy(
            tokens_hbm.at[pl.ds(i * part, part), :],
            tokens_ref.at[pl.ds(i * part, part), :],
            sems.at[i],
        )
        for i in range(parts)
    ]
    for copy in copies:
        copy.start()
    at = pl.multiple_of(group_ref[0] * share, share)
    share_copy = pltpu.make_async_copy(down_hbm.at[:, pl.ds(at, share), :], share_ref, share_sem)
    share_copy.start()
    adapter_copy.wait()
    place = slot_places(adapter_ref[...], me_ref[0], pool, local, depth, False)
    size = outs[0].shape[0]
    slots = len(outs) * size
    picker = jnp.where(iota((slots, rows), 0) == place, 1.0, 0.0).astype(jnp.bfloat16)
    for copy in copies:
        copy.wait()
    step = 512
    for at in range(0, width, step):
        block = jnp.dot(
            picker, tokens_ref[:, at : at + step], preferred_element_type=jnp.float32
        )
        for j, out in enumerate(outs):
            out[:, at : at + step] = block[j * size : (j + 1) * size].astype(jnp.bfloat16)
    share_copy.wait()


def base_kernel(
    core_ref,
    tokens_hbm,
    weight_hbm,
    down_hbm,
    up_hbm,
    theirs_ref,
    mine_ref,
    down_ref,
    up_ref,
    tokens_ref,
    weight_ref,
    other_sems,
    sems,
):
    rows, columns = mine_ref.shape
    steps = sems.shape[1]
    step = tokens_ref.shape[1] // steps
    copies = []
    for half in range(2):
        start = (1 - core_ref[0] if half == 0 else core_ref[0]) * columns
        start = pl.multiple_of(start, columns)
        for k in range(steps):
            copies.append(
                pltpu.make_async_copy(
                    weight_hbm.at[pl.ds(k * step, step), pl.ds(start, columns)],
                    weight_ref.at[half, pl.ds(k * step, step), :],
                    sems.at[half, k],
                )
            )
    tokens_copy = pltpu.make_async_copy(tokens_hbm, tokens_ref, other_sems.at[0])
    own = pl.multiple_of(core_ref[0] * columns, columns)
    factor_copies = [
        pltpu.make_async_copy(down_hbm, down_ref, other_sems.at[1]),
        pltpu.make_async_copy(up_hbm.at[:, :, pl.ds(own, columns)], up_ref, other_sems.at[2]),
    ]
    for copy in [tokens_copy] + copies + factor_copies:
        copy.start()
    tokens_copy.wait()
    for half, out in enumerate((theirs_ref, mine_ref)):
        for k in range(steps):
            copies[half * steps + k].wait()
            term = jnp.dot(
                tokens_ref[:, k * step : (k + 1) * step],
                weight_ref[half, k * step : (k + 1) * step, :],
                preferred_element_type=jnp.float32,
            )
            if k == 0:
                out[...] = term
            else:
                out[...] += term
    for copy in factor_copies:
        copy.wait()


def down_kernel(buffers, groups, local, depth, group_ref, down_ref, *refs):
    order = [0] + far_first(buffers)
    ins = [refs[order.index(j)] for j in range(buffers)]
    shares, out = refs[buffers : buffers + groups], refs[-1]
    rank = out.shape[1]
    share = shares[0].shape[1]
    total = None
    for k in range(groups):
        at = pl.multiple_of((group_ref[0] ^ k) * share, share)
        rows = jnp.concatenate([x[:, pl.ds(at, share)] for x in ins], axis=0)
        factors = [down_ref[a, pl.ds(at, share), :] for a in range(local)]
        factors += [shares[k][a] for a in range(local)]
        term = jnp.dot(
            rows, jnp.concatenate(factors, axis=1), preferred_element_type=jnp.float32
        )
        total = term if total is None else total + term
    for j in range(buffers):
        for i in range(2 * local):
            far, a = i // local, i % local
            source, target = (j * 2 * local + i) * depth, ((far * buffers + j) * local + a) * depth
            out[target : target + depth, :] = total[
                source : source + depth, i * rank : (i + 1) * rank
            ]


def code_terms(low, up, local, depth, outs, columns, scale=None):
    rows = low.shape[0]
    size = rows // len(outs)
    which = (iota((rows, 1), 0) // depth) % local
    if scale is not None:
        for a in range(local):
            low = jnp.where(which == a, low * scale[a : a + 1, :], low)
    both = jnp.concatenate(halves(low), axis=0)
    which = jnp.concatenate([which, which], axis=0)
    spread = jnp.concatenate(
        [jnp.where(which == a, both, jnp.zeros_like(both)) for a in range(local)], axis=1
    )
    term = jnp.dot(spread, jnp.concatenate(up, axis=0), preferred_element_type=jnp.float32)
    term = term[:rows] + term[rows:]
    top = jnp.max(jnp.abs(term), axis=1, keepdims=True)
    exponent = jnp.ceil(jnp.log2(jnp.maximum(top, 1e-30)) + 1e-3)
    code = jnp.clip(jnp.round(term * jnp.exp2(15.0 - exponent)), -32767.0, 32767.0)
    code = code.astype(jnp.int32)
    lane = iota((1, LANES), 1)
    biased = exponent.astype(jnp.int32) + EXPONENT_BIAS
    first = code[:, :LANES]
    marked = (first & -2) | ((biased >> jnp.minimum(lane, EXPONENT_BITS - 1)) & 1)
    first = jnp.where(lane < EXPONENT_BITS, marked, first).astype(jnp.int16)
    rest = code[:, LANES:].astype(jnp.int16)
    for j, out in enumerate(outs):
        out[:, :LANES] = first[j * size : (j + 1) * size]
        out[:, LANES:] = rest[j * size : (j + 1) * size]


def near_kernel(local, depth, low_ref, other_ref, factor_ref, up_ref, *outs):
    rows = low_ref.shape[0] // 2
    low = low_ref[:rows, :] + other_ref[:rows, :]
    up = [up_ref[a] for a in range(local)]
    code_terms(low, up, local, depth, outs, up_ref.shape[2], factor_ref[...])


def far_kernel(groups, local, depth, group_ref, low_ref, other_ref, *refs):
    shares, outs, up_ref = refs[:groups], refs[groups:-1], refs[-1]
    rows = low_ref.shape[0] // 2
    low = low_ref[rows:, :] + other_ref[rows:, :]
    share = shares[0].shape[2]
    for k in range(groups):
        at = pl.multiple_of((group_ref[0] ^ k) * share, share)
        up_ref[:, :, pl.ds(at, share)] = shares[k][...]
    up = [up_ref[a] for a in range(local)]
    code_terms(low, up, local, depth, outs, up_ref.shape[2])


def finish_kernel(
    buffers, pool, local, depth, me_ref, adapter_ref, mine_ref, other_ref, cos_ref, sin_ref, gain_ref, *refs
):
    order = [0] + return_order(buffers)
    ins = [refs[(1 - f) * buffers + order.index(j)] for f in range(2) for j in range(buffers)]
    out_hbm, out_ref, sems = refs[-3:]
    rows, columns = mine_ref.shape
    head = cos_ref.shape[1]
    place = to_column(slot_places(adapter_ref[...], me_ref[0], pool, local, depth, True))
    slots = len(ins) * ins[0].shape[0]
    picker = jnp.where(iota((rows, slots), 1) == place, 1.0, 0.0).astype(jnp.bfloat16)

    def picked(at, size):
        code = jnp.concatenate([x[:, at : at + size] for x in ins], axis=0).astype(jnp.int32)
        high = (code >> 8).astype(jnp.float32).astype(jnp.bfloat16)
        low = (code & 255).astype(jnp.float32).astype(jnp.bfloat16)
        high = jnp.dot(picker, high, preferred_element_type=jnp.float32)
        low = jnp.dot(picker, low, preferred_element_type=jnp.float32)
        return high * 256.0 + low

    lane = iota((1, LANES), 1)
    bits = picked(0, LANES).astype(jnp.int32) & 1
    bits = jnp.where(lane < EXPONENT_BITS, bits << jnp.minimum(lane, EXPONENT_BITS - 1), 0)
    exponent = jnp.sum(bits.astype(jnp.float32), axis=1, keepdims=True) - EXPONENT_BIAS
    scale = jnp.exp2(exponent - 15.0)
    cosine, sine, gain = cos_ref[...], sin_ref[...], gain_ref[...]
    entries = []
    for at in range(0, columns, 2 * head):
        projected = mine_ref[:, at : at + 2 * head] + other_ref[:, at : at + 2 * head]
        projected = projected + picked(at, 2 * head) * scale
        key, value = projected[:, :head], projected[:, head:]
        mean = jnp.mean(key * key, axis=1, keepdims=True)
        normed = key * lax.rsqrt(mean + NORM_EPS) * gain
        rotated = normed * cosine + pltpu.roll(normed, head // 2, 1) * sine
        entries += [rotated.astype(jnp.bfloat16), value.astype(jnp.bfloat16)]
    kinds, block = len(entries), 16
    n = kinds * block
    source = (iota((n, n), 0) % kinds) * block + iota((n, n), 0) // kinds
    order = jnp.where(iota((n, n), 1) == source, 1.0, 0.0).astype(jnp.bfloat16)
    copies = []
    for i in range(rows // block):
        stacked = jnp.concatenate([e[i * block : (i + 1) * block] for e in entries], axis=0)
        mixed = jnp.dot(order, stacked, preferred_element_type=jnp.float32)
        out_ref[i * n : (i + 1) * n, :] = mixed.astype(jnp.bfloat16)
        if i % 2:
            done = pl.ds((i - 1) * n, 2 * n)
            copies.append(
                pltpu.make_async_copy(out_ref.at[done, :], out_hbm.at[done, :], sems.at[i // 2])
            )
            copies[-1].start()
    for copy in copies:
        copy.wait()


def body(
    tokens,
    row_adapters,
    positions,
    key_value_weight,
    adapter_down,
    adapter_up,
    ranks,
    key_norm_gain,
):
    pool = lax.axis_size("pool")
    groups = lax.axis_size("groups")
    cores = lax.axis_size("tp")
    rows, width = tokens.shape
    local = adapter_down.shape[0]
    adapters = local * pool
    columns = key_value_weight.shape[1] // cores
    rank = adapter_down.shape[2]
    head = key_norm_gain.shape[0]
    depth = max(2, 2 * rows // adapters)
    buffers = pool // 2
    size = 2 * local * depth
    f32, bf16 = jnp.float32, jnp.bfloat16

    me = lax.axis_index("pool").astype(jnp.int32)[None]
    core = lax.axis_index("tp").astype(jnp.int32)[None]
    group = lax.axis_index("groups").astype(jnp.int32)[None]

    def exchange(x, axis, count, j):
        return lax.ppermute(x, axis, [(p, p ^ j) for p in range(count)])

    def hand_round(share):
        return [share] + [exchange(share, "groups", groups, k) for k in range(1, groups)]

    adapter_row = row_adapters.reshape(1, rows)
    down_share = width // groups
    parts = rows // 16
    down_part, *picked = pl.pallas_call(
        functools.partial(pick_kernel, pool, local, depth),
        in_specs=[SMEM] * 2 + [HBM] * 3,
        out_specs=[VMEM] * (1 + buffers),
        out_shape=[jax.ShapeDtypeStruct((local, down_share, rank), bf16)]
        + [jax.ShapeDtypeStruct((size, width), bf16)] * buffers,
        scratch_shapes=[
            pltpu.VMEM((1, rows), jnp.int32),
            pltpu.VMEM((rows, width), bf16),
            pltpu.SemaphoreType.DMA,
            pltpu.SemaphoreType.DMA((parts + 1,)),
        ],
        compiler_params=params(),
        cost_estimate=cost(2 * buffers * size * rows * width, 2 * (rows + buffers * size) * width),
        name="pick",
    )(me, group, in_hbm(adapter_row), in_hbm(tokens), in_hbm(adapter_down))
    far_down = exchange(down_part, "pool", pool, pool // 2)
    order = far_first(buffers)
    arrived = [picked[0]] + [exchange(picked[j], "pool", pool, j) for j in order]

    up_share = columns // groups
    ranks_now, adapter_up_now, _ = lax.optimization_barrier((ranks, adapter_up, picked))
    up_part, factor = pl.pallas_call(
        functools.partial(up_share_kernel, cores),
        in_specs=[SMEM] * 3 + [HBM],
        out_specs=[VMEM] * 2,
        out_shape=[
            jax.ShapeDtypeStruct((local, rank, up_share), bf16),
            jax.ShapeDtypeStruct((local, rank), f32),
        ],
        scratch_shapes=[
            pltpu.VMEM((local, rank, up_share), bf16),
            pltpu.SemaphoreType.DMA,
        ],
        compiler_params=params(),
        cost_estimate=cost(local * rank * up_share, 4 * local * rank * up_share),
        name="up_share",
    )(group, core, ranks_now, in_hbm(adapter_up_now))
    far_up = exchange(up_part, "pool", pool, pool // 2)

    steps = 5
    theirs, mine, own_down, own_up = pl.pallas_call(
        base_kernel,
        in_specs=[SMEM] + [HBM] * 4,
        out_specs=[VMEM] * 4,
        out_shape=[jax.ShapeDtypeStruct((rows, columns), f32)] * 2
        + [
            jax.ShapeDtypeStruct(adapter_down.shape, bf16),
            jax.ShapeDtypeStruct((local, rank, columns), bf16),
        ],
        scratch_shapes=[
            pltpu.VMEM((rows, width), bf16),
            pltpu.VMEM((2, width, columns), bf16),
            pltpu.SemaphoreType.DMA((3,)),
            pltpu.SemaphoreType.DMA((2, steps)),
        ],
        compiler_params=params(),
        cost_estimate=cost(4 * rows * width * columns, 4 * width * columns),
        name="base",
    )(
        core,
        in_hbm(tokens),
        in_hbm(key_value_weight),
        in_hbm(adapter_down),
        in_hbm(adapter_up),
    )
    far_down, theirs = lax.optimization_barrier((far_down, theirs))
    far_downs = hand_round(far_down)
    far_up, _ = lax.optimization_barrier((far_up, far_down))
    far_ups = hand_round(far_up)
    half_dim = head // 2
    frequency = jnp.power(
        f32(ROPE_THETA), -jnp.arange(half_dim, dtype=f32) * (2.0 / head)
    )
    angles = positions.astype(f32)[:, None] * frequency[None, :]
    cosine, sine = jnp.cos(angles), jnp.sin(angles)
    cosine = jnp.concatenate([cosine, cosine], axis=1)
    sine = jnp.concatenate([-sine, sine], axis=1)

    arrived[1], theirs = lax.optimization_barrier((arrived[1], theirs))
    other = exchange(theirs, "tp", cores, 1)
    arrived, mine, cosine, sine = lax.optimization_barrier((arrived, mine, cosine, sine))
    slots = buffers * size
    low = pl.pallas_call(
        functools.partial(down_kernel, buffers, groups, local, depth),
        in_specs=[SMEM] + [VMEM] * (1 + buffers + groups),
        out_specs=VMEM,
        out_shape=jax.ShapeDtypeStruct((slots, rank), f32),
        compiler_params=params(),
        cost_estimate=cost(4 * local * slots * rank * width, 2 * (slots + rank) * width),
        name="down",
    )(group, own_down, *arrived, *far_downs)
    low_other = exchange(low, "tp", cores, 1)

    half = local * depth
    coded = [jax.ShapeDtypeStruct((half, columns), jnp.int16)] * buffers
    order = return_order(buffers)

    def come_back(terms):
        return [terms[0]] + [exchange(terms[j], "pool", pool, j) for j in order]

    near = pl.pallas_call(
        functools.partial(near_kernel, local, depth),
        in_specs=[VMEM] * 4,
        out_specs=[VMEM] * buffers,
        out_shape=coded,
        compiler_params=params(),
        cost_estimate=cost(4 * local * slots * rank * columns, slots * columns),
        name="near_terms",
    )(low, low_other, factor, own_up)
    near, low, low_other = lax.optimization_barrier((near, low, low_other))
    returned = come_back(near)
    far = pl.pallas_call(
        functools.partial(far_kernel, groups, local, depth),
        in_specs=[SMEM] + [VMEM] * (2 + groups),
        out_specs=[VMEM] * buffers,
        out_shape=coded,
        scratch_shapes=[pltpu.VMEM((local, rank, columns), bf16)],
        compiler_params=params(),
        cost_estimate=cost(4 * local * slots * rank * columns, slots * columns),
        name="far_terms",
    )(group, low, low_other, *far_ups)
    far, returned[1] = lax.optimization_barrier((far, returned[1]))
    returned = come_back(far) + returned

    out = pl.pallas_call(
        functools.partial(finish_kernel, buffers, pool, local, depth),
        in_specs=[SMEM] + [VMEM] * (6 + 2 * buffers),
        out_specs=HBM,
        out_shape=jax.ShapeDtypeStruct((rows * columns // head, head), bf16),
        scratch_shapes=[
            pltpu.VMEM((rows * columns // head, head), bf16),
            pltpu.SemaphoreType.DMA((rows // 32,)),
        ],
        compiler_params=params(),
        cost_estimate=cost(4 * rows * slots * columns, 2 * slots * columns),
        name="finish",
    )(
        me,
        adapter_row,
        mine,
        other,
        cosine,
        sine,
        key_norm_gain.astype(f32)[None, :],
        *returned,
    )
    return out.reshape(rows, columns // (2 * head), 2, head)


def solution(mesh):
    return jax.shard_map(
        body,
        mesh=mesh,
        in_specs=(
            P(("groups", "pool"), "tp"),
            P(("groups", "pool"), None),
            P(("groups", "pool")),
            P("tp", None),
            P("pool", "tp", None),
            P("pool", None, None),
            P("pool"),
            P(),
        ),
        out_specs=P(("groups", "pool"), "tp", None, None),
        check_vma=False,
    )
```

```python
import functools

import jax
import jax.numpy as jnp
from jax import lax
from jax.experimental import pallas as pl
from jax.experimental.pallas import tpu as pltpu
from jax.sharding import PartitionSpec as P

ALPHA = 32
ROPE_THETA = 1000000.0
NORM_EPS = 1e-06
VMEM_LIMIT = 48 * 1024 * 1024
LANES = 128
EXPONENT_BITS = 8
EXPONENT_BIAS = 128

VMEM = pl.BlockSpec(memory_space=pltpu.VMEM)
HBM = pl.BlockSpec(memory_space=pltpu.HBM)
SMEM = pl.BlockSpec(memory_space=pltpu.SMEM)


def params(**kw):
    return pltpu.CompilerParams(vmem_limit_bytes=VMEM_LIMIT, **kw)


def cost(flops, bytes_accessed):
    return pl.CostEstimate(flops=flops, bytes_accessed=bytes_accessed, transcendentals=0)


def in_hbm(x):
    return pltpu.with_memory_space_constraint(x, pltpu.HBM)


def iota(shape, dim):
    return lax.broadcasted_iota(jnp.int32, shape, dim)


def to_column(row):
    n = row.shape[1]
    return jnp.sum(
        jnp.where(iota((n, n), 0) == iota((n, n), 1), row, 0), axis=1, keepdims=True
    )


def slot_places(row, me, pool, local, depth):
    n = row.shape[1]
    column = to_column(row)
    earlier = (column == row) & (iota((n, n), 0) < iota((n, n), 1))
    slot = jnp.sum(jnp.where(earlier, 1, 0), axis=0, keepdims=True)
    holder = row // local
    apart = holder ^ me
    buffer, far = apart % (pool // 2), apart // (pool // 2)
    return ((buffer * 2 + far) * local + (row - holder * local)) * depth + slot


def far_first(count):
    return sorted(range(1, count), key=lambda j: (-bin(j).count("1"), -j))


def return_order(count):
    order = far_first(count)
    return order[-1:] + order[:-1]


def halves(x):
    high = x.astype(jnp.bfloat16)
    low = (x - high.astype(jnp.float32)).astype(jnp.bfloat16)
    return high, low


def up_share_kernel(cores, group_ref, core_ref, ranks_ref, up_hbm, out_ref, factor_ref, own_ref, sem):
    local, rank, share = out_ref.shape
    at = core_ref[0] * (up_hbm.shape[2] // cores) + group_ref[0] * share
    copy = pltpu.make_async_copy(
        up_hbm.at[:, :, pl.ds(pl.multiple_of(at, share), share)], own_ref, sem
    )
    copy.start()
    copy.wait()
    for a in range(local):
        used = ranks_ref[a]

        def factor(shape, dim):
            scale = jnp.float32(ALPHA) / jnp.full(shape, used, jnp.int32).astype(jnp.float32)
            return jnp.where(iota(shape, dim) < used, scale, 0.0)

        factor_ref[a : a + 1, :] = factor((1, rank), 1)
        out_ref[a] = (own_ref[a].astype(jnp.float32) * factor((rank, 1), 0)).astype(jnp.bfloat16)


def pick_kernel(
    pool, local, depth, me_ref, group_ref, adapter_hbm, tokens_hbm, down_hbm, *refs
):
    share_ref, outs = refs[0], refs[1:-4]
    adapter_ref, tokens_ref, share_sem, sems = refs[-4:]
    rows, width = tokens_ref.shape
    share = share_ref.shape[1]
    parts = sems.shape[0] - 1
    part = rows // parts
    adapter_copy = pltpu.make_async_copy(adapter_hbm, adapter_ref, sems.at[parts])
    adapter_copy.start()
    copies = [
        pltpu.make_async_copy(
            tokens_hbm.at[pl.ds(i * part, part), :],
            tokens_ref.at[pl.ds(i * part, part), :],
            sems.at[i],
        )
        for i in range(parts)
    ]
    for copy in copies:
        copy.start()
    at = pl.multiple_of(group_ref[0] * share, share)
    share_copy = pltpu.make_async_copy(down_hbm.at[:, pl.ds(at, share), :], share_ref, share_sem)
    share_copy.start()
    adapter_copy.wait()
    place = slot_places(adapter_ref[...], me_ref[0], pool, local, depth)
    size = outs[0].shape[0]
    slots = len(outs) * size
    picker = jnp.where(iota((slots, rows), 0) == place, 1.0, 0.0).astype(jnp.bfloat16)
    for copy in copies:
        copy.wait()
    step = 512
    for at in range(0, width, step):
        block = jnp.dot(
            picker, tokens_ref[:, at : at + step], preferred_element_type=jnp.float32
        )
        for j, out in enumerate(outs):
            out[:, at : at + step] = block[j * size : (j + 1) * size].astype(jnp.bfloat16)
    share_copy.wait()


def base_kernel(
    core_ref,
    tokens_hbm,
    weight_hbm,
    down_hbm,
    up_hbm,
    theirs_ref,
    mine_ref,
    down_ref,
    up_ref,
    tokens_ref,
    weight_ref,
    other_sems,
    sems,
):
    rows, columns = mine_ref.shape
    steps = sems.shape[1]
    step = tokens_ref.shape[1] // steps
    copies = []
    for half in range(2):
        start = (1 - core_ref[0] if half == 0 else core_ref[0]) * columns
        start = pl.multiple_of(start, columns)
        for k in range(steps):
            copies.append(
                pltpu.make_async_copy(
                    weight_hbm.at[pl.ds(k * step, step), pl.ds(start, columns)],
                    weight_ref.at[half, pl.ds(k * step, step), :],
                    sems.at[half, k],
                )
            )
    tokens_copy = pltpu.make_async_copy(tokens_hbm, tokens_ref, other_sems.at[0])
    own = pl.multiple_of(core_ref[0] * columns, columns)
    factor_copies = [
        pltpu.make_async_copy(down_hbm, down_ref, other_sems.at[1]),
        pltpu.make_async_copy(up_hbm.at[:, :, pl.ds(own, columns)], up_ref, other_sems.at[2]),
    ]
    for copy in [tokens_copy] + copies + factor_copies:
        copy.start()
    tokens_copy.wait()
    for half, out in enumerate((theirs_ref, mine_ref)):
        for k in range(steps):
            copies[half * steps + k].wait()
            term = jnp.dot(
                tokens_ref[:, k * step : (k + 1) * step],
                weight_ref[half, k * step : (k + 1) * step, :],
                preferred_element_type=jnp.float32,
            )
            if k == 0:
                out[...] = term
            else:
                out[...] += term
    for copy in factor_copies:
        copy.wait()


def down_kernel(buffers, groups, local, depth, group_ref, down_ref, *refs):
    order = [0] + far_first(buffers)
    ins = [refs[order.index(j)] for j in range(buffers)]
    shares, out = refs[buffers : buffers + groups], refs[-1]
    rank = out.shape[1]
    share = shares[0].shape[1]
    total = None
    for k in range(groups):
        at = pl.multiple_of((group_ref[0] ^ k) * share, share)
        rows = jnp.concatenate([x[:, pl.ds(at, share)] for x in ins], axis=0)
        factors = [down_ref[a, pl.ds(at, share), :] for a in range(local)]
        factors += [shares[k][a] for a in range(local)]
        term = jnp.dot(
            rows, jnp.concatenate(factors, axis=1), preferred_element_type=jnp.float32
        )
        total = term if total is None else total + term
    which = (iota((total.shape[0], 1), 0) // depth) % (2 * local)
    low = total[:, :rank]
    for i in range(1, 2 * local):
        low = jnp.where(which == i, total[:, i * rank : (i + 1) * rank], low)
    out[...] = low


def up_kernel(
    buffers, groups, local, depth, group_ref, low_ref, other_ref, factor_ref, up_ref, *refs
):
    shares, outs, term_ref = refs[:groups], refs[groups : groups + buffers], refs[-1]
    rows, rank = low_ref.shape
    size = rows // buffers
    columns = up_ref.shape[2]
    share = columns // groups
    which = (iota((rows, 1), 0) // depth) % (2 * local)
    low = low_ref[...] + other_ref[...]
    for a in range(local):
        low = jnp.where(which == a, low * factor_ref[a : a + 1, :], low)
    both = jnp.concatenate(halves(low), axis=0)
    which = jnp.concatenate([which, which], axis=0)
    spread = jnp.concatenate(
        [jnp.where(which == i, both, jnp.zeros_like(both)) for i in range(2 * local)], axis=1
    )
    for k in range(groups):
        at = pl.multiple_of((group_ref[0] ^ k) * share, share)
        up = [up_ref[a, :, pl.ds(at, share)] for a in range(local)]
        up += [shares[k][a] for a in range(local)]
        term = jnp.dot(
            spread, jnp.concatenate(up, axis=0), preferred_element_type=jnp.float32
        )
        term_ref[:, pl.ds(at, share)] = term[:rows] + term[rows:]
    lane = iota((1, LANES), 1)
    for j, out in enumerate(outs):
        term = term_ref[j * size : (j + 1) * size, :]
        top = jnp.max(jnp.abs(term), axis=1, keepdims=True)
        exponent = jnp.ceil(jnp.log2(jnp.maximum(top, 1e-30)) + 1e-3)
        code = jnp.clip(jnp.round(term * jnp.exp2(15.0 - exponent)), -32767.0, 32767.0)
        code = code.astype(jnp.int32)
        biased = exponent.astype(jnp.int32) + EXPONENT_BIAS
        first = code[:, :LANES]
        marked = (first & -2) | ((biased >> jnp.minimum(lane, EXPONENT_BITS - 1)) & 1)
        first = jnp.where(lane < EXPONENT_BITS, marked, first)
        out[:, :LANES] = first.astype(jnp.int16)
        out[:, LANES:] = code[:, LANES:].astype(jnp.int16)


def finish_kernel(
    buffers, pool, local, depth, me_ref, adapter_ref, mine_ref, other_ref, cos_ref, sin_ref, gain_ref, *refs
):
    order = [0] + return_order(buffers)
    ins = [refs[order.index(j)] for j in range(buffers)]
    out_hbm, out_ref, sems = refs[-3:]
    rows, columns = mine_ref.shape
    head = cos_ref.shape[1]
    place = to_column(slot_places(adapter_ref[...], me_ref[0], pool, local, depth))
    slots = buffers * ins[0].shape[0]
    picker = jnp.where(iota((rows, slots), 1) == place, 1.0, 0.0).astype(jnp.bfloat16)

    def picked(at, size):
        code = jnp.concatenate([x[:, at : at + size] for x in ins], axis=0).astype(jnp.int32)
        high = (code >> 8).astype(jnp.float32).astype(jnp.bfloat16)
        low = (code & 255).astype(jnp.float32).astype(jnp.bfloat16)
        high = jnp.dot(picker, high, preferred_element_type=jnp.float32)
        low = jnp.dot(picker, low, preferred_element_type=jnp.float32)
        return high * 256.0 + low

    lane = iota((1, LANES), 1)
    bits = picked(0, LANES).astype(jnp.int32) & 1
    bits = jnp.where(lane < EXPONENT_BITS, bits << jnp.minimum(lane, EXPONENT_BITS - 1), 0)
    exponent = jnp.sum(bits.astype(jnp.float32), axis=1, keepdims=True) - EXPONENT_BIAS
    scale = jnp.exp2(exponent - 15.0)
    cosine, sine, gain = cos_ref[...], sin_ref[...], gain_ref[...]
    entries = []
    for at in range(0, columns, 2 * head):
        projected = mine_ref[:, at : at + 2 * head] + other_ref[:, at : at + 2 * head]
        projected = projected + picked(at, 2 * head) * scale
        key, value = projected[:, :head], projected[:, head:]
        mean = jnp.mean(key * key, axis=1, keepdims=True)
        normed = key * lax.rsqrt(mean + NORM_EPS) * gain
        rotated = normed * cosine + pltpu.roll(normed, head // 2, 1) * sine
        entries += [rotated.astype(jnp.bfloat16), value.astype(jnp.bfloat16)]
    kinds, block = len(entries), 16
    n = kinds * block
    source = (iota((n, n), 0) % kinds) * block + iota((n, n), 0) // kinds
    order = jnp.where(iota((n, n), 1) == source, 1.0, 0.0).astype(jnp.bfloat16)
    copies = []
    for i in range(rows // block):
        stacked = jnp.concatenate([e[i * block : (i + 1) * block] for e in entries], axis=0)
        mixed = jnp.dot(order, stacked, preferred_element_type=jnp.float32)
        out_ref[i * n : (i + 1) * n, :] = mixed.astype(jnp.bfloat16)
        if i % 2:
            done = pl.ds((i - 1) * n, 2 * n)
            copies.append(
                pltpu.make_async_copy(out_ref.at[done, :], out_hbm.at[done, :], sems.at[i // 2])
            )
            copies[-1].start()
    for copy in copies:
        copy.wait()


def body(
    tokens,
    row_adapters,
    positions,
    key_value_weight,
    adapter_down,
    adapter_up,
    ranks,
    key_norm_gain,
):
    pool = lax.axis_size("pool")
    groups = lax.axis_size("groups")
    cores = lax.axis_size("tp")
    rows, width = tokens.shape
    local = adapter_down.shape[0]
    adapters = local * pool
    columns = key_value_weight.shape[1] // cores
    rank = adapter_down.shape[2]
    head = key_norm_gain.shape[0]
    depth = max(2, 2 * rows // adapters)
    buffers = pool // 2
    size = 2 * local * depth
    f32, bf16 = jnp.float32, jnp.bfloat16

    me = lax.axis_index("pool").astype(jnp.int32)[None]
    core = lax.axis_index("tp").astype(jnp.int32)[None]
    group = lax.axis_index("groups").astype(jnp.int32)[None]

    def exchange(x, axis, count, j):
        return lax.ppermute(x, axis, [(p, p ^ j) for p in range(count)])

    def hand_round(share):
        return [share] + [exchange(share, "groups", groups, k) for k in range(1, groups)]

    adapter_row = row_adapters.reshape(1, rows)
    down_share = width // groups
    parts = rows // 16
    down_part, *picked = pl.pallas_call(
        functools.partial(pick_kernel, pool, local, depth),
        in_specs=[SMEM] * 2 + [HBM] * 3,
        out_specs=[VMEM] * (1 + buffers),
        out_shape=[jax.ShapeDtypeStruct((local, down_share, rank), bf16)]
        + [jax.ShapeDtypeStruct((size, width), bf16)] * buffers,
        scratch_shapes=[
            pltpu.VMEM((1, rows), jnp.int32),
            pltpu.VMEM((rows, width), bf16),
            pltpu.SemaphoreType.DMA,
            pltpu.SemaphoreType.DMA((parts + 1,)),
        ],
        compiler_params=params(),
        cost_estimate=cost(2 * buffers * size * rows * width, 2 * (rows + buffers * size) * width),
        name="pick",
    )(me, group, in_hbm(adapter_row), in_hbm(tokens), in_hbm(adapter_down))
    far_down = exchange(down_part, "pool", pool, pool // 2)
    up_share = columns // groups
    ranks_now, adapter_up_now, _ = lax.optimization_barrier((ranks, adapter_up, picked))
    up_part, factor = pl.pallas_call(
        functools.partial(up_share_kernel, cores),
        in_specs=[SMEM] * 3 + [HBM],
        out_specs=[VMEM] * 2,
        out_shape=[
            jax.ShapeDtypeStruct((local, rank, up_share), bf16),
            jax.ShapeDtypeStruct((local, rank), f32),
        ],
        scratch_shapes=[
            pltpu.VMEM((local, rank, up_share), bf16),
            pltpu.SemaphoreType.DMA,
        ],
        compiler_params=params(),
        cost_estimate=cost(local * rank * up_share, 4 * local * rank * up_share),
        name="up_share",
    )(group, core, ranks_now, in_hbm(adapter_up_now))
    far_up = exchange(up_part, "pool", pool, pool // 2)

    order = far_first(buffers)
    early, late = order[:1], order[1:]
    late_rows, _ = lax.optimization_barrier(([picked[j] for j in late], up_part))
    leaving = [picked[j] for j in early] + late_rows
    arrived = [picked[0]] + [exchange(x, "pool", pool, j) for x, j in zip(leaving, order)]

    steps = 5
    theirs, mine, own_down, own_up = pl.pallas_call(
        base_kernel,
        in_specs=[SMEM] + [HBM] * 4,
        out_specs=[VMEM] * 4,
        out_shape=[jax.ShapeDtypeStruct((rows, columns), f32)] * 2
        + [
            jax.ShapeDtypeStruct(adapter_down.shape, bf16),
            jax.ShapeDtypeStruct((local, rank, columns), bf16),
        ],
        scratch_shapes=[
            pltpu.VMEM((rows, width), bf16),
            pltpu.VMEM((2, width, columns), bf16),
            pltpu.SemaphoreType.DMA((3,)),
            pltpu.SemaphoreType.DMA((2, steps)),
        ],
        compiler_params=params(),
        cost_estimate=cost(4 * rows * width * columns, 4 * width * columns),
        name="base",
    )(
        core,
        in_hbm(tokens),
        in_hbm(key_value_weight),
        in_hbm(adapter_down),
        in_hbm(adapter_up),
    )
    far_down, theirs = lax.optimization_barrier((far_down, theirs))
    far_downs = hand_round(far_down)
    far_up, _ = lax.optimization_barrier((far_up, far_down))
    far_ups = hand_round(far_up)
    half_dim = head // 2
    frequency = jnp.power(
        f32(ROPE_THETA), -jnp.arange(half_dim, dtype=f32) * (2.0 / head)
    )
    angles = positions.astype(f32)[:, None] * frequency[None, :]
    cosine, sine = jnp.cos(angles), jnp.sin(angles)
    cosine = jnp.concatenate([cosine, cosine], axis=1)
    sine = jnp.concatenate([-sine, sine], axis=1)

    far_up, arrived[1], theirs = lax.optimization_barrier((far_up, arrived[1], theirs))
    other = exchange(theirs, "tp", cores, 1)
    arrived, mine, cosine, sine = lax.optimization_barrier((arrived, mine, cosine, sine))
    slots = buffers * size
    low = pl.pallas_call(
        functools.partial(down_kernel, buffers, groups, local, depth),
        in_specs=[SMEM] + [VMEM] * (1 + buffers + groups),
        out_specs=VMEM,
        out_shape=jax.ShapeDtypeStruct((slots, rank), f32),
        compiler_params=params(),
        cost_estimate=cost(4 * local * slots * rank * width, 2 * (slots + rank) * width),
        name="down",
    )(group, own_down, *arrived, *far_downs)
    low_other = exchange(low, "tp", cores, 1)

    terms = pl.pallas_call(
        functools.partial(up_kernel, buffers, groups, local, depth),
        in_specs=[SMEM] + [VMEM] * (4 + groups),
        out_specs=[VMEM] * buffers,
        out_shape=[jax.ShapeDtypeStruct((size, columns), jnp.int16)] * buffers,
        scratch_shapes=[pltpu.VMEM((slots, columns), f32)],
        compiler_params=params(),
        cost_estimate=cost(8 * local * slots * rank * columns, 2 * slots * columns),
        name="up",
    )(group, low, low_other, factor, own_up, *far_ups)
    order = return_order(buffers)
    returned = [terms[0]] + [exchange(terms[j], "pool", pool, j) for j in order]

    out = pl.pallas_call(
        functools.partial(finish_kernel, buffers, pool, local, depth),
        in_specs=[SMEM] + [VMEM] * (6 + buffers),
        out_specs=HBM,
        out_shape=jax.ShapeDtypeStruct((rows * columns // head, head), bf16),
        scratch_shapes=[
            pltpu.VMEM((rows * columns // head, head), bf16),
            pltpu.SemaphoreType.DMA((rows // 32,)),
        ],
        compiler_params=params(),
        cost_estimate=cost(4 * rows * slots * columns, 2 * slots * columns),
        name="finish",
    )(
        me,
        adapter_row,
        mine,
        other,
        cosine,
        sine,
        key_norm_gain.astype(f32)[None, :],
        *returned,
    )
    return out.reshape(rows, columns // (2 * head), 2, head)


def solution(mesh):
    return jax.shard_map(
        body,
        mesh=mesh,
        in_specs=(
            P(("groups", "pool"), "tp"),
            P(("groups", "pool"), None),
            P(("groups", "pool")),
            P("tp", None),
            P("pool", "tp", None),
            P("pool", None, None),
            P("pool"),
            P(),
        ),
        out_specs=P(("groups", "pool"), "tp", None, None),
        check_vma=False,
    )
```

```python
import functools

import jax
import jax.numpy as jnp
from jax import lax
from jax.experimental import pallas as pl
from jax.experimental.pallas import tpu as pltpu
from jax.sharding import PartitionSpec as P

ALPHA = 32
ROPE_THETA = 1000000.0
NORM_EPS = 1e-06
VMEM_LIMIT = 48 * 1024 * 1024
LANES = 128
EXPONENT_BITS = 8
EXPONENT_BIAS = 128

VMEM = pl.BlockSpec(memory_space=pltpu.VMEM)
HBM = pl.BlockSpec(memory_space=pltpu.HBM)
SMEM = pl.BlockSpec(memory_space=pltpu.SMEM)


def params(**kw):
    return pltpu.CompilerParams(vmem_limit_bytes=VMEM_LIMIT, **kw)


def cost(flops, bytes_accessed):
    return pl.CostEstimate(flops=flops, bytes_accessed=bytes_accessed, transcendentals=0)


def in_hbm(x):
    return pltpu.with_memory_space_constraint(x, pltpu.HBM)


def iota(shape, dim):
    return lax.broadcasted_iota(jnp.int32, shape, dim)


def to_column(row):
    n = row.shape[1]
    return jnp.sum(
        jnp.where(iota((n, n), 0) == iota((n, n), 1), row, 0), axis=1, keepdims=True
    )


def slot_places(row, me, pool, local, depth):
    n = row.shape[1]
    column = to_column(row)
    earlier = (column == row) & (iota((n, n), 0) < iota((n, n), 1))
    slot = jnp.sum(jnp.where(earlier, 1, 0), axis=0, keepdims=True)
    holder = row // local
    apart = holder ^ me
    buffer, far = apart % (pool // 2), apart // (pool // 2)
    return ((buffer * 2 + far) * local + (row - holder * local)) * depth + slot


def chunk_places(share):
    first = (share // LANES) * 4 // 5 * LANES
    return [(0, first), (first, share - first)]


def far_first(count):
    return sorted(range(1, count), key=lambda j: (-bin(j).count("1"), -j))


def return_order(count):
    order = far_first(count)
    return order[-1:] + order[:-1]


def halves(x):
    high = x.astype(jnp.bfloat16)
    low = (x - high.astype(jnp.float32)).astype(jnp.bfloat16)
    return high, low


def second_kernel(
    group_ref, core_ref, ranks_ref, down_hbm, up_hbm, out_ref, factor_ref, own_ref, sems
):
    local, rank, share = own_ref.shape
    rows = out_ref.shape[1] - share // LANES * rank
    columns = up_hbm.shape[2] // lax.axis_size("tp")
    at = core_ref[0] * columns + group_ref[0] * share
    copy = pltpu.make_async_copy(
        up_hbm.at[:, :, pl.ds(pl.multiple_of(at, share), share)], own_ref, sems.at[0]
    )
    copy.start()
    width = down_hbm.shape[1] // lax.axis_size("groups")
    start = pl.multiple_of((group_ref[0] + 1) * width - rows, LANES)
    down_copy = pltpu.make_async_copy(
        down_hbm.at[:, pl.ds(start, rows), :], out_ref.at[:, pl.ds(0, rows), :], sems.at[1]
    )
    down_copy.start()
    copy.wait()
    for a in range(local):
        used = ranks_ref[a]

        def factor(shape, dim):
            scale = jnp.float32(ALPHA) / jnp.full(shape, used, jnp.int32).astype(jnp.float32)
            return jnp.where(iota(shape, dim) < used, scale, 0.0)

        factor_ref[a : a + 1, :] = factor((1, rank), 1)
        scaled = (own_ref[a].astype(jnp.float32) * factor((rank, 1), 0)).astype(jnp.bfloat16)
        for i in range(share // LANES):
            top = rows + i * rank
            out_ref[a, top : top + rank, :] = scaled[:, i * LANES : (i + 1) * LANES]
    down_copy.wait()


def pick_kernel(
    pool, local, depth, me_ref, group_ref, adapter_hbm, tokens_hbm, down_hbm, *refs
):
    share_ref, outs = refs[0], refs[1:-4]
    adapter_ref, tokens_ref, share_sem, sems = refs[-4:]
    rows, width = tokens_ref.shape
    chunk = share_ref.shape[1]
    parts = sems.shape[0] - 1
    part = rows // parts
    adapter_copy = pltpu.make_async_copy(adapter_hbm, adapter_ref, sems.at[parts])
    adapter_copy.start()
    copies = [
        pltpu.make_async_copy(
            tokens_hbm.at[pl.ds(i * part, part), :],
            tokens_ref.at[pl.ds(i * part, part), :],
            sems.at[i],
        )
        for i in range(parts)
    ]
    for copy in copies:
        copy.start()
    at = pl.multiple_of(group_ref[0] * (down_hbm.shape[1] // lax.axis_size("groups")), LANES)
    share_copy = pltpu.make_async_copy(down_hbm.at[:, pl.ds(at, chunk), :], share_ref, share_sem)
    share_copy.start()
    adapter_copy.wait()
    place = slot_places(adapter_ref[...], me_ref[0], pool, local, depth)
    size = outs[0].shape[0]
    slots = len(outs) * size
    picker = jnp.where(iota((slots, rows), 0) == place, 1.0, 0.0).astype(jnp.bfloat16)
    for copy in copies:
        copy.wait()
    step = 512
    for at in range(0, width, step):
        block = jnp.dot(
            picker, tokens_ref[:, at : at + step], preferred_element_type=jnp.float32
        )
        for j, out in enumerate(outs):
            out[:, at : at + step] = block[j * size : (j + 1) * size].astype(jnp.bfloat16)
    share_copy.wait()


def base_kernel(
    core_ref,
    tokens_hbm,
    weight_hbm,
    down_hbm,
    up_hbm,
    theirs_ref,
    mine_ref,
    down_ref,
    up_ref,
    tokens_ref,
    weight_ref,
    other_sems,
    sems,
):
    rows, columns = mine_ref.shape
    steps = sems.shape[1]
    step = tokens_ref.shape[1] // steps
    copies = []
    for half in range(2):
        start = (1 - core_ref[0] if half == 0 else core_ref[0]) * columns
        start = pl.multiple_of(start, columns)
        for k in range(steps):
            copies.append(
                pltpu.make_async_copy(
                    weight_hbm.at[pl.ds(k * step, step), pl.ds(start, columns)],
                    weight_ref.at[half, pl.ds(k * step, step), :],
                    sems.at[half, k],
                )
            )
    tokens_copy = pltpu.make_async_copy(tokens_hbm, tokens_ref, other_sems.at[0])
    own = pl.multiple_of(core_ref[0] * columns, columns)
    factor_copies = [
        pltpu.make_async_copy(down_hbm, down_ref, other_sems.at[1]),
        pltpu.make_async_copy(up_hbm.at[:, :, pl.ds(own, columns)], up_ref, other_sems.at[2]),
    ]
    for copy in [tokens_copy] + copies + factor_copies:
        copy.start()
    tokens_copy.wait()
    for half, out in enumerate((theirs_ref, mine_ref)):
        for k in range(steps):
            copies[half * steps + k].wait()
            term = jnp.dot(
                tokens_ref[:, k * step : (k + 1) * step],
                weight_ref[half, k * step : (k + 1) * step, :],
                preferred_element_type=jnp.float32,
            )
            if k == 0:
                out[...] = term
            else:
                out[...] += term
    for copy in factor_copies:
        copy.wait()


def down_kernel(buffers, groups, local, depth, group_ref, down_ref, *refs):
    order = [0] + far_first(buffers)
    ins = [refs[order.index(j)] for j in range(buffers)]
    shares, out = refs[buffers:-1], refs[-1]
    rank = out.shape[1]
    share = ins[0].shape[1] // groups
    total = None
    for k in range(2 * groups):
        offset, chunk = chunk_places(share)[k // groups]
        at = pl.multiple_of((group_ref[0] ^ (k % groups)) * share + offset, LANES)
        rows = jnp.concatenate([x[:, pl.ds(at, chunk)] for x in ins], axis=0)
        factors = [down_ref[a, pl.ds(at, chunk), :] for a in range(local)]
        factors += [shares[k][a, :chunk, :] for a in range(local)]
        term = jnp.dot(
            rows, jnp.concatenate(factors, axis=1), preferred_element_type=jnp.float32
        )
        total = term if total is None else total + term
    which = (iota((total.shape[0], 1), 0) // depth) % (2 * local)
    low = total[:, :rank]
    for i in range(1, 2 * local):
        low = jnp.where(which == i, total[:, i * rank : (i + 1) * rank], low)
    out[...] = low


def up_kernel(
    buffers, groups, local, depth, group_ref, low_ref, other_ref, factor_ref, up_ref, *refs
):
    shares, outs, term_ref = refs[:groups], refs[groups : groups + buffers], refs[-1]
    rows, rank = low_ref.shape
    size = rows // buffers
    columns = up_ref.shape[2]
    share = columns // groups
    which = (iota((rows, 1), 0) // depth) % (2 * local)
    low = low_ref[...] + other_ref[...]
    for a in range(local):
        low = jnp.where(which == a, low * factor_ref[a : a + 1, :], low)
    both = jnp.concatenate(halves(low), axis=0)
    which = jnp.concatenate([which, which], axis=0)
    spread = jnp.concatenate(
        [jnp.where(which == i, both, jnp.zeros_like(both)) for i in range(2 * local)], axis=1
    )
    for k in range(groups):
        at = pl.multiple_of((group_ref[0] ^ k) * share, share)
        up = [up_ref[a, :, pl.ds(at, share)] for a in range(local)]
        top = shares[k].shape[1] - share // LANES * rank
        up += [
            jnp.concatenate(
                [
                    shares[k][a, top + i * rank : top + (i + 1) * rank, :]
                    for i in range(share // LANES)
                ],
                axis=1,
            )
            for a in range(local)
        ]
        term = jnp.dot(
            spread, jnp.concatenate(up, axis=0), preferred_element_type=jnp.float32
        )
        term_ref[:, pl.ds(at, share)] = term[:rows] + term[rows:]
    lane = iota((1, LANES), 1)
    for j, out in enumerate(outs):
        term = term_ref[j * size : (j + 1) * size, :]
        top = jnp.max(jnp.abs(term), axis=1, keepdims=True)
        exponent = jnp.ceil(jnp.log2(jnp.maximum(top, 1e-30)) + 1e-3)
        code = jnp.clip(jnp.round(term * jnp.exp2(15.0 - exponent)), -32767.0, 32767.0)
        code = code.astype(jnp.int32)
        biased = exponent.astype(jnp.int32) + EXPONENT_BIAS
        first = code[:, :LANES]
        marked = (first & -2) | ((biased >> jnp.minimum(lane, EXPONENT_BITS - 1)) & 1)
        first = jnp.where(lane < EXPONENT_BITS, marked, first)
        out[:, :LANES] = first.astype(jnp.int16)
        out[:, LANES:] = code[:, LANES:].astype(jnp.int16)


def finish_kernel(
    buffers, pool, local, depth, me_ref, adapter_ref, mine_ref, other_ref, cos_ref, sin_ref, gain_ref, *refs
):
    order = [0] + return_order(buffers)
    ins = [refs[order.index(j)] for j in range(buffers)]
    out_hbm, out_ref, sems = refs[-3:]
    rows, columns = mine_ref.shape
    head = cos_ref.shape[1]
    place = to_column(slot_places(adapter_ref[...], me_ref[0], pool, local, depth))
    slots = buffers * ins[0].shape[0]
    picker = jnp.where(iota((rows, slots), 1) == place, 1.0, 0.0).astype(jnp.bfloat16)

    def picked(at, size):
        code = jnp.concatenate([x[:, at : at + size] for x in ins], axis=0).astype(jnp.int32)
        high = (code >> 8).astype(jnp.float32).astype(jnp.bfloat16)
        low = (code & 255).astype(jnp.float32).astype(jnp.bfloat16)
        high = jnp.dot(picker, high, preferred_element_type=jnp.float32)
        low = jnp.dot(picker, low, preferred_element_type=jnp.float32)
        return high * 256.0 + low

    lane = iota((1, LANES), 1)
    bits = picked(0, LANES).astype(jnp.int32) & 1
    bits = jnp.where(lane < EXPONENT_BITS, bits << jnp.minimum(lane, EXPONENT_BITS - 1), 0)
    exponent = jnp.sum(bits.astype(jnp.float32), axis=1, keepdims=True) - EXPONENT_BIAS
    scale = jnp.exp2(exponent - 15.0)
    cosine, sine, gain = cos_ref[...], sin_ref[...], gain_ref[...]
    entries = []
    for at in range(0, columns, 2 * head):
        projected = mine_ref[:, at : at + 2 * head] + other_ref[:, at : at + 2 * head]
        projected = projected + picked(at, 2 * head) * scale
        key, value = projected[:, :head], projected[:, head:]
        mean = jnp.mean(key * key, axis=1, keepdims=True)
        normed = key * lax.rsqrt(mean + NORM_EPS) * gain
        rotated = normed * cosine + pltpu.roll(normed, head // 2, 1) * sine
        entries += [rotated.astype(jnp.bfloat16), value.astype(jnp.bfloat16)]
    kinds, block = len(entries), 16
    n = kinds * block
    source = (iota((n, n), 0) % kinds) * block + iota((n, n), 0) // kinds
    order = jnp.where(iota((n, n), 1) == source, 1.0, 0.0).astype(jnp.bfloat16)
    copies = []
    for i in range(rows // block):
        stacked = jnp.concatenate([e[i * block : (i + 1) * block] for e in entries], axis=0)
        mixed = jnp.dot(order, stacked, preferred_element_type=jnp.float32)
        out_ref[i * n : (i + 1) * n, :] = mixed.astype(jnp.bfloat16)
        if i % 2:
            done = pl.ds((i - 1) * n, 2 * n)
            copies.append(
                pltpu.make_async_copy(out_ref.at[done, :], out_hbm.at[done, :], sems.at[i // 2])
            )
            copies[-1].start()
    for copy in copies:
        copy.wait()


def body(
    tokens,
    row_adapters,
    positions,
    key_value_weight,
    adapter_down,
    adapter_up,
    ranks,
    key_norm_gain,
):
    pool = lax.axis_size("pool")
    groups = lax.axis_size("groups")
    cores = lax.axis_size("tp")
    rows, width = tokens.shape
    local = adapter_down.shape[0]
    adapters = local * pool
    columns = key_value_weight.shape[1] // cores
    rank = adapter_down.shape[2]
    head = key_norm_gain.shape[0]
    depth = max(2, 2 * rows // adapters)
    buffers = pool // 2
    size = 2 * local * depth
    f32, bf16 = jnp.float32, jnp.bfloat16

    me = lax.axis_index("pool").astype(jnp.int32)[None]
    core = lax.axis_index("tp").astype(jnp.int32)[None]
    group = lax.axis_index("groups").astype(jnp.int32)[None]

    def exchange(x, axis, count, j):
        return lax.ppermute(x, axis, [(p, p ^ j) for p in range(count)])

    def hand_round(share):
        return [share] + [exchange(share, "groups", groups, k) for k in range(1, groups)]

    adapter_row = row_adapters.reshape(1, rows)
    (_, first_rows), (_, second_rows) = chunk_places(width // groups)
    parts = rows // 16
    first, *picked = pl.pallas_call(
        functools.partial(pick_kernel, pool, local, depth),
        in_specs=[SMEM] * 2 + [HBM] * 3,
        out_specs=[VMEM] * (1 + buffers),
        out_shape=[jax.ShapeDtypeStruct((local, first_rows, rank), bf16)]
        + [jax.ShapeDtypeStruct((size, width), bf16)] * buffers,
        scratch_shapes=[
            pltpu.VMEM((1, rows), jnp.int32),
            pltpu.VMEM((rows, width), bf16),
            pltpu.SemaphoreType.DMA,
            pltpu.SemaphoreType.DMA((parts + 1,)),
        ],
        compiler_params=params(),
        cost_estimate=cost(2 * buffers * size * rows * width, 2 * (rows + buffers * size) * width),
        name="pick",
    )(me, group, in_hbm(adapter_row), in_hbm(tokens), in_hbm(adapter_down))
    far_first_part = exchange(first, "pool", pool, pool // 2)
    up_share = columns // groups
    ranks_now, adapter_up_now, _ = lax.optimization_barrier((ranks, adapter_up, picked))
    second, factor = pl.pallas_call(
        second_kernel,
        in_specs=[SMEM] * 3 + [HBM] * 2,
        out_specs=[VMEM] * 2,
        out_shape=[
            jax.ShapeDtypeStruct((local, second_rows + up_share // LANES * rank, rank), bf16),
            jax.ShapeDtypeStruct((local, rank), f32),
        ],
        scratch_shapes=[
            pltpu.VMEM((local, rank, up_share), bf16),
            pltpu.SemaphoreType.DMA((2,)),
        ],
        compiler_params=params(),
        cost_estimate=cost(local * rank * up_share, 4 * local * rank * (second_rows + up_share)),
        name="second_part",
    )(group, core, ranks_now, in_hbm(adapter_down), in_hbm(adapter_up_now))
    far_second_part = exchange(second, "pool", pool, pool // 2)

    order = far_first(buffers)
    early, late = order[:1], order[1:]
    late_rows, _ = lax.optimization_barrier(([picked[j] for j in late], second))
    leaving = [picked[j] for j in early] + late_rows
    arrived = [picked[0]] + [exchange(x, "pool", pool, j) for x, j in zip(leaving, order)]

    steps = 5
    theirs, mine, own_down, own_up = pl.pallas_call(
        base_kernel,
        in_specs=[SMEM] + [HBM] * 4,
        out_specs=[VMEM] * 4,
        out_shape=[jax.ShapeDtypeStruct((rows, columns), f32)] * 2
        + [
            jax.ShapeDtypeStruct(adapter_down.shape, bf16),
            jax.ShapeDtypeStruct((local, rank, columns), bf16),
        ],
        scratch_shapes=[
            pltpu.VMEM((rows, width), bf16),
            pltpu.VMEM((2, width, columns), bf16),
            pltpu.SemaphoreType.DMA((3,)),
            pltpu.SemaphoreType.DMA((2, steps)),
        ],
        compiler_params=params(),
        cost_estimate=cost(4 * rows * width * columns, 4 * width * columns),
        name="base",
    )(
        core,
        in_hbm(tokens),
        in_hbm(key_value_weight),
        in_hbm(adapter_down),
        in_hbm(adapter_up),
    )
    far_first_part, theirs = lax.optimization_barrier((far_first_part, theirs))
    firsts = hand_round(far_first_part)
    far_second_part, _ = lax.optimization_barrier((far_second_part, far_first_part))
    seconds = hand_round(far_second_part)

    half_dim = head // 2
    frequency = jnp.power(
        f32(ROPE_THETA), -jnp.arange(half_dim, dtype=f32) * (2.0 / head)
    )
    angles = positions.astype(f32)[:, None] * frequency[None, :]
    cosine, sine = jnp.cos(angles), jnp.sin(angles)
    cosine = jnp.concatenate([cosine, cosine], axis=1)
    sine = jnp.concatenate([-sine, sine], axis=1)

    arrived[1], theirs = lax.optimization_barrier((arrived[1], theirs))
    other = exchange(theirs, "tp", cores, 1)
    arrived, mine, cosine, sine = lax.optimization_barrier((arrived, mine, cosine, sine))
    slots = buffers * size
    low = pl.pallas_call(
        functools.partial(down_kernel, buffers, groups, local, depth),
        in_specs=[SMEM] + [VMEM] * (1 + buffers + 2 * groups),
        out_specs=VMEM,
        out_shape=jax.ShapeDtypeStruct((slots, rank), f32),
        compiler_params=params(),
        cost_estimate=cost(4 * local * slots * rank * width, 2 * (slots + rank) * width),
        name="down",
    )(group, own_down, *arrived, *firsts, *seconds)
    low_other = exchange(low, "tp", cores, 1)

    terms = pl.pallas_call(
        functools.partial(up_kernel, buffers, groups, local, depth),
        in_specs=[SMEM] + [VMEM] * (4 + groups),
        out_specs=[VMEM] * buffers,
        out_shape=[jax.ShapeDtypeStruct((size, columns), jnp.int16)] * buffers,
        scratch_shapes=[pltpu.VMEM((slots, columns), f32)],
        compiler_params=params(),
        cost_estimate=cost(8 * local * slots * rank * columns, 2 * slots * columns),
        name="up",
    )(group, low, low_other, factor, own_up, *seconds)
    order = return_order(buffers)
    returned = [terms[0]] + [exchange(terms[j], "pool", pool, j) for j in order]

    out = pl.pallas_call(
        functools.partial(finish_kernel, buffers, pool, local, depth),
        in_specs=[SMEM] + [VMEM] * (6 + buffers),
        out_specs=HBM,
        out_shape=jax.ShapeDtypeStruct((rows * columns // head, head), bf16),
        scratch_shapes=[
            pltpu.VMEM((rows * columns // head, head), bf16),
            pltpu.SemaphoreType.DMA((rows // 32,)),
        ],
        compiler_params=params(),
        cost_estimate=cost(4 * rows * slots * columns, 2 * slots * columns),
        name="finish",
    )(
        me,
        adapter_row,
        mine,
        other,
        cosine,
        sine,
        key_norm_gain.astype(f32)[None, :],
        *returned,
    )
    return out.reshape(rows, columns // (2 * head), 2, head)


def solution(mesh):
    return jax.shard_map(
        body,
        mesh=mesh,
        in_specs=(
            P(("groups", "pool"), "tp"),
            P(("groups", "pool"), None),
            P(("groups", "pool")),
            P("tp", None),
            P("pool", "tp", None),
            P("pool", None, None),
            P("pool"),
            P(),
        ),
        out_specs=P(("groups", "pool"), "tp", None, None),
        check_vma=False,
    )
```

```python
import functools

import jax
import jax.numpy as jnp
from jax import lax
from jax.experimental import pallas as pl
from jax.experimental.pallas import tpu as pltpu
from jax.sharding import PartitionSpec as P

ALPHA = 32
ROPE_THETA = 1000000.0
NORM_EPS = 1e-06
VMEM_LIMIT = 48 * 1024 * 1024
LANES = 128
EXPONENT_BITS = 8
EXPONENT_BIAS = 128

VMEM = pl.BlockSpec(memory_space=pltpu.VMEM)
HBM = pl.BlockSpec(memory_space=pltpu.HBM)
SMEM = pl.BlockSpec(memory_space=pltpu.SMEM)


def params(**kw):
    return pltpu.CompilerParams(vmem_limit_bytes=VMEM_LIMIT, **kw)


def cost(flops, bytes_accessed):
    return pl.CostEstimate(flops=flops, bytes_accessed=bytes_accessed, transcendentals=0)


def in_hbm(x):
    return pltpu.with_memory_space_constraint(x, pltpu.HBM)


def iota(shape, dim):
    return lax.broadcasted_iota(jnp.int32, shape, dim)


def to_column(row):
    n = row.shape[1]
    return jnp.sum(
        jnp.where(iota((n, n), 0) == iota((n, n), 1), row, 0), axis=1, keepdims=True
    )


def slot_places(row, me, pool, local, depth):
    n = row.shape[1]
    column = to_column(row)
    earlier = (column == row) & (iota((n, n), 0) < iota((n, n), 1))
    slot = jnp.sum(jnp.where(earlier, 1, 0), axis=0, keepdims=True)
    holder = row // local
    apart = holder ^ me
    buffer, far = apart % (pool // 2), apart // (pool // 2)
    return ((buffer * 2 + far) * local + (row - holder * local)) * depth + slot


def far_first(count):
    return sorted(range(1, count), key=lambda j: (-bin(j).count("1"), -j))


def return_order(count):
    near_first = far_first(count)[::-1]
    return near_first[1:2] + near_first[:1] + near_first[2:]


def halves(x):
    high = x.astype(jnp.bfloat16)
    low = (x - high.astype(jnp.float32)).astype(jnp.bfloat16)
    return high, low


def up_share_kernel(cores, group_ref, core_ref, ranks_ref, up_hbm, out_ref, factor_ref, own_ref, sem):
    local, rank, share = out_ref.shape
    at = core_ref[0] * (up_hbm.shape[2] // cores) + group_ref[0] * share
    copy = pltpu.make_async_copy(
        up_hbm.at[:, :, pl.ds(pl.multiple_of(at, share), share)], own_ref, sem
    )
    copy.start()
    copy.wait()
    for a in range(local):
        used = ranks_ref[a]

        def factor(shape, dim):
            scale = jnp.float32(ALPHA) / jnp.full(shape, used, jnp.int32).astype(jnp.float32)
            return jnp.where(iota(shape, dim) < used, scale, 0.0)

        factor_ref[a : a + 1, :] = factor((1, rank), 1)
        out_ref[a] = (own_ref[a].astype(jnp.float32) * factor((rank, 1), 0)).astype(jnp.bfloat16)


def pick_kernel(
    pool, local, depth, me_ref, group_ref, adapter_hbm, tokens_hbm, down_hbm, *refs
):
    share_ref, outs = refs[0], refs[1:-4]
    adapter_ref, tokens_ref, share_sem, sems = refs[-4:]
    rows, width = tokens_ref.shape
    share = share_ref.shape[1]
    parts = sems.shape[0] - 1
    part = rows // parts
    adapter_copy = pltpu.make_async_copy(adapter_hbm, adapter_ref, sems.at[parts])
    adapter_copy.start()
    copies = [
        pltpu.make_async_copy(
            tokens_hbm.at[pl.ds(i * part, part), :],
            tokens_ref.at[pl.ds(i * part, part), :],
            sems.at[i],
        )
        for i in range(parts)
    ]
    for copy in copies:
        copy.start()
    at = pl.multiple_of(group_ref[0] * share, share)
    share_copy = pltpu.make_async_copy(down_hbm.at[:, pl.ds(at, share), :], share_ref, share_sem)
    share_copy.start()
    adapter_copy.wait()
    place = slot_places(adapter_ref[...], me_ref[0], pool, local, depth)
    size = outs[0].shape[0]
    slots = len(outs) * size
    picker = jnp.where(iota((slots, rows), 0) == place, 1.0, 0.0).astype(jnp.bfloat16)
    for copy in copies:
        copy.wait()
    step = 512
    for at in range(0, width, step):
        block = jnp.dot(
            picker, tokens_ref[:, at : at + step], preferred_element_type=jnp.float32
        )
        for j, out in enumerate(outs):
            out[:, at : at + step] = block[j * size : (j + 1) * size].astype(jnp.bfloat16)
    share_copy.wait()


def base_kernel(
    core_ref,
    tokens_hbm,
    weight_hbm,
    down_hbm,
    up_hbm,
    theirs_ref,
    mine_ref,
    down_ref,
    up_ref,
    tokens_ref,
    weight_ref,
    other_sems,
    sems,
):
    rows, columns = mine_ref.shape
    steps = sems.shape[1]
    step = tokens_ref.shape[1] // steps
    copies = []
    for half in range(2):
        start = (1 - core_ref[0] if half == 0 else core_ref[0]) * columns
        start = pl.multiple_of(start, columns)
        for k in range(steps):
            copies.append(
                pltpu.make_async_copy(
                    weight_hbm.at[pl.ds(k * step, step), pl.ds(start, columns)],
                    weight_ref.at[half, pl.ds(k * step, step), :],
                    sems.at[half, k],
                )
            )
    tokens_copy = pltpu.make_async_copy(tokens_hbm, tokens_ref, other_sems.at[0])
    own = pl.multiple_of(core_ref[0] * columns, columns)
    factor_copies = [
        pltpu.make_async_copy(down_hbm, down_ref, other_sems.at[1]),
        pltpu.make_async_copy(up_hbm.at[:, :, pl.ds(own, columns)], up_ref, other_sems.at[2]),
    ]
    for copy in [tokens_copy] + copies + factor_copies:
        copy.start()
    tokens_copy.wait()
    for half, out in enumerate((theirs_ref, mine_ref)):
        for k in range(steps):
            copies[half * steps + k].wait()
            term = jnp.dot(
                tokens_ref[:, k * step : (k + 1) * step],
                weight_ref[half, k * step : (k + 1) * step, :],
                preferred_element_type=jnp.float32,
            )
            if k == 0:
                out[...] = term
            else:
                out[...] += term
    for copy in factor_copies:
        copy.wait()


def down_kernel(buffers, groups, local, depth, group_ref, down_ref, *refs):
    order = [0] + far_first(buffers)
    ins = [refs[order.index(j)] for j in range(buffers)]
    shares, out = refs[buffers : buffers + groups], refs[-1]
    rank = out.shape[1]
    share = shares[0].shape[1]
    total = None
    for k in range(groups):
        at = pl.multiple_of((group_ref[0] ^ k) * share, share)
        rows = jnp.concatenate([x[:, pl.ds(at, share)] for x in ins], axis=0)
        factors = [down_ref[a, pl.ds(at, share), :] for a in range(local)]
        factors += [shares[k][a] for a in range(local)]
        term = jnp.dot(
            rows, jnp.concatenate(factors, axis=1), preferred_element_type=jnp.float32
        )
        total = term if total is None else total + term
    which = (iota((total.shape[0], 1), 0) // depth) % (2 * local)
    low = total[:, :rank]
    for i in range(1, 2 * local):
        low = jnp.where(which == i, total[:, i * rank : (i + 1) * rank], low)
    out[...] = low


def up_kernel(
    buffers, groups, local, depth, group_ref, low_ref, other_ref, factor_ref, up_ref, *refs
):
    shares, outs, term_ref = refs[:groups], refs[groups : groups + buffers], refs[-1]
    rows, rank = low_ref.shape
    size = rows // buffers
    columns = up_ref.shape[2]
    share = columns // groups
    which = (iota((rows, 1), 0) // depth) % (2 * local)
    low = low_ref[...] + other_ref[...]
    for a in range(local):
        low = jnp.where(which == a, low * factor_ref[a : a + 1, :], low)
    both = jnp.concatenate(halves(low), axis=0)
    which = jnp.concatenate([which, which], axis=0)
    spread = jnp.concatenate(
        [jnp.where(which == i, both, jnp.zeros_like(both)) for i in range(2 * local)], axis=1
    )
    for k in range(groups):
        at = pl.multiple_of((group_ref[0] ^ k) * share, share)
        up = [up_ref[a, :, pl.ds(at, share)] for a in range(local)]
        up += [shares[k][a] for a in range(local)]
        term = jnp.dot(
            spread, jnp.concatenate(up, axis=0), preferred_element_type=jnp.float32
        )
        term_ref[:, pl.ds(at, share)] = term[:rows] + term[rows:]
    lane = iota((1, LANES), 1)
    for j, out in enumerate(outs):
        term = term_ref[j * size : (j + 1) * size, :]
        top = jnp.max(jnp.abs(term), axis=1, keepdims=True)
        exponent = jnp.ceil(jnp.log2(jnp.maximum(top, 1e-30)) + 1e-3)
        code = jnp.clip(jnp.round(term * jnp.exp2(15.0 - exponent)), -32767.0, 32767.0)
        code = code.astype(jnp.int32)
        biased = exponent.astype(jnp.int32) + EXPONENT_BIAS
        first = code[:, :LANES]
        marked = (first & -2) | ((biased >> jnp.minimum(lane, EXPONENT_BITS - 1)) & 1)
        first = jnp.where(lane < EXPONENT_BITS, marked, first)
        out[:, :LANES] = first.astype(jnp.int16)
        out[:, LANES:] = code[:, LANES:].astype(jnp.int16)


def finish_kernel(
    buffers, pool, local, depth, me_ref, adapter_ref, mine_ref, other_ref, cos_ref, sin_ref, gain_ref, *refs
):
    order = [0] + return_order(buffers)
    ins = [refs[order.index(j)] for j in range(buffers)]
    out_hbm, out_ref, sems = refs[-3:]
    rows, columns = mine_ref.shape
    head = cos_ref.shape[1]
    place = to_column(slot_places(adapter_ref[...], me_ref[0], pool, local, depth))
    slots = buffers * ins[0].shape[0]
    picker = jnp.where(iota((rows, slots), 1) == place, 1.0, 0.0).astype(jnp.bfloat16)

    def picked(at, size):
        code = jnp.concatenate([x[:, at : at + size] for x in ins], axis=0).astype(jnp.int32)
        high = (code >> 8).astype(jnp.float32).astype(jnp.bfloat16)
        low = (code & 255).astype(jnp.float32).astype(jnp.bfloat16)
        high = jnp.dot(picker, high, preferred_element_type=jnp.float32)
        low = jnp.dot(picker, low, preferred_element_type=jnp.float32)
        return high * 256.0 + low

    lane = iota((1, LANES), 1)
    bits = picked(0, LANES).astype(jnp.int32) & 1
    bits = jnp.where(lane < EXPONENT_BITS, bits << jnp.minimum(lane, EXPONENT_BITS - 1), 0)
    exponent = jnp.sum(bits.astype(jnp.float32), axis=1, keepdims=True) - EXPONENT_BIAS
    scale = jnp.exp2(exponent - 15.0)
    cosine, sine, gain = cos_ref[...], sin_ref[...], gain_ref[...]
    entries = []
    for at in range(0, columns, 2 * head):
        projected = mine_ref[:, at : at + 2 * head] + other_ref[:, at : at + 2 * head]
        projected = projected + picked(at, 2 * head) * scale
        key, value = projected[:, :head], projected[:, head:]
        mean = jnp.mean(key * key, axis=1, keepdims=True)
        normed = key * lax.rsqrt(mean + NORM_EPS) * gain
        rotated = normed * cosine + pltpu.roll(normed, head // 2, 1) * sine
        entries += [rotated.astype(jnp.bfloat16), value.astype(jnp.bfloat16)]
    kinds, block = len(entries), 16
    n = kinds * block
    source = (iota((n, n), 0) % kinds) * block + iota((n, n), 0) // kinds
    order = jnp.where(iota((n, n), 1) == source, 1.0, 0.0).astype(jnp.bfloat16)
    copies = []
    for i in range(rows // block):
        stacked = jnp.concatenate([e[i * block : (i + 1) * block] for e in entries], axis=0)
        mixed = jnp.dot(order, stacked, preferred_element_type=jnp.float32)
        out_ref[i * n : (i + 1) * n, :] = mixed.astype(jnp.bfloat16)
        if i % 2:
            done = pl.ds((i - 1) * n, 2 * n)
            copies.append(
                pltpu.make_async_copy(out_ref.at[done, :], out_hbm.at[done, :], sems.at[i // 2])
            )
            copies[-1].start()
    for copy in copies:
        copy.wait()


def body(
    tokens,
    row_adapters,
    positions,
    key_value_weight,
    adapter_down,
    adapter_up,
    ranks,
    key_norm_gain,
):
    pool = lax.axis_size("pool")
    groups = lax.axis_size("groups")
    cores = lax.axis_size("tp")
    rows, width = tokens.shape
    local = adapter_down.shape[0]
    adapters = local * pool
    columns = key_value_weight.shape[1] // cores
    rank = adapter_down.shape[2]
    head = key_norm_gain.shape[0]
    depth = max(2, 2 * rows // adapters)
    buffers = pool // 2
    size = 2 * local * depth
    f32, bf16 = jnp.float32, jnp.bfloat16

    me = lax.axis_index("pool").astype(jnp.int32)[None]
    core = lax.axis_index("tp").astype(jnp.int32)[None]
    group = lax.axis_index("groups").astype(jnp.int32)[None]

    def exchange(x, axis, count, j):
        return lax.ppermute(x, axis, [(p, p ^ j) for p in range(count)])

    def hand_round(share):
        return [share] + [exchange(share, "groups", groups, k) for k in range(1, groups)]

    adapter_row = row_adapters.reshape(1, rows)
    down_share = width // groups
    parts = rows // 16
    down_part, *picked = pl.pallas_call(
        functools.partial(pick_kernel, pool, local, depth),
        in_specs=[SMEM] * 2 + [HBM] * 3,
        out_specs=[VMEM] * (1 + buffers),
        out_shape=[jax.ShapeDtypeStruct((local, down_share, rank), bf16)]
        + [jax.ShapeDtypeStruct((size, width), bf16)] * buffers,
        scratch_shapes=[
            pltpu.VMEM((1, rows), jnp.int32),
            pltpu.VMEM((rows, width), bf16),
            pltpu.SemaphoreType.DMA,
            pltpu.SemaphoreType.DMA((parts + 1,)),
        ],
        compiler_params=params(),
        cost_estimate=cost(2 * buffers * size * rows * width, 2 * (rows + buffers * size) * width),
        name="pick",
    )(me, group, in_hbm(adapter_row), in_hbm(tokens), in_hbm(adapter_down))
    far_down = exchange(down_part, "pool", pool, pool // 2)
    up_share = columns // groups
    ranks_now, adapter_up_now, _ = lax.optimization_barrier((ranks, adapter_up, picked))
    up_part, factor = pl.pallas_call(
        functools.partial(up_share_kernel, cores),
        in_specs=[SMEM] * 3 + [HBM],
        out_specs=[VMEM] * 2,
        out_shape=[
            jax.ShapeDtypeStruct((local, rank, up_share), bf16),
            jax.ShapeDtypeStruct((local, rank), f32),
        ],
        scratch_shapes=[
            pltpu.VMEM((local, rank, up_share), bf16),
            pltpu.SemaphoreType.DMA,
        ],
        compiler_params=params(),
        cost_estimate=cost(local * rank * up_share, 4 * local * rank * up_share),
        name="up_share",
    )(group, core, ranks_now, in_hbm(adapter_up_now))
    far_up = exchange(up_part, "pool", pool, pool // 2)

    order = far_first(buffers)
    early, late = order[:1], order[1:]
    late_rows, _ = lax.optimization_barrier(([picked[j] for j in late], up_part))
    leaving = [picked[j] for j in early] + late_rows
    arrived = [picked[0]] + [exchange(x, "pool", pool, j) for x, j in zip(leaving, order)]

    steps = 5
    theirs, mine, own_down, own_up = pl.pallas_call(
        base_kernel,
        in_specs=[SMEM] + [HBM] * 4,
        out_specs=[VMEM] * 4,
        out_shape=[jax.ShapeDtypeStruct((rows, columns), f32)] * 2
        + [
            jax.ShapeDtypeStruct(adapter_down.shape, bf16),
            jax.ShapeDtypeStruct((local, rank, columns), bf16),
        ],
        scratch_shapes=[
            pltpu.VMEM((rows, width), bf16),
            pltpu.VMEM((2, width, columns), bf16),
            pltpu.SemaphoreType.DMA((3,)),
            pltpu.SemaphoreType.DMA((2, steps)),
        ],
        compiler_params=params(),
        cost_estimate=cost(4 * rows * width * columns, 4 * width * columns),
        name="base",
    )(
        core,
        in_hbm(tokens),
        in_hbm(key_value_weight),
        in_hbm(adapter_down),
        in_hbm(adapter_up),
    )
    far_down, theirs = lax.optimization_barrier((far_down, theirs))
    far_downs = hand_round(far_down)
    far_up, _ = lax.optimization_barrier((far_up, far_down))
    far_ups = hand_round(far_up)
    half_dim = head // 2
    frequency = jnp.power(
        f32(ROPE_THETA), -jnp.arange(half_dim, dtype=f32) * (2.0 / head)
    )
    angles = positions.astype(f32)[:, None] * frequency[None, :]
    cosine, sine = jnp.cos(angles), jnp.sin(angles)
    cosine = jnp.concatenate([cosine, cosine], axis=1)
    sine = jnp.concatenate([-sine, sine], axis=1)

    far_up, arrived[1], theirs = lax.optimization_barrier((far_up, arrived[1], theirs))
    other = exchange(theirs, "tp", cores, 1)
    arrived, mine, cosine, sine = lax.optimization_barrier((arrived, mine, cosine, sine))
    slots = buffers * size
    low = pl.pallas_call(
        functools.partial(down_kernel, buffers, groups, local, depth),
        in_specs=[SMEM] + [VMEM] * (1 + buffers + groups),
        out_specs=VMEM,
        out_shape=jax.ShapeDtypeStruct((slots, rank), f32),
        compiler_params=params(),
        cost_estimate=cost(4 * local * slots * rank * width, 2 * (slots + rank) * width),
        name="down",
    )(group, own_down, *arrived, *far_downs)
    low_other = exchange(low, "tp", cores, 1)

    terms = pl.pallas_call(
        functools.partial(up_kernel, buffers, groups, local, depth),
        in_specs=[SMEM] + [VMEM] * (4 + groups),
        out_specs=[VMEM] * buffers,
        out_shape=[jax.ShapeDtypeStruct((size, columns), jnp.int16)] * buffers,
        scratch_shapes=[pltpu.VMEM((slots, columns), f32)],
        compiler_params=params(),
        cost_estimate=cost(8 * local * slots * rank * columns, 2 * slots * columns),
        name="up",
    )(group, low, low_other, factor, own_up, *far_ups)
    order = return_order(buffers)
    returned = [terms[0]] + [exchange(terms[j], "pool", pool, j) for j in order]

    out = pl.pallas_call(
        functools.partial(finish_kernel, buffers, pool, local, depth),
        in_specs=[SMEM] + [VMEM] * (6 + buffers),
        out_specs=HBM,
        out_shape=jax.ShapeDtypeStruct((rows * columns // head, head), bf16),
        scratch_shapes=[
            pltpu.VMEM((rows * columns // head, head), bf16),
            pltpu.SemaphoreType.DMA((rows // 32,)),
        ],
        compiler_params=params(),
        cost_estimate=cost(4 * rows * slots * columns, 2 * slots * columns),
        name="finish",
    )(
        me,
        adapter_row,
        mine,
        other,
        cosine,
        sine,
        key_norm_gain.astype(f32)[None, :],
        *returned,
    )
    return out.reshape(rows, columns // (2 * head), 2, head)


def solution(mesh):
    return jax.shard_map(
        body,
        mesh=mesh,
        in_specs=(
            P(("groups", "pool"), "tp"),
            P(("groups", "pool"), None),
            P(("groups", "pool")),
            P("tp", None),
            P("pool", "tp", None),
            P("pool", None, None),
            P("pool"),
            P(),
        ),
        out_specs=P(("groups", "pool"), "tp", None, None),
        check_vma=False,
    )
```

```python
import functools

import jax
import jax.numpy as jnp
from jax import lax
from jax.experimental import pallas as pl
from jax.experimental.pallas import tpu as pltpu
from jax.sharding import PartitionSpec as P

ALPHA = 32
ROPE_THETA = 1000000.0
NORM_EPS = 1e-06
VMEM_LIMIT = 48 * 1024 * 1024
LANES = 128
EXPONENT_BITS = 8
EXPONENT_BIAS = 128

VMEM = pl.BlockSpec(memory_space=pltpu.VMEM)
HBM = pl.BlockSpec(memory_space=pltpu.HBM)
SMEM = pl.BlockSpec(memory_space=pltpu.SMEM)


def params(**kw):
    return pltpu.CompilerParams(vmem_limit_bytes=VMEM_LIMIT, **kw)


def cost(flops, bytes_accessed):
    return pl.CostEstimate(flops=flops, bytes_accessed=bytes_accessed, transcendentals=0)


def in_hbm(x):
    return pltpu.with_memory_space_constraint(x, pltpu.HBM)


def iota(shape, dim):
    return lax.broadcasted_iota(jnp.int32, shape, dim)


def to_column(row):
    n = row.shape[1]
    return jnp.sum(
        jnp.where(iota((n, n), 0) == iota((n, n), 1), row, 0), axis=1, keepdims=True
    )


def slot_places(row, me, pool, local, depth):
    n = row.shape[1]
    column = to_column(row)
    earlier = (column == row) & (iota((n, n), 0) < iota((n, n), 1))
    slot = jnp.sum(jnp.where(earlier, 1, 0), axis=0, keepdims=True)
    holder = row // local
    apart = holder ^ me
    buffer, far = apart % (pool // 2), apart // (pool // 2)
    return ((buffer * 2 + far) * local + (row - holder * local)) * depth + slot


def far_first(count):
    return sorted(range(1, count), key=lambda j: (-bin(j).count("1"), -j))


def return_order(count):
    order = far_first(count)
    return order[-1:] + order[:-1]


def halves(x):
    high = x.astype(jnp.bfloat16)
    low = (x - high.astype(jnp.float32)).astype(jnp.bfloat16)
    return high, low


def up_share_kernel(cores, group_ref, core_ref, ranks_ref, up_hbm, out_ref, factor_ref, own_ref, sem):
    local, rank, share = out_ref.shape
    at = core_ref[0] * (up_hbm.shape[2] // cores) + group_ref[0] * share
    copy = pltpu.make_async_copy(
        up_hbm.at[:, :, pl.ds(pl.multiple_of(at, share), share)], own_ref, sem
    )
    copy.start()
    copy.wait()
    for a in range(local):
        used = ranks_ref[a]

        def factor(shape, dim):
            scale = jnp.float32(ALPHA) / jnp.full(shape, used, jnp.int32).astype(jnp.float32)
            return jnp.where(iota(shape, dim) < used, scale, 0.0)

        factor_ref[a : a + 1, :] = factor((1, rank), 1)
        out_ref[a] = (own_ref[a].astype(jnp.float32) * factor((rank, 1), 0)).astype(jnp.bfloat16)


def pick_kernel(
    pool, local, depth, me_ref, group_ref, adapter_hbm, tokens_hbm, down_hbm, *refs
):
    share_ref, outs = refs[0], refs[1:-4]
    adapter_ref, tokens_ref, share_sem, sems = refs[-4:]
    rows, width = tokens_ref.shape
    share = share_ref.shape[1]
    parts = sems.shape[0] - 1
    part = rows // parts
    adapter_copy = pltpu.make_async_copy(adapter_hbm, adapter_ref, sems.at[parts])
    adapter_copy.start()
    copies = [
        pltpu.make_async_copy(
            tokens_hbm.at[pl.ds(i * part, part), :],
            tokens_ref.at[pl.ds(i * part, part), :],
            sems.at[i],
        )
        for i in range(parts)
    ]
    for copy in copies:
        copy.start()
    at = pl.multiple_of(group_ref[0] * share, share)
    share_copy = pltpu.make_async_copy(down_hbm.at[:, pl.ds(at, share), :], share_ref, share_sem)
    share_copy.start()
    adapter_copy.wait()
    place = slot_places(adapter_ref[...], me_ref[0], pool, local, depth)
    size = outs[0].shape[0]
    slots = len(outs) * size
    picker = jnp.where(iota((slots, rows), 0) == place, 1.0, 0.0).astype(jnp.bfloat16)
    for copy in copies:
        copy.wait()
    step = 512
    for at in range(0, width, step):
        block = jnp.dot(
            picker, tokens_ref[:, at : at + step], preferred_element_type=jnp.float32
        )
        for j, out in enumerate(outs):
            out[:, at : at + step] = block[j * size : (j + 1) * size].astype(jnp.bfloat16)
    share_copy.wait()


def base_kernel(
    core_ref,
    tokens_hbm,
    weight_hbm,
    down_hbm,
    up_hbm,
    theirs_ref,
    mine_ref,
    down_ref,
    up_ref,
    tokens_ref,
    weight_ref,
    other_sems,
    sems,
):
    rows, columns = mine_ref.shape
    steps = sems.shape[1]
    step = tokens_ref.shape[1] // steps
    copies = []
    for half in range(2):
        start = (1 - core_ref[0] if half == 0 else core_ref[0]) * columns
        start = pl.multiple_of(start, columns)
        for k in range(steps):
            copies.append(
                pltpu.make_async_copy(
                    weight_hbm.at[pl.ds(k * step, step), pl.ds(start, columns)],
                    weight_ref.at[half, pl.ds(k * step, step), :],
                    sems.at[half, k],
                )
            )
    tokens_copy = pltpu.make_async_copy(tokens_hbm, tokens_ref, other_sems.at[0])
    own = pl.multiple_of(core_ref[0] * columns, columns)
    factor_copies = [
        pltpu.make_async_copy(down_hbm, down_ref, other_sems.at[1]),
        pltpu.make_async_copy(up_hbm.at[:, :, pl.ds(own, columns)], up_ref, other_sems.at[2]),
    ]
    for copy in [tokens_copy] + copies + factor_copies:
        copy.start()
    tokens_copy.wait()
    for half, out in enumerate((theirs_ref, mine_ref)):
        for k in range(steps):
            copies[half * steps + k].wait()
            term = jnp.dot(
                tokens_ref[:, k * step : (k + 1) * step],
                weight_ref[half, k * step : (k + 1) * step, :],
                preferred_element_type=jnp.float32,
            )
            if k == 0:
                out[...] = term
            else:
                out[...] += term
    for copy in factor_copies:
        copy.wait()


def down_kernel(buffers, groups, local, depth, group_ref, down_ref, *refs):
    order = [0] + far_first(buffers)
    ins = [refs[order.index(j)] for j in range(buffers)]
    shares, out = refs[buffers : buffers + groups], refs[-1]
    rank = out.shape[1]
    share = shares[0].shape[1]
    total = None
    for k in range(groups):
        at = pl.multiple_of((group_ref[0] ^ k) * share, share)
        rows = jnp.concatenate([x[:, pl.ds(at, share)] for x in ins], axis=0)
        factors = [down_ref[a, pl.ds(at, share), :] for a in range(local)]
        factors += [shares[k][a] for a in range(local)]
        term = jnp.dot(
            rows, jnp.concatenate(factors, axis=1), preferred_element_type=jnp.float32
        )
        total = term if total is None else total + term
    which = (iota((total.shape[0], 1), 0) // depth) % (2 * local)
    low = total[:, :rank]
    for i in range(1, 2 * local):
        low = jnp.where(which == i, total[:, i * rank : (i + 1) * rank], low)
    out[...] = low


def up_kernel(
    buffers, groups, local, depth, group_ref, low_ref, other_ref, factor_ref, up_ref, *refs
):
    shares, outs, term_ref = refs[:groups], refs[groups : groups + buffers], refs[-1]
    rows, rank = low_ref.shape
    size = rows // buffers
    columns = up_ref.shape[2]
    share = columns // groups
    which = (iota((rows, 1), 0) // depth) % (2 * local)
    low = low_ref[...] + other_ref[...]
    for a in range(local):
        low = jnp.where(which == a, low * factor_ref[a : a + 1, :], low)
    both = jnp.concatenate(halves(low), axis=0)
    which = jnp.concatenate([which, which], axis=0)
    spread = jnp.concatenate(
        [jnp.where(which == i, both, jnp.zeros_like(both)) for i in range(2 * local)], axis=1
    )
    for k in range(groups):
        at = pl.multiple_of((group_ref[0] ^ k) * share, share)
        up = [up_ref[a, :, pl.ds(at, share)] for a in range(local)]
        up += [shares[k][a] for a in range(local)]
        term = jnp.dot(
            spread, jnp.concatenate(up, axis=0), preferred_element_type=jnp.float32
        )
        term_ref[:, pl.ds(at, share)] = term[:rows] + term[rows:]
    lane = iota((1, LANES), 1)
    for j, out in enumerate(outs):
        term = term_ref[j * size : (j + 1) * size, :]
        top = jnp.max(jnp.abs(term), axis=1, keepdims=True)
        exponent = jnp.ceil(jnp.log2(jnp.maximum(top, 1e-30)) + 1e-3)
        code = jnp.clip(jnp.round(term * jnp.exp2(15.0 - exponent)), -32767.0, 32767.0)
        code = code.astype(jnp.int32)
        biased = exponent.astype(jnp.int32) + EXPONENT_BIAS
        first = code[:, :LANES]
        marked = (first & -2) | ((biased >> jnp.minimum(lane, EXPONENT_BITS - 1)) & 1)
        first = jnp.where(lane < EXPONENT_BITS, marked, first)
        out[:, :LANES] = first.astype(jnp.int16)
        out[:, LANES:] = code[:, LANES:].astype(jnp.int16)


def planes(codes, at, size):
    code = jnp.concatenate([x[:, at : at + size] for x in codes], axis=0).astype(jnp.int32)
    high = (code >> 8).astype(jnp.float32).astype(jnp.bfloat16)
    low = (code & 255).astype(jnp.float32).astype(jnp.bfloat16)
    return high, low


def decoded(picker, plane):
    high = jnp.dot(picker, plane[0], preferred_element_type=jnp.float32)
    low = jnp.dot(picker, plane[1], preferred_element_type=jnp.float32)
    return high * 256.0 + low


def scale_of(first):
    lane = iota((1, LANES), 1)
    bits = first.astype(jnp.int32) & 1
    bits = jnp.where(lane < EXPONENT_BITS, bits << jnp.minimum(lane, EXPONENT_BITS - 1), 0)
    exponent = jnp.sum(bits.astype(jnp.float32), axis=1, keepdims=True) - EXPONENT_BIAS
    return jnp.exp2(exponent - 15.0)


def start_rows_kernel(
    buffers, pool, local, depth, me_ref, adapter_ref, mine_ref, other_ref, own_ref, partial_ref, picker_ref
):
    rows, columns = mine_ref.shape
    size = own_ref.shape[0]
    place = to_column(slot_places(adapter_ref[...], me_ref[0], pool, local, depth))
    picker = jnp.where(iota((rows, size), 1) == place, 1.0, 0.0).astype(jnp.bfloat16)
    scale = scale_of(decoded(picker, planes([own_ref], 0, LANES)))
    for at in range(0, columns, 256):
        term = decoded(picker, planes([own_ref], at, 256)) * scale
        partial_ref[:, at : at + 256] = (
            mine_ref[:, at : at + 256] + other_ref[:, at : at + 256] + term
        )
    slots = (buffers - 1) * size
    picker_ref[...] = jnp.where(iota((rows, slots), 1) == place - size, 1.0, 0.0).astype(
        jnp.bfloat16
    )


def finish_kernel(buffers, partial_ref, picker_ref, cos_ref, sin_ref, gain_ref, *refs):
    order = return_order(buffers)
    ins = [refs[order.index(j)] for j in range(1, buffers)]
    out_hbm, out_ref, sems = refs[-3:]
    rows, columns = partial_ref.shape
    head = cos_ref.shape[1]
    gain = gain_ref[...]
    kinds, block = columns // head, 16
    n = kinds * block
    source = (iota((n, n), 0) % kinds) * block + iota((n, n), 0) // kinds
    mix = jnp.where(iota((n, n), 1) == source, 1.0, 0.0).astype(jnp.bfloat16)
    plane = [planes(ins, at, 2 * head) for at in range(0, columns, 2 * head)]
    first = planes(ins, 0, LANES)
    copies = []
    part = rows // 2
    for begin in range(0, rows, part):
        here = slice(begin, begin + part)
        picker = picker_ref[here, :]
        scale = scale_of(decoded(picker, first))
        cosine, sine = cos_ref[here, :], sin_ref[here, :]
        entries = []
        for at in range(0, columns, 2 * head):
            projected = partial_ref[here, at : at + 2 * head]
            projected = projected + decoded(picker, plane[at // (2 * head)]) * scale
            key, value = projected[:, :head], projected[:, head:]
            mean = jnp.mean(key * key, axis=1, keepdims=True)
            normed = key * lax.rsqrt(mean + NORM_EPS) * gain
            rotated = normed * cosine + pltpu.roll(normed, head // 2, 1) * sine
            entries += [rotated.astype(jnp.bfloat16), value.astype(jnp.bfloat16)]
        for i in range(part // block):
            stacked = jnp.concatenate([e[i * block : (i + 1) * block] for e in entries], axis=0)
            mixed = jnp.dot(mix, stacked, preferred_element_type=jnp.float32)
            top = begin * kinds + i * n
            out_ref[top : top + n, :] = mixed.astype(jnp.bfloat16)
        done = pl.ds(begin * kinds, part * kinds)
        copies.append(
            pltpu.make_async_copy(
                out_ref.at[done, :], out_hbm.at[done, :], sems.at[begin // part]
            )
        )
        copies[-1].start()
    for copy in copies:
        copy.wait()


def body(
    tokens,
    row_adapters,
    positions,
    key_value_weight,
    adapter_down,
    adapter_up,
    ranks,
    key_norm_gain,
):
    pool = lax.axis_size("pool")
    groups = lax.axis_size("groups")
    cores = lax.axis_size("tp")
    rows, width = tokens.shape
    local = adapter_down.shape[0]
    adapters = local * pool
    columns = key_value_weight.shape[1] // cores
    rank = adapter_down.shape[2]
    head = key_norm_gain.shape[0]
    depth = max(2, 2 * rows // adapters)
    buffers = pool // 2
    size = 2 * local * depth
    f32, bf16 = jnp.float32, jnp.bfloat16

    me = lax.axis_index("pool").astype(jnp.int32)[None]
    core = lax.axis_index("tp").astype(jnp.int32)[None]
    group = lax.axis_index("groups").astype(jnp.int32)[None]

    def exchange(x, axis, count, j):
        return lax.ppermute(x, axis, [(p, p ^ j) for p in range(count)])

    def hand_round(share):
        return [share] + [exchange(share, "groups", groups, k) for k in range(1, groups)]

    adapter_row = row_adapters.reshape(1, rows)
    down_share = width // groups
    parts = rows // 16
    down_part, *picked = pl.pallas_call(
        functools.partial(pick_kernel, pool, local, depth),
        in_specs=[SMEM] * 2 + [HBM] * 3,
        out_specs=[VMEM] * (1 + buffers),
        out_shape=[jax.ShapeDtypeStruct((local, down_share, rank), bf16)]
        + [jax.ShapeDtypeStruct((size, width), bf16)] * buffers,
        scratch_shapes=[
            pltpu.VMEM((1, rows), jnp.int32),
            pltpu.VMEM((rows, width), bf16),
            pltpu.SemaphoreType.DMA,
            pltpu.SemaphoreType.DMA((parts + 1,)),
        ],
        compiler_params=params(),
        cost_estimate=cost(2 * buffers * size * rows * width, 2 * (rows + buffers * size) * width),
        name="pick",
    )(me, group, in_hbm(adapter_row), in_hbm(tokens), in_hbm(adapter_down))
    far_down = exchange(down_part, "pool", pool, pool // 2)
    up_share = columns // groups
    ranks_now, adapter_up_now, _ = lax.optimization_barrier((ranks, adapter_up, picked))
    up_part, factor = pl.pallas_call(
        functools.partial(up_share_kernel, cores),
        in_specs=[SMEM] * 3 + [HBM],
        out_specs=[VMEM] * 2,
        out_shape=[
            jax.ShapeDtypeStruct((local, rank, up_share), bf16),
            jax.ShapeDtypeStruct((local, rank), f32),
        ],
        scratch_shapes=[
            pltpu.VMEM((local, rank, up_share), bf16),
            pltpu.SemaphoreType.DMA,
        ],
        compiler_params=params(),
        cost_estimate=cost(local * rank * up_share, 4 * local * rank * up_share),
        name="up_share",
    )(group, core, ranks_now, in_hbm(adapter_up_now))
    far_up = exchange(up_part, "pool", pool, pool // 2)

    order = far_first(buffers)
    early, late = order[:1], order[1:]
    late_rows, _ = lax.optimization_barrier(([picked[j] for j in late], up_part))
    leaving = [picked[j] for j in early] + late_rows
    arrived = [picked[0]] + [exchange(x, "pool", pool, j) for x, j in zip(leaving, order)]

    steps = 5
    theirs, mine, own_down, own_up = pl.pallas_call(
        base_kernel,
        in_specs=[SMEM] + [HBM] * 4,
        out_specs=[VMEM] * 4,
        out_shape=[jax.ShapeDtypeStruct((rows, columns), f32)] * 2
        + [
            jax.ShapeDtypeStruct(adapter_down.shape, bf16),
            jax.ShapeDtypeStruct((local, rank, columns), bf16),
        ],
        scratch_shapes=[
            pltpu.VMEM((rows, width), bf16),
            pltpu.VMEM((2, width, columns), bf16),
            pltpu.SemaphoreType.DMA((3,)),
            pltpu.SemaphoreType.DMA((2, steps)),
        ],
        compiler_params=params(),
        cost_estimate=cost(4 * rows * width * columns, 4 * width * columns),
        name="base",
    )(
        core,
        in_hbm(tokens),
        in_hbm(key_value_weight),
        in_hbm(adapter_down),
        in_hbm(adapter_up),
    )
    far_down, theirs = lax.optimization_barrier((far_down, theirs))
    far_downs = hand_round(far_down)
    far_up, _ = lax.optimization_barrier((far_up, far_down))
    far_ups = hand_round(far_up)
    half_dim = head // 2
    frequency = jnp.power(
        f32(ROPE_THETA), -jnp.arange(half_dim, dtype=f32) * (2.0 / head)
    )
    angles = positions.astype(f32)[:, None] * frequency[None, :]
    cosine, sine = jnp.cos(angles), jnp.sin(angles)
    cosine = jnp.concatenate([cosine, cosine], axis=1)
    sine = jnp.concatenate([-sine, sine], axis=1)

    far_up, arrived[1], theirs = lax.optimization_barrier((far_up, arrived[1], theirs))
    other = exchange(theirs, "tp", cores, 1)
    arrived, mine, cosine, sine = lax.optimization_barrier((arrived, mine, cosine, sine))
    slots = buffers * size
    low = pl.pallas_call(
        functools.partial(down_kernel, buffers, groups, local, depth),
        in_specs=[SMEM] + [VMEM] * (1 + buffers + groups),
        out_specs=VMEM,
        out_shape=jax.ShapeDtypeStruct((slots, rank), f32),
        compiler_params=params(),
        cost_estimate=cost(4 * local * slots * rank * width, 2 * (slots + rank) * width),
        name="down",
    )(group, own_down, *arrived, *far_downs)
    low_other = exchange(low, "tp", cores, 1)

    terms = pl.pallas_call(
        functools.partial(up_kernel, buffers, groups, local, depth),
        in_specs=[SMEM] + [VMEM] * (4 + groups),
        out_specs=[VMEM] * buffers,
        out_shape=[jax.ShapeDtypeStruct((size, columns), jnp.int16)] * buffers,
        scratch_shapes=[pltpu.VMEM((slots, columns), f32)],
        compiler_params=params(),
        cost_estimate=cost(8 * local * slots * rank * columns, 2 * slots * columns),
        name="up",
    )(group, low, low_other, factor, own_up, *far_ups)
    order = return_order(buffers)
    returned = [exchange(terms[j], "pool", pool, j) for j in order]

    partial, picker = pl.pallas_call(
        functools.partial(start_rows_kernel, buffers, pool, local, depth),
        in_specs=[SMEM] + [VMEM] * 4,
        out_specs=[VMEM] * 2,
        out_shape=[
            jax.ShapeDtypeStruct((rows, columns), f32),
            jax.ShapeDtypeStruct((rows, slots - size), bf16),
        ],
        compiler_params=params(),
        cost_estimate=cost(4 * rows * size * columns, 12 * rows * columns),
        name="start_rows",
    )(me, adapter_row, mine, other, terms[0])
    out = pl.pallas_call(
        functools.partial(finish_kernel, buffers),
        in_specs=[VMEM] * (4 + buffers),
        out_specs=HBM,
        out_shape=jax.ShapeDtypeStruct((rows * columns // head, head), bf16),
        scratch_shapes=[
            pltpu.VMEM((rows * columns // head, head), bf16),
            pltpu.SemaphoreType.DMA((2,)),
        ],
        compiler_params=params(),
        cost_estimate=cost(4 * rows * slots * columns, 2 * slots * columns),
        name="finish",
    )(partial, picker, cosine, sine, key_norm_gain.astype(f32)[None, :], *returned)
    return out.reshape(rows, columns // (2 * head), 2, head)


def solution(mesh):
    return jax.shard_map(
        body,
        mesh=mesh,
        in_specs=(
            P(("groups", "pool"), "tp"),
            P(("groups", "pool"), None),
            P(("groups", "pool")),
            P("tp", None),
            P("pool", "tp", None),
            P("pool", None, None),
            P("pool"),
            P(),
        ),
        out_specs=P(("groups", "pool"), "tp", None, None),
        check_vma=False,
    )
```

```python
import functools

import jax
import jax.numpy as jnp
from jax import lax
from jax.experimental import pallas as pl
from jax.experimental.pallas import tpu as pltpu
from jax.sharding import PartitionSpec as P

ALPHA = 32
ROPE_THETA = 1000000.0
NORM_EPS = 1e-06
VMEM_LIMIT = 48 * 1024 * 1024
LANES = 128
EXPONENT_BITS = 8
EXPONENT_BIAS = 128

VMEM = pl.BlockSpec(memory_space=pltpu.VMEM)
HBM = pl.BlockSpec(memory_space=pltpu.HBM)
SMEM = pl.BlockSpec(memory_space=pltpu.SMEM)


def params(**kw):
    return pltpu.CompilerParams(vmem_limit_bytes=VMEM_LIMIT, **kw)


def cost(flops, bytes_accessed):
    return pl.CostEstimate(flops=flops, bytes_accessed=bytes_accessed, transcendentals=0)


def in_hbm(x):
    return pltpu.with_memory_space_constraint(x, pltpu.HBM)


def iota(shape, dim):
    return lax.broadcasted_iota(jnp.int32, shape, dim)


def to_column(row):
    n = row.shape[1]
    return jnp.sum(
        jnp.where(iota((n, n), 0) == iota((n, n), 1), row, 0), axis=1, keepdims=True
    )


def slot_places(row, me, pool, local, depth):
    n = row.shape[1]
    column = to_column(row)
    earlier = (column == row) & (iota((n, n), 0) < iota((n, n), 1))
    slot = jnp.sum(jnp.where(earlier, 1, 0), axis=0, keepdims=True)
    holder = row // local
    apart = holder ^ me
    buffer, far = apart % (pool // 2), apart // (pool // 2)
    return ((buffer * 2 + far) * local + (row - holder * local)) * depth + slot


def far_first(count):
    return sorted(range(1, count), key=lambda j: (-bin(j).count("1"), -j))


def return_order(count):
    order = far_first(count)
    return order[-1:] + order[:-1]


def halves(x):
    high = x.astype(jnp.bfloat16)
    low = (x - high.astype(jnp.float32)).astype(jnp.bfloat16)
    return high, low


def up_share_kernel(cores, group_ref, core_ref, ranks_ref, up_hbm, out_ref, factor_ref, own_ref, sem):
    local, rank, share = out_ref.shape
    at = core_ref[0] * (up_hbm.shape[2] // cores) + group_ref[0] * share
    copy = pltpu.make_async_copy(
        up_hbm.at[:, :, pl.ds(pl.multiple_of(at, share), share)], own_ref, sem
    )
    copy.start()
    copy.wait()
    for a in range(local):
        used = ranks_ref[a]

        def factor(shape, dim):
            scale = jnp.float32(ALPHA) / jnp.full(shape, used, jnp.int32).astype(jnp.float32)
            return jnp.where(iota(shape, dim) < used, scale, 0.0)

        factor_ref[a : a + 1, :] = factor((1, rank), 1)
        out_ref[a] = (own_ref[a].astype(jnp.float32) * factor((rank, 1), 0)).astype(jnp.bfloat16)


def pick_kernel(
    pool, local, depth, me_ref, group_ref, adapter_hbm, tokens_hbm, down_hbm, *refs
):
    share_ref, outs = refs[0], refs[1:-4]
    adapter_ref, tokens_ref, share_sem, sems = refs[-4:]
    rows, width = tokens_ref.shape
    share = share_ref.shape[1]
    parts = sems.shape[0] - 1
    part = rows // parts
    adapter_copy = pltpu.make_async_copy(adapter_hbm, adapter_ref, sems.at[parts])
    adapter_copy.start()
    copies = [
        pltpu.make_async_copy(
            tokens_hbm.at[pl.ds(i * part, part), :],
            tokens_ref.at[pl.ds(i * part, part), :],
            sems.at[i],
        )
        for i in range(parts)
    ]
    for copy in copies:
        copy.start()
    at = pl.multiple_of(group_ref[0] * share, share)
    share_copy = pltpu.make_async_copy(down_hbm.at[:, pl.ds(at, share), :], share_ref, share_sem)
    share_copy.start()
    adapter_copy.wait()
    place = slot_places(adapter_ref[...], me_ref[0], pool, local, depth)
    size = outs[0].shape[0]
    slots = len(outs) * size
    picker = jnp.where(iota((slots, rows), 0) == place, 1.0, 0.0).astype(jnp.bfloat16)
    for copy in copies:
        copy.wait()
    step = 512
    for at in range(0, width, step):
        block = jnp.dot(
            picker, tokens_ref[:, at : at + step], preferred_element_type=jnp.float32
        )
        for j, out in enumerate(outs):
            out[:, at : at + step] = block[j * size : (j + 1) * size].astype(jnp.bfloat16)
    share_copy.wait()


def base_kernel(
    core_ref,
    tokens_hbm,
    weight_hbm,
    down_hbm,
    up_hbm,
    theirs_ref,
    mine_ref,
    down_ref,
    up_ref,
    tokens_ref,
    weight_ref,
    other_sems,
    sems,
):
    rows, columns = mine_ref.shape
    steps = sems.shape[1]
    step = tokens_ref.shape[1] // steps
    copies = []
    for half in range(2):
        start = (1 - core_ref[0] if half == 0 else core_ref[0]) * columns
        start = pl.multiple_of(start, columns)
        for k in range(steps):
            copies.append(
                pltpu.make_async_copy(
                    weight_hbm.at[pl.ds(k * step, step), pl.ds(start, columns)],
                    weight_ref.at[half, pl.ds(k * step, step), :],
                    sems.at[half, k],
                )
            )
    tokens_copy = pltpu.make_async_copy(tokens_hbm, tokens_ref, other_sems.at[0])
    own = pl.multiple_of(core_ref[0] * columns, columns)
    factor_copies = [
        pltpu.make_async_copy(down_hbm, down_ref, other_sems.at[1]),
        pltpu.make_async_copy(up_hbm.at[:, :, pl.ds(own, columns)], up_ref, other_sems.at[2]),
    ]
    for copy in [tokens_copy] + copies + factor_copies:
        copy.start()
    tokens_copy.wait()
    for half, out in enumerate((theirs_ref, mine_ref)):
        for k in range(steps):
            copies[half * steps + k].wait()
            term = jnp.dot(
                tokens_ref[:, k * step : (k + 1) * step],
                weight_ref[half, k * step : (k + 1) * step, :],
                preferred_element_type=jnp.float32,
            )
            if k == 0:
                out[...] = term
            else:
                out[...] += term
    for copy in factor_copies:
        copy.wait()


def down_kernel(buffers, groups, local, depth, group_ref, down_ref, *refs):
    order = [0] + far_first(buffers)
    ins = [refs[order.index(j)] for j in range(buffers)]
    shares, out = refs[buffers : buffers + groups], refs[-1]
    rank = out.shape[1]
    share = shares[0].shape[1]
    total = None
    for k in range(groups):
        at = pl.multiple_of((group_ref[0] ^ k) * share, share)
        rows = jnp.concatenate([x[:, pl.ds(at, share)] for x in ins], axis=0)
        factors = [down_ref[a, pl.ds(at, share), :] for a in range(local)]
        factors += [shares[k][a] for a in range(local)]
        term = jnp.dot(
            rows, jnp.concatenate(factors, axis=1), preferred_element_type=jnp.float32
        )
        total = term if total is None else total + term
    which = (iota((total.shape[0], 1), 0) // depth) % (2 * local)
    low = total[:, :rank]
    for i in range(1, 2 * local):
        low = jnp.where(which == i, total[:, i * rank : (i + 1) * rank], low)
    out[...] = low


def up_kernel(
    buffers, groups, local, depth, group_ref, low_ref, other_ref, factor_ref, up_ref, *refs
):
    shares, outs, term_ref = refs[:groups], refs[groups : groups + buffers], refs[-1]
    rows, rank = low_ref.shape
    size = rows // buffers
    columns = up_ref.shape[2]
    share = columns // groups
    which = (iota((rows, 1), 0) // depth) % (2 * local)
    low = low_ref[...] + other_ref[...]
    for a in range(local):
        low = jnp.where(which == a, low * factor_ref[a : a + 1, :], low)
    both = jnp.concatenate(halves(low), axis=0)
    which = jnp.concatenate([which, which], axis=0)
    spread = jnp.concatenate(
        [jnp.where(which == i, both, jnp.zeros_like(both)) for i in range(2 * local)], axis=1
    )
    for k in range(groups):
        at = pl.multiple_of((group_ref[0] ^ k) * share, share)
        up = [up_ref[a, :, pl.ds(at, share)] for a in range(local)]
        up += [shares[k][a] for a in range(local)]
        term = jnp.dot(
            spread, jnp.concatenate(up, axis=0), preferred_element_type=jnp.float32
        )
        term_ref[:, pl.ds(at, share)] = term[:rows] + term[rows:]
    lane = iota((1, LANES), 1)
    for j, out in enumerate(outs):
        term = term_ref[j * size : (j + 1) * size, :]
        top = jnp.max(jnp.abs(term), axis=1, keepdims=True)
        exponent = jnp.ceil(jnp.log2(jnp.maximum(top, 1e-30)) + 1e-3)
        code = jnp.clip(jnp.round(term * jnp.exp2(15.0 - exponent)), -32767.0, 32767.0)
        code = code.astype(jnp.int32)
        biased = exponent.astype(jnp.int32) + EXPONENT_BIAS
        first = code[:, :LANES]
        marked = (first & -2) | ((biased >> jnp.minimum(lane, EXPONENT_BITS - 1)) & 1)
        first = jnp.where(lane < EXPONENT_BITS, marked, first)
        out[:, :LANES] = first.astype(jnp.int16)
        out[:, LANES:] = code[:, LANES:].astype(jnp.int16)


def planes(codes, at, size):
    code = jnp.concatenate([x[:, at : at + size] for x in codes], axis=0).astype(jnp.int32)
    high = (code >> 8).astype(jnp.float32).astype(jnp.bfloat16)
    low = (code & 255).astype(jnp.float32).astype(jnp.bfloat16)
    return high, low


def decoded(picker, plane):
    high = jnp.dot(picker, plane[0], preferred_element_type=jnp.float32)
    low = jnp.dot(picker, plane[1], preferred_element_type=jnp.float32)
    return high * 256.0 + low


def scale_of(first):
    lane = iota((1, LANES), 1)
    bits = first.astype(jnp.int32) & 1
    bits = jnp.where(lane < EXPONENT_BITS, bits << jnp.minimum(lane, EXPONENT_BITS - 1), 0)
    exponent = jnp.sum(bits.astype(jnp.float32), axis=1, keepdims=True) - EXPONENT_BIAS
    return jnp.exp2(exponent - 15.0)


def start_rows_kernel(
    buffers, pool, local, depth, me_ref, adapter_ref, mine_ref, other_ref, own_ref, partial_ref, picker_ref
):
    rows, columns = mine_ref.shape
    size = own_ref.shape[0]
    place = to_column(slot_places(adapter_ref[...], me_ref[0], pool, local, depth))
    picker = jnp.where(iota((rows, size), 1) == place, 1.0, 0.0).astype(jnp.bfloat16)
    scale = scale_of(decoded(picker, planes([own_ref], 0, LANES)))
    for at in range(0, columns, 256):
        term = decoded(picker, planes([own_ref], at, 256)) * scale
        partial_ref[:, at : at + 256] = (
            mine_ref[:, at : at + 256] + other_ref[:, at : at + 256] + term
        )
    slots = (buffers - 1) * size
    picker_ref[...] = jnp.where(iota((rows, slots), 1) == place - size, 1.0, 0.0).astype(
        jnp.bfloat16
    )


def finish_kernel(buffers, partial_ref, picker_ref, cos_ref, sin_ref, gain_ref, *refs):
    order = return_order(buffers)
    ins = [refs[order.index(j)] for j in range(1, buffers)]
    out_hbm, entry_ref, out_ref, sems = refs[-4:]
    rows, columns = partial_ref.shape
    head = cos_ref.shape[1]
    kinds = columns // head
    gain, cosine, sine, picker = gain_ref[...], cos_ref[...], sin_ref[...], picker_ref[...]
    scale = scale_of(decoded(picker, planes(ins, 0, LANES)))
    for at in range(0, columns, 2 * head):
        projected = partial_ref[:, at : at + 2 * head]
        projected = projected + decoded(picker, planes(ins, at, 2 * head)) * scale
        key, value = projected[:, :head], projected[:, head:]
        mean = jnp.mean(key * key, axis=1, keepdims=True)
        normed = key * lax.rsqrt(mean + NORM_EPS) * gain
        rotated = normed * cosine + pltpu.roll(normed, head // 2, 1) * sine
        entry_ref[pl.ds(at // head, rows, stride=kinds), :] = rotated
        entry_ref[pl.ds(at // head + 1, rows, stride=kinds), :] = value
    copies = []
    part = rows * kinds // sems.shape[0]
    for i in range(sems.shape[0]):
        done = pl.ds(i * part, part)
        out_ref[done, :] = entry_ref[done, :].astype(jnp.bfloat16)
        copies.append(pltpu.make_async_copy(out_ref.at[done, :], out_hbm.at[done, :], sems.at[i]))
        copies[-1].start()
    for copy in copies:
        copy.wait()


def body(
    tokens,
    row_adapters,
    positions,
    key_value_weight,
    adapter_down,
    adapter_up,
    ranks,
    key_norm_gain,
):
    pool = lax.axis_size("pool")
    groups = lax.axis_size("groups")
    cores = lax.axis_size("tp")
    rows, width = tokens.shape
    local = adapter_down.shape[0]
    adapters = local * pool
    columns = key_value_weight.shape[1] // cores
    rank = adapter_down.shape[2]
    head = key_norm_gain.shape[0]
    depth = max(2, 2 * rows // adapters)
    buffers = pool // 2
    size = 2 * local * depth
    f32, bf16 = jnp.float32, jnp.bfloat16

    me = lax.axis_index("pool").astype(jnp.int32)[None]
    core = lax.axis_index("tp").astype(jnp.int32)[None]
    group = lax.axis_index("groups").astype(jnp.int32)[None]

    def exchange(x, axis, count, j):
        return lax.ppermute(x, axis, [(p, p ^ j) for p in range(count)])

    def hand_round(share):
        return [share] + [exchange(share, "groups", groups, k) for k in range(1, groups)]

    adapter_row = row_adapters.reshape(1, rows)
    down_share = width // groups
    parts = rows // 16
    down_part, *picked = pl.pallas_call(
        functools.partial(pick_kernel, pool, local, depth),
        in_specs=[SMEM] * 2 + [HBM] * 3,
        out_specs=[VMEM] * (1 + buffers),
        out_shape=[jax.ShapeDtypeStruct((local, down_share, rank), bf16)]
        + [jax.ShapeDtypeStruct((size, width), bf16)] * buffers,
        scratch_shapes=[
            pltpu.VMEM((1, rows), jnp.int32),
            pltpu.VMEM((rows, width), bf16),
            pltpu.SemaphoreType.DMA,
            pltpu.SemaphoreType.DMA((parts + 1,)),
        ],
        compiler_params=params(),
        cost_estimate=cost(2 * buffers * size * rows * width, 2 * (rows + buffers * size) * width),
        name="pick",
    )(me, group, in_hbm(adapter_row), in_hbm(tokens), in_hbm(adapter_down))
    far_down = exchange(down_part, "pool", pool, pool // 2)
    up_share = columns // groups
    ranks_now, adapter_up_now, _ = lax.optimization_barrier((ranks, adapter_up, picked))
    up_part, factor = pl.pallas_call(
        functools.partial(up_share_kernel, cores),
        in_specs=[SMEM] * 3 + [HBM],
        out_specs=[VMEM] * 2,
        out_shape=[
            jax.ShapeDtypeStruct((local, rank, up_share), bf16),
            jax.ShapeDtypeStruct((local, rank), f32),
        ],
        scratch_shapes=[
            pltpu.VMEM((local, rank, up_share), bf16),
            pltpu.SemaphoreType.DMA,
        ],
        compiler_params=params(),
        cost_estimate=cost(local * rank * up_share, 4 * local * rank * up_share),
        name="up_share",
    )(group, core, ranks_now, in_hbm(adapter_up_now))
    far_up = exchange(up_part, "pool", pool, pool // 2)

    order = far_first(buffers)
    early, late = order[:1], order[1:]
    late_rows, _ = lax.optimization_barrier(([picked[j] for j in late], up_part))
    leaving = [picked[j] for j in early] + late_rows
    arrived = [picked[0]] + [exchange(x, "pool", pool, j) for x, j in zip(leaving, order)]

    steps = 5
    theirs, mine, own_down, own_up = pl.pallas_call(
        base_kernel,
        in_specs=[SMEM] + [HBM] * 4,
        out_specs=[VMEM] * 4,
        out_shape=[jax.ShapeDtypeStruct((rows, columns), f32)] * 2
        + [
            jax.ShapeDtypeStruct(adapter_down.shape, bf16),
            jax.ShapeDtypeStruct((local, rank, columns), bf16),
        ],
        scratch_shapes=[
            pltpu.VMEM((rows, width), bf16),
            pltpu.VMEM((2, width, columns), bf16),
            pltpu.SemaphoreType.DMA((3,)),
            pltpu.SemaphoreType.DMA((2, steps)),
        ],
        compiler_params=params(),
        cost_estimate=cost(4 * rows * width * columns, 4 * width * columns),
        name="base",
    )(
        core,
        in_hbm(tokens),
        in_hbm(key_value_weight),
        in_hbm(adapter_down),
        in_hbm(adapter_up),
    )
    far_down, theirs = lax.optimization_barrier((far_down, theirs))
    far_downs = hand_round(far_down)
    far_up, _ = lax.optimization_barrier((far_up, far_down))
    far_ups = hand_round(far_up)
    half_dim = head // 2
    frequency = jnp.power(
        f32(ROPE_THETA), -jnp.arange(half_dim, dtype=f32) * (2.0 / head)
    )
    angles = positions.astype(f32)[:, None] * frequency[None, :]
    cosine, sine = jnp.cos(angles), jnp.sin(angles)
    cosine = jnp.concatenate([cosine, cosine], axis=1)
    sine = jnp.concatenate([-sine, sine], axis=1)

    far_up, arrived[1], theirs = lax.optimization_barrier((far_up, arrived[1], theirs))
    other = exchange(theirs, "tp", cores, 1)
    arrived, mine, cosine, sine = lax.optimization_barrier((arrived, mine, cosine, sine))
    slots = buffers * size
    low = pl.pallas_call(
        functools.partial(down_kernel, buffers, groups, local, depth),
        in_specs=[SMEM] + [VMEM] * (1 + buffers + groups),
        out_specs=VMEM,
        out_shape=jax.ShapeDtypeStruct((slots, rank), f32),
        compiler_params=params(),
        cost_estimate=cost(4 * local * slots * rank * width, 2 * (slots + rank) * width),
        name="down",
    )(group, own_down, *arrived, *far_downs)
    low_other = exchange(low, "tp", cores, 1)

    terms = pl.pallas_call(
        functools.partial(up_kernel, buffers, groups, local, depth),
        in_specs=[SMEM] + [VMEM] * (4 + groups),
        out_specs=[VMEM] * buffers,
        out_shape=[jax.ShapeDtypeStruct((size, columns), jnp.int16)] * buffers,
        scratch_shapes=[pltpu.VMEM((slots, columns), f32)],
        compiler_params=params(),
        cost_estimate=cost(8 * local * slots * rank * columns, 2 * slots * columns),
        name="up",
    )(group, low, low_other, factor, own_up, *far_ups)
    order = return_order(buffers)
    returned = [exchange(terms[j], "pool", pool, j) for j in order]

    partial, picker = pl.pallas_call(
        functools.partial(start_rows_kernel, buffers, pool, local, depth),
        in_specs=[SMEM] + [VMEM] * 4,
        out_specs=[VMEM] * 2,
        out_shape=[
            jax.ShapeDtypeStruct((rows, columns), f32),
            jax.ShapeDtypeStruct((rows, slots - size), bf16),
        ],
        compiler_params=params(),
        cost_estimate=cost(4 * rows * size * columns, 12 * rows * columns),
        name="start_rows",
    )(me, adapter_row, mine, other, terms[0])
    out = pl.pallas_call(
        functools.partial(finish_kernel, buffers),
        in_specs=[VMEM] * (4 + buffers),
        out_specs=HBM,
        out_shape=jax.ShapeDtypeStruct((rows * columns // head, head), bf16),
        scratch_shapes=[
            pltpu.VMEM((rows * columns // head, head), f32),
            pltpu.VMEM((rows * columns // head, head), bf16),
            pltpu.SemaphoreType.DMA((4,)),
        ],
        compiler_params=params(),
        cost_estimate=cost(4 * rows * slots * columns, 2 * slots * columns),
        name="finish",
    )(partial, picker, cosine, sine, key_norm_gain.astype(f32)[None, :], *returned)
    return out.reshape(rows, columns // (2 * head), 2, head)


def solution(mesh):
    return jax.shard_map(
        body,
        mesh=mesh,
        in_specs=(
            P(("groups", "pool"), "tp"),
            P(("groups", "pool"), None),
            P(("groups", "pool")),
            P("tp", None),
            P("pool", "tp", None),
            P("pool", None, None),
            P("pool"),
            P(),
        ),
        out_specs=P(("groups", "pool"), "tp", None, None),
        check_vma=False,
    )
```

```python
import functools

import jax
import jax.numpy as jnp
from jax import lax
from jax.experimental import pallas as pl
from jax.experimental.pallas import tpu as pltpu
from jax.sharding import PartitionSpec as P

ALPHA = 32
ROPE_THETA = 1000000.0
NORM_EPS = 1e-06
VMEM_LIMIT = 48 * 1024 * 1024
LANES = 128
EXPONENT_BITS = 8
EXPONENT_BIAS = 128

VMEM = pl.BlockSpec(memory_space=pltpu.VMEM)
HBM = pl.BlockSpec(memory_space=pltpu.HBM)
SMEM = pl.BlockSpec(memory_space=pltpu.SMEM)


def params(**kw):
    return pltpu.CompilerParams(vmem_limit_bytes=VMEM_LIMIT, **kw)


def cost(flops, bytes_accessed):
    return pl.CostEstimate(flops=flops, bytes_accessed=bytes_accessed, transcendentals=0)


def in_hbm(x):
    return pltpu.with_memory_space_constraint(x, pltpu.HBM)


def iota(shape, dim):
    return lax.broadcasted_iota(jnp.int32, shape, dim)


def to_column(row):
    n = row.shape[1]
    return jnp.sum(
        jnp.where(iota((n, n), 0) == iota((n, n), 1), row, 0), axis=1, keepdims=True
    )


def slot_places(row, me, pool, local, depth):
    n = row.shape[1]
    column = to_column(row)
    earlier = (column == row) & (iota((n, n), 0) < iota((n, n), 1))
    slot = jnp.sum(jnp.where(earlier, 1, 0), axis=0, keepdims=True)
    holder = row // local
    apart = holder ^ me
    buffer, far = apart % (pool // 2), apart // (pool // 2)
    return ((buffer * 2 + far) * local + (row - holder * local)) * depth + slot


def far_first(count):
    return sorted(range(1, count), key=lambda j: (-bin(j).count("1"), -j))


def return_order(count):
    order = far_first(count)
    return order[-1:] + order[:-1]


def halves(x):
    high = x.astype(jnp.bfloat16)
    low = (x - high.astype(jnp.float32)).astype(jnp.bfloat16)
    return high, low


def up_share_kernel(cores, group_ref, core_ref, ranks_ref, up_hbm, out_ref, factor_ref, own_ref, sem):
    local, rank, share = out_ref.shape
    at = core_ref[0] * (up_hbm.shape[2] // cores) + group_ref[0] * share
    copy = pltpu.make_async_copy(
        up_hbm.at[:, :, pl.ds(pl.multiple_of(at, share), share)], own_ref, sem
    )
    copy.start()
    copy.wait()
    for a in range(local):
        used = ranks_ref[a]

        def factor(shape, dim):
            scale = jnp.float32(ALPHA) / jnp.full(shape, used, jnp.int32).astype(jnp.float32)
            return jnp.where(iota(shape, dim) < used, scale, 0.0)

        factor_ref[a : a + 1, :] = factor((1, rank), 1)
        out_ref[a] = (own_ref[a].astype(jnp.float32) * factor((rank, 1), 0)).astype(jnp.bfloat16)


def pick_kernel(
    pool, local, depth, me_ref, group_ref, adapter_hbm, tokens_hbm, down_hbm, *refs
):
    share_ref, outs = refs[0], refs[1:-4]
    adapter_ref, tokens_ref, share_sem, sems = refs[-4:]
    rows, width = tokens_ref.shape
    share = share_ref.shape[1]
    parts = sems.shape[0] - 1
    part = rows // parts
    adapter_copy = pltpu.make_async_copy(adapter_hbm, adapter_ref, sems.at[parts])
    adapter_copy.start()
    copies = [
        pltpu.make_async_copy(
            tokens_hbm.at[pl.ds(i * part, part), :],
            tokens_ref.at[pl.ds(i * part, part), :],
            sems.at[i],
        )
        for i in range(parts)
    ]
    for copy in copies:
        copy.start()
    at = pl.multiple_of(group_ref[0] * share, share)
    share_copy = pltpu.make_async_copy(down_hbm.at[:, pl.ds(at, share), :], share_ref, share_sem)
    share_copy.start()
    adapter_copy.wait()
    place = slot_places(adapter_ref[...], me_ref[0], pool, local, depth)
    size = outs[0].shape[0]
    slots = len(outs) * size
    picker = jnp.where(iota((slots, rows), 0) == place, 1.0, 0.0).astype(jnp.bfloat16)
    for copy in copies:
        copy.wait()
    step = 512
    for at in range(0, width, step):
        block = jnp.dot(
            picker, tokens_ref[:, at : at + step], preferred_element_type=jnp.float32
        )
        for j, out in enumerate(outs):
            out[:, at : at + step] = block[j * size : (j + 1) * size].astype(jnp.bfloat16)
    share_copy.wait()


def base_kernel(
    core_ref,
    tokens_hbm,
    weight_hbm,
    down_hbm,
    up_hbm,
    theirs_ref,
    mine_ref,
    down_ref,
    up_ref,
    tokens_ref,
    weight_ref,
    other_sems,
    sems,
):
    rows, columns = mine_ref.shape
    steps = sems.shape[1]
    step = tokens_ref.shape[1] // steps
    copies = []
    for half in range(2):
        start = (1 - core_ref[0] if half == 0 else core_ref[0]) * columns
        start = pl.multiple_of(start, columns)
        for k in range(steps):
            copies.append(
                pltpu.make_async_copy(
                    weight_hbm.at[pl.ds(k * step, step), pl.ds(start, columns)],
                    weight_ref.at[half, pl.ds(k * step, step), :],
                    sems.at[half, k],
                )
            )
    tokens_copy = pltpu.make_async_copy(tokens_hbm, tokens_ref, other_sems.at[0])
    own = pl.multiple_of(core_ref[0] * columns, columns)
    factor_copies = [
        pltpu.make_async_copy(down_hbm, down_ref, other_sems.at[1]),
        pltpu.make_async_copy(up_hbm.at[:, :, pl.ds(own, columns)], up_ref, other_sems.at[2]),
    ]
    for copy in [tokens_copy] + copies + factor_copies:
        copy.start()
    tokens_copy.wait()
    for half, out in enumerate((theirs_ref, mine_ref)):
        for k in range(steps):
            copies[half * steps + k].wait()
            term = jnp.dot(
                tokens_ref[:, k * step : (k + 1) * step],
                weight_ref[half, k * step : (k + 1) * step, :],
                preferred_element_type=jnp.float32,
            )
            if k == 0:
                out[...] = term
            else:
                out[...] += term
    for copy in factor_copies:
        copy.wait()


def down_kernel(buffers, groups, local, depth, group_ref, down_ref, *refs):
    order = [0] + far_first(buffers)
    ins = [refs[order.index(j)] for j in range(buffers)]
    shares, out = refs[buffers : buffers + groups], refs[-1]
    rank = out.shape[1]
    share = shares[0].shape[1]
    total = None
    for k in range(groups):
        at = pl.multiple_of((group_ref[0] ^ k) * share, share)
        rows = jnp.concatenate([x[:, pl.ds(at, share)] for x in ins], axis=0)
        factors = [down_ref[a, pl.ds(at, share), :] for a in range(local)]
        factors += [shares[k][a] for a in range(local)]
        term = jnp.dot(
            rows, jnp.concatenate(factors, axis=1), preferred_element_type=jnp.float32
        )
        total = term if total is None else total + term
    which = (iota((total.shape[0], 1), 0) // depth) % (2 * local)
    low = total[:, :rank]
    for i in range(1, 2 * local):
        low = jnp.where(which == i, total[:, i * rank : (i + 1) * rank], low)
    out[...] = low


def up_kernel(
    buffers, groups, local, depth, group_ref, low_ref, other_ref, factor_ref, up_ref, *refs
):
    shares, outs, term_ref = refs[:groups], refs[groups : groups + buffers], refs[-1]
    rows, rank = low_ref.shape
    size = rows // buffers
    columns = up_ref.shape[2]
    share = columns // groups
    which = (iota((rows, 1), 0) // depth) % (2 * local)
    low = low_ref[...] + other_ref[...]
    for a in range(local):
        low = jnp.where(which == a, low * factor_ref[a : a + 1, :], low)
    both = jnp.concatenate(halves(low), axis=0)
    which = jnp.concatenate([which, which], axis=0)
    spread = jnp.concatenate(
        [jnp.where(which == i, both, jnp.zeros_like(both)) for i in range(2 * local)], axis=1
    )
    for k in range(groups):
        at = pl.multiple_of((group_ref[0] ^ k) * share, share)
        up = [up_ref[a, :, pl.ds(at, share)] for a in range(local)]
        up += [shares[k][a] for a in range(local)]
        term = jnp.dot(
            spread, jnp.concatenate(up, axis=0), preferred_element_type=jnp.float32
        )
        term_ref[:, pl.ds(at, share)] = term[:rows] + term[rows:]
    lane = iota((1, LANES), 1)
    for j, out in enumerate(outs):
        term = term_ref[j * size : (j + 1) * size, :]
        top = jnp.max(jnp.abs(term), axis=1, keepdims=True)
        exponent = jnp.ceil(jnp.log2(jnp.maximum(top, 1e-30)) + 1e-3)
        code = jnp.clip(jnp.round(term * jnp.exp2(15.0 - exponent)), -32767.0, 32767.0)
        code = code.astype(jnp.int32)
        biased = exponent.astype(jnp.int32) + EXPONENT_BIAS
        first = code[:, :LANES]
        marked = (first & -2) | ((biased >> jnp.minimum(lane, EXPONENT_BITS - 1)) & 1)
        first = jnp.where(lane < EXPONENT_BITS, marked, first)
        out[:, :LANES] = first.astype(jnp.int16)
        out[:, LANES:] = code[:, LANES:].astype(jnp.int16)


def planes(codes, at, size):
    code = jnp.concatenate([x[:, at : at + size] for x in codes], axis=0).astype(jnp.int32)
    high = (code >> 8).astype(jnp.float32).astype(jnp.bfloat16)
    low = (code & 255).astype(jnp.float32).astype(jnp.bfloat16)
    return high, low


def decoded(picker, plane):
    high = jnp.dot(picker, plane[0], preferred_element_type=jnp.float32)
    low = jnp.dot(picker, plane[1], preferred_element_type=jnp.float32)
    return high * 256.0 + low


def scale_of(first):
    lane = iota((1, LANES), 1)
    bits = first.astype(jnp.int32) & 1
    bits = jnp.where(lane < EXPONENT_BITS, bits << jnp.minimum(lane, EXPONENT_BITS - 1), 0)
    exponent = jnp.sum(bits.astype(jnp.float32), axis=1, keepdims=True) - EXPONENT_BIAS
    return jnp.exp2(exponent - 15.0)


def start_rows_kernel(
    buffers, pool, local, depth, me_ref, adapter_ref, mine_ref, other_ref, own_ref, partial_ref, picker_ref
):
    rows, columns = mine_ref.shape
    size = own_ref.shape[0]
    place = to_column(slot_places(adapter_ref[...], me_ref[0], pool, local, depth))
    picker = jnp.where(iota((rows, size), 1) == place, 1.0, 0.0).astype(jnp.bfloat16)
    scale = scale_of(decoded(picker, planes([own_ref], 0, LANES)))
    for at in range(0, columns, 256):
        term = decoded(picker, planes([own_ref], at, 256)) * scale
        partial_ref[:, at : at + 256] = (
            mine_ref[:, at : at + 256] + other_ref[:, at : at + 256] + term
        )
    slots = (buffers - 1) * size
    picker_ref[...] = jnp.where(iota((rows, slots), 1) == place - size, 1.0, 0.0).astype(
        jnp.bfloat16
    )


def finish_kernel(buffers, partial_ref, picker_ref, cos_ref, sin_ref, gain_ref, *refs):
    order = return_order(buffers)
    ins = [refs[order.index(j)] for j in range(1, buffers)]
    out_hbm, entry_ref, out_ref, sems = refs[-4:]
    rows, columns = partial_ref.shape
    head = cos_ref.shape[1]
    kinds = columns // head
    gain, cosine, sine, picker = gain_ref[...], cos_ref[...], sin_ref[...], picker_ref[...]
    scale = scale_of(decoded(picker, planes(ins, 0, LANES)))
    for at in range(0, columns, 2 * head):
        projected = partial_ref[:, at : at + 2 * head]
        projected = projected + decoded(picker, planes(ins, at, 2 * head)) * scale
        key, value = projected[:, :head], projected[:, head:]
        mean = jnp.mean(key * key, axis=1, keepdims=True)
        normed = key * lax.rsqrt(mean + NORM_EPS) * gain
        rotated = normed * cosine + pltpu.roll(normed, head // 2, 1) * sine
        entry_ref[pl.ds(at // head, rows, stride=kinds), :] = rotated
        entry_ref[pl.ds(at // head + 1, rows, stride=kinds), :] = value
    copies = []
    part = rows * kinds // sems.shape[0]
    for i in range(sems.shape[0]):
        done = pl.ds(i * part, part)
        out_ref[done, :] = entry_ref[done, :].astype(jnp.bfloat16)
        copies.append(pltpu.make_async_copy(out_ref.at[done, :], out_hbm.at[done, :], sems.at[i]))
        copies[-1].start()
    for copy in copies:
        copy.wait()


def body(
    tokens,
    row_adapters,
    positions,
    key_value_weight,
    adapter_down,
    adapter_up,
    ranks,
    key_norm_gain,
):
    pool = lax.axis_size("pool")
    groups = lax.axis_size("groups")
    cores = lax.axis_size("tp")
    rows, width = tokens.shape
    local = adapter_down.shape[0]
    adapters = local * pool
    columns = key_value_weight.shape[1] // cores
    rank = adapter_down.shape[2]
    head = key_norm_gain.shape[0]
    depth = max(2, 2 * rows // adapters)
    buffers = pool // 2
    size = 2 * local * depth
    f32, bf16 = jnp.float32, jnp.bfloat16

    me = lax.axis_index("pool").astype(jnp.int32)[None]
    core = lax.axis_index("tp").astype(jnp.int32)[None]
    group = lax.axis_index("groups").astype(jnp.int32)[None]

    def exchange(x, axis, count, j):
        return lax.ppermute(x, axis, [(p, p ^ j) for p in range(count)])

    def hand_round(share):
        return [share] + [exchange(share, "groups", groups, k) for k in range(1, groups)]

    adapter_row = row_adapters.reshape(1, rows)
    down_share = width // groups
    parts = rows // 16
    down_part, *picked = pl.pallas_call(
        functools.partial(pick_kernel, pool, local, depth),
        in_specs=[SMEM] * 2 + [HBM] * 3,
        out_specs=[VMEM] * (1 + buffers),
        out_shape=[jax.ShapeDtypeStruct((local, down_share, rank), bf16)]
        + [jax.ShapeDtypeStruct((size, width), bf16)] * buffers,
        scratch_shapes=[
            pltpu.VMEM((1, rows), jnp.int32),
            pltpu.VMEM((rows, width), bf16),
            pltpu.SemaphoreType.DMA,
            pltpu.SemaphoreType.DMA((parts + 1,)),
        ],
        compiler_params=params(),
        cost_estimate=cost(2 * buffers * size * rows * width, 2 * (rows + buffers * size) * width),
        name="pick",
    )(me, group, in_hbm(adapter_row), in_hbm(tokens), in_hbm(adapter_down))
    far_down = exchange(down_part, "pool", pool, pool // 2)
    up_share = columns // groups
    ranks_now, adapter_up_now, _ = lax.optimization_barrier((ranks, adapter_up, picked))
    up_part, factor = pl.pallas_call(
        functools.partial(up_share_kernel, cores),
        in_specs=[SMEM] * 3 + [HBM],
        out_specs=[VMEM] * 2,
        out_shape=[
            jax.ShapeDtypeStruct((local, rank, up_share), bf16),
            jax.ShapeDtypeStruct((local, rank), f32),
        ],
        scratch_shapes=[
            pltpu.VMEM((local, rank, up_share), bf16),
            pltpu.SemaphoreType.DMA,
        ],
        compiler_params=params(),
        cost_estimate=cost(local * rank * up_share, 4 * local * rank * up_share),
        name="up_share",
    )(group, core, ranks_now, in_hbm(adapter_up_now))
    far_up = exchange(up_part, "pool", pool, pool // 2)

    order = far_first(buffers)
    early, late = order[:1], order[1:]
    late_rows, _ = lax.optimization_barrier(([picked[j] for j in late], up_part))
    leaving = [picked[j] for j in early] + late_rows
    arrived = [picked[0]] + [exchange(x, "pool", pool, j) for x, j in zip(leaving, order)]

    steps = 5
    theirs, mine, own_down, own_up = pl.pallas_call(
        base_kernel,
        in_specs=[SMEM] + [HBM] * 4,
        out_specs=[VMEM] * 4,
        out_shape=[jax.ShapeDtypeStruct((rows, columns), f32)] * 2
        + [
            jax.ShapeDtypeStruct(adapter_down.shape, bf16),
            jax.ShapeDtypeStruct((local, rank, columns), bf16),
        ],
        scratch_shapes=[
            pltpu.VMEM((rows, width), bf16),
            pltpu.VMEM((2, width, columns), bf16),
            pltpu.SemaphoreType.DMA((3,)),
            pltpu.SemaphoreType.DMA((2, steps)),
        ],
        compiler_params=params(),
        cost_estimate=cost(4 * rows * width * columns, 4 * width * columns),
        name="base",
    )(
        core,
        in_hbm(tokens),
        in_hbm(key_value_weight),
        in_hbm(adapter_down),
        in_hbm(adapter_up),
    )
    far_down, theirs = lax.optimization_barrier((far_down, theirs))
    far_downs = hand_round(far_down)
    far_up, arrived[-1] = lax.optimization_barrier((far_up, arrived[-1]))
    far_ups = hand_round(far_up)
    half_dim = head // 2
    frequency = jnp.power(
        f32(ROPE_THETA), -jnp.arange(half_dim, dtype=f32) * (2.0 / head)
    )
    angles = positions.astype(f32)[:, None] * frequency[None, :]
    cosine, sine = jnp.cos(angles), jnp.sin(angles)
    cosine = jnp.concatenate([cosine, cosine], axis=1)
    sine = jnp.concatenate([-sine, sine], axis=1)

    far_up, arrived[-1], theirs = lax.optimization_barrier((far_up, arrived[-1], theirs))
    other = exchange(theirs, "tp", cores, 1)
    arrived, mine, cosine, sine = lax.optimization_barrier((arrived, mine, cosine, sine))
    slots = buffers * size
    low = pl.pallas_call(
        functools.partial(down_kernel, buffers, groups, local, depth),
        in_specs=[SMEM] + [VMEM] * (1 + buffers + groups),
        out_specs=VMEM,
        out_shape=jax.ShapeDtypeStruct((slots, rank), f32),
        compiler_params=params(),
        cost_estimate=cost(4 * local * slots * rank * width, 2 * (slots + rank) * width),
        name="down",
    )(group, own_down, *arrived, *far_downs)
    low_other = exchange(low, "tp", cores, 1)

    terms = pl.pallas_call(
        functools.partial(up_kernel, buffers, groups, local, depth),
        in_specs=[SMEM] + [VMEM] * (4 + groups),
        out_specs=[VMEM] * buffers,
        out_shape=[jax.ShapeDtypeStruct((size, columns), jnp.int16)] * buffers,
        scratch_shapes=[pltpu.VMEM((slots, columns), f32)],
        compiler_params=params(),
        cost_estimate=cost(8 * local * slots * rank * columns, 2 * slots * columns),
        name="up",
    )(group, low, low_other, factor, own_up, *far_ups)
    order = return_order(buffers)
    returned = [exchange(terms[j], "pool", pool, j) for j in order]

    partial, picker = pl.pallas_call(
        functools.partial(start_rows_kernel, buffers, pool, local, depth),
        in_specs=[SMEM] + [VMEM] * 4,
        out_specs=[VMEM] * 2,
        out_shape=[
            jax.ShapeDtypeStruct((rows, columns), f32),
            jax.ShapeDtypeStruct((rows, slots - size), bf16),
        ],
        compiler_params=params(),
        cost_estimate=cost(4 * rows * size * columns, 12 * rows * columns),
        name="start_rows",
    )(me, adapter_row, mine, other, terms[0])
    out = pl.pallas_call(
        functools.partial(finish_kernel, buffers),
        in_specs=[VMEM] * (4 + buffers),
        out_specs=HBM,
        out_shape=jax.ShapeDtypeStruct((rows * columns // head, head), bf16),
        scratch_shapes=[
            pltpu.VMEM((rows * columns // head, head), f32),
            pltpu.VMEM((rows * columns // head, head), bf16),
            pltpu.SemaphoreType.DMA((4,)),
        ],
        compiler_params=params(),
        cost_estimate=cost(4 * rows * slots * columns, 2 * slots * columns),
        name="finish",
    )(partial, picker, cosine, sine, key_norm_gain.astype(f32)[None, :], *returned)
    return out.reshape(rows, columns // (2 * head), 2, head)


def solution(mesh):
    return jax.shard_map(
        body,
        mesh=mesh,
        in_specs=(
            P(("groups", "pool"), "tp"),
            P(("groups", "pool"), None),
            P(("groups", "pool")),
            P("tp", None),
            P("pool", "tp", None),
            P("pool", None, None),
            P("pool"),
            P(),
        ),
        out_specs=P(("groups", "pool"), "tp", None, None),
        check_vma=False,
    )
```

```python
import functools

import jax
import jax.numpy as jnp
from jax import lax
from jax.experimental import pallas as pl
from jax.experimental.pallas import tpu as pltpu
from jax.sharding import PartitionSpec as P

ALPHA = 32
ROPE_THETA = 1000000.0
NORM_EPS = 1e-06
VMEM_LIMIT = 48 * 1024 * 1024
LANES = 128
EXPONENT_BITS = 8
EXPONENT_BIAS = 128

VMEM = pl.BlockSpec(memory_space=pltpu.VMEM)
HBM = pl.BlockSpec(memory_space=pltpu.HBM)
SMEM = pl.BlockSpec(memory_space=pltpu.SMEM)


def params(**kw):
    return pltpu.CompilerParams(vmem_limit_bytes=VMEM_LIMIT, **kw)


def cost(flops, bytes_accessed):
    return pl.CostEstimate(flops=flops, bytes_accessed=bytes_accessed, transcendentals=0)


def in_hbm(x):
    return pltpu.with_memory_space_constraint(x, pltpu.HBM)


def iota(shape, dim):
    return lax.broadcasted_iota(jnp.int32, shape, dim)


def to_column(row):
    n = row.shape[1]
    return jnp.sum(
        jnp.where(iota((n, n), 0) == iota((n, n), 1), row, 0), axis=1, keepdims=True
    )


def slot_places(row, me, pool, local, depth):
    n = row.shape[1]
    column = to_column(row)
    earlier = (column == row) & (iota((n, n), 0) < iota((n, n), 1))
    slot = jnp.sum(jnp.where(earlier, 1, 0), axis=0, keepdims=True)
    holder = row // local
    apart = holder ^ me
    buffer, far = apart % (pool // 2), apart // (pool // 2)
    return ((buffer * 2 + far) * local + (row - holder * local)) * depth + slot


def far_first(count):
    return sorted(range(1, count), key=lambda j: (-bin(j).count("1"), -j))


def return_order(count):
    order = far_first(count)
    return order[-1:] + order[:-1]


def halves(x):
    high = x.astype(jnp.bfloat16)
    low = (x - high.astype(jnp.float32)).astype(jnp.bfloat16)
    return high, low


def up_share_kernel(cores, group_ref, core_ref, ranks_ref, up_hbm, out_ref, factor_ref, own_ref, sem):
    local, rank, share = out_ref.shape
    at = core_ref[0] * (up_hbm.shape[2] // cores) + group_ref[0] * share
    copy = pltpu.make_async_copy(
        up_hbm.at[:, :, pl.ds(pl.multiple_of(at, share), share)], own_ref, sem
    )
    copy.start()
    copy.wait()
    for a in range(local):
        used = ranks_ref[a]

        def factor(shape, dim):
            scale = jnp.float32(ALPHA) / jnp.full(shape, used, jnp.int32).astype(jnp.float32)
            return jnp.where(iota(shape, dim) < used, scale, 0.0)

        factor_ref[a : a + 1, :] = factor((1, rank), 1)
        out_ref[a] = (own_ref[a].astype(jnp.float32) * factor((rank, 1), 0)).astype(jnp.bfloat16)


def down_share_kernel(group_ref, down_hbm, out_ref, sem):
    share = out_ref.shape[1]
    at = pl.multiple_of(group_ref[0] * share, share)
    copy = pltpu.make_async_copy(down_hbm.at[:, pl.ds(at, share), :], out_ref, sem)
    copy.start()
    copy.wait()


def pick_kernel(
    pool, local, depth, me_ref, adapter_hbm, tokens_hbm, *refs
):
    outs, (adapter_ref, tokens_ref, sems) = refs[:-3], refs[-3:]
    rows, width = tokens_ref.shape
    parts = sems.shape[0] - 1
    part = rows // parts
    adapter_copy = pltpu.make_async_copy(adapter_hbm, adapter_ref, sems.at[parts])
    adapter_copy.start()
    copies = [
        pltpu.make_async_copy(
            tokens_hbm.at[pl.ds(i * part, part), :],
            tokens_ref.at[pl.ds(i * part, part), :],
            sems.at[i],
        )
        for i in range(parts)
    ]
    for copy in copies:
        copy.start()
    adapter_copy.wait()
    place = slot_places(adapter_ref[...], me_ref[0], pool, local, depth)
    size = outs[0].shape[0]
    slots = len(outs) * size
    picker = jnp.where(iota((slots, rows), 0) == place, 1.0, 0.0).astype(jnp.bfloat16)
    for copy in copies:
        copy.wait()
    step = 512
    for at in range(0, width, step):
        block = jnp.dot(
            picker, tokens_ref[:, at : at + step], preferred_element_type=jnp.float32
        )
        for j, out in enumerate(outs):
            out[:, at : at + step] = block[j * size : (j + 1) * size].astype(jnp.bfloat16)


def base_kernel(
    core_ref,
    tokens_hbm,
    weight_hbm,
    down_hbm,
    up_hbm,
    theirs_ref,
    mine_ref,
    down_ref,
    up_ref,
    tokens_ref,
    weight_ref,
    other_sems,
    sems,
):
    rows, columns = mine_ref.shape
    steps = sems.shape[1]
    step = tokens_ref.shape[1] // steps
    copies = []
    for half in range(2):
        start = (1 - core_ref[0] if half == 0 else core_ref[0]) * columns
        start = pl.multiple_of(start, columns)
        for k in range(steps):
            copies.append(
                pltpu.make_async_copy(
                    weight_hbm.at[pl.ds(k * step, step), pl.ds(start, columns)],
                    weight_ref.at[half, pl.ds(k * step, step), :],
                    sems.at[half, k],
                )
            )
    tokens_copy = pltpu.make_async_copy(tokens_hbm, tokens_ref, other_sems.at[0])
    own = pl.multiple_of(core_ref[0] * columns, columns)
    factor_copies = [
        pltpu.make_async_copy(down_hbm, down_ref, other_sems.at[1]),
        pltpu.make_async_copy(up_hbm.at[:, :, pl.ds(own, columns)], up_ref, other_sems.at[2]),
    ]
    for copy in [tokens_copy] + copies + factor_copies:
        copy.start()
    tokens_copy.wait()
    for half, out in enumerate((theirs_ref, mine_ref)):
        for k in range(steps):
            copies[half * steps + k].wait()
            term = jnp.dot(
                tokens_ref[:, k * step : (k + 1) * step],
                weight_ref[half, k * step : (k + 1) * step, :],
                preferred_element_type=jnp.float32,
            )
            if k == 0:
                out[...] = term
            else:
                out[...] += term
    for copy in factor_copies:
        copy.wait()


def down_kernel(buffers, groups, local, depth, group_ref, down_ref, *refs):
    order = [0] + far_first(buffers)
    ins = [refs[order.index(j)] for j in range(buffers)]
    shares, out = refs[buffers : buffers + groups], refs[-1]
    rank = out.shape[1]
    share = shares[0].shape[1]
    total = None
    for k in range(groups):
        at = pl.multiple_of((group_ref[0] ^ k) * share, share)
        rows = jnp.concatenate([x[:, pl.ds(at, share)] for x in ins], axis=0)
        factors = [down_ref[a, pl.ds(at, share), :] for a in range(local)]
        factors += [shares[k][a] for a in range(local)]
        term = jnp.dot(
            rows, jnp.concatenate(factors, axis=1), preferred_element_type=jnp.float32
        )
        total = term if total is None else total + term
    which = (iota((total.shape[0], 1), 0) // depth) % (2 * local)
    low = total[:, :rank]
    for i in range(1, 2 * local):
        low = jnp.where(which == i, total[:, i * rank : (i + 1) * rank], low)
    out[...] = low


def up_kernel(
    buffers, groups, local, depth, group_ref, low_ref, other_ref, factor_ref, up_ref, *refs
):
    shares, outs, term_ref = refs[:groups], refs[groups : groups + buffers], refs[-1]
    rows, rank = low_ref.shape
    size = rows // buffers
    columns = up_ref.shape[2]
    share = columns // groups
    which = (iota((rows, 1), 0) // depth) % (2 * local)
    low = low_ref[...] + other_ref[...]
    for a in range(local):
        low = jnp.where(which == a, low * factor_ref[a : a + 1, :], low)
    both = jnp.concatenate(halves(low), axis=0)
    which = jnp.concatenate([which, which], axis=0)
    spread = jnp.concatenate(
        [jnp.where(which == i, both, jnp.zeros_like(both)) for i in range(2 * local)], axis=1
    )
    for k in range(groups):
        at = pl.multiple_of((group_ref[0] ^ k) * share, share)
        up = [up_ref[a, :, pl.ds(at, share)] for a in range(local)]
        up += [shares[k][a] for a in range(local)]
        term = jnp.dot(
            spread, jnp.concatenate(up, axis=0), preferred_element_type=jnp.float32
        )
        term_ref[:, pl.ds(at, share)] = term[:rows] + term[rows:]
    lane = iota((1, LANES), 1)
    for j, out in enumerate(outs):
        term = term_ref[j * size : (j + 1) * size, :]
        top = jnp.max(jnp.abs(term), axis=1, keepdims=True)
        exponent = jnp.ceil(jnp.log2(jnp.maximum(top, 1e-30)) + 1e-3)
        code = jnp.clip(jnp.round(term * jnp.exp2(15.0 - exponent)), -32767.0, 32767.0)
        code = code.astype(jnp.int32)
        biased = exponent.astype(jnp.int32) + EXPONENT_BIAS
        first = code[:, :LANES]
        marked = (first & -2) | ((biased >> jnp.minimum(lane, EXPONENT_BITS - 1)) & 1)
        first = jnp.where(lane < EXPONENT_BITS, marked, first)
        out[:, :LANES] = first.astype(jnp.int16)
        out[:, LANES:] = code[:, LANES:].astype(jnp.int16)


def planes(codes, at, size):
    code = jnp.concatenate([x[:, at : at + size] for x in codes], axis=0).astype(jnp.int32)
    high = (code >> 8).astype(jnp.float32).astype(jnp.bfloat16)
    low = (code & 255).astype(jnp.float32).astype(jnp.bfloat16)
    return high, low


def decoded(picker, plane):
    high = jnp.dot(picker, plane[0], preferred_element_type=jnp.float32)
    low = jnp.dot(picker, plane[1], preferred_element_type=jnp.float32)
    return high * 256.0 + low


def scale_of(first):
    lane = iota((1, LANES), 1)
    bits = first.astype(jnp.int32) & 1
    bits = jnp.where(lane < EXPONENT_BITS, bits << jnp.minimum(lane, EXPONENT_BITS - 1), 0)
    exponent = jnp.sum(bits.astype(jnp.float32), axis=1, keepdims=True) - EXPONENT_BIAS
    return jnp.exp2(exponent - 15.0)


def start_rows_kernel(
    buffers, pool, local, depth, me_ref, adapter_ref, mine_ref, other_ref, own_ref, partial_ref, picker_ref
):
    rows, columns = mine_ref.shape
    size = own_ref.shape[0]
    place = to_column(slot_places(adapter_ref[...], me_ref[0], pool, local, depth))
    picker = jnp.where(iota((rows, size), 1) == place, 1.0, 0.0).astype(jnp.bfloat16)
    scale = scale_of(decoded(picker, planes([own_ref], 0, LANES)))
    for at in range(0, columns, 256):
        term = decoded(picker, planes([own_ref], at, 256)) * scale
        partial_ref[:, at : at + 256] = (
            mine_ref[:, at : at + 256] + other_ref[:, at : at + 256] + term
        )
    slots = (buffers - 1) * size
    picker_ref[...] = jnp.where(iota((rows, slots), 1) == place - size, 1.0, 0.0).astype(
        jnp.bfloat16
    )


def finish_kernel(buffers, partial_ref, picker_ref, cos_ref, sin_ref, gain_ref, *refs):
    order = return_order(buffers)
    ins = [refs[order.index(j)] for j in range(1, buffers)]
    out_hbm, entry_ref, out_ref, sems = refs[-4:]
    rows, columns = partial_ref.shape
    head = cos_ref.shape[1]
    kinds = columns // head
    gain, cosine, sine, picker = gain_ref[...], cos_ref[...], sin_ref[...], picker_ref[...]
    scale = scale_of(decoded(picker, planes(ins, 0, LANES)))
    for at in range(0, columns, 2 * head):
        projected = partial_ref[:, at : at + 2 * head]
        projected = projected + decoded(picker, planes(ins, at, 2 * head)) * scale
        key, value = projected[:, :head], projected[:, head:]
        mean = jnp.mean(key * key, axis=1, keepdims=True)
        normed = key * lax.rsqrt(mean + NORM_EPS) * gain
        rotated = normed * cosine + pltpu.roll(normed, head // 2, 1) * sine
        entry_ref[pl.ds(at // head, rows, stride=kinds), :] = rotated
        entry_ref[pl.ds(at // head + 1, rows, stride=kinds), :] = value
    copies = []
    part = rows * kinds // sems.shape[0]
    for i in range(sems.shape[0]):
        done = pl.ds(i * part, part)
        out_ref[done, :] = entry_ref[done, :].astype(jnp.bfloat16)
        copies.append(pltpu.make_async_copy(out_ref.at[done, :], out_hbm.at[done, :], sems.at[i]))
        copies[-1].start()
    for copy in copies:
        copy.wait()


def body(
    tokens,
    row_adapters,
    positions,
    key_value_weight,
    adapter_down,
    adapter_up,
    ranks,
    key_norm_gain,
):
    pool = lax.axis_size("pool")
    groups = lax.axis_size("groups")
    cores = lax.axis_size("tp")
    rows, width = tokens.shape
    local = adapter_down.shape[0]
    adapters = local * pool
    columns = key_value_weight.shape[1] // cores
    rank = adapter_down.shape[2]
    head = key_norm_gain.shape[0]
    depth = max(2, 2 * rows // adapters)
    buffers = pool // 2
    size = 2 * local * depth
    f32, bf16 = jnp.float32, jnp.bfloat16

    me = lax.axis_index("pool").astype(jnp.int32)[None]
    core = lax.axis_index("tp").astype(jnp.int32)[None]
    group = lax.axis_index("groups").astype(jnp.int32)[None]

    def exchange(x, axis, count, j):
        return lax.ppermute(x, axis, [(p, p ^ j) for p in range(count)])

    def hand_round(share):
        return [share] + [exchange(share, "groups", groups, k) for k in range(1, groups)]

    adapter_row = row_adapters.reshape(1, rows)
    down_share = width // groups
    parts = rows // 16
    down_part = pl.pallas_call(
        down_share_kernel,
        in_specs=[SMEM, HBM],
        out_specs=VMEM,
        out_shape=jax.ShapeDtypeStruct((local, down_share, rank), bf16),
        scratch_shapes=[pltpu.SemaphoreType.DMA],
        compiler_params=params(),
        cost_estimate=cost(0, 4 * local * rank * down_share),
        name="down_share",
    )(group, in_hbm(adapter_down))
    tokens_now, _ = lax.optimization_barrier((tokens, down_part))
    picked = pl.pallas_call(
        functools.partial(pick_kernel, pool, local, depth),
        in_specs=[SMEM] + [HBM] * 2,
        out_specs=[VMEM] * buffers,
        out_shape=[jax.ShapeDtypeStruct((size, width), bf16)] * buffers,
        scratch_shapes=[
            pltpu.VMEM((1, rows), jnp.int32),
            pltpu.VMEM((rows, width), bf16),
            pltpu.SemaphoreType.DMA((parts + 1,)),
        ],
        compiler_params=params(),
        cost_estimate=cost(2 * buffers * size * rows * width, 2 * (rows + buffers * size) * width),
        name="pick",
    )(me, in_hbm(adapter_row), in_hbm(tokens_now))
    far_down = exchange(down_part, "pool", pool, pool // 2)
    up_share = columns // groups
    ranks_now, adapter_up_now, _ = lax.optimization_barrier((ranks, adapter_up, picked))
    up_part, factor = pl.pallas_call(
        functools.partial(up_share_kernel, cores),
        in_specs=[SMEM] * 3 + [HBM],
        out_specs=[VMEM] * 2,
        out_shape=[
            jax.ShapeDtypeStruct((local, rank, up_share), bf16),
            jax.ShapeDtypeStruct((local, rank), f32),
        ],
        scratch_shapes=[
            pltpu.VMEM((local, rank, up_share), bf16),
            pltpu.SemaphoreType.DMA,
        ],
        compiler_params=params(),
        cost_estimate=cost(local * rank * up_share, 4 * local * rank * up_share),
        name="up_share",
    )(group, core, ranks_now, in_hbm(adapter_up_now))
    far_up = exchange(up_part, "pool", pool, pool // 2)

    order = far_first(buffers)
    early, late = order[:1], order[1:]
    late_rows, _ = lax.optimization_barrier(([picked[j] for j in late], up_part))
    leaving = [picked[j] for j in early] + late_rows
    arrived = [picked[0]] + [exchange(x, "pool", pool, j) for x, j in zip(leaving, order)]

    steps = 5
    theirs, mine, own_down, own_up = pl.pallas_call(
        base_kernel,
        in_specs=[SMEM] + [HBM] * 4,
        out_specs=[VMEM] * 4,
        out_shape=[jax.ShapeDtypeStruct((rows, columns), f32)] * 2
        + [
            jax.ShapeDtypeStruct(adapter_down.shape, bf16),
            jax.ShapeDtypeStruct((local, rank, columns), bf16),
        ],
        scratch_shapes=[
            pltpu.VMEM((rows, width), bf16),
            pltpu.VMEM((2, width, columns), bf16),
            pltpu.SemaphoreType.DMA((3,)),
            pltpu.SemaphoreType.DMA((2, steps)),
        ],
        compiler_params=params(),
        cost_estimate=cost(4 * rows * width * columns, 4 * width * columns),
        name="base",
    )(
        core,
        in_hbm(tokens),
        in_hbm(key_value_weight),
        in_hbm(adapter_down),
        in_hbm(adapter_up),
    )
    far_down, theirs = lax.optimization_barrier((far_down, theirs))
    far_downs = hand_round(far_down)
    far_up, _ = lax.optimization_barrier((far_up, far_down))
    far_ups = hand_round(far_up)
    half_dim = head // 2
    frequency = jnp.power(
        f32(ROPE_THETA), -jnp.arange(half_dim, dtype=f32) * (2.0 / head)
    )
    angles = positions.astype(f32)[:, None] * frequency[None, :]
    cosine, sine = jnp.cos(angles), jnp.sin(angles)
    cosine = jnp.concatenate([cosine, cosine], axis=1)
    sine = jnp.concatenate([-sine, sine], axis=1)

    far_up, arrived[1], theirs = lax.optimization_barrier((far_up, arrived[1], theirs))
    other = exchange(theirs, "tp", cores, 1)
    arrived, mine, cosine, sine = lax.optimization_barrier((arrived, mine, cosine, sine))
    slots = buffers * size
    low = pl.pallas_call(
        functools.partial(down_kernel, buffers, groups, local, depth),
        in_specs=[SMEM] + [VMEM] * (1 + buffers + groups),
        out_specs=VMEM,
        out_shape=jax.ShapeDtypeStruct((slots, rank), f32),
        compiler_params=params(),
        cost_estimate=cost(4 * local * slots * rank * width, 2 * (slots + rank) * width),
        name="down",
    )(group, own_down, *arrived, *far_downs)
    low_other = exchange(low, "tp", cores, 1)

    terms = pl.pallas_call(
        functools.partial(up_kernel, buffers, groups, local, depth),
        in_specs=[SMEM] + [VMEM] * (4 + groups),
        out_specs=[VMEM] * buffers,
        out_shape=[jax.ShapeDtypeStruct((size, columns), jnp.int16)] * buffers,
        scratch_shapes=[pltpu.VMEM((slots, columns), f32)],
        compiler_params=params(),
        cost_estimate=cost(8 * local * slots * rank * columns, 2 * slots * columns),
        name="up",
    )(group, low, low_other, factor, own_up, *far_ups)
    order = return_order(buffers)
    returned = [exchange(terms[j], "pool", pool, j) for j in order]

    partial, picker = pl.pallas_call(
        functools.partial(start_rows_kernel, buffers, pool, local, depth),
        in_specs=[SMEM] + [VMEM] * 4,
        out_specs=[VMEM] * 2,
        out_shape=[
            jax.ShapeDtypeStruct((rows, columns), f32),
            jax.ShapeDtypeStruct((rows, slots - size), bf16),
        ],
        compiler_params=params(),
        cost_estimate=cost(4 * rows * size * columns, 12 * rows * columns),
        name="start_rows",
    )(me, adapter_row, mine, other, terms[0])
    out = pl.pallas_call(
        functools.partial(finish_kernel, buffers),
        in_specs=[VMEM] * (4 + buffers),
        out_specs=HBM,
        out_shape=jax.ShapeDtypeStruct((rows * columns // head, head), bf16),
        scratch_shapes=[
            pltpu.VMEM((rows * columns // head, head), f32),
            pltpu.VMEM((rows * columns // head, head), bf16),
            pltpu.SemaphoreType.DMA((4,)),
        ],
        compiler_params=params(),
        cost_estimate=cost(4 * rows * slots * columns, 2 * slots * columns),
        name="finish",
    )(partial, picker, cosine, sine, key_norm_gain.astype(f32)[None, :], *returned)
    return out.reshape(rows, columns // (2 * head), 2, head)


def solution(mesh):
    return jax.shard_map(
        body,
        mesh=mesh,
        in_specs=(
            P(("groups", "pool"), "tp"),
            P(("groups", "pool"), None),
            P(("groups", "pool")),
            P("tp", None),
            P("pool", "tp", None),
            P("pool", None, None),
            P("pool"),
            P(),
        ),
        out_specs=P(("groups", "pool"), "tp", None, None),
        check_vma=False,
    )
```

```python
import functools

import jax
import jax.numpy as jnp
from jax import lax
from jax.experimental import pallas as pl
from jax.experimental.pallas import tpu as pltpu
from jax.sharding import PartitionSpec as P

ALPHA = 32
ROPE_THETA = 1000000.0
NORM_EPS = 1e-06
VMEM_LIMIT = 48 * 1024 * 1024
LANES = 128
EXPONENT_BITS = 8
EXPONENT_BIAS = 128

VMEM = pl.BlockSpec(memory_space=pltpu.VMEM)
HBM = pl.BlockSpec(memory_space=pltpu.HBM)
SMEM = pl.BlockSpec(memory_space=pltpu.SMEM)


def params(**kw):
    return pltpu.CompilerParams(vmem_limit_bytes=VMEM_LIMIT, **kw)


def cost(flops, bytes_accessed):
    return pl.CostEstimate(flops=flops, bytes_accessed=bytes_accessed, transcendentals=0)


def in_hbm(x):
    return pltpu.with_memory_space_constraint(x, pltpu.HBM)


def iota(shape, dim):
    return lax.broadcasted_iota(jnp.int32, shape, dim)


def to_column(row):
    n = row.shape[1]
    return jnp.sum(
        jnp.where(iota((n, n), 0) == iota((n, n), 1), row, 0), axis=1, keepdims=True
    )


def slot_places(row, me, pool, local, depth):
    n = row.shape[1]
    column = to_column(row)
    earlier = (column == row) & (iota((n, n), 0) < iota((n, n), 1))
    slot = jnp.sum(jnp.where(earlier, 1, 0), axis=0, keepdims=True)
    holder = row // local
    apart = holder ^ me
    buffer, far = apart % (pool // 2), apart // (pool // 2)
    return ((buffer * 2 + far) * local + (row - holder * local)) * depth + slot


def far_first(count):
    return sorted(range(1, count), key=lambda j: (-bin(j).count("1"), -j))


def return_order(count):
    order = far_first(count)
    return order[-1:] + order[:-1]


def halves(x):
    high = x.astype(jnp.bfloat16)
    low = (x - high.astype(jnp.float32)).astype(jnp.bfloat16)
    return high, low


def up_share_kernel(cores, group_ref, core_ref, ranks_ref, up_hbm, out_ref, factor_ref, own_ref, sem):
    local, rank, share = out_ref.shape
    at = core_ref[0] * (up_hbm.shape[2] // cores) + group_ref[0] * share
    copy = pltpu.make_async_copy(
        up_hbm.at[:, :, pl.ds(pl.multiple_of(at, share), share)], own_ref, sem
    )
    copy.start()
    copy.wait()
    for a in range(local):
        used = ranks_ref[a]

        def factor(shape, dim):
            scale = jnp.float32(ALPHA) / jnp.full(shape, used, jnp.int32).astype(jnp.float32)
            return jnp.where(iota(shape, dim) < used, scale, 0.0)

        factor_ref[a : a + 1, :] = factor((1, rank), 1)
        out_ref[a] = (own_ref[a].astype(jnp.float32) * factor((rank, 1), 0)).astype(jnp.bfloat16)


def pick_kernel(
    pool, local, depth, me_ref, group_ref, adapter_hbm, tokens_hbm, down_hbm, *refs
):
    share_ref, outs = refs[0], refs[1:-4]
    adapter_ref, tokens_ref, share_sem, sems = refs[-4:]
    rows, width = tokens_ref.shape
    share = share_ref.shape[1]
    parts = sems.shape[0] - 1
    part = width // parts
    adapter_copy = pltpu.make_async_copy(adapter_hbm, adapter_ref, sems.at[parts])
    adapter_copy.start()
    copies = [
        pltpu.make_async_copy(
            tokens_hbm.at[:, pl.ds(i * part, part)],
            tokens_ref.at[:, pl.ds(i * part, part)],
            sems.at[i],
        )
        for i in range(parts)
    ]
    for copy in copies:
        copy.start()
    at = pl.multiple_of(group_ref[0] * share, share)
    share_copy = pltpu.make_async_copy(down_hbm.at[:, pl.ds(at, share), :], share_ref, share_sem)
    share_copy.start()
    adapter_copy.wait()
    place = slot_places(adapter_ref[...], me_ref[0], pool, local, depth)
    size = outs[0].shape[0]
    slots = len(outs) * size
    picker = jnp.where(iota((slots, rows), 0) == place, 1.0, 0.0).astype(jnp.bfloat16)
    for i, copy in enumerate(copies):
        copy.wait()
        here = slice(i * part, (i + 1) * part)
        block = jnp.dot(picker, tokens_ref[:, here], preferred_element_type=jnp.float32)
        for j, out in enumerate(outs):
            out[:, here] = block[j * size : (j + 1) * size].astype(jnp.bfloat16)
    share_copy.wait()


def base_kernel(
    core_ref,
    tokens_hbm,
    weight_hbm,
    down_hbm,
    up_hbm,
    theirs_ref,
    mine_ref,
    down_ref,
    up_ref,
    tokens_ref,
    weight_ref,
    other_sems,
    sems,
):
    rows, columns = mine_ref.shape
    steps = sems.shape[1]
    step = tokens_ref.shape[1] // steps
    copies = []
    for half in range(2):
        start = (1 - core_ref[0] if half == 0 else core_ref[0]) * columns
        start = pl.multiple_of(start, columns)
        for k in range(steps):
            copies.append(
                pltpu.make_async_copy(
                    weight_hbm.at[pl.ds(k * step, step), pl.ds(start, columns)],
                    weight_ref.at[half, pl.ds(k * step, step), :],
                    sems.at[half, k],
                )
            )
    tokens_copy = pltpu.make_async_copy(tokens_hbm, tokens_ref, other_sems.at[0])
    own = pl.multiple_of(core_ref[0] * columns, columns)
    factor_copies = [
        pltpu.make_async_copy(down_hbm, down_ref, other_sems.at[1]),
        pltpu.make_async_copy(up_hbm.at[:, :, pl.ds(own, columns)], up_ref, other_sems.at[2]),
    ]
    for copy in [tokens_copy] + copies + factor_copies:
        copy.start()
    tokens_copy.wait()
    for half, out in enumerate((theirs_ref, mine_ref)):
        for k in range(steps):
            copies[half * steps + k].wait()
            term = jnp.dot(
                tokens_ref[:, k * step : (k + 1) * step],
                weight_ref[half, k * step : (k + 1) * step, :],
                preferred_element_type=jnp.float32,
            )
            if k == 0:
                out[...] = term
            else:
                out[...] += term
    for copy in factor_copies:
        copy.wait()


def down_kernel(buffers, groups, local, depth, group_ref, down_ref, *refs):
    order = [0] + far_first(buffers)
    ins = [refs[order.index(j)] for j in range(buffers)]
    shares, out = refs[buffers : buffers + groups], refs[-1]
    rank = out.shape[1]
    share = shares[0].shape[1]
    total = None
    for k in range(groups):
        at = pl.multiple_of((group_ref[0] ^ k) * share, share)
        rows = jnp.concatenate([x[:, pl.ds(at, share)] for x in ins], axis=0)
        factors = [down_ref[a, pl.ds(at, share), :] for a in range(local)]
        factors += [shares[k][a] for a in range(local)]
        term = jnp.dot(
            rows, jnp.concatenate(factors, axis=1), preferred_element_type=jnp.float32
        )
        total = term if total is None else total + term
    which = (iota((total.shape[0], 1), 0) // depth) % (2 * local)
    low = total[:, :rank]
    for i in range(1, 2 * local):
        low = jnp.where(which == i, total[:, i * rank : (i + 1) * rank], low)
    out[...] = low


def up_kernel(
    buffers, groups, local, depth, group_ref, low_ref, other_ref, factor_ref, up_ref, *refs
):
    shares, outs, term_ref = refs[:groups], refs[groups : groups + buffers], refs[-1]
    rows, rank = low_ref.shape
    size = rows // buffers
    columns = up_ref.shape[2]
    share = columns // groups
    which = (iota((rows, 1), 0) // depth) % (2 * local)
    low = low_ref[...] + other_ref[...]
    for a in range(local):
        low = jnp.where(which == a, low * factor_ref[a : a + 1, :], low)
    both = jnp.concatenate(halves(low), axis=0)
    which = jnp.concatenate([which, which], axis=0)
    spread = jnp.concatenate(
        [jnp.where(which == i, both, jnp.zeros_like(both)) for i in range(2 * local)], axis=1
    )
    for k in range(groups):
        at = pl.multiple_of((group_ref[0] ^ k) * share, share)
        up = [up_ref[a, :, pl.ds(at, share)] for a in range(local)]
        up += [shares[k][a] for a in range(local)]
        term = jnp.dot(
            spread, jnp.concatenate(up, axis=0), preferred_element_type=jnp.float32
        )
        term_ref[:, pl.ds(at, share)] = term[:rows] + term[rows:]
    lane = iota((1, LANES), 1)
    for j, out in enumerate(outs):
        term = term_ref[j * size : (j + 1) * size, :]
        top = jnp.max(jnp.abs(term), axis=1, keepdims=True)
        exponent = jnp.ceil(jnp.log2(jnp.maximum(top, 1e-30)) + 1e-3)
        code = jnp.clip(jnp.round(term * jnp.exp2(15.0 - exponent)), -32767.0, 32767.0)
        code = code.astype(jnp.int32)
        biased = exponent.astype(jnp.int32) + EXPONENT_BIAS
        first = code[:, :LANES]
        marked = (first & -2) | ((biased >> jnp.minimum(lane, EXPONENT_BITS - 1)) & 1)
        first = jnp.where(lane < EXPONENT_BITS, marked, first)
        out[:, :LANES] = first.astype(jnp.int16)
        out[:, LANES:] = code[:, LANES:].astype(jnp.int16)


def planes(codes, at, size):
    code = jnp.concatenate([x[:, at : at + size] for x in codes], axis=0).astype(jnp.int32)
    high = (code >> 8).astype(jnp.float32).astype(jnp.bfloat16)
    low = (code & 255).astype(jnp.float32).astype(jnp.bfloat16)
    return high, low


def decoded(picker, plane):
    high = jnp.dot(picker, plane[0], preferred_element_type=jnp.float32)
    low = jnp.dot(picker, plane[1], preferred_element_type=jnp.float32)
    return high * 256.0 + low


def scale_of(first):
    lane = iota((1, LANES), 1)
    bits = first.astype(jnp.int32) & 1
    bits = jnp.where(lane < EXPONENT_BITS, bits << jnp.minimum(lane, EXPONENT_BITS - 1), 0)
    exponent = jnp.sum(bits.astype(jnp.float32), axis=1, keepdims=True) - EXPONENT_BIAS
    return jnp.exp2(exponent - 15.0)


def start_rows_kernel(
    buffers, pool, local, depth, me_ref, adapter_ref, mine_ref, other_ref, own_ref, partial_ref, picker_ref
):
    rows, columns = mine_ref.shape
    size = own_ref.shape[0]
    place = to_column(slot_places(adapter_ref[...], me_ref[0], pool, local, depth))
    picker = jnp.where(iota((rows, size), 1) == place, 1.0, 0.0).astype(jnp.bfloat16)
    scale = scale_of(decoded(picker, planes([own_ref], 0, LANES)))
    for at in range(0, columns, 256):
        term = decoded(picker, planes([own_ref], at, 256)) * scale
        partial_ref[:, at : at + 256] = (
            mine_ref[:, at : at + 256] + other_ref[:, at : at + 256] + term
        )
    slots = (buffers - 1) * size
    picker_ref[...] = jnp.where(iota((rows, slots), 1) == place - size, 1.0, 0.0).astype(
        jnp.bfloat16
    )


def finish_kernel(buffers, partial_ref, picker_ref, cos_ref, sin_ref, gain_ref, *refs):
    order = return_order(buffers)
    ins = [refs[order.index(j)] for j in range(1, buffers)]
    out_hbm, entry_ref, out_ref, sems = refs[-4:]
    rows, columns = partial_ref.shape
    head = cos_ref.shape[1]
    kinds = columns // head
    gain, cosine, sine, picker = gain_ref[...], cos_ref[...], sin_ref[...], picker_ref[...]
    scale = scale_of(decoded(picker, planes(ins, 0, LANES)))
    for at in range(0, columns, 2 * head):
        projected = partial_ref[:, at : at + 2 * head]
        projected = projected + decoded(picker, planes(ins, at, 2 * head)) * scale
        key, value = projected[:, :head], projected[:, head:]
        mean = jnp.mean(key * key, axis=1, keepdims=True)
        normed = key * lax.rsqrt(mean + NORM_EPS) * gain
        rotated = normed * cosine + pltpu.roll(normed, head // 2, 1) * sine
        entry_ref[pl.ds(at // head, rows, stride=kinds), :] = rotated
        entry_ref[pl.ds(at // head + 1, rows, stride=kinds), :] = value
    copies = []
    part = rows * kinds // sems.shape[0]
    for i in range(sems.shape[0]):
        done = pl.ds(i * part, part)
        out_ref[done, :] = entry_ref[done, :].astype(jnp.bfloat16)
        copies.append(pltpu.make_async_copy(out_ref.at[done, :], out_hbm.at[done, :], sems.at[i]))
        copies[-1].start()
    for copy in copies:
        copy.wait()


def body(
    tokens,
    row_adapters,
    positions,
    key_value_weight,
    adapter_down,
    adapter_up,
    ranks,
    key_norm_gain,
):
    pool = lax.axis_size("pool")
    groups = lax.axis_size("groups")
    cores = lax.axis_size("tp")
    rows, width = tokens.shape
    local = adapter_down.shape[0]
    adapters = local * pool
    columns = key_value_weight.shape[1] // cores
    rank = adapter_down.shape[2]
    head = key_norm_gain.shape[0]
    depth = max(2, 2 * rows // adapters)
    buffers = pool // 2
    size = 2 * local * depth
    f32, bf16 = jnp.float32, jnp.bfloat16

    me = lax.axis_index("pool").astype(jnp.int32)[None]
    core = lax.axis_index("tp").astype(jnp.int32)[None]
    group = lax.axis_index("groups").astype(jnp.int32)[None]

    def exchange(x, axis, count, j):
        return lax.ppermute(x, axis, [(p, p ^ j) for p in range(count)])

    def hand_round(share):
        return [share] + [exchange(share, "groups", groups, k) for k in range(1, groups)]

    adapter_row = row_adapters.reshape(1, rows)
    down_share = width // groups
    parts = 10
    down_part, *picked = pl.pallas_call(
        functools.partial(pick_kernel, pool, local, depth),
        in_specs=[SMEM] * 2 + [HBM] * 3,
        out_specs=[VMEM] * (1 + buffers),
        out_shape=[jax.ShapeDtypeStruct((local, down_share, rank), bf16)]
        + [jax.ShapeDtypeStruct((size, width), bf16)] * buffers,
        scratch_shapes=[
            pltpu.VMEM((1, rows), jnp.int32),
            pltpu.VMEM((rows, width), bf16),
            pltpu.SemaphoreType.DMA,
            pltpu.SemaphoreType.DMA((parts + 1,)),
        ],
        compiler_params=params(),
        cost_estimate=cost(2 * buffers * size * rows * width, 2 * (rows + buffers * size) * width),
        name="pick",
    )(me, group, in_hbm(adapter_row), in_hbm(tokens), in_hbm(adapter_down))
    far_down = exchange(down_part, "pool", pool, pool // 2)
    up_share = columns // groups
    ranks_now, adapter_up_now, _ = lax.optimization_barrier((ranks, adapter_up, picked))
    up_part, factor = pl.pallas_call(
        functools.partial(up_share_kernel, cores),
        in_specs=[SMEM] * 3 + [HBM],
        out_specs=[VMEM] * 2,
        out_shape=[
            jax.ShapeDtypeStruct((local, rank, up_share), bf16),
            jax.ShapeDtypeStruct((local, rank), f32),
        ],
        scratch_shapes=[
            pltpu.VMEM((local, rank, up_share), bf16),
            pltpu.SemaphoreType.DMA,
        ],
        compiler_params=params(),
        cost_estimate=cost(local * rank * up_share, 4 * local * rank * up_share),
        name="up_share",
    )(group, core, ranks_now, in_hbm(adapter_up_now))
    far_up = exchange(up_part, "pool", pool, pool // 2)

    order = far_first(buffers)
    early, late = order[:1], order[1:]
    late_rows, _ = lax.optimization_barrier(([picked[j] for j in late], up_part))
    leaving = [picked[j] for j in early] + late_rows
    arrived = [picked[0]] + [exchange(x, "pool", pool, j) for x, j in zip(leaving, order)]

    steps = 5
    theirs, mine, own_down, own_up = pl.pallas_call(
        base_kernel,
        in_specs=[SMEM] + [HBM] * 4,
        out_specs=[VMEM] * 4,
        out_shape=[jax.ShapeDtypeStruct((rows, columns), f32)] * 2
        + [
            jax.ShapeDtypeStruct(adapter_down.shape, bf16),
            jax.ShapeDtypeStruct((local, rank, columns), bf16),
        ],
        scratch_shapes=[
            pltpu.VMEM((rows, width), bf16),
            pltpu.VMEM((2, width, columns), bf16),
            pltpu.SemaphoreType.DMA((3,)),
            pltpu.SemaphoreType.DMA((2, steps)),
        ],
        compiler_params=params(),
        cost_estimate=cost(4 * rows * width * columns, 4 * width * columns),
        name="base",
    )(
        core,
        in_hbm(tokens),
        in_hbm(key_value_weight),
        in_hbm(adapter_down),
        in_hbm(adapter_up),
    )
    far_down, theirs = lax.optimization_barrier((far_down, theirs))
    far_downs = hand_round(far_down)
    far_up, _ = lax.optimization_barrier((far_up, far_down))
    far_ups = hand_round(far_up)
    half_dim = head // 2
    frequency = jnp.power(
        f32(ROPE_THETA), -jnp.arange(half_dim, dtype=f32) * (2.0 / head)
    )
    angles = positions.astype(f32)[:, None] * frequency[None, :]
    cosine, sine = jnp.cos(angles), jnp.sin(angles)
    cosine = jnp.concatenate([cosine, cosine], axis=1)
    sine = jnp.concatenate([-sine, sine], axis=1)

    far_up, arrived[1], theirs = lax.optimization_barrier((far_up, arrived[1], theirs))
    other = exchange(theirs, "tp", cores, 1)
    arrived, mine, cosine, sine = lax.optimization_barrier((arrived, mine, cosine, sine))
    slots = buffers * size
    low = pl.pallas_call(
        functools.partial(down_kernel, buffers, groups, local, depth),
        in_specs=[SMEM] + [VMEM] * (1 + buffers + groups),
        out_specs=VMEM,
        out_shape=jax.ShapeDtypeStruct((slots, rank), f32),
        compiler_params=params(),
        cost_estimate=cost(4 * local * slots * rank * width, 2 * (slots + rank) * width),
        name="down",
    )(group, own_down, *arrived, *far_downs)
    low_other = exchange(low, "tp", cores, 1)

    terms = pl.pallas_call(
        functools.partial(up_kernel, buffers, groups, local, depth),
        in_specs=[SMEM] + [VMEM] * (4 + groups),
        out_specs=[VMEM] * buffers,
        out_shape=[jax.ShapeDtypeStruct((size, columns), jnp.int16)] * buffers,
        scratch_shapes=[pltpu.VMEM((slots, columns), f32)],
        compiler_params=params(),
        cost_estimate=cost(8 * local * slots * rank * columns, 2 * slots * columns),
        name="up",
    )(group, low, low_other, factor, own_up, *far_ups)
    order = return_order(buffers)
    returned = [exchange(terms[j], "pool", pool, j) for j in order]

    partial, picker = pl.pallas_call(
        functools.partial(start_rows_kernel, buffers, pool, local, depth),
        in_specs=[SMEM] + [VMEM] * 4,
        out_specs=[VMEM] * 2,
        out_shape=[
            jax.ShapeDtypeStruct((rows, columns), f32),
            jax.ShapeDtypeStruct((rows, slots - size), bf16),
        ],
        compiler_params=params(),
        cost_estimate=cost(4 * rows * size * columns, 12 * rows * columns),
        name="start_rows",
    )(me, adapter_row, mine, other, terms[0])
    out = pl.pallas_call(
        functools.partial(finish_kernel, buffers),
        in_specs=[VMEM] * (4 + buffers),
        out_specs=HBM,
        out_shape=jax.ShapeDtypeStruct((rows * columns // head, head), bf16),
        scratch_shapes=[
            pltpu.VMEM((rows * columns // head, head), f32),
            pltpu.VMEM((rows * columns // head, head), bf16),
            pltpu.SemaphoreType.DMA((4,)),
        ],
        compiler_params=params(),
        cost_estimate=cost(4 * rows * slots * columns, 2 * slots * columns),
        name="finish",
    )(partial, picker, cosine, sine, key_norm_gain.astype(f32)[None, :], *returned)
    return out.reshape(rows, columns // (2 * head), 2, head)


def solution(mesh):
    return jax.shard_map(
        body,
        mesh=mesh,
        in_specs=(
            P(("groups", "pool"), "tp"),
            P(("groups", "pool"), None),
            P(("groups", "pool")),
            P("tp", None),
            P("pool", "tp", None),
            P("pool", None, None),
            P("pool"),
            P(),
        ),
        out_specs=P(("groups", "pool"), "tp", None, None),
        check_vma=False,
    )
```

```python
import functools

import jax
import jax.numpy as jnp
from jax import lax
from jax.experimental import pallas as pl
from jax.experimental.pallas import tpu as pltpu
from jax.sharding import PartitionSpec as P

ALPHA = 32
ROPE_THETA = 1000000.0
NORM_EPS = 1e-06
VMEM_LIMIT = 48 * 1024 * 1024
LANES = 128
EXPONENT_BITS = 8
EXPONENT_BIAS = 128

VMEM = pl.BlockSpec(memory_space=pltpu.VMEM)
HBM = pl.BlockSpec(memory_space=pltpu.HBM)
SMEM = pl.BlockSpec(memory_space=pltpu.SMEM)


def params(**kw):
    return pltpu.CompilerParams(vmem_limit_bytes=VMEM_LIMIT, **kw)


def cost(flops, bytes_accessed):
    return pl.CostEstimate(flops=flops, bytes_accessed=bytes_accessed, transcendentals=0)


def in_hbm(x):
    return pltpu.with_memory_space_constraint(x, pltpu.HBM)


def iota(shape, dim):
    return lax.broadcasted_iota(jnp.int32, shape, dim)


def to_column(row):
    n = row.shape[1]
    return jnp.sum(
        jnp.where(iota((n, n), 0) == iota((n, n), 1), row, 0), axis=1, keepdims=True
    )


def slot_places(row, me, pool, local, depth):
    n = row.shape[1]
    column = to_column(row)
    earlier = (column == row) & (iota((n, n), 0) < iota((n, n), 1))
    slot = jnp.sum(jnp.where(earlier, 1, 0), axis=0, keepdims=True)
    holder = row // local
    apart = holder ^ me
    buffer, far = apart % (pool // 2), apart // (pool // 2)
    return ((buffer * 2 + far) * local + (row - holder * local)) * depth + slot


def far_first(count):
    return sorted(range(1, count), key=lambda j: (-bin(j).count("1"), -j))


def return_order(count):
    order = far_first(count)
    return order[-1:] + order[:-1]


def halves(x):
    high = x.astype(jnp.bfloat16)
    low = (x - high.astype(jnp.float32)).astype(jnp.bfloat16)
    return high, low


def up_share_kernel(cores, group_ref, core_ref, ranks_ref, up_hbm, out_ref, factor_ref, own_ref, sem):
    local, rank, share = out_ref.shape
    at = core_ref[0] * (up_hbm.shape[2] // cores) + group_ref[0] * share
    copy = pltpu.make_async_copy(
        up_hbm.at[:, :, pl.ds(pl.multiple_of(at, share), share)], own_ref, sem
    )
    copy.start()
    copy.wait()
    for a in range(local):
        used = ranks_ref[a]

        def factor(shape, dim):
            scale = jnp.float32(ALPHA) / jnp.full(shape, used, jnp.int32).astype(jnp.float32)
            return jnp.where(iota(shape, dim) < used, scale, 0.0)

        factor_ref[a : a + 1, :] = factor((1, rank), 1)
        out_ref[a] = (own_ref[a].astype(jnp.float32) * factor((rank, 1), 0)).astype(jnp.bfloat16)


def fetch_kernel(group_ref, down_hbm, adapter_hbm, tokens_hbm, share_ref, adapter_ref, tokens_ref, sems):
    share = share_ref.shape[1]
    at = pl.multiple_of(group_ref[0] * share, share)
    copies = [
        pltpu.make_async_copy(down_hbm.at[:, pl.ds(at, share), :], share_ref, sems.at[0]),
        pltpu.make_async_copy(adapter_hbm, adapter_ref, sems.at[1]),
    ]
    parts = sems.shape[0] - 2
    part = tokens_ref.shape[0] // parts
    for i in range(parts):
        here = pl.ds(i * part, part)
        copies.append(
            pltpu.make_async_copy(tokens_hbm.at[here, :], tokens_ref.at[here, :], sems.at[2 + i])
        )
    for copy in copies:
        copy.start()
    for copy in copies:
        copy.wait()


def pick_kernel(pool, local, depth, me_ref, adapter_ref, tokens_ref, *outs):
    rows, width = tokens_ref.shape
    place = slot_places(adapter_ref[...], me_ref[0], pool, local, depth)
    size = outs[0].shape[0]
    slots = len(outs) * size
    picker = jnp.where(iota((slots, rows), 0) == place, 1.0, 0.0).astype(jnp.bfloat16)
    step = 512
    for at in range(0, width, step):
        block = jnp.dot(
            picker, tokens_ref[:, at : at + step], preferred_element_type=jnp.float32
        )
        for j, out in enumerate(outs):
            out[:, at : at + step] = block[j * size : (j + 1) * size].astype(jnp.bfloat16)


def base_kernel(
    core_ref,
    tokens_hbm,
    weight_hbm,
    down_hbm,
    up_hbm,
    theirs_ref,
    mine_ref,
    down_ref,
    up_ref,
    tokens_ref,
    weight_ref,
    other_sems,
    sems,
):
    rows, columns = mine_ref.shape
    steps = sems.shape[1]
    step = tokens_ref.shape[1] // steps
    copies = []
    for half in range(2):
        start = (1 - core_ref[0] if half == 0 else core_ref[0]) * columns
        start = pl.multiple_of(start, columns)
        for k in range(steps):
            copies.append(
                pltpu.make_async_copy(
                    weight_hbm.at[pl.ds(k * step, step), pl.ds(start, columns)],
                    weight_ref.at[half, pl.ds(k * step, step), :],
                    sems.at[half, k],
                )
            )
    tokens_copy = pltpu.make_async_copy(tokens_hbm, tokens_ref, other_sems.at[0])
    own = pl.multiple_of(core_ref[0] * columns, columns)
    factor_copies = [
        pltpu.make_async_copy(down_hbm, down_ref, other_sems.at[1]),
        pltpu.make_async_copy(up_hbm.at[:, :, pl.ds(own, columns)], up_ref, other_sems.at[2]),
    ]
    for copy in [tokens_copy] + copies + factor_copies:
        copy.start()
    tokens_copy.wait()
    for half, out in enumerate((theirs_ref, mine_ref)):
        for k in range(steps):
            copies[half * steps + k].wait()
            term = jnp.dot(
                tokens_ref[:, k * step : (k + 1) * step],
                weight_ref[half, k * step : (k + 1) * step, :],
                preferred_element_type=jnp.float32,
            )
            if k == 0:
                out[...] = term
            else:
                out[...] += term
    for copy in factor_copies:
        copy.wait()


def down_kernel(buffers, groups, local, depth, group_ref, down_ref, *refs):
    order = [0] + far_first(buffers)
    ins = [refs[order.index(j)] for j in range(buffers)]
    shares, out = refs[buffers : buffers + groups], refs[-1]
    rank = out.shape[1]
    share = shares[0].shape[1]
    total = None
    for k in range(groups):
        at = pl.multiple_of((group_ref[0] ^ k) * share, share)
        rows = jnp.concatenate([x[:, pl.ds(at, share)] for x in ins], axis=0)
        factors = [down_ref[a, pl.ds(at, share), :] for a in range(local)]
        factors += [shares[k][a] for a in range(local)]
        term = jnp.dot(
            rows, jnp.concatenate(factors, axis=1), preferred_element_type=jnp.float32
        )
        total = term if total is None else total + term
    which = (iota((total.shape[0], 1), 0) // depth) % (2 * local)
    low = total[:, :rank]
    for i in range(1, 2 * local):
        low = jnp.where(which == i, total[:, i * rank : (i + 1) * rank], low)
    out[...] = low


def up_kernel(
    buffers, groups, local, depth, group_ref, low_ref, other_ref, factor_ref, up_ref, *refs
):
    shares, outs, term_ref = refs[:groups], refs[groups : groups + buffers], refs[-1]
    rows, rank = low_ref.shape
    size = rows // buffers
    columns = up_ref.shape[2]
    share = columns // groups
    which = (iota((rows, 1), 0) // depth) % (2 * local)
    low = low_ref[...] + other_ref[...]
    for a in range(local):
        low = jnp.where(which == a, low * factor_ref[a : a + 1, :], low)
    both = jnp.concatenate(halves(low), axis=0)
    which = jnp.concatenate([which, which], axis=0)
    spread = jnp.concatenate(
        [jnp.where(which == i, both, jnp.zeros_like(both)) for i in range(2 * local)], axis=1
    )
    for k in range(groups):
        at = pl.multiple_of((group_ref[0] ^ k) * share, share)
        up = [up_ref[a, :, pl.ds(at, share)] for a in range(local)]
        up += [shares[k][a] for a in range(local)]
        term = jnp.dot(
            spread, jnp.concatenate(up, axis=0), preferred_element_type=jnp.float32
        )
        term_ref[:, pl.ds(at, share)] = term[:rows] + term[rows:]
    lane = iota((1, LANES), 1)
    for j, out in enumerate(outs):
        term = term_ref[j * size : (j + 1) * size, :]
        top = jnp.max(jnp.abs(term), axis=1, keepdims=True)
        exponent = jnp.ceil(jnp.log2(jnp.maximum(top, 1e-30)) + 1e-3)
        code = jnp.clip(jnp.round(term * jnp.exp2(15.0 - exponent)), -32767.0, 32767.0)
        code = code.astype(jnp.int32)
        biased = exponent.astype(jnp.int32) + EXPONENT_BIAS
        first = code[:, :LANES]
        marked = (first & -2) | ((biased >> jnp.minimum(lane, EXPONENT_BITS - 1)) & 1)
        first = jnp.where(lane < EXPONENT_BITS, marked, first)
        out[:, :LANES] = first.astype(jnp.int16)
        out[:, LANES:] = code[:, LANES:].astype(jnp.int16)


def planes(codes, at, size):
    code = jnp.concatenate([x[:, at : at + size] for x in codes], axis=0).astype(jnp.int32)
    high = (code >> 8).astype(jnp.float32).astype(jnp.bfloat16)
    low = (code & 255).astype(jnp.float32).astype(jnp.bfloat16)
    return high, low


def decoded(picker, plane):
    high = jnp.dot(picker, plane[0], preferred_element_type=jnp.float32)
    low = jnp.dot(picker, plane[1], preferred_element_type=jnp.float32)
    return high * 256.0 + low


def scale_of(first):
    lane = iota((1, LANES), 1)
    bits = first.astype(jnp.int32) & 1
    bits = jnp.where(lane < EXPONENT_BITS, bits << jnp.minimum(lane, EXPONENT_BITS - 1), 0)
    exponent = jnp.sum(bits.astype(jnp.float32), axis=1, keepdims=True) - EXPONENT_BIAS
    return jnp.exp2(exponent - 15.0)


def start_rows_kernel(
    buffers, pool, local, depth, me_ref, adapter_ref, mine_ref, other_ref, own_ref, partial_ref, picker_ref
):
    rows, columns = mine_ref.shape
    size = own_ref.shape[0]
    place = to_column(slot_places(adapter_ref[...], me_ref[0], pool, local, depth))
    picker = jnp.where(iota((rows, size), 1) == place, 1.0, 0.0).astype(jnp.bfloat16)
    scale = scale_of(decoded(picker, planes([own_ref], 0, LANES)))
    for at in range(0, columns, 256):
        term = decoded(picker, planes([own_ref], at, 256)) * scale
        partial_ref[:, at : at + 256] = (
            mine_ref[:, at : at + 256] + other_ref[:, at : at + 256] + term
        )
    slots = (buffers - 1) * size
    picker_ref[...] = jnp.where(iota((rows, slots), 1) == place - size, 1.0, 0.0).astype(
        jnp.bfloat16
    )


def finish_kernel(buffers, partial_ref, picker_ref, cos_ref, sin_ref, gain_ref, *refs):
    order = return_order(buffers)
    ins = [refs[order.index(j)] for j in range(1, buffers)]
    out_hbm, entry_ref, out_ref, sems = refs[-4:]
    rows, columns = partial_ref.shape
    head = cos_ref.shape[1]
    kinds = columns // head
    gain, cosine, sine, picker = gain_ref[...], cos_ref[...], sin_ref[...], picker_ref[...]
    scale = scale_of(decoded(picker, planes(ins, 0, LANES)))
    for at in range(0, columns, 2 * head):
        projected = partial_ref[:, at : at + 2 * head]
        projected = projected + decoded(picker, planes(ins, at, 2 * head)) * scale
        key, value = projected[:, :head], projected[:, head:]
        mean = jnp.mean(key * key, axis=1, keepdims=True)
        normed = key * lax.rsqrt(mean + NORM_EPS) * gain
        rotated = normed * cosine + pltpu.roll(normed, head // 2, 1) * sine
        entry_ref[pl.ds(at // head, rows, stride=kinds), :] = rotated
        entry_ref[pl.ds(at // head + 1, rows, stride=kinds), :] = value
    copies = []
    part = rows * kinds // sems.shape[0]
    for i in range(sems.shape[0]):
        done = pl.ds(i * part, part)
        out_ref[done, :] = entry_ref[done, :].astype(jnp.bfloat16)
        copies.append(pltpu.make_async_copy(out_ref.at[done, :], out_hbm.at[done, :], sems.at[i]))
        copies[-1].start()
    for copy in copies:
        copy.wait()


def body(
    tokens,
    row_adapters,
    positions,
    key_value_weight,
    adapter_down,
    adapter_up,
    ranks,
    key_norm_gain,
):
    pool = lax.axis_size("pool")
    groups = lax.axis_size("groups")
    cores = lax.axis_size("tp")
    rows, width = tokens.shape
    local = adapter_down.shape[0]
    adapters = local * pool
    columns = key_value_weight.shape[1] // cores
    rank = adapter_down.shape[2]
    head = key_norm_gain.shape[0]
    depth = max(2, 2 * rows // adapters)
    buffers = pool // 2
    size = 2 * local * depth
    f32, bf16 = jnp.float32, jnp.bfloat16

    me = lax.axis_index("pool").astype(jnp.int32)[None]
    core = lax.axis_index("tp").astype(jnp.int32)[None]
    group = lax.axis_index("groups").astype(jnp.int32)[None]

    def exchange(x, axis, count, j):
        return lax.ppermute(x, axis, [(p, p ^ j) for p in range(count)])

    def hand_round(share):
        return [share] + [exchange(share, "groups", groups, k) for k in range(1, groups)]

    adapter_row = row_adapters.reshape(1, rows)
    down_share = width // groups
    parts = rows // 16
    down_part, adapter_now, tokens_now = pl.pallas_call(
        fetch_kernel,
        in_specs=[SMEM] + [HBM] * 3,
        out_specs=[VMEM] * 3,
        out_shape=[
            jax.ShapeDtypeStruct((local, down_share, rank), bf16),
            jax.ShapeDtypeStruct((1, rows), jnp.int32),
            jax.ShapeDtypeStruct((rows, width), bf16),
        ],
        scratch_shapes=[pltpu.SemaphoreType.DMA((parts + 2,))],
        compiler_params=params(),
        cost_estimate=cost(0, 4 * (local * rank * down_share + rows * width)),
        name="fetch",
    )(group, in_hbm(adapter_down), in_hbm(adapter_row), in_hbm(tokens))
    picked = pl.pallas_call(
        functools.partial(pick_kernel, pool, local, depth),
        in_specs=[SMEM] + [VMEM] * 2,
        out_specs=[VMEM] * buffers,
        out_shape=[jax.ShapeDtypeStruct((size, width), bf16)] * buffers,
        compiler_params=params(),
        cost_estimate=cost(2 * buffers * size * rows * width, 2 * (rows + buffers * size) * width),
        name="pick",
    )(me, adapter_now, tokens_now)
    far_down = exchange(down_part, "pool", pool, pool // 2)
    up_share = columns // groups
    ranks_now, adapter_up_now, _ = lax.optimization_barrier((ranks, adapter_up, picked))
    up_part, factor = pl.pallas_call(
        functools.partial(up_share_kernel, cores),
        in_specs=[SMEM] * 3 + [HBM],
        out_specs=[VMEM] * 2,
        out_shape=[
            jax.ShapeDtypeStruct((local, rank, up_share), bf16),
            jax.ShapeDtypeStruct((local, rank), f32),
        ],
        scratch_shapes=[
            pltpu.VMEM((local, rank, up_share), bf16),
            pltpu.SemaphoreType.DMA,
        ],
        compiler_params=params(),
        cost_estimate=cost(local * rank * up_share, 4 * local * rank * up_share),
        name="up_share",
    )(group, core, ranks_now, in_hbm(adapter_up_now))
    far_up = exchange(up_part, "pool", pool, pool // 2)

    order = far_first(buffers)
    early, late = order[:1], order[1:]
    late_rows, _ = lax.optimization_barrier(([picked[j] for j in late], up_part))
    leaving = [picked[j] for j in early] + late_rows
    arrived = [picked[0]] + [exchange(x, "pool", pool, j) for x, j in zip(leaving, order)]

    steps = 5
    theirs, mine, own_down, own_up = pl.pallas_call(
        base_kernel,
        in_specs=[SMEM] + [HBM] * 4,
        out_specs=[VMEM] * 4,
        out_shape=[jax.ShapeDtypeStruct((rows, columns), f32)] * 2
        + [
            jax.ShapeDtypeStruct(adapter_down.shape, bf16),
            jax.ShapeDtypeStruct((local, rank, columns), bf16),
        ],
        scratch_shapes=[
            pltpu.VMEM((rows, width), bf16),
            pltpu.VMEM((2, width, columns), bf16),
            pltpu.SemaphoreType.DMA((3,)),
            pltpu.SemaphoreType.DMA((2, steps)),
        ],
        compiler_params=params(),
        cost_estimate=cost(4 * rows * width * columns, 4 * width * columns),
        name="base",
    )(
        core,
        in_hbm(tokens),
        in_hbm(key_value_weight),
        in_hbm(adapter_down),
        in_hbm(adapter_up),
    )
    far_down, theirs = lax.optimization_barrier((far_down, theirs))
    far_downs = hand_round(far_down)
    far_up, _ = lax.optimization_barrier((far_up, far_down))
    far_ups = hand_round(far_up)
    half_dim = head // 2
    frequency = jnp.power(
        f32(ROPE_THETA), -jnp.arange(half_dim, dtype=f32) * (2.0 / head)
    )
    angles = positions.astype(f32)[:, None] * frequency[None, :]
    cosine, sine = jnp.cos(angles), jnp.sin(angles)
    cosine = jnp.concatenate([cosine, cosine], axis=1)
    sine = jnp.concatenate([-sine, sine], axis=1)

    far_up, arrived[1], theirs = lax.optimization_barrier((far_up, arrived[1], theirs))
    other = exchange(theirs, "tp", cores, 1)
    arrived, mine, cosine, sine = lax.optimization_barrier((arrived, mine, cosine, sine))
    slots = buffers * size
    low = pl.pallas_call(
        functools.partial(down_kernel, buffers, groups, local, depth),
        in_specs=[SMEM] + [VMEM] * (1 + buffers + groups),
        out_specs=VMEM,
        out_shape=jax.ShapeDtypeStruct((slots, rank), f32),
        compiler_params=params(),
        cost_estimate=cost(4 * local * slots * rank * width, 2 * (slots + rank) * width),
        name="down",
    )(group, own_down, *arrived, *far_downs)
    low_other = exchange(low, "tp", cores, 1)

    terms = pl.pallas_call(
        functools.partial(up_kernel, buffers, groups, local, depth),
        in_specs=[SMEM] + [VMEM] * (4 + groups),
        out_specs=[VMEM] * buffers,
        out_shape=[jax.ShapeDtypeStruct((size, columns), jnp.int16)] * buffers,
        scratch_shapes=[pltpu.VMEM((slots, columns), f32)],
        compiler_params=params(),
        cost_estimate=cost(8 * local * slots * rank * columns, 2 * slots * columns),
        name="up",
    )(group, low, low_other, factor, own_up, *far_ups)
    order = return_order(buffers)
    returned = [exchange(terms[j], "pool", pool, j) for j in order]

    partial, picker = pl.pallas_call(
        functools.partial(start_rows_kernel, buffers, pool, local, depth),
        in_specs=[SMEM] + [VMEM] * 4,
        out_specs=[VMEM] * 2,
        out_shape=[
            jax.ShapeDtypeStruct((rows, columns), f32),
            jax.ShapeDtypeStruct((rows, slots - size), bf16),
        ],
        compiler_params=params(),
        cost_estimate=cost(4 * rows * size * columns, 12 * rows * columns),
        name="start_rows",
    )(me, adapter_row, mine, other, terms[0])
    out = pl.pallas_call(
        functools.partial(finish_kernel, buffers),
        in_specs=[VMEM] * (4 + buffers),
        out_specs=HBM,
        out_shape=jax.ShapeDtypeStruct((rows * columns // head, head), bf16),
        scratch_shapes=[
            pltpu.VMEM((rows * columns // head, head), f32),
            pltpu.VMEM((rows * columns // head, head), bf16),
            pltpu.SemaphoreType.DMA((4,)),
        ],
        compiler_params=params(),
        cost_estimate=cost(4 * rows * slots * columns, 2 * slots * columns),
        name="finish",
    )(partial, picker, cosine, sine, key_norm_gain.astype(f32)[None, :], *returned)
    return out.reshape(rows, columns // (2 * head), 2, head)


def solution(mesh):
    return jax.shard_map(
        body,
        mesh=mesh,
        in_specs=(
            P(("groups", "pool"), "tp"),
            P(("groups", "pool"), None),
            P(("groups", "pool")),
            P("tp", None),
            P("pool", "tp", None),
            P("pool", None, None),
            P("pool"),
            P(),
        ),
        out_specs=P(("groups", "pool"), "tp", None, None),
        check_vma=False,
    )
```

```python
import functools

import jax
import jax.numpy as jnp
from jax import lax
from jax.experimental import pallas as pl
from jax.experimental.pallas import tpu as pltpu
from jax.sharding import PartitionSpec as P

ALPHA = 32
ROPE_THETA = 1000000.0
NORM_EPS = 1e-06
VMEM_LIMIT = 48 * 1024 * 1024
LANES = 128
EXPONENT_BITS = 8
EXPONENT_BIAS = 128

VMEM = pl.BlockSpec(memory_space=pltpu.VMEM)
HBM = pl.BlockSpec(memory_space=pltpu.HBM)
SMEM = pl.BlockSpec(memory_space=pltpu.SMEM)


def params(**kw):
    return pltpu.CompilerParams(vmem_limit_bytes=VMEM_LIMIT, **kw)


def cost(flops, bytes_accessed):
    return pl.CostEstimate(flops=flops, bytes_accessed=bytes_accessed, transcendentals=0)


def in_hbm(x):
    return pltpu.with_memory_space_constraint(x, pltpu.HBM)


def iota(shape, dim):
    return lax.broadcasted_iota(jnp.int32, shape, dim)


def to_column(row):
    n = row.shape[1]
    return jnp.sum(
        jnp.where(iota((n, n), 0) == iota((n, n), 1), row, 0), axis=1, keepdims=True
    )


def slot_places(row, me, pool, local, depth):
    n = row.shape[1]
    column = to_column(row)
    earlier = (column == row) & (iota((n, n), 0) < iota((n, n), 1))
    slot = jnp.sum(jnp.where(earlier, 1, 0), axis=0, keepdims=True)
    holder = row // local
    apart = holder ^ me
    buffer, far = apart % (pool // 2), apart // (pool // 2)
    return ((buffer * 2 + far) * local + (row - holder * local)) * depth + slot


def far_first(count):
    return sorted(range(1, count), key=lambda j: (-bin(j).count("1"), -j))


def return_order(count):
    order = far_first(count)
    return order[-1:] + order[:-1]


def halves(x):
    high = x.astype(jnp.bfloat16)
    low = (x - high.astype(jnp.float32)).astype(jnp.bfloat16)
    return high, low


def up_share_kernel(cores, group_ref, core_ref, ranks_ref, up_hbm, out_ref, factor_ref, own_ref, sem):
    local, rank, share = out_ref.shape
    at = core_ref[0] * (up_hbm.shape[2] // cores) + group_ref[0] * share
    copy = pltpu.make_async_copy(
        up_hbm.at[:, :, pl.ds(pl.multiple_of(at, share), share)], own_ref, sem
    )
    copy.start()
    copy.wait()
    for a in range(local):
        used = ranks_ref[a]

        def factor(shape, dim):
            scale = jnp.float32(ALPHA) / jnp.full(shape, used, jnp.int32).astype(jnp.float32)
            return jnp.where(iota(shape, dim) < used, scale, 0.0)

        factor_ref[a : a + 1, :] = factor((1, rank), 1)
        out_ref[a] = (own_ref[a].astype(jnp.float32) * factor((rank, 1), 0)).astype(jnp.bfloat16)


def fetch_kernel(group_ref, down_hbm, adapter_hbm, tokens_hbm, share_ref, adapter_ref, tokens_ref, sems):
    share = share_ref.shape[1]
    at = pl.multiple_of(group_ref[0] * share, share)
    copies = [
        pltpu.make_async_copy(down_hbm.at[:, pl.ds(at, share), :], share_ref, sems.at[0]),
        pltpu.make_async_copy(adapter_hbm, adapter_ref, sems.at[1]),
    ]
    parts = sems.shape[0] - 2
    part = tokens_ref.shape[0] // parts
    for i in range(parts):
        here = pl.ds(i * part, part)
        copies.append(
            pltpu.make_async_copy(tokens_hbm.at[here, :], tokens_ref.at[here, :], sems.at[2 + i])
        )
    for copy in copies:
        copy.start()
    for copy in copies:
        copy.wait()


def pick_kernel(pool, local, depth, me_ref, adapter_ref, tokens_ref, *outs):
    rows, width = tokens_ref.shape
    place = slot_places(adapter_ref[...], me_ref[0], pool, local, depth)
    size = outs[0].shape[0]
    slots = len(outs) * size
    picker = jnp.where(iota((slots, rows), 0) == place, 1.0, 0.0).astype(jnp.bfloat16)
    step = 512
    for at in range(0, width, step):
        block = jnp.dot(
            picker, tokens_ref[:, at : at + step], preferred_element_type=jnp.float32
        )
        for j, out in enumerate(outs):
            out[:, at : at + step] = block[j * size : (j + 1) * size].astype(jnp.bfloat16)


def base_kernel(
    core_ref,
    tokens_hbm,
    weight_hbm,
    down_hbm,
    up_hbm,
    theirs_ref,
    mine_ref,
    down_ref,
    up_ref,
    tokens_ref,
    weight_ref,
    other_sems,
    sems,
):
    rows, columns = mine_ref.shape
    steps = sems.shape[1]
    step = tokens_ref.shape[1] // steps
    copies = []
    for half in range(2):
        start = (1 - core_ref[0] if half == 0 else core_ref[0]) * columns
        start = pl.multiple_of(start, columns)
        for k in range(steps):
            copies.append(
                pltpu.make_async_copy(
                    weight_hbm.at[pl.ds(k * step, step), pl.ds(start, columns)],
                    weight_ref.at[half, pl.ds(k * step, step), :],
                    sems.at[half, k],
                )
            )
    tokens_copy = pltpu.make_async_copy(tokens_hbm, tokens_ref, other_sems.at[0])
    own = pl.multiple_of(core_ref[0] * columns, columns)
    factor_copies = [
        pltpu.make_async_copy(down_hbm, down_ref, other_sems.at[1]),
        pltpu.make_async_copy(up_hbm.at[:, :, pl.ds(own, columns)], up_ref, other_sems.at[2]),
    ]
    for copy in [tokens_copy] + copies + factor_copies:
        copy.start()
    tokens_copy.wait()
    for half, out in enumerate((theirs_ref, mine_ref)):
        for k in range(steps):
            copies[half * steps + k].wait()
            term = jnp.dot(
                tokens_ref[:, k * step : (k + 1) * step],
                weight_ref[half, k * step : (k + 1) * step, :],
                preferred_element_type=jnp.float32,
            )
            if k == 0:
                out[...] = term
            else:
                out[...] += term
    for copy in factor_copies:
        copy.wait()


def down_kernel(buffers, groups, local, depth, group_ref, down_ref, *refs):
    order = [0] + far_first(buffers)
    ins = [refs[order.index(j)] for j in range(buffers)]
    shares, out = refs[buffers : buffers + groups], refs[-1]
    rank = out.shape[1]
    share = shares[0].shape[1]
    total = None
    for k in range(groups):
        at = pl.multiple_of((group_ref[0] ^ k) * share, share)
        rows = jnp.concatenate([x[:, pl.ds(at, share)] for x in ins], axis=0)
        factors = [down_ref[a, pl.ds(at, share), :] for a in range(local)]
        factors += [shares[k][a] for a in range(local)]
        term = jnp.dot(
            rows, jnp.concatenate(factors, axis=1), preferred_element_type=jnp.float32
        )
        total = term if total is None else total + term
    which = (iota((total.shape[0], 1), 0) // depth) % (2 * local)
    low = total[:, :rank]
    for i in range(1, 2 * local):
        low = jnp.where(which == i, total[:, i * rank : (i + 1) * rank], low)
    out[...] = low


def up_kernel(
    buffers, groups, local, depth, group_ref, low_ref, other_ref, factor_ref, up_ref, *refs
):
    shares, outs, term_ref = refs[:groups], refs[groups : groups + buffers], refs[-1]
    rows, rank = low_ref.shape
    size = rows // buffers
    columns = up_ref.shape[2]
    share = columns // groups
    which = (iota((rows, 1), 0) // depth) % (2 * local)
    low = low_ref[...] + other_ref[...]
    for a in range(local):
        low = jnp.where(which == a, low * factor_ref[a : a + 1, :], low)
    both = jnp.concatenate(halves(low), axis=0)
    which = jnp.concatenate([which, which], axis=0)
    spread = jnp.concatenate(
        [jnp.where(which == i, both, jnp.zeros_like(both)) for i in range(2 * local)], axis=1
    )
    for k in range(groups):
        at = pl.multiple_of((group_ref[0] ^ k) * share, share)
        up = [up_ref[a, :, pl.ds(at, share)] for a in range(local)]
        up += [shares[k][a] for a in range(local)]
        term = jnp.dot(
            spread, jnp.concatenate(up, axis=0), preferred_element_type=jnp.float32
        )
        term_ref[:, pl.ds(at, share)] = term[:rows] + term[rows:]
    lane = iota((1, LANES), 1)
    for j, out in enumerate(outs):
        term = term_ref[j * size : (j + 1) * size, :]
        top = jnp.max(jnp.abs(term), axis=1, keepdims=True)
        exponent = jnp.ceil(jnp.log2(jnp.maximum(top, 1e-30)) + 1e-3)
        code = jnp.clip(jnp.round(term * jnp.exp2(15.0 - exponent)), -32767.0, 32767.0)
        code = code.astype(jnp.int32)
        biased = exponent.astype(jnp.int32) + EXPONENT_BIAS
        first = code[:, :LANES]
        marked = (first & -2) | ((biased >> jnp.minimum(lane, EXPONENT_BITS - 1)) & 1)
        first = jnp.where(lane < EXPONENT_BITS, marked, first)
        out[:, :LANES] = first.astype(jnp.int16)
        out[:, LANES:] = code[:, LANES:].astype(jnp.int16)


def planes(codes, at, size):
    code = jnp.concatenate([x[:, at : at + size] for x in codes], axis=0).astype(jnp.int32)
    high = (code >> 8).astype(jnp.float32).astype(jnp.bfloat16)
    low = (code & 255).astype(jnp.float32).astype(jnp.bfloat16)
    return high, low


def decoded(picker, plane):
    high = jnp.dot(picker, plane[0], preferred_element_type=jnp.float32)
    low = jnp.dot(picker, plane[1], preferred_element_type=jnp.float32)
    return high * 256.0 + low


def scale_of(first):
    lane = iota((1, LANES), 1)
    bits = first.astype(jnp.int32) & 1
    bits = jnp.where(lane < EXPONENT_BITS, bits << jnp.minimum(lane, EXPONENT_BITS - 1), 0)
    exponent = jnp.sum(bits.astype(jnp.float32), axis=1, keepdims=True) - EXPONENT_BIAS
    return jnp.exp2(exponent - 15.0)


def start_rows_kernel(
    buffers, pool, local, depth, me_ref, adapter_ref, mine_ref, other_ref, own_ref, partial_ref, picker_ref
):
    rows, columns = mine_ref.shape
    size = own_ref.shape[0]
    place = to_column(slot_places(adapter_ref[...], me_ref[0], pool, local, depth))
    picker = jnp.where(iota((rows, size), 1) == place, 1.0, 0.0).astype(jnp.bfloat16)
    scale = scale_of(decoded(picker, planes([own_ref], 0, LANES)))
    for at in range(0, columns, 256):
        term = decoded(picker, planes([own_ref], at, 256)) * scale
        partial_ref[:, at : at + 256] = (
            mine_ref[:, at : at + 256] + other_ref[:, at : at + 256] + term
        )
    slots = (buffers - 1) * size
    picker_ref[...] = jnp.where(iota((rows, slots), 1) == place - size, 1.0, 0.0).astype(
        jnp.bfloat16
    )


def finish_kernel(buffers, partial_ref, picker_ref, cos_ref, sin_ref, gain_ref, *refs):
    order = return_order(buffers)
    ins = [refs[order.index(j)] for j in range(1, buffers)]
    out_hbm, entry_ref, out_ref, sems = refs[-4:]
    rows, columns = partial_ref.shape
    head = cos_ref.shape[1]
    kinds = columns // head
    gain, cosine, sine, picker = gain_ref[...], cos_ref[...], sin_ref[...], picker_ref[...]
    scale = scale_of(decoded(picker, planes(ins, 0, LANES)))
    for at in range(0, columns, 2 * head):
        projected = partial_ref[:, at : at + 2 * head]
        projected = projected + decoded(picker, planes(ins, at, 2 * head)) * scale
        key, value = projected[:, :head], projected[:, head:]
        mean = jnp.mean(key * key, axis=1, keepdims=True)
        normed = key * lax.rsqrt(mean + NORM_EPS) * gain
        rotated = normed * cosine + pltpu.roll(normed, head // 2, 1) * sine
        entry_ref[pl.ds(at // head, rows, stride=kinds), :] = rotated
        entry_ref[pl.ds(at // head + 1, rows, stride=kinds), :] = value
    copies = []
    part = rows * kinds // sems.shape[0]
    for i in range(sems.shape[0]):
        done = pl.ds(i * part, part)
        out_ref[done, :] = entry_ref[done, :].astype(jnp.bfloat16)
        copies.append(pltpu.make_async_copy(out_ref.at[done, :], out_hbm.at[done, :], sems.at[i]))
        copies[-1].start()
    for copy in copies:
        copy.wait()


def body(
    tokens,
    row_adapters,
    positions,
    key_value_weight,
    adapter_down,
    adapter_up,
    ranks,
    key_norm_gain,
):
    pool = lax.axis_size("pool")
    groups = lax.axis_size("groups")
    cores = lax.axis_size("tp")
    rows, width = tokens.shape
    local = adapter_down.shape[0]
    adapters = local * pool
    columns = key_value_weight.shape[1] // cores
    rank = adapter_down.shape[2]
    head = key_norm_gain.shape[0]
    depth = max(2, 2 * rows // adapters)
    buffers = pool // 2
    size = 2 * local * depth
    f32, bf16 = jnp.float32, jnp.bfloat16

    me = lax.axis_index("pool").astype(jnp.int32)[None]
    core = lax.axis_index("tp").astype(jnp.int32)[None]
    group = lax.axis_index("groups").astype(jnp.int32)[None]

    def exchange(x, axis, count, j):
        return lax.ppermute(x, axis, [(p, p ^ j) for p in range(count)])

    def hand_round(share):
        return [share] + [exchange(share, "groups", groups, k) for k in range(1, groups)]

    adapter_row = row_adapters.reshape(1, rows)
    down_share = width // groups
    parts = rows // 16
    down_part, adapter_now, tokens_now = pl.pallas_call(
        fetch_kernel,
        in_specs=[SMEM] + [HBM] * 3,
        out_specs=[VMEM] * 3,
        out_shape=[
            jax.ShapeDtypeStruct((local, down_share, rank), bf16),
            jax.ShapeDtypeStruct((1, rows), jnp.int32),
            jax.ShapeDtypeStruct((rows, width), bf16),
        ],
        scratch_shapes=[pltpu.SemaphoreType.DMA((parts + 2,))],
        compiler_params=params(),
        cost_estimate=cost(0, 4 * (local * rank * down_share + rows * width)),
        name="fetch",
    )(group, in_hbm(adapter_down), in_hbm(adapter_row), in_hbm(tokens))
    picked = pl.pallas_call(
        functools.partial(pick_kernel, pool, local, depth),
        in_specs=[SMEM] + [VMEM] * 2,
        out_specs=[VMEM] * buffers,
        out_shape=[jax.ShapeDtypeStruct((size, width), bf16)] * buffers,
        compiler_params=params(),
        cost_estimate=cost(2 * buffers * size * rows * width, 2 * (rows + buffers * size) * width),
        name="pick",
    )(me, adapter_now, tokens_now)
    far_down = exchange(down_part, "pool", pool, pool // 2)
    up_share = columns // groups
    ranks_now, adapter_up_now, _ = lax.optimization_barrier((ranks, adapter_up, picked))
    up_part, factor = pl.pallas_call(
        functools.partial(up_share_kernel, cores),
        in_specs=[SMEM] * 3 + [HBM],
        out_specs=[VMEM] * 2,
        out_shape=[
            jax.ShapeDtypeStruct((local, rank, up_share), bf16),
            jax.ShapeDtypeStruct((local, rank), f32),
        ],
        scratch_shapes=[
            pltpu.VMEM((local, rank, up_share), bf16),
            pltpu.SemaphoreType.DMA,
        ],
        compiler_params=params(),
        cost_estimate=cost(local * rank * up_share, 4 * local * rank * up_share),
        name="up_share",
    )(group, core, ranks_now, in_hbm(adapter_up_now))
    far_up = exchange(up_part, "pool", pool, pool // 2)

    order = far_first(buffers)
    early, late = order[:-1], order[-1:]
    late_rows, _ = lax.optimization_barrier(([picked[j] for j in late], up_part))
    leaving = [picked[j] for j in early] + late_rows
    arrived = [picked[0]] + [exchange(x, "pool", pool, j) for x, j in zip(leaving, order)]

    steps = 5
    theirs, mine, own_down, own_up = pl.pallas_call(
        base_kernel,
        in_specs=[SMEM] + [HBM] * 4,
        out_specs=[VMEM] * 4,
        out_shape=[jax.ShapeDtypeStruct((rows, columns), f32)] * 2
        + [
            jax.ShapeDtypeStruct(adapter_down.shape, bf16),
            jax.ShapeDtypeStruct((local, rank, columns), bf16),
        ],
        scratch_shapes=[
            pltpu.VMEM((rows, width), bf16),
            pltpu.VMEM((2, width, columns), bf16),
            pltpu.SemaphoreType.DMA((3,)),
            pltpu.SemaphoreType.DMA((2, steps)),
        ],
        compiler_params=params(),
        cost_estimate=cost(4 * rows * width * columns, 4 * width * columns),
        name="base",
    )(
        core,
        in_hbm(tokens),
        in_hbm(key_value_weight),
        in_hbm(adapter_down),
        in_hbm(adapter_up),
    )
    far_down, theirs = lax.optimization_barrier((far_down, theirs))
    far_downs = hand_round(far_down)
    far_up, _ = lax.optimization_barrier((far_up, far_down))
    far_ups = hand_round(far_up)
    half_dim = head // 2
    frequency = jnp.power(
        f32(ROPE_THETA), -jnp.arange(half_dim, dtype=f32) * (2.0 / head)
    )
    angles = positions.astype(f32)[:, None] * frequency[None, :]
    cosine, sine = jnp.cos(angles), jnp.sin(angles)
    cosine = jnp.concatenate([cosine, cosine], axis=1)
    sine = jnp.concatenate([-sine, sine], axis=1)

    far_up, arrived[1], theirs = lax.optimization_barrier((far_up, arrived[1], theirs))
    other = exchange(theirs, "tp", cores, 1)
    arrived, mine, cosine, sine = lax.optimization_barrier((arrived, mine, cosine, sine))
    slots = buffers * size
    low = pl.pallas_call(
        functools.partial(down_kernel, buffers, groups, local, depth),
        in_specs=[SMEM] + [VMEM] * (1 + buffers + groups),
        out_specs=VMEM,
        out_shape=jax.ShapeDtypeStruct((slots, rank), f32),
        compiler_params=params(),
        cost_estimate=cost(4 * local * slots * rank * width, 2 * (slots + rank) * width),
        name="down",
    )(group, own_down, *arrived, *far_downs)
    low_other = exchange(low, "tp", cores, 1)

    terms = pl.pallas_call(
        functools.partial(up_kernel, buffers, groups, local, depth),
        in_specs=[SMEM] + [VMEM] * (4 + groups),
        out_specs=[VMEM] * buffers,
        out_shape=[jax.ShapeDtypeStruct((size, columns), jnp.int16)] * buffers,
        scratch_shapes=[pltpu.VMEM((slots, columns), f32)],
        compiler_params=params(),
        cost_estimate=cost(8 * local * slots * rank * columns, 2 * slots * columns),
        name="up",
    )(group, low, low_other, factor, own_up, *far_ups)
    order = return_order(buffers)
    returned = [exchange(terms[j], "pool", pool, j) for j in order]

    partial, picker = pl.pallas_call(
        functools.partial(start_rows_kernel, buffers, pool, local, depth),
        in_specs=[SMEM] + [VMEM] * 4,
        out_specs=[VMEM] * 2,
        out_shape=[
            jax.ShapeDtypeStruct((rows, columns), f32),
            jax.ShapeDtypeStruct((rows, slots - size), bf16),
        ],
        compiler_params=params(),
        cost_estimate=cost(4 * rows * size * columns, 12 * rows * columns),
        name="start_rows",
    )(me, adapter_row, mine, other, terms[0])
    out = pl.pallas_call(
        functools.partial(finish_kernel, buffers),
        in_specs=[VMEM] * (4 + buffers),
        out_specs=HBM,
        out_shape=jax.ShapeDtypeStruct((rows * columns // head, head), bf16),
        scratch_shapes=[
            pltpu.VMEM((rows * columns // head, head), f32),
            pltpu.VMEM((rows * columns // head, head), bf16),
            pltpu.SemaphoreType.DMA((4,)),
        ],
        compiler_params=params(),
        cost_estimate=cost(4 * rows * slots * columns, 2 * slots * columns),
        name="finish",
    )(partial, picker, cosine, sine, key_norm_gain.astype(f32)[None, :], *returned)
    return out.reshape(rows, columns // (2 * head), 2, head)


def solution(mesh):
    return jax.shard_map(
        body,
        mesh=mesh,
        in_specs=(
            P(("groups", "pool"), "tp"),
            P(("groups", "pool"), None),
            P(("groups", "pool")),
            P("tp", None),
            P("pool", "tp", None),
            P("pool", None, None),
            P("pool"),
            P(),
        ),
        out_specs=P(("groups", "pool"), "tp", None, None),
        check_vma=False,
    )
```

```python
import functools

import jax
import jax.numpy as jnp
from jax import lax
from jax.experimental import pallas as pl
from jax.experimental.pallas import tpu as pltpu
from jax.sharding import PartitionSpec as P

ALPHA = 32
ROPE_THETA = 1000000.0
NORM_EPS = 1e-06
VMEM_LIMIT = 48 * 1024 * 1024
LANES = 128
EXPONENT_BITS = 8
EXPONENT_BIAS = 128

VMEM = pl.BlockSpec(memory_space=pltpu.VMEM)
HBM = pl.BlockSpec(memory_space=pltpu.HBM)
SMEM = pl.BlockSpec(memory_space=pltpu.SMEM)


def params(**kw):
    return pltpu.CompilerParams(vmem_limit_bytes=VMEM_LIMIT, **kw)


def cost(flops, bytes_accessed):
    return pl.CostEstimate(flops=flops, bytes_accessed=bytes_accessed, transcendentals=0)


def in_hbm(x):
    return pltpu.with_memory_space_constraint(x, pltpu.HBM)


def iota(shape, dim):
    return lax.broadcasted_iota(jnp.int32, shape, dim)


def to_column(row):
    n = row.shape[1]
    return jnp.sum(
        jnp.where(iota((n, n), 0) == iota((n, n), 1), row, 0), axis=1, keepdims=True
    )


def slot_places(row, me, pool, local, depth):
    n = row.shape[1]
    column = to_column(row)
    earlier = (column == row) & (iota((n, n), 0) < iota((n, n), 1))
    slot = jnp.sum(jnp.where(earlier, 1, 0), axis=0, keepdims=True)
    holder = row // local
    apart = holder ^ me
    buffer, far = apart % (pool // 2), apart // (pool // 2)
    return ((buffer * 2 + far) * local + (row - holder * local)) * depth + slot


def far_first(count):
    return sorted(range(1, count), key=lambda j: (-bin(j).count("1"), -j))


def return_order(count):
    order = far_first(count)
    return order[-1:] + order[:-1]


def halves(x):
    high = x.astype(jnp.bfloat16)
    low = (x - high.astype(jnp.float32)).astype(jnp.bfloat16)
    return high, low


def scale_up_kernel(ranks_ref, own_ref, out_ref, factor_ref):
    local, rank, _ = out_ref.shape
    for a in range(local):
        used = ranks_ref[a]

        def factor(shape, dim):
            scale = jnp.float32(ALPHA) / jnp.full(shape, used, jnp.int32).astype(jnp.float32)
            return jnp.where(iota(shape, dim) < used, scale, 0.0)

        factor_ref[a : a + 1, :] = factor((1, rank), 1)
        out_ref[a] = (own_ref[a].astype(jnp.float32) * factor((rank, 1), 0)).astype(jnp.bfloat16)


def fetch_kernel(
    columns,
    group_ref,
    core_ref,
    down_hbm,
    up_hbm,
    adapter_hbm,
    tokens_hbm,
    share_ref,
    up_ref,
    adapter_ref,
    tokens_ref,
    sems,
):
    share, up_share = share_ref.shape[1], up_ref.shape[2]
    up_at = pl.multiple_of(core_ref[0] * columns + group_ref[0] * up_share, up_share)
    at = pl.multiple_of(group_ref[0] * share, share)
    copies = [
        pltpu.make_async_copy(down_hbm.at[:, pl.ds(at, share), :], share_ref, sems.at[0]),
        pltpu.make_async_copy(adapter_hbm, adapter_ref, sems.at[1]),
    ]
    parts = sems.shape[0] - 3
    part = tokens_ref.shape[0] // parts
    for i in range(parts):
        here = pl.ds(i * part, part)
        copies.append(
            pltpu.make_async_copy(tokens_hbm.at[here, :], tokens_ref.at[here, :], sems.at[3 + i])
        )
    copies.append(
        pltpu.make_async_copy(up_hbm.at[:, :, pl.ds(up_at, up_share)], up_ref, sems.at[2])
    )
    for copy in copies:
        copy.start()
    for copy in copies:
        copy.wait()


def pick_kernel(pool, local, depth, me_ref, adapter_ref, tokens_ref, *outs):
    rows, width = tokens_ref.shape
    place = slot_places(adapter_ref[...], me_ref[0], pool, local, depth)
    size = outs[0].shape[0]
    slots = len(outs) * size
    picker = jnp.where(iota((slots, rows), 0) == place, 1.0, 0.0).astype(jnp.bfloat16)
    step = 512
    for at in range(0, width, step):
        block = jnp.dot(
            picker, tokens_ref[:, at : at + step], preferred_element_type=jnp.float32
        )
        for j, out in enumerate(outs):
            out[:, at : at + step] = block[j * size : (j + 1) * size].astype(jnp.bfloat16)


def base_kernel(
    core_ref,
    tokens_hbm,
    weight_hbm,
    down_hbm,
    up_hbm,
    theirs_ref,
    mine_ref,
    down_ref,
    up_ref,
    tokens_ref,
    weight_ref,
    other_sems,
    sems,
):
    rows, columns = mine_ref.shape
    steps = sems.shape[1]
    step = tokens_ref.shape[1] // steps
    copies = []
    for half in range(2):
        start = (1 - core_ref[0] if half == 0 else core_ref[0]) * columns
        start = pl.multiple_of(start, columns)
        for k in range(steps):
            copies.append(
                pltpu.make_async_copy(
                    weight_hbm.at[pl.ds(k * step, step), pl.ds(start, columns)],
                    weight_ref.at[half, pl.ds(k * step, step), :],
                    sems.at[half, k],
                )
            )
    tokens_copy = pltpu.make_async_copy(tokens_hbm, tokens_ref, other_sems.at[0])
    own = pl.multiple_of(core_ref[0] * columns, columns)
    factor_copies = [
        pltpu.make_async_copy(down_hbm, down_ref, other_sems.at[1]),
        pltpu.make_async_copy(up_hbm.at[:, :, pl.ds(own, columns)], up_ref, other_sems.at[2]),
    ]
    for copy in [tokens_copy] + copies + factor_copies:
        copy.start()
    tokens_copy.wait()
    for half, out in enumerate((theirs_ref, mine_ref)):
        for k in range(steps):
            copies[half * steps + k].wait()
            term = jnp.dot(
                tokens_ref[:, k * step : (k + 1) * step],
                weight_ref[half, k * step : (k + 1) * step, :],
                preferred_element_type=jnp.float32,
            )
            if k == 0:
                out[...] = term
            else:
                out[...] += term
    for copy in factor_copies:
        copy.wait()


def down_kernel(buffers, groups, local, depth, group_ref, down_ref, *refs):
    order = [0] + far_first(buffers)
    ins = [refs[order.index(j)] for j in range(buffers)]
    shares, out = refs[buffers : buffers + groups], refs[-1]
    rank = out.shape[1]
    share = shares[0].shape[1]
    total = None
    for k in range(groups):
        at = pl.multiple_of((group_ref[0] ^ k) * share, share)
        rows = jnp.concatenate([x[:, pl.ds(at, share)] for x in ins], axis=0)
        factors = [down_ref[a, pl.ds(at, share), :] for a in range(local)]
        factors += [shares[k][a] for a in range(local)]
        term = jnp.dot(
            rows, jnp.concatenate(factors, axis=1), preferred_element_type=jnp.float32
        )
        total = term if total is None else total + term
    which = (iota((total.shape[0], 1), 0) // depth) % (2 * local)
    low = total[:, :rank]
    for i in range(1, 2 * local):
        low = jnp.where(which == i, total[:, i * rank : (i + 1) * rank], low)
    out[...] = low


def up_kernel(
    buffers, groups, local, depth, group_ref, low_ref, other_ref, factor_ref, up_ref, *refs
):
    shares, outs, term_ref = refs[:groups], refs[groups : groups + buffers], refs[-1]
    rows, rank = low_ref.shape
    size = rows // buffers
    columns = up_ref.shape[2]
    share = columns // groups
    which = (iota((rows, 1), 0) // depth) % (2 * local)
    low = low_ref[...] + other_ref[...]
    for a in range(local):
        low = jnp.where(which == a, low * factor_ref[a : a + 1, :], low)
    both = jnp.concatenate(halves(low), axis=0)
    which = jnp.concatenate([which, which], axis=0)
    spread = jnp.concatenate(
        [jnp.where(which == i, both, jnp.zeros_like(both)) for i in range(2 * local)], axis=1
    )
    for k in range(groups):
        at = pl.multiple_of((group_ref[0] ^ k) * share, share)
        up = [up_ref[a, :, pl.ds(at, share)] for a in range(local)]
        up += [shares[k][a] for a in range(local)]
        term = jnp.dot(
            spread, jnp.concatenate(up, axis=0), preferred_element_type=jnp.float32
        )
        term_ref[:, pl.ds(at, share)] = term[:rows] + term[rows:]
    lane = iota((1, LANES), 1)
    for j, out in enumerate(outs):
        term = term_ref[j * size : (j + 1) * size, :]
        top = jnp.max(jnp.abs(term), axis=1, keepdims=True)
        exponent = jnp.ceil(jnp.log2(jnp.maximum(top, 1e-30)) + 1e-3)
        code = jnp.clip(jnp.round(term * jnp.exp2(15.0 - exponent)), -32767.0, 32767.0)
        code = code.astype(jnp.int32)
        biased = exponent.astype(jnp.int32) + EXPONENT_BIAS
        first = code[:, :LANES]
        marked = (first & -2) | ((biased >> jnp.minimum(lane, EXPONENT_BITS - 1)) & 1)
        first = jnp.where(lane < EXPONENT_BITS, marked, first)
        out[:, :LANES] = first.astype(jnp.int16)
        out[:, LANES:] = code[:, LANES:].astype(jnp.int16)


def planes(codes, at, size):
    code = jnp.concatenate([x[:, at : at + size] for x in codes], axis=0).astype(jnp.int32)
    high = (code >> 8).astype(jnp.float32).astype(jnp.bfloat16)
    low = (code & 255).astype(jnp.float32).astype(jnp.bfloat16)
    return high, low


def decoded(picker, plane):
    high = jnp.dot(picker, plane[0], preferred_element_type=jnp.float32)
    low = jnp.dot(picker, plane[1], preferred_element_type=jnp.float32)
    return high * 256.0 + low


def scale_of(first):
    lane = iota((1, LANES), 1)
    bits = first.astype(jnp.int32) & 1
    bits = jnp.where(lane < EXPONENT_BITS, bits << jnp.minimum(lane, EXPONENT_BITS - 1), 0)
    exponent = jnp.sum(bits.astype(jnp.float32), axis=1, keepdims=True) - EXPONENT_BIAS
    return jnp.exp2(exponent - 15.0)


def start_rows_kernel(
    buffers, pool, local, depth, me_ref, adapter_ref, mine_ref, other_ref, own_ref, partial_ref, picker_ref
):
    rows, columns = mine_ref.shape
    size = own_ref.shape[0]
    place = to_column(slot_places(adapter_ref[...], me_ref[0], pool, local, depth))
    picker = jnp.where(iota((rows, size), 1) == place, 1.0, 0.0).astype(jnp.bfloat16)
    scale = scale_of(decoded(picker, planes([own_ref], 0, LANES)))
    for at in range(0, columns, 256):
        term = decoded(picker, planes([own_ref], at, 256)) * scale
        partial_ref[:, at : at + 256] = (
            mine_ref[:, at : at + 256] + other_ref[:, at : at + 256] + term
        )
    slots = (buffers - 1) * size
    picker_ref[...] = jnp.where(iota((rows, slots), 1) == place - size, 1.0, 0.0).astype(
        jnp.bfloat16
    )


def finish_kernel(buffers, partial_ref, picker_ref, cos_ref, sin_ref, gain_ref, *refs):
    order = return_order(buffers)
    ins = [refs[order.index(j)] for j in range(1, buffers)]
    out_hbm, entry_ref, out_ref, sems = refs[-4:]
    rows, columns = partial_ref.shape
    head = cos_ref.shape[1]
    kinds = columns // head
    gain, cosine, sine, picker = gain_ref[...], cos_ref[...], sin_ref[...], picker_ref[...]
    scale = scale_of(decoded(picker, planes(ins, 0, LANES)))
    for at in range(0, columns, 2 * head):
        projected = partial_ref[:, at : at + 2 * head]
        projected = projected + decoded(picker, planes(ins, at, 2 * head)) * scale
        key, value = projected[:, :head], projected[:, head:]
        mean = jnp.mean(key * key, axis=1, keepdims=True)
        normed = key * lax.rsqrt(mean + NORM_EPS) * gain
        rotated = normed * cosine + pltpu.roll(normed, head // 2, 1) * sine
        entry_ref[pl.ds(at // head, rows, stride=kinds), :] = rotated
        entry_ref[pl.ds(at // head + 1, rows, stride=kinds), :] = value
    copies = []
    part = rows * kinds // sems.shape[0]
    for i in range(sems.shape[0]):
        done = pl.ds(i * part, part)
        out_ref[done, :] = entry_ref[done, :].astype(jnp.bfloat16)
        copies.append(pltpu.make_async_copy(out_ref.at[done, :], out_hbm.at[done, :], sems.at[i]))
        copies[-1].start()
    for copy in copies:
        copy.wait()


def body(
    tokens,
    row_adapters,
    positions,
    key_value_weight,
    adapter_down,
    adapter_up,
    ranks,
    key_norm_gain,
):
    pool = lax.axis_size("pool")
    groups = lax.axis_size("groups")
    cores = lax.axis_size("tp")
    rows, width = tokens.shape
    local = adapter_down.shape[0]
    adapters = local * pool
    columns = key_value_weight.shape[1] // cores
    rank = adapter_down.shape[2]
    head = key_norm_gain.shape[0]
    depth = max(2, 2 * rows // adapters)
    buffers = pool // 2
    size = 2 * local * depth
    f32, bf16 = jnp.float32, jnp.bfloat16

    me = lax.axis_index("pool").astype(jnp.int32)[None]
    core = lax.axis_index("tp").astype(jnp.int32)[None]
    group = lax.axis_index("groups").astype(jnp.int32)[None]

    def exchange(x, axis, count, j):
        return lax.ppermute(x, axis, [(p, p ^ j) for p in range(count)])

    def hand_round(share):
        return [share] + [exchange(share, "groups", groups, k) for k in range(1, groups)]

    adapter_row = row_adapters.reshape(1, rows)
    down_share = width // groups
    parts = rows // 16
    up_share = columns // groups
    down_part, up_own, adapter_now, tokens_now = pl.pallas_call(
        functools.partial(fetch_kernel, columns),
        in_specs=[SMEM] * 2 + [HBM] * 4,
        out_specs=[VMEM] * 4,
        out_shape=[
            jax.ShapeDtypeStruct((local, down_share, rank), bf16),
            jax.ShapeDtypeStruct((local, rank, up_share), bf16),
            jax.ShapeDtypeStruct((1, rows), jnp.int32),
            jax.ShapeDtypeStruct((rows, width), bf16),
        ],
        scratch_shapes=[pltpu.SemaphoreType.DMA((parts + 3,))],
        compiler_params=params(),
        cost_estimate=cost(0, 4 * (local * rank * down_share + rows * width)),
        name="fetch",
    )(
        group,
        core,
        in_hbm(adapter_down),
        in_hbm(adapter_up),
        in_hbm(adapter_row),
        in_hbm(tokens),
    )
    picked = pl.pallas_call(
        functools.partial(pick_kernel, pool, local, depth),
        in_specs=[SMEM] + [VMEM] * 2,
        out_specs=[VMEM] * buffers,
        out_shape=[jax.ShapeDtypeStruct((size, width), bf16)] * buffers,
        compiler_params=params(),
        cost_estimate=cost(2 * buffers * size * rows * width, 2 * (rows + buffers * size) * width),
        name="pick",
    )(me, adapter_now, tokens_now)
    far_down = exchange(down_part, "pool", pool, pool // 2)
    ranks_now, up_own, _ = lax.optimization_barrier((ranks, up_own, picked))
    up_part, factor = pl.pallas_call(
        scale_up_kernel,
        in_specs=[SMEM, VMEM],
        out_specs=[VMEM] * 2,
        out_shape=[
            jax.ShapeDtypeStruct((local, rank, up_share), bf16),
            jax.ShapeDtypeStruct((local, rank), f32),
        ],
        compiler_params=params(),
        cost_estimate=cost(local * rank * up_share, 4 * local * rank * up_share),
        name="scale_up",
    )(ranks_now, up_own)
    far_up = exchange(up_part, "pool", pool, pool // 2)

    order = far_first(buffers)
    early, late = order[:1], order[1:]
    late_rows, _ = lax.optimization_barrier(([picked[j] for j in late], up_part))
    leaving = [picked[j] for j in early] + late_rows
    arrived = [picked[0]] + [exchange(x, "pool", pool, j) for x, j in zip(leaving, order)]

    steps = 5
    theirs, mine, own_down, own_up = pl.pallas_call(
        base_kernel,
        in_specs=[SMEM] + [HBM] * 4,
        out_specs=[VMEM] * 4,
        out_shape=[jax.ShapeDtypeStruct((rows, columns), f32)] * 2
        + [
            jax.ShapeDtypeStruct(adapter_down.shape, bf16),
            jax.ShapeDtypeStruct((local, rank, columns), bf16),
        ],
        scratch_shapes=[
            pltpu.VMEM((rows, width), bf16),
            pltpu.VMEM((2, width, columns), bf16),
            pltpu.SemaphoreType.DMA((3,)),
            pltpu.SemaphoreType.DMA((2, steps)),
        ],
        compiler_params=params(),
        cost_estimate=cost(4 * rows * width * columns, 4 * width * columns),
        name="base",
    )(
        core,
        in_hbm(tokens),
        in_hbm(key_value_weight),
        in_hbm(adapter_down),
        in_hbm(adapter_up),
    )
    far_down, theirs = lax.optimization_barrier((far_down, theirs))
    far_downs = hand_round(far_down)
    far_up, _ = lax.optimization_barrier((far_up, far_down))
    far_ups = hand_round(far_up)
    half_dim = head // 2
    frequency = jnp.power(
        f32(ROPE_THETA), -jnp.arange(half_dim, dtype=f32) * (2.0 / head)
    )
    angles = positions.astype(f32)[:, None] * frequency[None, :]
    cosine, sine = jnp.cos(angles), jnp.sin(angles)
    cosine = jnp.concatenate([cosine, cosine], axis=1)
    sine = jnp.concatenate([-sine, sine], axis=1)

    far_up, arrived[1], theirs = lax.optimization_barrier((far_up, arrived[1], theirs))
    other = exchange(theirs, "tp", cores, 1)
    arrived, mine, cosine, sine = lax.optimization_barrier((arrived, mine, cosine, sine))
    slots = buffers * size
    low = pl.pallas_call(
        functools.partial(down_kernel, buffers, groups, local, depth),
        in_specs=[SMEM] + [VMEM] * (1 + buffers + groups),
        out_specs=VMEM,
        out_shape=jax.ShapeDtypeStruct((slots, rank), f32),
        compiler_params=params(),
        cost_estimate=cost(4 * local * slots * rank * width, 2 * (slots + rank) * width),
        name="down",
    )(group, own_down, *arrived, *far_downs)
    low_other = exchange(low, "tp", cores, 1)

    terms = pl.pallas_call(
        functools.partial(up_kernel, buffers, groups, local, depth),
        in_specs=[SMEM] + [VMEM] * (4 + groups),
        out_specs=[VMEM] * buffers,
        out_shape=[jax.ShapeDtypeStruct((size, columns), jnp.int16)] * buffers,
        scratch_shapes=[pltpu.VMEM((slots, columns), f32)],
        compiler_params=params(),
        cost_estimate=cost(8 * local * slots * rank * columns, 2 * slots * columns),
        name="up",
    )(group, low, low_other, factor, own_up, *far_ups)
    order = return_order(buffers)
    returned = [exchange(terms[j], "pool", pool, j) for j in order]

    partial, picker = pl.pallas_call(
        functools.partial(start_rows_kernel, buffers, pool, local, depth),
        in_specs=[SMEM] + [VMEM] * 4,
        out_specs=[VMEM] * 2,
        out_shape=[
            jax.ShapeDtypeStruct((rows, columns), f32),
            jax.ShapeDtypeStruct((rows, slots - size), bf16),
        ],
        compiler_params=params(),
        cost_estimate=cost(4 * rows * size * columns, 12 * rows * columns),
        name="start_rows",
    )(me, adapter_row, mine, other, terms[0])
    out = pl.pallas_call(
        functools.partial(finish_kernel, buffers),
        in_specs=[VMEM] * (4 + buffers),
        out_specs=HBM,
        out_shape=jax.ShapeDtypeStruct((rows * columns // head, head), bf16),
        scratch_shapes=[
            pltpu.VMEM((rows * columns // head, head), f32),
            pltpu.VMEM((rows * columns // head, head), bf16),
            pltpu.SemaphoreType.DMA((4,)),
        ],
        compiler_params=params(),
        cost_estimate=cost(4 * rows * slots * columns, 2 * slots * columns),
        name="finish",
    )(partial, picker, cosine, sine, key_norm_gain.astype(f32)[None, :], *returned)
    return out.reshape(rows, columns // (2 * head), 2, head)


def solution(mesh):
    return jax.shard_map(
        body,
        mesh=mesh,
        in_specs=(
            P(("groups", "pool"), "tp"),
            P(("groups", "pool"), None),
            P(("groups", "pool")),
            P("tp", None),
            P("pool", "tp", None),
            P("pool", None, None),
            P("pool"),
            P(),
        ),
        out_specs=P(("groups", "pool"), "tp", None, None),
        check_vma=False,
    )
```

```python
import functools

import jax
import jax.numpy as jnp
from jax import lax
from jax.experimental import pallas as pl
from jax.experimental.pallas import tpu as pltpu
from jax.sharding import PartitionSpec as P

ALPHA = 32
ROPE_THETA = 1000000.0
NORM_EPS = 1e-06
VMEM_LIMIT = 48 * 1024 * 1024
LANES = 128
EXPONENT_BITS = 8
EXPONENT_BIAS = 128

VMEM = pl.BlockSpec(memory_space=pltpu.VMEM)
HBM = pl.BlockSpec(memory_space=pltpu.HBM)
SMEM = pl.BlockSpec(memory_space=pltpu.SMEM)


def params(**kw):
    return pltpu.CompilerParams(vmem_limit_bytes=VMEM_LIMIT, **kw)


def cost(flops, bytes_accessed):
    return pl.CostEstimate(flops=flops, bytes_accessed=bytes_accessed, transcendentals=0)


def in_hbm(x):
    return pltpu.with_memory_space_constraint(x, pltpu.HBM)


def iota(shape, dim):
    return lax.broadcasted_iota(jnp.int32, shape, dim)


def to_column(row):
    n = row.shape[1]
    return jnp.sum(
        jnp.where(iota((n, n), 0) == iota((n, n), 1), row, 0), axis=1, keepdims=True
    )


def slot_places(row, me, pool, local, depth):
    n = row.shape[1]
    column = to_column(row)
    earlier = (column == row) & (iota((n, n), 0) < iota((n, n), 1))
    slot = jnp.sum(jnp.where(earlier, 1, 0), axis=0, keepdims=True)
    holder = row // local
    apart = holder ^ me
    buffer, far = apart % (pool // 2), apart // (pool // 2)
    return ((buffer * 2 + far) * local + (row - holder * local)) * depth + slot


def far_first(count):
    return sorted(range(1, count), key=lambda j: (-bin(j).count("1"), -j))


def return_order(count):
    order = far_first(count)
    return order[-1:] + order[:-1]


def halves(x):
    high = x.astype(jnp.bfloat16)
    low = (x - high.astype(jnp.float32)).astype(jnp.bfloat16)
    return high, low


def scale_up_kernel(ranks_ref, own_ref, out_ref, factor_ref):
    local, rank, _ = out_ref.shape
    for a in range(local):
        used = ranks_ref[a]

        def factor(shape, dim):
            scale = jnp.float32(ALPHA) / jnp.full(shape, used, jnp.int32).astype(jnp.float32)
            return jnp.where(iota(shape, dim) < used, scale, 0.0)

        factor_ref[a : a + 1, :] = factor((1, rank), 1)
        out_ref[a] = (own_ref[a].astype(jnp.float32) * factor((rank, 1), 0)).astype(jnp.bfloat16)


def fetch_kernel(
    columns,
    group_ref,
    core_ref,
    down_hbm,
    up_hbm,
    adapter_hbm,
    tokens_hbm,
    share_ref,
    up_ref,
    adapter_ref,
    tokens_ref,
    sems,
):
    share, up_share = share_ref.shape[1], up_ref.shape[2]
    up_at = pl.multiple_of(core_ref[0] * columns + group_ref[0] * up_share, up_share)
    at = pl.multiple_of(group_ref[0] * share, share)
    copies = [
        pltpu.make_async_copy(down_hbm.at[:, pl.ds(at, share), :], share_ref, sems.at[0]),
        pltpu.make_async_copy(adapter_hbm, adapter_ref, sems.at[1]),
    ]
    parts = sems.shape[0] - 3
    part = tokens_ref.shape[0] // parts
    for i in range(parts):
        here = pl.ds(i * part, part)
        copies.append(
            pltpu.make_async_copy(tokens_hbm.at[here, :], tokens_ref.at[here, :], sems.at[3 + i])
        )
    copies.append(
        pltpu.make_async_copy(up_hbm.at[:, :, pl.ds(up_at, up_share)], up_ref, sems.at[2])
    )
    for copy in copies:
        copy.start()
    for copy in copies:
        copy.wait()


def pick_kernel(pool, local, depth, me_ref, adapter_ref, tokens_ref, *outs):
    rows, width = tokens_ref.shape
    place = slot_places(adapter_ref[...], me_ref[0], pool, local, depth)
    size = outs[0].shape[0]
    slots = len(outs) * size
    picker = jnp.where(iota((slots, rows), 0) == place, 1.0, 0.0).astype(jnp.bfloat16)
    step = 512
    for at in range(0, width, step):
        block = jnp.dot(
            picker, tokens_ref[:, at : at + step], preferred_element_type=jnp.float32
        )
        for j, out in enumerate(outs):
            out[:, at : at + step] = block[j * size : (j + 1) * size].astype(jnp.bfloat16)


def base_kernel(
    core_ref,
    tokens_hbm,
    weight_hbm,
    down_hbm,
    up_hbm,
    theirs_ref,
    mine_ref,
    down_ref,
    up_ref,
    tokens_ref,
    weight_ref,
    other_sems,
    sems,
):
    rows, columns = mine_ref.shape
    steps = sems.shape[1]
    step = tokens_ref.shape[1] // steps
    copies = []
    for half in range(2):
        start = (1 - core_ref[0] if half == 0 else core_ref[0]) * columns
        start = pl.multiple_of(start, columns)
        for k in range(steps):
            copies.append(
                pltpu.make_async_copy(
                    weight_hbm.at[pl.ds(k * step, step), pl.ds(start, columns)],
                    weight_ref.at[half, pl.ds(k * step, step), :],
                    sems.at[half, k],
                )
            )
    tokens_copy = pltpu.make_async_copy(tokens_hbm, tokens_ref, other_sems.at[0])
    own = pl.multiple_of(core_ref[0] * columns, columns)
    factor_copies = [
        pltpu.make_async_copy(down_hbm, down_ref, other_sems.at[1]),
        pltpu.make_async_copy(up_hbm.at[:, :, pl.ds(own, columns)], up_ref, other_sems.at[2]),
    ]
    for copy in [tokens_copy] + copies + factor_copies:
        copy.start()
    tokens_copy.wait()
    for half, out in enumerate((theirs_ref, mine_ref)):
        for k in range(steps):
            copies[half * steps + k].wait()
            term = jnp.dot(
                tokens_ref[:, k * step : (k + 1) * step],
                weight_ref[half, k * step : (k + 1) * step, :],
                preferred_element_type=jnp.float32,
            )
            if k == 0:
                out[...] = term
            else:
                out[...] += term
    for copy in factor_copies:
        copy.wait()


def down_kernel(buffers, groups, local, depth, group_ref, down_ref, *refs):
    order = [0] + far_first(buffers)
    ins = [refs[order.index(j)] for j in range(buffers)]
    shares, out = refs[buffers : buffers + groups], refs[-1]
    rank = out.shape[1]
    share = shares[0].shape[1]
    total = None
    for k in range(groups):
        at = pl.multiple_of((group_ref[0] ^ k) * share, share)
        rows = jnp.concatenate([x[:, pl.ds(at, share)] for x in ins], axis=0)
        factors = [down_ref[a, pl.ds(at, share), :] for a in range(local)]
        factors += [shares[k][a] for a in range(local)]
        term = jnp.dot(
            rows, jnp.concatenate(factors, axis=1), preferred_element_type=jnp.float32
        )
        total = term if total is None else total + term
    which = (iota((total.shape[0], 1), 0) // depth) % (2 * local)
    low = total[:, :rank]
    for i in range(1, 2 * local):
        low = jnp.where(which == i, total[:, i * rank : (i + 1) * rank], low)
    out[...] = low


def up_kernel(
    buffers, groups, local, depth, group_ref, low_ref, other_ref, factor_ref, up_ref, *refs
):
    shares, outs, term_ref = refs[:groups], refs[groups : groups + buffers], refs[-1]
    rows, rank = low_ref.shape
    size = rows // buffers
    columns = up_ref.shape[2]
    share = columns // groups
    which = (iota((rows, 1), 0) // depth) % (2 * local)
    low = low_ref[...] + other_ref[...]
    for a in range(local):
        low = jnp.where(which == a, low * factor_ref[a : a + 1, :], low)
    both = jnp.concatenate(halves(low), axis=0)
    which = jnp.concatenate([which, which], axis=0)
    spread = jnp.concatenate(
        [jnp.where(which == i, both, jnp.zeros_like(both)) for i in range(2 * local)], axis=1
    )
    for k in range(groups):
        at = pl.multiple_of((group_ref[0] ^ k) * share, share)
        up = [up_ref[a, :, pl.ds(at, share)] for a in range(local)]
        up += [shares[k][a] for a in range(local)]
        term = jnp.dot(
            spread, jnp.concatenate(up, axis=0), preferred_element_type=jnp.float32
        )
        term_ref[:, pl.ds(at, share)] = term[:rows] + term[rows:]
    lane = iota((1, LANES), 1)
    for j, out in enumerate(outs):
        term = term_ref[j * size : (j + 1) * size, :]
        top = jnp.max(jnp.abs(term), axis=1, keepdims=True)
        exponent = jnp.ceil(jnp.log2(jnp.maximum(top, 1e-30)) + 1e-3)
        code = jnp.round(term * jnp.exp2(15.0 - exponent)).astype(jnp.int32)
        biased = exponent.astype(jnp.int32) + EXPONENT_BIAS
        first = code[:, :LANES]
        marked = (first & -2) | ((biased >> jnp.minimum(lane, EXPONENT_BITS - 1)) & 1)
        first = jnp.where(lane < EXPONENT_BITS, marked, first)
        out[:, :LANES] = first.astype(jnp.int16)
        out[:, LANES:] = code[:, LANES:].astype(jnp.int16)


def planes(codes, at, size):
    code = jnp.concatenate([x[:, at : at + size] for x in codes], axis=0).astype(jnp.int32)
    high = (code >> 8).astype(jnp.float32).astype(jnp.bfloat16)
    low = (code & 255).astype(jnp.float32).astype(jnp.bfloat16)
    return high, low


def decoded(picker, plane):
    high = jnp.dot(picker, plane[0], preferred_element_type=jnp.float32)
    low = jnp.dot(picker, plane[1], preferred_element_type=jnp.float32)
    return high * 256.0 + low


def scale_of(first):
    lane = iota((1, LANES), 1)
    bits = first.astype(jnp.int32) & 1
    bits = jnp.where(lane < EXPONENT_BITS, bits << jnp.minimum(lane, EXPONENT_BITS - 1), 0)
    exponent = jnp.sum(bits.astype(jnp.float32), axis=1, keepdims=True) - EXPONENT_BIAS
    return jnp.exp2(exponent - 15.0)


def start_rows_kernel(
    buffers, pool, local, depth, me_ref, adapter_ref, mine_ref, other_ref, own_ref, partial_ref, picker_ref
):
    rows, columns = mine_ref.shape
    size = own_ref.shape[0]
    place = to_column(slot_places(adapter_ref[...], me_ref[0], pool, local, depth))
    picker = jnp.where(iota((rows, size), 1) == place, 1.0, 0.0).astype(jnp.bfloat16)
    scale = scale_of(decoded(picker, planes([own_ref], 0, LANES)))
    for at in range(0, columns, 256):
        term = decoded(picker, planes([own_ref], at, 256)) * scale
        partial_ref[:, at : at + 256] = (
            mine_ref[:, at : at + 256] + other_ref[:, at : at + 256] + term
        )
    slots = (buffers - 1) * size
    picker_ref[...] = jnp.where(iota((rows, slots), 1) == place - size, 1.0, 0.0).astype(
        jnp.bfloat16
    )


def finish_kernel(buffers, partial_ref, picker_ref, cos_ref, sin_ref, gain_ref, *refs):
    order = return_order(buffers)
    ins = [refs[order.index(j)] for j in range(1, buffers)]
    out_hbm, entry_ref, out_ref, sems = refs[-4:]
    rows, columns = partial_ref.shape
    head = cos_ref.shape[1]
    kinds = columns // head
    gain, cosine, sine, picker = gain_ref[...], cos_ref[...], sin_ref[...], picker_ref[...]
    scale = scale_of(decoded(picker, planes(ins, 0, LANES)))
    for at in range(0, columns, 2 * head):
        projected = partial_ref[:, at : at + 2 * head]
        projected = projected + decoded(picker, planes(ins, at, 2 * head)) * scale
        key, value = projected[:, :head], projected[:, head:]
        mean = jnp.mean(key * key, axis=1, keepdims=True)
        normed = key * lax.rsqrt(mean + NORM_EPS) * gain
        rotated = normed * cosine + pltpu.roll(normed, head // 2, 1) * sine
        entry_ref[pl.ds(at // head, rows, stride=kinds), :] = rotated
        entry_ref[pl.ds(at // head + 1, rows, stride=kinds), :] = value
    copies = []
    part = rows * kinds // sems.shape[0]
    for i in range(sems.shape[0]):
        done = pl.ds(i * part, part)
        out_ref[done, :] = entry_ref[done, :].astype(jnp.bfloat16)
        copies.append(pltpu.make_async_copy(out_ref.at[done, :], out_hbm.at[done, :], sems.at[i]))
        copies[-1].start()
    for copy in copies:
        copy.wait()


def body(
    tokens,
    row_adapters,
    positions,
    key_value_weight,
    adapter_down,
    adapter_up,
    ranks,
    key_norm_gain,
):
    pool = lax.axis_size("pool")
    groups = lax.axis_size("groups")
    cores = lax.axis_size("tp")
    rows, width = tokens.shape
    local = adapter_down.shape[0]
    adapters = local * pool
    columns = key_value_weight.shape[1] // cores
    rank = adapter_down.shape[2]
    head = key_norm_gain.shape[0]
    depth = max(2, 2 * rows // adapters)
    buffers = pool // 2
    size = 2 * local * depth
    f32, bf16 = jnp.float32, jnp.bfloat16

    me = lax.axis_index("pool").astype(jnp.int32)[None]
    core = lax.axis_index("tp").astype(jnp.int32)[None]
    group = lax.axis_index("groups").astype(jnp.int32)[None]

    def exchange(x, axis, count, j):
        return lax.ppermute(x, axis, [(p, p ^ j) for p in range(count)])

    def hand_round(share):
        return [share] + [exchange(share, "groups", groups, k) for k in range(1, groups)]

    adapter_row = row_adapters.reshape(1, rows)
    down_share = width // groups
    parts = rows // 16
    up_share = columns // groups
    down_part, up_own, adapter_now, tokens_now = pl.pallas_call(
        functools.partial(fetch_kernel, columns),
        in_specs=[SMEM] * 2 + [HBM] * 4,
        out_specs=[VMEM] * 4,
        out_shape=[
            jax.ShapeDtypeStruct((local, down_share, rank), bf16),
            jax.ShapeDtypeStruct((local, rank, up_share), bf16),
            jax.ShapeDtypeStruct((1, rows), jnp.int32),
            jax.ShapeDtypeStruct((rows, width), bf16),
        ],
        scratch_shapes=[pltpu.SemaphoreType.DMA((parts + 3,))],
        compiler_params=params(),
        cost_estimate=cost(0, 4 * (local * rank * down_share + rows * width)),
        name="fetch",
    )(
        group,
        core,
        in_hbm(adapter_down),
        in_hbm(adapter_up),
        in_hbm(adapter_row),
        in_hbm(tokens),
    )
    picked = pl.pallas_call(
        functools.partial(pick_kernel, pool, local, depth),
        in_specs=[SMEM] + [VMEM] * 2,
        out_specs=[VMEM] * buffers,
        out_shape=[jax.ShapeDtypeStruct((size, width), bf16)] * buffers,
        compiler_params=params(),
        cost_estimate=cost(2 * buffers * size * rows * width, 2 * (rows + buffers * size) * width),
        name="pick",
    )(me, adapter_now, tokens_now)
    far_down = exchange(down_part, "pool", pool, pool // 2)
    ranks_now, up_own, _ = lax.optimization_barrier((ranks, up_own, picked))
    up_part, factor = pl.pallas_call(
        scale_up_kernel,
        in_specs=[SMEM, VMEM],
        out_specs=[VMEM] * 2,
        out_shape=[
            jax.ShapeDtypeStruct((local, rank, up_share), bf16),
            jax.ShapeDtypeStruct((local, rank), f32),
        ],
        compiler_params=params(),
        cost_estimate=cost(local * rank * up_share, 4 * local * rank * up_share),
        name="scale_up",
    )(ranks_now, up_own)
    far_up = exchange(up_part, "pool", pool, pool // 2)

    order = far_first(buffers)
    early, late = order[:1], order[1:]
    late_rows, _ = lax.optimization_barrier(([picked[j] for j in late], up_part))
    leaving = [picked[j] for j in early] + late_rows
    arrived = [picked[0]] + [exchange(x, "pool", pool, j) for x, j in zip(leaving, order)]

    steps = 5
    theirs, mine, own_down, own_up = pl.pallas_call(
        base_kernel,
        in_specs=[SMEM] + [HBM] * 4,
        out_specs=[VMEM] * 4,
        out_shape=[jax.ShapeDtypeStruct((rows, columns), f32)] * 2
        + [
            jax.ShapeDtypeStruct(adapter_down.shape, bf16),
            jax.ShapeDtypeStruct((local, rank, columns), bf16),
        ],
        scratch_shapes=[
            pltpu.VMEM((rows, width), bf16),
            pltpu.VMEM((2, width, columns), bf16),
            pltpu.SemaphoreType.DMA((3,)),
            pltpu.SemaphoreType.DMA((2, steps)),
        ],
        compiler_params=params(),
        cost_estimate=cost(4 * rows * width * columns, 4 * width * columns),
        name="base",
    )(
        core,
        in_hbm(tokens),
        in_hbm(key_value_weight),
        in_hbm(adapter_down),
        in_hbm(adapter_up),
    )
    far_down, theirs = lax.optimization_barrier((far_down, theirs))
    far_downs = hand_round(far_down)
    far_up, _ = lax.optimization_barrier((far_up, far_down))
    far_ups = hand_round(far_up)
    half_dim = head // 2
    frequency = jnp.power(
        f32(ROPE_THETA), -jnp.arange(half_dim, dtype=f32) * (2.0 / head)
    )
    angles = positions.astype(f32)[:, None] * frequency[None, :]
    cosine, sine = jnp.cos(angles), jnp.sin(angles)
    cosine = jnp.concatenate([cosine, cosine], axis=1)
    sine = jnp.concatenate([-sine, sine], axis=1)

    far_up, arrived[1], theirs = lax.optimization_barrier((far_up, arrived[1], theirs))
    other = exchange(theirs, "tp", cores, 1)
    arrived, mine, cosine, sine = lax.optimization_barrier((arrived, mine, cosine, sine))
    slots = buffers * size
    low = pl.pallas_call(
        functools.partial(down_kernel, buffers, groups, local, depth),
        in_specs=[SMEM] + [VMEM] * (1 + buffers + groups),
        out_specs=VMEM,
        out_shape=jax.ShapeDtypeStruct((slots, rank), f32),
        compiler_params=params(),
        cost_estimate=cost(4 * local * slots * rank * width, 2 * (slots + rank) * width),
        name="down",
    )(group, own_down, *arrived, *far_downs)
    low_other = exchange(low, "tp", cores, 1)

    terms = pl.pallas_call(
        functools.partial(up_kernel, buffers, groups, local, depth),
        in_specs=[SMEM] + [VMEM] * (4 + groups),
        out_specs=[VMEM] * buffers,
        out_shape=[jax.ShapeDtypeStruct((size, columns), jnp.int16)] * buffers,
        scratch_shapes=[pltpu.VMEM((slots, columns), f32)],
        compiler_params=params(),
        cost_estimate=cost(8 * local * slots * rank * columns, 2 * slots * columns),
        name="up",
    )(group, low, low_other, factor, own_up, *far_ups)
    order = return_order(buffers)
    returned = [exchange(terms[j], "pool", pool, j) for j in order]

    partial, picker = pl.pallas_call(
        functools.partial(start_rows_kernel, buffers, pool, local, depth),
        in_specs=[SMEM] + [VMEM] * 4,
        out_specs=[VMEM] * 2,
        out_shape=[
            jax.ShapeDtypeStruct((rows, columns), f32),
            jax.ShapeDtypeStruct((rows, slots - size), bf16),
        ],
        compiler_params=params(),
        cost_estimate=cost(4 * rows * size * columns, 12 * rows * columns),
        name="start_rows",
    )(me, adapter_row, mine, other, terms[0])
    out = pl.pallas_call(
        functools.partial(finish_kernel, buffers),
        in_specs=[VMEM] * (4 + buffers),
        out_specs=HBM,
        out_shape=jax.ShapeDtypeStruct((rows * columns // head, head), bf16),
        scratch_shapes=[
            pltpu.VMEM((rows * columns // head, head), f32),
            pltpu.VMEM((rows * columns // head, head), bf16),
            pltpu.SemaphoreType.DMA((4,)),
        ],
        compiler_params=params(),
        cost_estimate=cost(4 * rows * slots * columns, 2 * slots * columns),
        name="finish",
    )(partial, picker, cosine, sine, key_norm_gain.astype(f32)[None, :], *returned)
    return out.reshape(rows, columns // (2 * head), 2, head)


def solution(mesh):
    return jax.shard_map(
        body,
        mesh=mesh,
        in_specs=(
            P(("groups", "pool"), "tp"),
            P(("groups", "pool"), None),
            P(("groups", "pool")),
            P("tp", None),
            P("pool", "tp", None),
            P("pool", None, None),
            P("pool"),
            P(),
        ),
        out_specs=P(("groups", "pool"), "tp", None, None),
        check_vma=False,
    )
```
